512 devices in a mesh: fine: 128 (over z_hi, y, x, core), sub: 4 (over z_lo).
Axes of the slice: x: 4, y: 8, z: 8 (z_hi: 2, z_lo: 4; z = z_hi * 4 + z_lo), core: 2. Of those that a mesh axis runs over, the one named last changes fastest.
Arguments:
- rhs: float32 [1024, 128, 128], P('fine', 'sub'), may hold values from -6 to 6
- density: float32 [1024, 128, 128], P('fine', 'sub'), may hold values from 0.2 to 5
Outputs:
- solution: float32 [1024, 128, 128], P('fine', 'sub')
- residual: float32 [1024, 128, 128], P('fine', 'sub')
The draws below stay inside these ranges and needn't reach their ends.
All inputs are finite; a program needn't handle non-finite values.
Results may differ from the reference program's by a relative error of at most 0.00014.
Values sent between devices are 32-bit elements; how exact they have to be, the bound alone decides.
A program may use at most 64 MiB of HBM per device.

```python
import math
from functools import partial
import jax
import jax.numpy as jnp

NY = 128
DEGREE = 4
CYCLES = 2
NZ = 1024
NX = 128


def draw_rhs(key, part):
    key = jax.random.fold_in(key, 7)
    values = jnp.clip(jax.random.normal(key, (NZ, NX, NY), jnp.float32), -6.0, 6.0)
    return values


def block_scale(rng, shape, cuts, least, largest):
    loudness = 1.0
    for axis_at, parts in cuts:
        draws = jax.random.uniform(jax.random.fold_in(jax.random.fold_in(rng, 6), axis_at), (parts,), jnp.float32, least / len(cuts), largest / len(cuts))
        loudness = loudness * jnp.repeat(jnp.exp(draws), shape[axis_at] // parts).reshape((-1,) + (1,) * (len(shape) - 1 - axis_at))
    return loudness


def setup_inputs(seed: int = 0) -> dict:
    key_of = jax.random.split(jax.random.key(seed), 3)
    rhs = draw_rhs(jax.random.fold_in(key_of[2], 71), 0)
    density = jnp.clip(jnp.exp(math.log(5.0) - 3.218876 * jax.random.uniform(key_of[1], (NZ, NX, NY), jnp.float32) ** block_scale(key_of[1], (NZ, NX, NY), ((0, 128), (1, 4)), -0.2, 0.2)), 0.2, 5.0)
    return {"rhs": rhs, "density": density}


def restrict(field):
    depth, rows, cols = field.shape
    blocks = field.reshape(depth // 2, 2, rows // 2, 2, cols // 2, 2)
    return jnp.sum(blocks, axis=(1, 3, 5)) * 0.125


def prolong(field):
    return jnp.repeat(jnp.repeat(jnp.repeat(field, 2, axis=0), 2, axis=1), 2, axis=2)


def face_terms(padded, scale):
    face_z = scale * 2.0 / (padded[1:, 1:-1, 1:-1] + padded[:-1, 1:-1, 1:-1])
    face_x = scale * 2.0 / (padded[1:-1, 1:, 1:-1] + padded[1:-1, :-1, 1:-1])
    face_y = scale * 2.0 / (padded[1:-1, 1:-1, 1:] + padded[1:-1, 1:-1, :-1])
    diagonal = face_z[1:] + face_z[:-1] + face_x[:, 1:] + face_x[:, :-1] + face_y[:, :, 1:] + face_y[:, :, :-1]
    return face_z, face_x, face_y, diagonal, 1.0 / diagonal


def stencil(padded, terms):
    face_z, face_x, face_y, diagonal, inverse = terms
    result = diagonal * padded[1:-1, 1:-1, 1:-1]
    result = result - face_z[1:] * padded[2:, 1:-1, 1:-1] - face_z[:-1] * padded[:-2, 1:-1, 1:-1]
    result = result - face_x[:, 1:] * padded[1:-1, 2:, 1:-1] - face_x[:, :-1] * padded[1:-1, :-2, 1:-1]
    result = result - face_y[:, :, 1:] * padded[1:-1, 1:-1, 2:] - face_y[:, :, :-1] * padded[1:-1, 1:-1, :-2]
    return result


def chebyshev(source, operate, terms, lower):
    upper = 2.0
    theta = 0.5 * (upper + lower)
    delta = 0.5 * (upper - lower)
    sigma = theta / delta
    ratio = 1.0 / sigma
    inverse = terms[4]
    remain = source
    update = source * inverse / theta
    answer = update
    for sweep in range(DEGREE - 1):
        remain = remain - operate(update)
        next_ratio = 1.0 / (2.0 * sigma - ratio)
        update = (next_ratio * ratio) * update + (2.0 * next_ratio / delta) * (remain * inverse)
        answer = answer + update
        ratio = next_ratio
    return answer


def apply_level(field, level, all_terms):
    return stencil(jnp.pad(field, 1), all_terms[level])


def reference(rhs, density):
    densities = [density]
    for level in range(1, 6):
        densities.append(restrict(densities[-1]))
    all_terms = [face_terms(jnp.pad(densities[level], 1), 0.25 ** level) for level in range(6)]
    solution = jnp.zeros_like(rhs)
    for cycle in range(CYCLES):
        if cycle == 0:
            source = rhs
        else:
            source = rhs - apply_level(solution, 0, all_terms)
        residuals = [source]
        for level in range(1, 6):
            residuals.append(restrict(residuals[-1]))
        offset = jnp.sum(residuals[5]) / jnp.sum(all_terms[5][3])
        correction = chebyshev(residuals[5], partial(apply_level, level=5, all_terms=all_terms), all_terms[5], 0.05) + offset
        for level in range(4, -1, -1):
            smoothed = chebyshev(residuals[level], partial(apply_level, level=level, all_terms=all_terms), all_terms[level], 0.5)
            correction = smoothed + prolong(correction)
        solution = solution + 0.4 * correction
    residual = rhs - apply_level(solution, 0, all_terms)
    return solution, residual
```

```python
import functools

import jax
import jax.numpy as jnp
from jax import lax
from jax.experimental import pallas as pl
from jax.experimental.pallas import tpu as pltpu
from jax.sharding import PartitionSpec as P

DEGREE = 4
CYCLES = 2
MESH = pl.DeviceIdType.MESH
HIGHEST = lax.Precision.HIGHEST
F32 = jnp.float32
ROW = 8
PLANES = (8, 4, 2)
ROWS = (32, 16, 8)


def chebyshev_constants(lower):
    upper = 2.0
    theta = 0.5 * (upper + lower)
    delta = 0.5 * (upper - lower)
    sigma = theta / delta
    ratio = 1.0 / sigma
    steps = []
    for _ in range(DEGREE - 1):
        next_ratio = 1.0 / (2.0 * sigma - ratio)
        steps.append((next_ratio * ratio, 2.0 * next_ratio / delta))
        ratio = next_ratio
    return 1.0 / theta, steps


def iota(shape, dim):
    return lax.broadcasted_iota(jnp.int32, shape, dim)


def roll(value, shift, axis):
    return pltpu.roll(value, shift % value.shape[axis], axis)


def matmul(left, right):
    return jnp.dot(left, right, precision=HIGHEST, preferred_element_type=F32)


def one_hot(condition):
    return jnp.where(condition, 1.0, 0.0).astype(F32)


def restrict_block(source, first, planes, rows, stride, work):
    field = source[first : first + planes, 0:rows, :]
    field = field.reshape(planes // 2, 2, rows, 128)
    work[0 : planes // 2, 0:rows, :] = field[:, 0] + field[:, 1]
    half = rows // 2
    both = (
        work[0 : planes // 2, pl.ds(0, half, stride=2), :]
        + work[0 : planes // 2, pl.ds(1, half, stride=2), :]
    )
    lane = iota(both.shape, 2)
    even = (lane // stride) % 2 == 0
    other = jnp.where(even, roll(both, -stride, 2), roll(both, stride, 2))
    return (both + other) * 0.125


def fine_coefficients(level, dens, coef):
    own = ROWS[level]
    scale = 2.0 * 0.25**level
    stride = 2**level
    planes = PLANES[level] + 8
    face_z, face_x, face_y, diagonal, inverse = coef
    shape = (own + 16, 128)

    def compress(value):
        tail = jnp.where(
            iota((8, 128), 0) < 4, value[own : own + 8], value[own + 8 : own + 16]
        )
        return jnp.concatenate([value[0:own], tail], axis=0)

    def plane(p, carry):
        here = dens[p + 1]
        above = dens[p + 2]
        below = dens[p]
        lane = iota(shape, 1)
        right = roll(here, -1, 0)
        up = scale / jnp.maximum(here + above, 0.1)
        down = scale / jnp.maximum(here + below, 0.1)
        x_face = scale / jnp.maximum(here + right, 0.1)
        ahead = jnp.where(lane >= 128 - stride, 0.0, roll(here, -stride, 1))
        behind = jnp.where(lane < stride, 0.0, roll(here, stride, 1))
        y_face = scale / jnp.maximum(here + ahead, 0.1)
        y_back = scale / jnp.maximum(here + behind, 0.1)
        diag = up + down + x_face + roll(x_face, 1, 0) + y_face + y_back
        inside = here > 0.0
        face_z[p] = compress(jnp.where(inside & (above > 0.0), up, 0.0))
        face_x[p] = compress(jnp.where(inside & (right > 0.0), x_face, 0.0))
        face_y[p] = compress(jnp.where(lane >= 128 - stride, 0.0, y_face))
        diagonal[p] = compress(diag)
        inverse[p] = compress(1.0 / diag)
        return carry

    lax.fori_loop(0, planes, plane, 0)


def fine_apply(field, p, coef, q, stride):
    face_z, face_x, face_y, diagonal, _ = coef
    here = field[p]
    x_face = face_x[q]
    y_face = face_y[q]
    result = diagonal[q] * here
    result = result - face_z[q] * field[p + 1] - face_z[q - 1] * field[p - 1]
    result = result - x_face * roll(here, -1, 0) - roll(x_face * here, 1, 0)
    result = result - y_face * roll(here, -stride, 1) - roll(y_face * here, stride, 1)
    return result


def fine_smooth(level, source, coef, remain, updates, answer):
    planes = PLANES[level] + 8
    stride = 2**level
    inverse = coef[4]
    first, steps = chebyshev_constants(0.5)
    d0, d1, d2 = updates

    def start(p, carry):
        d0[p] = source[p] * inverse[p] * first
        return carry

    lax.fori_loop(0, planes, start, 0)
    chain = (d0, d1, d2)
    for sweep in range(3):
        old = chain[sweep]
        keep, add = steps[sweep]

        def step(p, carry, sweep=sweep, old=old, keep=keep, add=add):
            left = source[p] if sweep == 0 else remain[p]
            left = left - fine_apply(old, p, coef, p, stride)
            new = keep * old[p] + add * (left * inverse[p])
            if sweep < 2:
                remain[p] = left
                chain[sweep + 1][p] = new
            else:
                answer[p] = d0[p] + d1[p] + d2[p] + new
            return carry

        lax.fori_loop(sweep + 1, planes - sweep - 1, step, 0)


def packed_coefficients(dens, ny, nx, scale):
    rows = dens.shape[0]
    z = iota(dens.shape, 0)
    lane = iota(dens.shape, 1)
    y = lane % ny
    x = lane // ny
    scale = 2.0 * scale

    def neighbour(shift, axis, outside):
        return jnp.where(outside, 0.0, roll(dens, shift, axis))

    above = neighbour(-1, 0, z == rows - 1)
    below = neighbour(1, 0, z == 0)
    right = neighbour(-ny, 1, x >= nx - 1)
    left = neighbour(ny, 1, x == 0)
    ahead = neighbour(-1, 1, y == ny - 1)
    behind = neighbour(1, 1, y == 0)

    def face(other):
        return scale / jnp.maximum(dens + other, 0.1)

    up, x_face, y_face = face(above), face(right), face(ahead)
    diagonal = up + face(below) + x_face + face(left) + y_face + face(behind)
    inside = dens > 0.0

    def inner(value, other):
        return jnp.where(inside & (other > 0.0), value, 0.0)

    return (
        inner(up, above),
        inner(x_face, right),
        inner(y_face, ahead),
        jnp.where(inside, diagonal, 0.0),
        jnp.where(inside, 1.0 / diagonal, 0.0),
    )


def packed_apply(field, coef, ny):
    face_z, face_x, face_y, diagonal, _ = coef
    result = diagonal * field
    result = result - face_z * roll(field, -1, 0) - roll(face_z * field, 1, 0)
    result = result - face_x * roll(field, -ny, 1) - roll(face_x * field, ny, 1)
    result = result - face_y * roll(field, -1, 1) - roll(face_y * field, 1, 1)
    return result


def packed_smooth(source, coef, ny, lower):
    first, steps = chebyshev_constants(lower)
    inverse = coef[4]
    update = source * inverse * first
    answer = update
    for keep, add in steps:
        source = source - packed_apply(update, coef, ny)
        update = keep * update + add * (source * inverse)
        answer = answer + update
    return answer


def halo_pieces(with_density):
    up = {1: [], 2: [], 3: []}
    down = {1: [], 2: [], 3: []}
    if with_density:
        up[1] += [("D0", 8, 0, 5), ("D1", 5, 1, 4), ("D2", 5, 3, 2)]
        down[1] += [("D0", 5, 13, 5), ("D1", 5, 9, 4), ("D2", 5, 7, 2)]
        up[2] += [("D1", 8, 0, 1), ("D2", 5, 1, 2)]
        down[2] += [("D1", 5, 13, 1), ("D2", 5, 9, 2)]
        up[3] += [("D2", 6, 0, 1)]
        down[3] += [("D2", 5, 11, 1)]
    up[1] += [("R0", 8, 0, 4), ("R1", 4, 0, 4), ("R2", 4, 2, 2)]
    down[1] += [("R0", 4, 12, 4), ("R1", 4, 8, 4), ("R2", 4, 6, 2)]
    up[2] += [("R2", 4, 0, 2)]
    down[2] += [("R2", 4, 8, 2)]
    return up, down


def part_rows(name, part):
    own = ROWS[int(name[1])]
    if part == "a":
        return 0, own
    return (own, own + 16) if name[0] == "D" else (own, own + 8)


def z_messages(with_density):
    up, down = halo_pieces(with_density)
    result = []
    for part in "ab":
        for distance in (1, 2, 3):
            for shift, pieces in ((distance, up[distance]), (-distance, down[distance])):
                if pieces:
                    result.append((part, shift, pieces))
    return result


def tiles_of(part, pieces):
    total = 0
    for name, _, _, count in pieces:
        low, high = part_rows(name, part)
        total += count * (high - low) // 8
    return total


def x_tiles(with_density):
    return sum(PLANES) * (2 if with_density else 1)


def buffer_shapes(with_density):
    tiles = [x_tiles(with_density)] * 2
    tiles += [tiles_of(part, pieces) for part, _, pieces in z_messages(with_density)]
    shapes = [pltpu.VMEM((count, 8, 128), F32) for count in tiles]
    return shapes


def n_halo(with_density):
    return 2 + len(z_messages(with_density))


class Phase:
    def __init__(self, refs, place, with_density, send, recv, coarse, send_sem, recv_sem):
        self.refs = refs
        self.k, self.s, self.nf, self.ns = place
        self.dense = with_density
        self.send, self.recv = send, recv
        self.row, self.row_in, self.sub_in, self.group, self.low, self.high, self.quad_in = coarse
        self.send_sem, self.recv_sem = send_sem, recv_sem
        self.started = []
        self.count = 0
        self.z = z_messages(with_density)
        self.i = self.k % ROW
        self.g = self.k // ROW
        self.ng = self.nf // ROW

    def start(self, source, target, k, s):
        index = self.count
        self.count += 1
        copy = pltpu.make_async_remote_copy(
            src_ref=source,
            dst_ref=target,
            send_sem=self.send_sem.at[index],
            recv_sem=self.recv_sem.at[index],
            device_id=(k, s),
            device_id_type=MESH,
        )
        copy.start()
        self.started.append(copy)
        return copy

    def pack_x(self):
        for which in (0, 1):
            at = 0
            for name in ("D", "R") if self.dense else ("R",):
                for level in range(3):
                    ref = self.refs[name + str(level)]
                    lead = 5 if name == "D" else 4
                    row = ROWS[level] - 8 if which == 0 else 0
                    count = PLANES[level]
                    self.send[which][at : at + count] = ref[
                        lead : lead + count, row : row + 8, :
                    ]
                    at += count

    def pack_z(self, part):
        for index, (kind, _, pieces) in enumerate(self.z):
            if kind != part:
                continue
            at = 0
            for name, source, _, count in pieces:
                low, high = part_rows(name, part)
                tiles = count * (high - low) // 8
                block = self.refs[name][source : source + count, low:high, :]
                self.send[2 + index][at : at + tiles] = block.reshape(tiles, 8, 128)
                at += tiles

    def start_x(self):
        up, down = (self.s + 1) % self.ns, (self.s + self.ns - 1) % self.ns
        self.x_copies = [
            self.start(self.send[0], self.recv[0], self.k, up),
            self.start(self.send[1], self.recv[1], self.k, down),
        ]

    def start_z(self, part):
        copies = []
        for index, (kind, shift, _) in enumerate(self.z):
            if kind == part:
                target = (self.k + shift + self.nf) % self.nf
                copies.append(
                    (index, self.start(self.send[2 + index], self.recv[2 + index], target, self.s))
                )
        return copies

    def unpack_x(self):
        for copy in self.x_copies:
            copy.wait_recv()
        low_in = jnp.where(self.s > 0, 1.0, 0.0).astype(F32)
        high_in = jnp.where(self.s < self.ns - 1, 1.0, 0.0).astype(F32)
        at = 0
        if self.dense:
            for level in range(3):
                ref, own, count = self.refs["D" + str(level)], ROWS[level], PLANES[level]
                ref[5 : 5 + count, own : own + 8, :] = self.recv[1][at : at + count] * high_in
                ref[5 : 5 + count, own + 8 : own + 16, :] = self.recv[0][at : at + count] * low_in
                at += count
        for level in range(3):
            ref, own, count = self.refs["R" + str(level)], ROWS[level], PLANES[level]
            first = iota((count, 8, 128), 1) < 4
            ref[4 : 4 + count, own : own + 8, :] = jnp.where(
                first, self.recv[1][at : at + count], self.recv[0][at : at + count]
            )
            at += count

    def unpack_z(self, copies):
        for index, copy in copies:
            part, shift, pieces = self.z[index]
            copy.wait_recv()
            if shift > 0:
                inside = self.k >= shift
            else:
                inside = self.k < self.nf + shift
            factor = jnp.where(inside, 1.0, 0.0).astype(F32)
            at = 0
            for name, _, target, count in pieces:
                low, high = part_rows(name, part)
                tiles = count * (high - low) // 8
                block = self.recv[2 + index][at : at + tiles]
                if name[0] == "D":
                    block = block * factor
                self.refs[name][target : target + count, low:high, :] = block.reshape(
                    count, high - low, 128
                )
                at += tiles

    def pack_row(self, pair):
        line, lane = iota((128, 128), 0), iota((128, 128), 1)
        spread = matmul(pair[...], one_hot(line == 8 * (lane % 16)))
        mine = iota((8, 128), 1) // 16 == iota((8, 128), 0)
        row = jnp.sum(jnp.where(mine, spread, 0.0), axis=0, keepdims=True)
        self.row[...] = row
        self.row_in[self.i] = row

    def start_rows(self):
        self.row_copies = []
        for delta in range(1, ROW):
            target = self.g * ROW + (self.i + delta) % ROW
            self.row_copies.append(
                self.start(self.row, self.row_in.at[self.i], target, self.s)
            )

    def start_subs(self):
        for copy in self.row_copies:
            copy.wait_recv()
        line = iota((8, 128), 0)
        tile = jnp.zeros((8, 128), F32)
        for index in range(ROW):
            tile = jnp.where(line == index, self.row_in[index], tile)
        self.sub_in[self.s] = tile
        self.sub_copies = []
        for delta in range(1, 4):
            self.sub_copies.append(
                self.start(
                    self.sub_in.at[self.s],
                    self.sub_in.at[self.s],
                    self.k,
                    (self.s + delta) % self.ns,
                )
            )

    def start_groups(self, work):
        for copy in self.sub_copies:
            copy.wait_recv()
        tiles = [self.sub_in[index] for index in range(4)]
        turned = [roll(tile, 64, 1) for tile in tiles]
        left = iota((8, 128), 1) < 64
        for half in range(2):
            a, b = 2 * half, 2 * half + 1
            self.group[half] = jnp.where(left, tiles[a], turned[b])
            if self.dense:
                self.group[2 + half] = jnp.where(left, turned[a], tiles[b])
        quads = jnp.zeros((8, 128), F32)
        for half in range(4 if self.dense else 2):
            line, lane = iota((128, 128), 0), iota((128, 128), 1)
            x, y = line // 16 + 8 * (half % 2), line % 16
            home = (x // 2) * 8 + y // 2 + 64 * (half // 2)
            quads = quads + matmul(self.group[half], one_hot(home == lane))
        work[...] = quads
        four = (work[pl.ds(0, 4, stride=2), :] + work[pl.ds(1, 4, stride=2), :]) * 0.125
        self.quad_in[self.g, 0:4, :] = four
        self.quad_in[self.g, 4:8, :] = four
        up = ((self.g + 1) % self.ng) * ROW + self.i
        down = ((self.g + self.ng - 1) % self.ng) * ROW + self.i
        self.group_copies = [
            self.start(self.group, self.low, up, self.s),
            self.start(self.group, self.high, down, self.s),
        ]
        for delta in range(1, self.ng):
            target = ((self.g + delta) % self.ng) * ROW + self.i
            self.group_copies.append(
                self.start(
                    self.quad_in.at[self.g], self.quad_in.at[self.g], target, self.s
                )
            )

    def wait_groups(self):
        for copy in self.group_copies:
            copy.wait_recv()

    def finish(self):
        for copy in self.started:
            copy.wait_send()


def split_packed(value):
    left = iota(value.shape, 1) < 64
    return jnp.where(left, value, 0.0), jnp.where(left, roll(value, 64, 1), 0.0)


def kernel(nf, ns, rhs, density, solution, residual, *scratch):
    scratch = list(scratch)

    def take(count):
        taken = scratch[:count]
        del scratch[:count]
        return taken

    refs = {}
    for name in ("D0", "D1", "D2", "R0", "R1", "R2"):
        (refs[name],) = take(1)
    fine_coef = [take(5) for _ in range(3)]
    remains = take(3)
    updates = [take(3) for _ in range(3)]
    answers = take(3)
    (work, tile_work, pair, sol, spread, level4, level5, dens3, dens4, dens5) = take(10)
    phases = []
    k, s = lax.axis_index("fine"), lax.axis_index("sub")
    for with_density in (True, False):
        count = n_halo(with_density)
        send, recv, coarse = take(count), take(count), take(7)
        send_sem, recv_sem = take(2)
        phases.append(
            Phase(refs, (k, s, nf, ns), with_density, send, recv, coarse, send_sem, recv_sem)
        )
    ng = nf // ROW
    i, g = k % ROW, k // ROW

    barrier = pltpu.get_barrier_semaphore()
    partners = []
    for shift in (1, 2, 3):
        partners += [((k + shift) % nf, s), ((k + nf - shift) % nf, s)]
    partners += [(k, (s + delta) % ns) for delta in range(1, ns)]
    partners += [(g * ROW + (i + delta) % ROW, s) for delta in range(1, ROW)]
    partners += [(((g + delta) % ng) * ROW + i, s) for delta in range(1, ng)]
    for partner in partners:
        pl.semaphore_signal(barrier, inc=1, device_id=partner, device_id_type=MESH)

    def restrict_all(name, lead, first_row):
        for level in range(2):
            refs[name + str(level + 1)][
                lead : lead + PLANES[level + 1], 0 : ROWS[level + 1], :
            ] = restrict_block(
                refs[name + str(level)], lead, PLANES[level], ROWS[level], 2**level, work
            )
        three = restrict_block(refs[name + "2"], lead, PLANES[2], ROWS[2], 4, work)
        pair[first_row : first_row + 4, :] = three.reshape(4, 128)

    refs["R0"][4:12, 0:32, :] = rhs[...]
    refs["D0"][5:13, 0:32, :] = density[...]

    for cycle in range(CYCLES):
        phase = phases[cycle]
        restrict_all("R", 4, 0)
        if cycle == 0:
            restrict_all("D", 5, 4)
        phase.pack_row(pair)
        if cycle == 0:
            pl.semaphore_wait(barrier, len(partners))
        phase.start_rows()
        phase.pack_x()
        phase.start_x()
        phase.pack_z("a")
        a_copies = phase.start_z("a")
        phase.start_subs()
        phase.unpack_x()
        phase.pack_z("b")
        b_copies = phase.start_z("b")
        phase.start_groups(tile_work)
        phase.unpack_z(a_copies)
        phase.unpack_z(b_copies)
        for level in range(3):
            if cycle == 0:
                fine_coefficients(level, refs["D" + str(level)], fine_coef[level])
            fine_smooth(
                level,
                refs["R" + str(level)],
                fine_coef[level],
                remains[level],
                updates[level],
                answers[level],
            )
        phase.wait_groups()

        for tile in range(ng // 2):
            level4[8 * tile : 8 * tile + 8, :] = jnp.where(
                iota((8, 128), 0) < 4, phase.quad_in[2 * tile], phase.quad_in[2 * tile + 1]
            )
        n4, n5 = 4 * ng, 2 * ng
        line, lane = iota((128, 128), 0), iota((128, 128), 1)
        inner = line % 64
        home = (inner // 16) * 4 + (inner % 8) // 2 + 64 * (line // 64)
        pairs5 = level4[pl.ds(0, n5, stride=2), :] + level4[pl.ds(1, n5, stride=2), :]
        packed5 = matmul(pairs5, one_hot(home == lane)) * 0.125
        source4, density4 = split_packed(level4[...])
        source5, density5 = split_packed(packed5)
        low_in = jnp.where(g > 0, 1.0, 0.0).astype(F32)
        high_in = jnp.where(g < ng - 1, 1.0, 0.0).astype(F32)
        if cycle == 0:
            dens4[...] = density4
            dens5[...] = density5
            for half in range(2):
                cols = slice(128 * half, 128 * half + 128)
                dens3[0:8, cols] = phase.low[2 + half] * low_in
                dens3[8:16, cols] = phase.group[2 + half]
                dens3[16:24, cols] = phase.high[2 + half] * high_in
        coef5 = packed_coefficients(dens5[...], 4, 4, 0.25**5)
        total = jnp.sum(jnp.sum(source5, axis=0, keepdims=True), axis=1, keepdims=True)
        weight = jnp.sum(jnp.sum(coef5[3], axis=0, keepdims=True), axis=1, keepdims=True)
        c5 = packed_smooth(source5, coef5, 4, 0.05) + total / weight
        coef4 = packed_coefficients(dens4[...], 8, 8, 0.25**4)
        s4 = packed_smooth(source4, coef4, 8, 0.5)
        up5 = matmul(
            c5, one_hot((line == ((lane // 16) * 4 + (lane % 8) // 2)) & (lane < 64))
        )
        level5[pl.ds(0, n5, stride=2), :] = up5
        level5[pl.ds(1, n5, stride=2), :] = up5
        c4 = s4 + level5[...]

        source3 = jnp.concatenate(
            [
                jnp.concatenate([phase.low[0], phase.low[1]], axis=1),
                jnp.concatenate([phase.group[0], phase.group[1]], axis=1),
                jnp.concatenate([phase.high[0], phase.high[1]], axis=1),
            ],
            axis=0,
        )
        coef3 = packed_coefficients(dens3[...], 16, 16, 0.25**3)
        s3 = packed_smooth(source3, coef3, 16, 0.5)
        near3 = iota((8, 24), 1) == iota((8, 24), 0) + (i + 7)
        near4 = iota((8, n4), 1) == (iota((8, n4), 0) + (k + 1)) // 2 - 1
        wide = iota((128, 256), 1)
        lift = one_hot(iota((128, 256), 0) == (wide // 32) * 8 + (wide % 16) // 2)
        slabs = matmul(one_hot(near3), s3) + matmul(matmul(one_hot(near4), c4), lift)

        row = iota((16, 256), 0)
        x3 = jnp.where(row < 8, 0, jnp.where(row < 12, 0, -8)) + row // 2 + 4 * s
        here = iota((16, 256), 1) // 16 == x3
        picked = jnp.concatenate(
            [jnp.where(here, slabs[t : t + 1, :], 0.0) for t in range(3)], axis=0
        )
        fan = one_hot(iota((256, 128), 0) % 16 == iota((256, 128), 1) // 8)
        spread[0:3, 0:16, :] = matmul(picked, fan).reshape(3, 16, 128)

        for level in (2, 1, 0):
            rows = ROWS[level]
            answer = answers[level]
            planes = PLANES[level] + 2

            def add(p, carry, answer=answer):
                answer[p + 3] = answer[p + 3] + spread[(p + 1) // 2, 0 : answer.shape[1], :]
                return carry

            lax.fori_loop(0, planes, add, 0)
            if level > 0:
                value = answer[3 : 3 + planes, 0:rows, :]
                ends = answer[3 : 3 + planes, rows : rows + 8, :]
                spread[0:planes, pl.ds(0, rows, stride=2), :] = value
                spread[0:planes, pl.ds(1, rows, stride=2), :] = value
                first = iota((planes, 8, 128), 1) < 4
                spread[0:planes, 2 * rows : 2 * rows + 8, :] = jnp.where(
                    first, ends[:, 0:1, :], ends[:, 7:8, :]
                )

        def advance(p, carry, cycle=cycle):
            if cycle == 0:
                sol[p] = 0.4 * answers[0][p + 3]
            else:
                sol[p] = sol[p] + 0.4 * answers[0][p + 3]
            return carry

        lax.fori_loop(0, PLANES[0] + 2, advance, 0)

        def defect(p, carry, cycle=cycle):
            applied = fine_apply(sol, p + 1, fine_coef[0], p + 4, 1)
            left = rhs[p] - applied[0:32, :]
            if cycle == 0:
                refs["R0"][p + 4, 0:32, :] = left
            else:
                residual[p] = left
                solution[p] = sol[p + 1, 0:32, :]
            return carry

        if cycle == 0:
            lax.fori_loop(0, PLANES[0], defect, 0)
        else:
            lax.fori_loop(0, PLANES[0], defect, 0)

    for phase in phases:
        phase.finish()


def scratch_shapes(ng):
    shapes = []
    for level in range(3):
        shapes.append(pltpu.VMEM((PLANES[level] + 10, ROWS[level] + 16, 128), F32))
    extents = [(PLANES[level] + 8, ROWS[level] + 8, 128) for level in range(3)]
    shapes += [pltpu.VMEM(extent, F32) for extent in extents]
    for extent in extents:
        shapes += [pltpu.VMEM(extent, F32)] * 5
    shapes += [pltpu.VMEM(extent, F32) for extent in extents]
    for extent in extents:
        shapes += [pltpu.VMEM(extent, F32)] * 3
    shapes += [pltpu.VMEM(extent, F32) for extent in extents]
    shapes += [
        pltpu.VMEM((4, 32, 128), F32),
        pltpu.VMEM((8, 128), F32),
        pltpu.VMEM((8, 128), F32),
        pltpu.VMEM((10, 40, 128), F32),
        pltpu.VMEM((6, 40, 128), F32),
        pltpu.VMEM((4 * ng, 128), F32),
        pltpu.VMEM((4 * ng, 128), F32),
        pltpu.VMEM((24, 256), F32),
        pltpu.VMEM((4 * ng, 128), F32),
        pltpu.VMEM((2 * ng, 128), F32),
    ]
    for with_density in (True, False):
        halo = buffer_shapes(with_density)
        shapes += halo + halo
        tiles = 4 if with_density else 2
        shapes += [
            pltpu.VMEM((1, 128), F32),
            pltpu.VMEM((ROW, 1, 128), F32),
            pltpu.VMEM((4, 8, 128), F32),
            pltpu.VMEM((tiles, 8, 128), F32),
            pltpu.VMEM((tiles, 8, 128), F32),
            pltpu.VMEM((tiles, 8, 128), F32),
            pltpu.VMEM((ng, 8, 128), F32),
        ]
        copies = n_halo(with_density) + (ROW - 1) + 3 + 2 + (ng - 1)
        shapes += [pltpu.SemaphoreType.DMA((copies,)), pltpu.SemaphoreType.DMA((copies,))]
    return shapes


def solution(mesh):
    nf, ns = mesh.shape["fine"], mesh.shape["sub"]

    def body(rhs, density):
        return pl.pallas_call(
            functools.partial(kernel, nf, ns),
            out_shape=(
                jax.ShapeDtypeStruct(rhs.shape, F32),
                jax.ShapeDtypeStruct(rhs.shape, F32),
            ),
            in_specs=[pl.BlockSpec(memory_space=pltpu.VMEM)] * 2,
            out_specs=[pl.BlockSpec(memory_space=pltpu.VMEM)] * 2,
            scratch_shapes=scratch_shapes(nf // ROW),
            compiler_params=pltpu.CompilerParams(
                collective_id=0, has_side_effects=True, vmem_limit_bytes=32 * 1024 * 1024
            ),
        )(rhs, density)

    return jax.shard_map(
        body,
        mesh=mesh,
        in_specs=(P("fine", "sub", None), P("fine", "sub", None)),
        out_specs=(P("fine", "sub", None), P("fine", "sub", None)),
        check_vma=False,
    )
```

```python
import functools

import jax
import jax.numpy as jnp
from jax import lax
from jax.experimental import pallas as pl
from jax.experimental.pallas import tpu as pltpu
from jax.sharding import PartitionSpec as P

DEGREE = 4
CYCLES = 2
MESH = pl.DeviceIdType.MESH
HIGHEST = lax.Precision.HIGHEST
F32 = jnp.float32
ROW = 8
PLANES = (8, 4, 2)
ROWS = (32, 16, 8)


def chebyshev_constants(lower):
    upper = 2.0
    theta = 0.5 * (upper + lower)
    delta = 0.5 * (upper - lower)
    sigma = theta / delta
    ratio = 1.0 / sigma
    steps = []
    for _ in range(DEGREE - 1):
        next_ratio = 1.0 / (2.0 * sigma - ratio)
        steps.append((next_ratio * ratio, 2.0 * next_ratio / delta))
        ratio = next_ratio
    return 1.0 / theta, steps


def iota(shape, dim):
    return lax.broadcasted_iota(jnp.int32, shape, dim)


def roll(value, shift, axis):
    return pltpu.roll(value, shift % value.shape[axis], axis)


def matmul(left, right):
    return jnp.dot(left, right, precision=HIGHEST, preferred_element_type=F32)


def invert(value):
    return pltpu.reciprocal(value, full_range=False)


def one_hot(condition):
    return jnp.where(condition, 1.0, 0.0).astype(F32)


def restrict_block(source, first, planes, rows, stride, work):
    field = source[first : first + planes, 0:rows, :]
    field = field.reshape(planes // 2, 2, rows, 128)
    work[0 : planes // 2, 0:rows, :] = field[:, 0] + field[:, 1]
    half = rows // 2
    both = (
        work[0 : planes // 2, pl.ds(0, half, stride=2), :]
        + work[0 : planes // 2, pl.ds(1, half, stride=2), :]
    )
    lane = iota(both.shape, 2)
    even = (lane // stride) % 2 == 0
    other = jnp.where(even, roll(both, -stride, 2), roll(both, stride, 2))
    return (both + other) * 0.125


def fine_coefficients(level, dens, coef):
    own = ROWS[level]
    scale = 2.0 * 0.25**level
    stride = 2**level
    planes = PLANES[level] + 8
    face_z, face_x, face_y, diagonal, inverse = coef
    shape = (own + 16, 128)

    def compress(value):
        tail = jnp.where(
            iota((8, 128), 0) < 4, value[own : own + 8], value[own + 8 : own + 16]
        )
        return jnp.concatenate([value[0:own], tail], axis=0)

    def plane(p, down):
        here = dens[p + 1]
        above = dens[p + 2]
        lane = iota(shape, 1)
        right = roll(here, -1, 0)
        up = scale * invert(jnp.maximum(here + above, 0.1))
        x_face = scale * invert(jnp.maximum(here + right, 0.1))
        ahead = jnp.where(lane >= 128 - stride, 0.0, roll(here, -stride, 1))
        behind = jnp.where(lane < stride, 0.0, roll(here, stride, 1))
        y_face = scale * invert(jnp.maximum(here + ahead, 0.1))
        y_back = scale * invert(jnp.maximum(here + behind, 0.1))
        diag = up + down + x_face + roll(x_face, 1, 0) + y_face + y_back
        inside = here > 0.0
        face_z[p] = compress(jnp.where(inside & (above > 0.0), up, 0.0))
        face_x[p] = compress(jnp.where(inside & (right > 0.0), x_face, 0.0))
        face_y[p] = compress(jnp.where(lane >= 128 - stride, 0.0, y_face))
        diagonal[p] = compress(diag)
        inverse[p] = compress(invert(diag))
        return up

    lowest = scale * invert(jnp.maximum(dens[0] + dens[1], 0.1))
    lax.fori_loop(0, planes, plane, lowest, unroll=True)


def fine_apply(field, p, coef, q, stride):
    face_z, face_x, face_y, diagonal, _ = coef
    here = field[p]
    x_face = face_x[q]
    y_face = face_y[q]
    result = diagonal[q] * here
    result = result - face_z[q] * field[p + 1] - face_z[q - 1] * field[p - 1]
    result = result - x_face * roll(here, -1, 0) - roll(x_face * here, 1, 0)
    result = result - y_face * roll(here, -stride, 1) - roll(y_face * here, stride, 1)
    return result


def fine_smooth(level, source, coef, remain, updates, answer):
    planes = PLANES[level] + 8
    stride = 2**level
    inverse = coef[4]
    first, steps = chebyshev_constants(0.5)
    d0, d1, d2 = updates

    def start(p, carry):
        d0[p] = source[p] * inverse[p] * first
        return carry

    lax.fori_loop(0, planes, start, 0, unroll=True)
    chain = (d0, d1, d2)
    for sweep in range(3):
        old = chain[sweep]
        keep, add = steps[sweep]

        def step(p, carry, sweep=sweep, old=old, keep=keep, add=add):
            left = source[p] if sweep == 0 else remain[p]
            left = left - fine_apply(old, p, coef, p, stride)
            new = keep * old[p] + add * (left * inverse[p])
            if sweep < 2:
                remain[p] = left
                chain[sweep + 1][p] = new
            else:
                answer[p] = d0[p] + d1[p] + d2[p] + new
            return carry

        lax.fori_loop(sweep + 1, planes - sweep - 1, step, 0, unroll=True)


def packed_coefficients(dens, ny, nx, scale):
    rows = dens.shape[0]
    z = iota(dens.shape, 0)
    lane = iota(dens.shape, 1)
    y = lane % ny
    x = lane // ny
    scale = 2.0 * scale

    def neighbour(shift, axis, outside):
        return jnp.where(outside, 0.0, roll(dens, shift, axis))

    above = neighbour(-1, 0, z == rows - 1)
    below = neighbour(1, 0, z == 0)
    right = neighbour(-ny, 1, x >= nx - 1)
    left = neighbour(ny, 1, x == 0)
    ahead = neighbour(-1, 1, y == ny - 1)
    behind = neighbour(1, 1, y == 0)

    def face(other):
        return scale * invert(jnp.maximum(dens + other, 0.1))

    up, x_face, y_face = face(above), face(right), face(ahead)
    diagonal = up + face(below) + x_face + face(left) + y_face + face(behind)
    inside = dens > 0.0

    def inner(value, other):
        return jnp.where(inside & (other > 0.0), value, 0.0)

    return (
        inner(up, above),
        inner(x_face, right),
        inner(y_face, ahead),
        jnp.where(inside, diagonal, 0.0),
        jnp.where(inside, invert(diagonal), 0.0),
    )


def packed_apply(field, coef, ny):
    face_z, face_x, face_y, diagonal, _ = coef
    result = diagonal * field
    result = result - face_z * roll(field, -1, 0) - roll(face_z * field, 1, 0)
    result = result - face_x * roll(field, -ny, 1) - roll(face_x * field, ny, 1)
    result = result - face_y * roll(field, -1, 1) - roll(face_y * field, 1, 1)
    return result


def packed_smooth(source, coef, ny, lower):
    first, steps = chebyshev_constants(lower)
    inverse = coef[4]
    update = source * inverse * first
    answer = update
    for keep, add in steps:
        source = source - packed_apply(update, coef, ny)
        update = keep * update + add * (source * inverse)
        answer = answer + update
    return answer


def halo_pieces(with_density):
    up = {1: [], 2: [], 3: []}
    down = {1: [], 2: [], 3: []}
    if with_density:
        up[1] += [("D0", 8, 0, 5), ("D1", 5, 1, 4), ("D2", 5, 3, 2)]
        down[1] += [("D0", 5, 13, 5), ("D1", 5, 9, 4), ("D2", 5, 7, 2)]
        up[2] += [("D1", 8, 0, 1), ("D2", 5, 1, 2)]
        down[2] += [("D1", 5, 13, 1), ("D2", 5, 9, 2)]
        up[3] += [("D2", 6, 0, 1)]
        down[3] += [("D2", 5, 11, 1)]
    up[1] += [("R0", 8, 0, 4), ("R1", 4, 0, 4), ("R2", 4, 2, 2)]
    down[1] += [("R0", 4, 12, 4), ("R1", 4, 8, 4), ("R2", 4, 6, 2)]
    up[2] += [("R2", 4, 0, 2)]
    down[2] += [("R2", 4, 8, 2)]
    return up, down


def part_rows(name, part):
    own = ROWS[int(name[1])]
    if part == "a":
        return 0, own
    return (own, own + 16) if name[0] == "D" else (own, own + 8)


def z_messages(with_density):
    up, down = halo_pieces(with_density)
    result = []
    for part in "ab":
        for distance in (1, 2, 3):
            for shift, pieces in ((distance, up[distance]), (-distance, down[distance])):
                if pieces:
                    result.append((part, shift, pieces))
    return result


def tiles_of(part, pieces):
    total = 0
    for name, _, _, count in pieces:
        low, high = part_rows(name, part)
        total += count * (high - low) // 8
    return total


def x_tiles(with_density):
    return sum(PLANES) * (2 if with_density else 1)


def buffer_shapes(with_density):
    tiles = [x_tiles(with_density)] * 2
    tiles += [tiles_of(part, pieces) for part, _, pieces in z_messages(with_density)]
    shapes = [pltpu.VMEM((count, 8, 128), F32) for count in tiles]
    return shapes


def n_halo(with_density):
    return 2 + len(z_messages(with_density))


class Phase:
    def __init__(self, refs, place, with_density, send, recv, coarse, send_sem, recv_sem):
        self.refs = refs
        self.k, self.s, self.nf, self.ns = place
        self.dense = with_density
        self.send, self.recv = send, recv
        self.row, self.row_in, self.sub_in, self.group, self.low, self.high, self.quad_in = coarse
        self.send_sem, self.recv_sem = send_sem, recv_sem
        self.started = []
        self.count = 0
        self.z = z_messages(with_density)
        self.i = self.k % ROW
        self.g = self.k // ROW
        self.ng = self.nf // ROW

    def start(self, source, target, k, s):
        index = self.count
        self.count += 1
        copy = pltpu.make_async_remote_copy(
            src_ref=source,
            dst_ref=target,
            send_sem=self.send_sem.at[index],
            recv_sem=self.recv_sem.at[index],
            device_id=(k, s),
            device_id_type=MESH,
        )
        copy.start()
        self.started.append(copy)
        return copy

    def pack_x(self):
        for which in (0, 1):
            at = 0
            for name in ("D", "R") if self.dense else ("R",):
                for level in range(3):
                    ref = self.refs[name + str(level)]
                    lead = 5 if name == "D" else 4
                    row = ROWS[level] - 8 if which == 0 else 0
                    count = PLANES[level]
                    self.send[which][at : at + count] = ref[
                        lead : lead + count, row : row + 8, :
                    ]
                    at += count

    def pack_z(self, part):
        for index, (kind, _, pieces) in enumerate(self.z):
            if kind != part:
                continue
            at = 0
            for name, source, _, count in pieces:
                low, high = part_rows(name, part)
                tiles = count * (high - low) // 8
                block = self.refs[name][source : source + count, low:high, :]
                self.send[2 + index][at : at + tiles] = block.reshape(tiles, 8, 128)
                at += tiles

    def start_x(self):
        up, down = (self.s + 1) % self.ns, (self.s + self.ns - 1) % self.ns
        self.x_copies = [
            self.start(self.send[0], self.recv[0], self.k, up),
            self.start(self.send[1], self.recv[1], self.k, down),
        ]

    def start_z(self, part):
        copies = []
        for index, (kind, shift, _) in enumerate(self.z):
            if kind == part:
                target = (self.k + shift + self.nf) % self.nf
                copies.append(
                    (index, self.start(self.send[2 + index], self.recv[2 + index], target, self.s))
                )
        return copies

    def unpack_x(self):
        for copy in self.x_copies:
            copy.wait_recv()
        low_in = jnp.where(self.s > 0, 1.0, 0.0).astype(F32)
        high_in = jnp.where(self.s < self.ns - 1, 1.0, 0.0).astype(F32)
        at = 0
        if self.dense:
            for level in range(3):
                ref, own, count = self.refs["D" + str(level)], ROWS[level], PLANES[level]
                ref[5 : 5 + count, own : own + 8, :] = self.recv[1][at : at + count] * high_in
                ref[5 : 5 + count, own + 8 : own + 16, :] = self.recv[0][at : at + count] * low_in
                at += count
        for level in range(3):
            ref, own, count = self.refs["R" + str(level)], ROWS[level], PLANES[level]
            first = iota((count, 8, 128), 1) < 4
            ref[4 : 4 + count, own : own + 8, :] = jnp.where(
                first, self.recv[1][at : at + count], self.recv[0][at : at + count]
            )
            at += count

    def unpack_z(self, copies):
        for index, copy in copies:
            part, shift, pieces = self.z[index]
            copy.wait_recv()
            if shift > 0:
                inside = self.k >= shift
            else:
                inside = self.k < self.nf + shift
            factor = jnp.where(inside, 1.0, 0.0).astype(F32)
            at = 0
            for name, _, target, count in pieces:
                low, high = part_rows(name, part)
                tiles = count * (high - low) // 8
                block = self.recv[2 + index][at : at + tiles]
                if name[0] == "D":
                    block = block * factor
                self.refs[name][target : target + count, low:high, :] = block.reshape(
                    count, high - low, 128
                )
                at += tiles

    def pack_row(self, pair):
        line, lane = iota((128, 128), 0), iota((128, 128), 1)
        spread = matmul(pair[...], one_hot(line == 8 * (lane % 16)))
        mine = iota((8, 128), 1) // 16 == iota((8, 128), 0)
        row = jnp.sum(jnp.where(mine, spread, 0.0), axis=0, keepdims=True)
        self.row[...] = row
        self.row_in[self.i] = row

    def start_rows(self):
        self.row_copies = []
        for delta in range(1, ROW):
            target = self.g * ROW + (self.i + delta) % ROW
            self.row_copies.append(
                self.start(self.row, self.row_in.at[self.i], target, self.s)
            )

    def start_subs(self):
        for copy in self.row_copies:
            copy.wait_recv()
        line = iota((8, 128), 0)
        tile = jnp.zeros((8, 128), F32)
        for index in range(ROW):
            tile = jnp.where(line == index, self.row_in[index], tile)
        self.sub_in[self.s] = tile
        self.sub_copies = []
        for delta in range(1, 4):
            self.sub_copies.append(
                self.start(
                    self.sub_in.at[self.s],
                    self.sub_in.at[self.s],
                    self.k,
                    (self.s + delta) % self.ns,
                )
            )

    def start_groups(self, work):
        for copy in self.sub_copies:
            copy.wait_recv()
        tiles = [self.sub_in[index] for index in range(4)]
        turned = [roll(tile, 64, 1) for tile in tiles]
        left = iota((8, 128), 1) < 64
        for half in range(2):
            a, b = 2 * half, 2 * half + 1
            self.group[half] = jnp.where(left, tiles[a], turned[b])
            if self.dense:
                self.group[2 + half] = jnp.where(left, turned[a], tiles[b])
        quads = jnp.zeros((8, 128), F32)
        for half in range(4 if self.dense else 2):
            line, lane = iota((128, 128), 0), iota((128, 128), 1)
            x, y = line // 16 + 8 * (half % 2), line % 16
            home = (x // 2) * 8 + y // 2 + 64 * (half // 2)
            quads = quads + matmul(self.group[half], one_hot(home == lane))
        work[...] = quads
        four = (work[pl.ds(0, 4, stride=2), :] + work[pl.ds(1, 4, stride=2), :]) * 0.125
        self.quad_in[self.g, 0:4, :] = four
        self.quad_in[self.g, 4:8, :] = four
        up = ((self.g + 1) % self.ng) * ROW + self.i
        down = ((self.g + self.ng - 1) % self.ng) * ROW + self.i
        self.group_copies = [
            self.start(self.group, self.low, up, self.s),
            self.start(self.group, self.high, down, self.s),
        ]
        for delta in range(1, self.ng):
            target = ((self.g + delta) % self.ng) * ROW + self.i
            self.group_copies.append(
                self.start(
                    self.quad_in.at[self.g], self.quad_in.at[self.g], target, self.s
                )
            )

    def wait_groups(self):
        for copy in self.group_copies:
            copy.wait_recv()

    def finish(self):
        for copy in self.started:
            copy.wait_send()


def split_packed(value):
    left = iota(value.shape, 1) < 64
    return jnp.where(left, value, 0.0), jnp.where(left, roll(value, 64, 1), 0.0)


def kernel(nf, ns, rhs, density, solution, residual, *scratch):
    scratch = list(scratch)

    def take(count):
        taken = scratch[:count]
        del scratch[:count]
        return taken

    refs = {}
    for name in ("D0", "D1", "D2", "R0", "R1", "R2"):
        (refs[name],) = take(1)
    fine_coef = [take(5) for _ in range(3)]
    remains = take(3)
    updates = [take(3) for _ in range(3)]
    answers = take(3)
    (work, tile_work, pair, sol, spread, level4, level5, dens3) = take(8)
    coarse_coef = [take(5) for _ in range(3)]
    phases = []
    k, s = lax.axis_index("fine"), lax.axis_index("sub")
    for with_density in (True, False):
        count = n_halo(with_density)
        send, recv, coarse = take(count), take(count), take(7)
        send_sem, recv_sem = take(2)
        phases.append(
            Phase(refs, (k, s, nf, ns), with_density, send, recv, coarse, send_sem, recv_sem)
        )
    ng = nf // ROW
    i, g = k % ROW, k // ROW

    barrier = pltpu.get_barrier_semaphore()
    partners = []
    for shift in (1, 2, 3):
        partners += [((k + shift) % nf, s), ((k + nf - shift) % nf, s)]
    partners += [(k, (s + delta) % ns) for delta in range(1, ns)]
    partners += [(g * ROW + (i + delta) % ROW, s) for delta in range(1, ROW)]
    partners += [(((g + delta) % ng) * ROW + i, s) for delta in range(1, ng)]
    for partner in partners:
        pl.semaphore_signal(barrier, inc=1, device_id=partner, device_id_type=MESH)

    def restrict_all(name, lead, first_row):
        for level in range(2):
            refs[name + str(level + 1)][
                lead : lead + PLANES[level + 1], 0 : ROWS[level + 1], :
            ] = restrict_block(
                refs[name + str(level)], lead, PLANES[level], ROWS[level], 2**level, work
            )
        three = restrict_block(refs[name + "2"], lead, PLANES[2], ROWS[2], 4, work)
        pair[first_row : first_row + 4, :] = three.reshape(4, 128)

    refs["R0"][4:12, 0:32, :] = rhs[...]
    refs["D0"][5:13, 0:32, :] = density[...]

    for cycle in range(CYCLES):
        phase = phases[cycle]
        restrict_all("R", 4, 0)
        if cycle == 0:
            restrict_all("D", 5, 4)
        phase.pack_row(pair)
        if cycle == 0:
            pl.semaphore_wait(barrier, len(partners))
        phase.start_rows()
        phase.pack_x()
        phase.start_x()
        phase.pack_z("a")
        a_copies = phase.start_z("a")
        phase.start_subs()
        phase.unpack_x()
        phase.pack_z("b")
        b_copies = phase.start_z("b")
        phase.start_groups(tile_work)
        phase.unpack_z(a_copies)
        phase.unpack_z(b_copies)
        for level in range(3):
            if cycle == 0:
                fine_coefficients(level, refs["D" + str(level)], fine_coef[level])
            fine_smooth(
                level,
                refs["R" + str(level)],
                fine_coef[level],
                remains[level],
                updates[level],
                answers[level],
            )
        phase.wait_groups()

        for tile in range(ng // 2):
            level4[8 * tile : 8 * tile + 8, :] = jnp.where(
                iota((8, 128), 0) < 4, phase.quad_in[2 * tile], phase.quad_in[2 * tile + 1]
            )
        n4, n5 = 4 * ng, 2 * ng
        line, lane = iota((128, 128), 0), iota((128, 128), 1)
        inner = line % 64
        home = (inner // 16) * 4 + (inner % 8) // 2 + 64 * (line // 64)
        pairs5 = level4[pl.ds(0, n5, stride=2), :] + level4[pl.ds(1, n5, stride=2), :]
        packed5 = matmul(pairs5, one_hot(home == lane)) * 0.125
        source4, density4 = split_packed(level4[...])
        source5, density5 = split_packed(packed5)
        low_in = jnp.where(g > 0, 1.0, 0.0).astype(F32)
        high_in = jnp.where(g < ng - 1, 1.0, 0.0).astype(F32)
        if cycle == 0:
            for half in range(2):
                cols = slice(128 * half, 128 * half + 128)
                dens3[0:8, cols] = phase.low[2 + half] * low_in
                dens3[8:16, cols] = phase.group[2 + half]
                dens3[16:24, cols] = phase.high[2 + half] * high_in
            for index, (dens, ny) in enumerate(
                ((dens3[...], 16), (density4, 8), (density5, 4))
            ):
                values = packed_coefficients(dens, ny, ny, 0.25 ** (3 + index))
                for ref, value in zip(coarse_coef[index], values):
                    ref[...] = value
        coef3, coef4, coef5 = ([ref[...] for ref in refs5] for refs5 in coarse_coef)
        total = jnp.sum(jnp.sum(source5, axis=0, keepdims=True), axis=1, keepdims=True)
        weight = jnp.sum(jnp.sum(coef5[3], axis=0, keepdims=True), axis=1, keepdims=True)
        c5 = packed_smooth(source5, coef5, 4, 0.05) + total / weight
        s4 = packed_smooth(source4, coef4, 8, 0.5)
        up5 = matmul(
            c5, one_hot((line == ((lane // 16) * 4 + (lane % 8) // 2)) & (lane < 64))
        )
        level5[pl.ds(0, n5, stride=2), :] = up5
        level5[pl.ds(1, n5, stride=2), :] = up5
        c4 = s4 + level5[...]

        source3 = jnp.concatenate(
            [
                jnp.concatenate([phase.low[0], phase.low[1]], axis=1),
                jnp.concatenate([phase.group[0], phase.group[1]], axis=1),
                jnp.concatenate([phase.high[0], phase.high[1]], axis=1),
            ],
            axis=0,
        )
        s3 = packed_smooth(source3, coef3, 16, 0.5)
        near3 = iota((8, 24), 1) == iota((8, 24), 0) + (i + 7)
        near4 = iota((8, n4), 1) == (iota((8, n4), 0) + (k + 1)) // 2 - 1
        wide = iota((128, 256), 1)
        lift = one_hot(iota((128, 256), 0) == (wide // 32) * 8 + (wide % 16) // 2)
        slabs = matmul(one_hot(near3), s3) + matmul(matmul(one_hot(near4), c4), lift)

        row = iota((16, 256), 0)
        x3 = jnp.where(row < 8, 0, jnp.where(row < 12, 0, -8)) + row // 2 + 4 * s
        here = iota((16, 256), 1) // 16 == x3
        picked = jnp.concatenate(
            [jnp.where(here, slabs[t : t + 1, :], 0.0) for t in range(3)], axis=0
        )
        fan = one_hot(iota((256, 128), 0) % 16 == iota((256, 128), 1) // 8)
        spread[0:3, 0:16, :] = matmul(picked, fan).reshape(3, 16, 128)

        for level in (2, 1, 0):
            rows = ROWS[level]
            answer = answers[level]
            planes = PLANES[level] + 2

            def add(p, carry, answer=answer):
                answer[p + 3] = answer[p + 3] + spread[(p + 1) // 2, 0 : answer.shape[1], :]
                return carry

            lax.fori_loop(0, planes, add, 0, unroll=True)
            if level > 0:
                value = answer[3 : 3 + planes, 0:rows, :]
                ends = answer[3 : 3 + planes, rows : rows + 8, :]
                spread[0:planes, pl.ds(0, rows, stride=2), :] = value
                spread[0:planes, pl.ds(1, rows, stride=2), :] = value
                first = iota((planes, 8, 128), 1) < 4
                spread[0:planes, 2 * rows : 2 * rows + 8, :] = jnp.where(
                    first, ends[:, 0:1, :], ends[:, 7:8, :]
                )

        def advance(p, carry, cycle=cycle):
            if cycle == 0:
                sol[p] = 0.4 * answers[0][p + 3]
            else:
                sol[p] = sol[p] + 0.4 * answers[0][p + 3]
            return carry

        lax.fori_loop(0, PLANES[0] + 2, advance, 0, unroll=True)

        def defect(p, carry, cycle=cycle):
            applied = fine_apply(sol, p + 1, fine_coef[0], p + 4, 1)
            left = rhs[p] - applied[0:32, :]
            if cycle == 0:
                refs["R0"][p + 4, 0:32, :] = left
            else:
                residual[p] = left
                solution[p] = sol[p + 1, 0:32, :]
            return carry

        if cycle == 0:
            lax.fori_loop(0, PLANES[0], defect, 0, unroll=True)
        else:
            lax.fori_loop(0, PLANES[0], defect, 0, unroll=True)

    for phase in phases:
        phase.finish()


def scratch_shapes(ng):
    shapes = []
    for level in range(3):
        shapes.append(pltpu.VMEM((PLANES[level] + 10, ROWS[level] + 16, 128), F32))
    extents = [(PLANES[level] + 8, ROWS[level] + 8, 128) for level in range(3)]
    shapes += [pltpu.VMEM(extent, F32) for extent in extents]
    for extent in extents:
        shapes += [pltpu.VMEM(extent, F32)] * 5
    shapes += [pltpu.VMEM(extent, F32) for extent in extents]
    for extent in extents:
        shapes += [pltpu.VMEM(extent, F32)] * 3
    shapes += [pltpu.VMEM(extent, F32) for extent in extents]
    shapes += [
        pltpu.VMEM((4, 32, 128), F32),
        pltpu.VMEM((8, 128), F32),
        pltpu.VMEM((8, 128), F32),
        pltpu.VMEM((10, 40, 128), F32),
        pltpu.VMEM((6, 40, 128), F32),
        pltpu.VMEM((4 * ng, 128), F32),
        pltpu.VMEM((4 * ng, 128), F32),
        pltpu.VMEM((24, 256), F32),
    ]
    for extent in ((24, 256), (4 * ng, 128), (2 * ng, 128)):
        shapes += [pltpu.VMEM(extent, F32)] * 5
    for with_density in (True, False):
        halo = buffer_shapes(with_density)
        shapes += halo + halo
        tiles = 4 if with_density else 2
        shapes += [
            pltpu.VMEM((1, 128), F32),
            pltpu.VMEM((ROW, 1, 128), F32),
            pltpu.VMEM((4, 8, 128), F32),
            pltpu.VMEM((tiles, 8, 128), F32),
            pltpu.VMEM((tiles, 8, 128), F32),
            pltpu.VMEM((tiles, 8, 128), F32),
            pltpu.VMEM((ng, 8, 128), F32),
        ]
        copies = n_halo(with_density) + (ROW - 1) + 3 + 2 + (ng - 1)
        shapes += [pltpu.SemaphoreType.DMA((copies,)), pltpu.SemaphoreType.DMA((copies,))]
    return shapes


def solution(mesh):
    nf, ns = mesh.shape["fine"], mesh.shape["sub"]

    def body(rhs, density):
        return pl.pallas_call(
            functools.partial(kernel, nf, ns),
            out_shape=(
                jax.ShapeDtypeStruct(rhs.shape, F32),
                jax.ShapeDtypeStruct(rhs.shape, F32),
            ),
            in_specs=[pl.BlockSpec(memory_space=pltpu.VMEM)] * 2,
            out_specs=[pl.BlockSpec(memory_space=pltpu.VMEM)] * 2,
            scratch_shapes=scratch_shapes(nf // ROW),
            compiler_params=pltpu.CompilerParams(
                collective_id=0, has_side_effects=True, vmem_limit_bytes=32 * 1024 * 1024
            ),
        )(rhs, density)

    return jax.shard_map(
        body,
        mesh=mesh,
        in_specs=(P("fine", "sub", None), P("fine", "sub", None)),
        out_specs=(P("fine", "sub", None), P("fine", "sub", None)),
        check_vma=False,
    )
```

```python
import functools

import jax
import jax.numpy as jnp
from jax import lax
from jax.experimental import pallas as pl
from jax.experimental.pallas import tpu as pltpu
from jax.sharding import PartitionSpec as P

DEGREE = 4
CYCLES = 2
MESH = pl.DeviceIdType.MESH
F32 = jnp.float32
BF16 = jnp.bfloat16
ROW = 8
PLANES = (8, 4, 2)
ROWS = (32, 16, 8)


def chebyshev_constants(lower):
    upper = 2.0
    theta = 0.5 * (upper + lower)
    delta = 0.5 * (upper - lower)
    sigma = theta / delta
    ratio = 1.0 / sigma
    steps = []
    for _ in range(DEGREE - 1):
        next_ratio = 1.0 / (2.0 * sigma - ratio)
        steps.append((next_ratio * ratio, 2.0 * next_ratio / delta))
        ratio = next_ratio
    return 1.0 / theta, steps


def iota(shape, dim):
    return lax.broadcasted_iota(jnp.int32, shape, dim)


def roll(value, shift, axis):
    return pltpu.roll(value, shift % value.shape[axis], axis)


def invert(value):
    return pltpu.reciprocal(value, full_range=False)


def one_hot(condition):
    return jnp.where(condition, 1.0, 0.0).astype(F32)


def one_hot_matmul(value, matrix):
    count = value.shape[0]
    first = value.astype(BF16).astype(F32)
    rest = value - first
    second = rest.astype(BF16).astype(F32)
    parts = jnp.concatenate([first, second, rest - second], axis=0).astype(BF16)
    product = jnp.dot(parts, matrix, preferred_element_type=F32)
    return product[0:count] + product[count : 2 * count] + product[2 * count :]


def restrict_block(source, first, planes, rows, stride, work):
    field = source[first : first + planes, 0:rows, :]
    field = field.reshape(planes // 2, 2, rows, 128)
    work[0 : planes // 2, 0:rows, :] = field[:, 0] + field[:, 1]
    half = rows // 2
    both = (
        work[0 : planes // 2, pl.ds(0, half, stride=2), :]
        + work[0 : planes // 2, pl.ds(1, half, stride=2), :]
    )
    lane = iota(both.shape, 2)
    even = (lane // stride) % 2 == 0
    other = jnp.where(even, roll(both, -stride, 2), roll(both, stride, 2))
    return (both + other) * 0.125


def fine_coefficients(level, dens, coef):
    own = ROWS[level]
    scale = 2.0 * 0.25**level
    stride = 2**level
    planes = PLANES[level] + 8
    face_z, face_x, face_y, diagonal, inverse = coef
    shape = (own + 16, 128)

    def compress(value):
        tail = jnp.where(
            iota((8, 128), 0) < 4, value[own : own + 8], value[own + 8 : own + 16]
        )
        return jnp.concatenate([value[0:own], tail], axis=0)

    def plane(p, down):
        here = dens[p + 1]
        above = dens[p + 2]
        lane = iota(shape, 1)
        right = roll(here, -1, 0)
        up = scale * invert(jnp.maximum(here + above, 0.1))
        x_face = scale * invert(jnp.maximum(here + right, 0.1))
        ahead = jnp.where(lane >= 128 - stride, 0.0, roll(here, -stride, 1))
        behind = jnp.where(lane < stride, 0.0, roll(here, stride, 1))
        y_face = scale * invert(jnp.maximum(here + ahead, 0.1))
        y_back = scale * invert(jnp.maximum(here + behind, 0.1))
        diag = up + down + x_face + roll(x_face, 1, 0) + y_face + y_back
        inside = here > 0.0
        face_z[p] = compress(jnp.where(inside & (above > 0.0), up, 0.0))
        face_x[p] = compress(jnp.where(inside & (right > 0.0), x_face, 0.0))
        face_y[p] = compress(jnp.where(lane >= 128 - stride, 0.0, y_face))
        diagonal[p] = compress(diag)
        inverse[p] = compress(invert(diag))
        return up

    lowest = scale * invert(jnp.maximum(dens[0] + dens[1], 0.1))
    lax.fori_loop(0, planes, plane, lowest, unroll=True)


def fine_apply(field, p, coef, q, stride):
    face_z, face_x, face_y, diagonal, _ = coef
    here = field[p]
    x_face = face_x[q]
    y_face = face_y[q]
    result = diagonal[q] * here
    result = result - face_z[q] * field[p + 1] - face_z[q - 1] * field[p - 1]
    result = result - x_face * roll(here, -1, 0) - roll(x_face * here, 1, 0)
    result = result - y_face * roll(here, -stride, 1) - roll(y_face * here, stride, 1)
    return result


def fine_smooth(level, source, coef, remain, updates, answer):
    planes = PLANES[level] + 8
    stride = 2**level
    inverse = coef[4]
    first, steps = chebyshev_constants(0.5)
    d0, d1, d2 = updates

    def start(p, carry):
        d0[p] = source[p] * inverse[p] * first
        return carry

    lax.fori_loop(0, planes, start, 0, unroll=True)
    chain = (d0, d1, d2)
    for sweep in range(3):
        old = chain[sweep]
        keep, add = steps[sweep]

        def step(p, carry, sweep=sweep, old=old, keep=keep, add=add):
            left = source[p] if sweep == 0 else remain[p]
            left = left - fine_apply(old, p, coef, p, stride)
            new = keep * old[p] + add * (left * inverse[p])
            if sweep < 2:
                remain[p] = left
                chain[sweep + 1][p] = new
            else:
                answer[p] = d0[p] + d1[p] + d2[p] + new
            return carry

        lax.fori_loop(sweep + 1, planes - sweep - 1, step, 0, unroll=True)


def packed_coefficients(dens, ny, nx, scale):
    rows = dens.shape[0]
    z = iota(dens.shape, 0)
    lane = iota(dens.shape, 1)
    y = lane % ny
    x = lane // ny
    scale = 2.0 * scale

    def neighbour(shift, axis, outside):
        return jnp.where(outside, 0.0, roll(dens, shift, axis))

    above = neighbour(-1, 0, z == rows - 1)
    below = neighbour(1, 0, z == 0)
    right = neighbour(-ny, 1, x >= nx - 1)
    left = neighbour(ny, 1, x == 0)
    ahead = neighbour(-1, 1, y == ny - 1)
    behind = neighbour(1, 1, y == 0)

    def face(other):
        return scale * invert(jnp.maximum(dens + other, 0.1))

    up, x_face, y_face = face(above), face(right), face(ahead)
    diagonal = up + face(below) + x_face + face(left) + y_face + face(behind)
    inside = dens > 0.0

    def inner(value, other):
        return jnp.where(inside & (other > 0.0), value, 0.0)

    return (
        inner(up, above),
        inner(x_face, right),
        inner(y_face, ahead),
        jnp.where(inside, diagonal, 0.0),
        jnp.where(inside, invert(diagonal), 0.0),
    )


def packed_apply(field, coef, ny):
    face_z, face_x, face_y, diagonal, _ = coef
    result = diagonal * field
    result = result - face_z * roll(field, -1, 0) - roll(face_z * field, 1, 0)
    result = result - face_x * roll(field, -ny, 1) - roll(face_x * field, ny, 1)
    result = result - face_y * roll(field, -1, 1) - roll(face_y * field, 1, 1)
    return result


def packed_smooth(source, coef, ny, lower):
    first, steps = chebyshev_constants(lower)
    inverse = coef[4]
    update = source * inverse * first
    answer = update
    for keep, add in steps:
        source = source - packed_apply(update, coef, ny)
        update = keep * update + add * (source * inverse)
        answer = answer + update
    return answer


SMALL = {
    ("a", 1): ((("D1", 5, 1, 4), ("D2", 5, 3, 2)), (("R1", 4, 0, 4), ("R2", 4, 2, 2))),
    ("a", -1): ((("D1", 5, 9, 4), ("D2", 5, 7, 2)), (("R1", 4, 8, 4), ("R2", 4, 6, 2))),
    ("a", 2): ((("D1", 8, 0, 1), ("D2", 5, 1, 2)), (("R2", 4, 0, 2),)),
    ("a", -2): ((("D1", 5, 13, 1), ("D2", 5, 9, 2)), (("R2", 4, 8, 2),)),
    ("a", 3): ((("D2", 6, 0, 1),), ()),
    ("a", -3): ((("D2", 5, 11, 1),), ()),
    ("b", 1): ((("D1", 5, 1, 4), ("D2", 5, 3, 2)), (("R1", 4, 0, 4), ("R2", 4, 2, 2))),
    ("b", -1): ((("D1", 5, 9, 4), ("D2", 5, 7, 2)), (("R1", 4, 8, 4), ("R2", 4, 6, 2))),
    ("b", 2): ((("D2", 5, 1, 2),), (("R2", 4, 0, 2),)),
    ("b", -2): ((("D2", 5, 9, 2),), (("R2", 4, 8, 2),)),
}
LARGE = {
    ("a", 1): ((("D0", 8, 0, 5),), (("R0", 8, 0, 4),)),
    ("a", -1): ((("D0", 5, 13, 5),), (("R0", 4, 12, 4),)),
    ("b", 1): ((("D0", 9, 1, 4),), (("R0", 9, 1, 3),)),
    ("b", -1): ((("D0", 5, 13, 4),), (("R0", 4, 12, 3),)),
}


def z_messages(with_density):
    result = []
    for which, table in (("small", SMALL), ("large", LARGE)):
        for (part, shift), (density, field) in table.items():
            pieces = (density if with_density else ()) + field
            if pieces:
                result.append((which, part, shift, pieces))
    return result


def paired(name, tiles):
    return name[1] != "0" and tiles % 2 == 0


def piece_tiles(part, piece):
    name, _, _, count = piece
    tiles = count * (ROWS[int(name[1])] // 8 if part == "a" else 1)
    return tiles // 2 if paired(name, tiles) else tiles


def x_pieces(with_density):
    result = []
    for level in range(3):
        count = PLANES[level]
        if with_density:
            result.append(("D%d" % level, count, count // 2 if level else count))
        result.append(("R%d" % level, count, (4, 1, 1)[level]))
    return result


def buffer_shapes(with_density):
    tiles = [sum(sent for _, _, sent in x_pieces(with_density))] * 2
    for _, part, _, pieces in z_messages(with_density):
        tiles.append(sum(piece_tiles(part, piece) for piece in pieces))
    return [pltpu.VMEM((count, 8, 128), F32) for count in tiles]


def n_halo(with_density):
    return 2 + len(z_messages(with_density))


def even_lanes(tiles):
    return iota((tiles, 8, 128), 2) % 2 == 0


def upper_rows(tiles):
    return iota((tiles, 8, 128), 1) < 4


def pack_lanes(block):
    half = block.shape[0] // 2
    return jnp.where(even_lanes(half), block[0:half], block[half:])


def unpack_lanes(block):
    even = even_lanes(block.shape[0])
    return jnp.concatenate(
        [jnp.where(even, block, roll(block, 1, 2)), jnp.where(even, roll(block, -1, 2), block)],
        axis=0,
    )


class Phase:
    def __init__(self, refs, place, with_density, send, recv, coarse, send_sem, recv_sem):
        self.refs = refs
        self.k, self.s, self.nf, self.ns = place
        self.dense = with_density
        self.send, self.recv = send, recv
        self.row, self.row_in, self.sub_in, self.group, self.low, self.high, self.quad_in = coarse
        self.send_sem, self.recv_sem = send_sem, recv_sem
        self.started = []
        self.count = 0
        self.z = z_messages(with_density)
        self.copies = {}
        self.i = self.k % ROW
        self.g = self.k // ROW
        self.ng = self.nf // ROW

    def start(self, source, target, k, s):
        index = self.count
        self.count += 1
        copy = pltpu.make_async_remote_copy(
            src_ref=source,
            dst_ref=target,
            send_sem=self.send_sem.at[index],
            recv_sem=self.recv_sem.at[index],
            device_id=(k, s),
            device_id_type=MESH,
        )
        copy.start()
        self.started.append(copy)
        return copy

    def pack_x(self):
        for which in (0, 1):
            at = 0
            for name, count, sent in x_pieces(self.dense):
                level = int(name[1])
                lead = 5 if name[0] == "D" else 4
                row = ROWS[level] - 8 if which == 0 else 0
                block = self.refs[name][lead : lead + count, row : row + 8, :]
                if level:
                    block = pack_lanes(block)
                if block.shape[0] > sent:
                    near, far = block[0:sent], roll(block[sent:], 4, 1)
                    upper = upper_rows(sent)
                    if which == 0:
                        block = jnp.where(upper, far, near)
                    else:
                        block = jnp.where(upper, near, far)
                self.send[which][at : at + sent] = block
                at += sent

    def start_x(self):
        up, down = (self.s + 1) % self.ns, (self.s + self.ns - 1) % self.ns
        self.x_copies = [
            self.start(self.send[0], self.recv[0], self.k, up),
            self.start(self.send[1], self.recv[1], self.k, down),
        ]

    def unpack_x(self):
        for copy in self.x_copies:
            copy.wait_recv()
        low_in = jnp.where(self.s > 0, 1.0, 0.0).astype(F32)
        high_in = jnp.where(self.s < self.ns - 1, 1.0, 0.0).astype(F32)
        at = 0
        for name, count, sent in x_pieces(self.dense):
            level = int(name[1])
            own = ROWS[level]
            lead = 5 if name[0] == "D" else 4
            low, high = self.recv[0][at : at + sent], self.recv[1][at : at + sent]
            at += sent
            ref = self.refs[name]
            if name[0] == "D":
                if level:
                    low, high = unpack_lanes(low), unpack_lanes(high)
                ref[lead : lead + count, own : own + 8, :] = high * high_in
                ref[lead : lead + count, own + 8 : own + 16, :] = low * low_in
                continue
            upper = upper_rows(sent)
            block = jnp.where(upper, high, low)
            if sent < (count // 2 if level else count):
                far = roll(jnp.where(upper, low, high), 4, 1)
                block = jnp.concatenate([block, far], axis=0)
            if level:
                block = unpack_lanes(block)
            ref[lead : lead + count, own : own + 8, :] = block

    def pack_z(self, part):
        for index, (_, kind, _, pieces) in enumerate(self.z):
            if kind != part:
                continue
            at = 0
            for piece in pieces:
                name, source, _, count = piece
                ref, own = self.refs[name], ROWS[int(name[1])]
                if part == "a":
                    block = ref[source : source + count, 0:own, :]
                    block = block.reshape(count * own // 8, 8, 128)
                else:
                    block = ref[source : source + count, own : own + 8, :]
                    if name[0] == "D":
                        low = ref[source : source + count, own + 8 : own + 16, :]
                        block = jnp.where(upper_rows(count), block, low)
                if paired(name, block.shape[0]):
                    block = pack_lanes(block)
                self.send[2 + index][at : at + block.shape[0]] = block
                at += block.shape[0]

    def start_z(self, which, part):
        for index, (size, kind, shift, _) in enumerate(self.z):
            if (size, kind) == (which, part):
                target = (self.k + shift + self.nf) % self.nf
                self.copies[index] = self.start(
                    self.send[2 + index], self.recv[2 + index], target, self.s
                )

    def unpack_z(self, which):
        for index, (size, part, shift, pieces) in enumerate(self.z):
            if size != which:
                continue
            self.copies[index].wait_recv()
            inside = self.k >= shift if shift > 0 else self.k < self.nf + shift
            factor = jnp.where(inside, 1.0, 0.0).astype(F32)
            at = 0
            for piece in pieces:
                name, _, target, count = piece
                ref, own = self.refs[name], ROWS[int(name[1])]
                sent = piece_tiles(part, piece)
                block = self.recv[2 + index][at : at + sent]
                at += sent
                if name[0] == "D":
                    block = block * factor
                if sent < (count * own // 8 if part == "a" else count):
                    block = unpack_lanes(block)
                if part == "a":
                    ref[target : target + count, 0:own, :] = block.reshape(count, own, 128)
                else:
                    ref[target : target + count, own : own + 8, :] = block
                    if name[0] == "D":
                        ref[target : target + count, own + 8 : own + 16, :] = block

    def pack_row(self, pair, spread_row):
        spread = one_hot_matmul(pair[...], spread_row[...])[0:8]
        mine = iota((8, 128), 1) // 16 == iota((8, 128), 0)
        row = jnp.sum(jnp.where(mine, spread, 0.0), axis=0, keepdims=True)
        self.row[...] = row
        self.row_in[self.i] = row

    def start_rows(self):
        self.row_copies = []
        for delta in range(1, ROW):
            target = self.g * ROW + (self.i + delta) % ROW
            self.row_copies.append(
                self.start(self.row, self.row_in.at[self.i], target, self.s)
            )

    def start_subs(self):
        for copy in self.row_copies:
            copy.wait_recv()
        line = iota((8, 128), 0)
        tile = jnp.zeros((8, 128), F32)
        for index in range(ROW):
            tile = jnp.where(line == index, self.row_in[index], tile)
        self.sub_in[self.s] = tile
        self.sub_copies = []
        for delta in range(1, 4):
            self.sub_copies.append(
                self.start(
                    self.sub_in.at[self.s],
                    self.sub_in.at[self.s],
                    self.k,
                    (self.s + delta) % self.ns,
                )
            )

    def start_groups(self, work, pool):
        for copy in self.sub_copies:
            copy.wait_recv()
        tiles = [self.sub_in[index] for index in range(4)]
        turned = [roll(tile, 64, 1) for tile in tiles]
        left = iota((8, 128), 1) < 64
        fields = []
        for half in range(2):
            a, b = 2 * half, 2 * half + 1
            fields.append(jnp.where(left, tiles[a], turned[b]))
        if self.dense:
            for half in range(2):
                a, b = 2 * half, 2 * half + 1
                fields.append(jnp.where(left, turned[a], tiles[b]))
        for index, field in enumerate(fields):
            self.group[index] = field
        up = ((self.g + 1) % self.ng) * ROW + self.i
        down = ((self.g + self.ng - 1) % self.ng) * ROW + self.i
        self.group_copies = [
            self.start(self.group, self.low, up, self.s),
            self.start(self.group, self.high, down, self.s),
        ]
        wide = jnp.concatenate(fields, axis=1)
        wide = jnp.concatenate([wide, jnp.zeros(wide.shape, F32)], axis=0)
        sums = one_hot_matmul(wide, pool[0 : wide.shape[1], :])[0:8]
        work[...] = sums[:, 0:128]
        four = (work[pl.ds(0, 4, stride=2), :] + work[pl.ds(1, 4, stride=2), :]) * 0.125
        self.quad_in[self.g, 0:4, :] = four
        five = sums[:, 128:256]
        five = five + roll(five, -1, 0)
        five = (five + roll(five, -2, 0)) * (0.125 * 0.125)
        line = iota((8, 128), 0)
        five = jnp.where(line % 2 == 0, five[0:1], five[4:5])
        self.quad_in[self.g, 4:8, :] = five[4:8]
        for delta in range(1, self.ng):
            target = ((self.g + delta) % self.ng) * ROW + self.i
            self.group_copies.append(
                self.start(
                    self.quad_in.at[self.g], self.quad_in.at[self.g], target, self.s
                )
            )

    def wait_groups(self):
        for copy in self.group_copies:
            copy.wait_recv()

    def finish(self, first, last):
        for copy in self.started[first:last]:
            copy.wait_send()


def split_packed(value):
    left = iota(value.shape, 1) < 64
    return jnp.where(left, value, 0.0), jnp.where(left, roll(value, 64, 1), 0.0)


def build_matrices(spread_row, pool, fan):
    line, lane = iota((128, 128), 0), iota((128, 128), 1)
    spread_row[...] = one_hot(line == 8 * (lane % 16)).astype(BF16)
    for half in range(4):
        x, y = line // 16 + 8 * (half % 2), line % 16
        rows = slice(128 * half, 128 * half + 128)
        home4 = (x // 2) * 8 + y // 2 + 64 * (half // 2)
        home5 = (x // 4) * 4 + y // 4 + 64 * (half // 2)
        pool[rows, 0:128] = one_hot(home4 == lane).astype(BF16)
        pool[rows, 128:256] = one_hot(home5 == lane).astype(BF16)
    three = one_hot(line % 16 == lane // 8).astype(BF16)
    fan[0:128, :] = three
    fan[128:256, :] = three
    fan[256:384, :] = one_hot(line % 8 == lane // 16).astype(BF16)
    fan[384:512, :] = one_hot(line % 4 == lane // 32).astype(BF16)


def kernel(nf, ns, rhs_in, density_in, solution, residual, *scratch):
    scratch = list(scratch)

    def take(count):
        taken = scratch[:count]
        del scratch[:count]
        return taken

    refs = {}
    for name in ("D0", "D1", "D2", "R0", "R1", "R2"):
        (refs[name],) = take(1)
    fine_coef = [take(5) for _ in range(3)]
    remains = take(3)
    updates = [take(3) for _ in range(3)]
    answers = take(3)
    (rhs, load_sem, work, tile_work, pair, sol, spread) = take(7)
    (spread_row, pool, fan, keep3, keep4, keep5, dens3) = take(7)
    coarse_coef = [take(5) for _ in range(3)]
    phases = []
    k, s = lax.axis_index("fine"), lax.axis_index("sub")
    for with_density in (True, False):
        count = n_halo(with_density)
        send, recv, coarse = take(count), take(count), take(7)
        send_sem, recv_sem = take(2)
        phases.append(
            Phase(refs, (k, s, nf, ns), with_density, send, recv, coarse, send_sem, recv_sem)
        )
    ng = nf // ROW
    i, g = k % ROW, k // ROW

    loads = [
        pltpu.make_async_copy(density_in, refs["D0"].at[5:13, 0:32, :], load_sem.at[0]),
        pltpu.make_async_copy(rhs_in, refs["R0"].at[4:12, 0:32, :], load_sem.at[1]),
        pltpu.make_async_copy(rhs_in, rhs, load_sem.at[2]),
    ]
    for load in loads:
        load.start()

    barrier = pltpu.get_barrier_semaphore()
    partners = []
    for shift in (1, 2, 3):
        partners += [((k + shift) % nf, s), ((k + nf - shift) % nf, s)]
    partners += [(k, (s + delta) % ns) for delta in range(1, ns)]
    partners += [(g * ROW + (i + delta) % ROW, s) for delta in range(1, ROW)]
    partners += [(((g + delta) % ng) * ROW + i, s) for delta in range(1, ng)]
    for partner in partners:
        pl.semaphore_signal(barrier, inc=1, device_id=partner, device_id_type=MESH)

    for level in range(3):
        for name, lead in (("D", 5), ("R", 4)):
            ref = refs[name + str(level)]
            planes, rows, _ = ref.shape
            blank = jnp.zeros((lead, rows, 128), F32)
            ref[0:lead] = blank
            ref[planes - lead : planes] = blank
    for ref in (keep4, keep5):
        rows = ref.shape[0]
        ref[0:8, :] = jnp.zeros((8, 128), F32)
        ref[rows - 8 : rows, :] = jnp.zeros((8, 128), F32)
    pair[...] = jnp.zeros((16, 128), F32)

    def restrict_all(name, lead, first_row):
        for level in range(2):
            refs[name + str(level + 1)][
                lead : lead + PLANES[level + 1], 0 : ROWS[level + 1], :
            ] = restrict_block(
                refs[name + str(level)], lead, PLANES[level], ROWS[level], 2**level, work
            )
        three = restrict_block(refs[name + "2"], lead, PLANES[2], ROWS[2], 4, work)
        pair[first_row : first_row + 4, :] = three.reshape(4, 128)

    def smooth(level, cycle):
        if cycle == 0:
            fine_coefficients(level, refs["D" + str(level)], fine_coef[level])
        fine_smooth(
            level,
            refs["R" + str(level)],
            fine_coef[level],
            remains[level],
            updates[level],
            answers[level],
        )

    for load in loads:
        load.wait()

    for cycle in range(CYCLES):
        phase = phases[cycle]
        restrict_all("R", 4, 0)
        if cycle == 0:
            restrict_all("D", 5, 4)
            build_matrices(spread_row, pool, fan)
        phase.pack_row(pair, spread_row)
        if cycle == 0:
            phase.pack_x()
            phase.pack_z("a")
            pl.semaphore_wait(barrier, len(partners))
        phase.start_rows()
        if cycle == 1:
            phase.pack_x()
        phase.start_x()
        if cycle == 1:
            phase.pack_z("a")
        phase.start_z("small", "a")
        phase.start_z("large", "a")
        phase.start_subs()
        phase.unpack_x()
        phase.pack_z("b")
        phase.start_z("small", "b")
        phase.start_z("large", "b")
        phase.start_groups(tile_work, pool)
        if cycle == 1:
            phases[0].finish(0, None)
        phase.unpack_z("small")
        smooth(2, cycle)
        smooth(1, cycle)
        if cycle == 1:
            phase.finish(0, -(ng + 1))
        phase.wait_groups()

        tiles = [phase.quad_in[index] for index in range(ng)]
        line = iota((8, 128), 0)
        packed4, packed5 = [], []
        for index in range(0, ng, 2):
            packed4.append(jnp.where(line < 4, tiles[index], roll(tiles[index + 1], 4, 0)))
        for index in range(0, ng, 4):
            first = jnp.where(line < 6, tiles[index], tiles[index + 1])
            second = jnp.where(line < 6, tiles[index + 2], tiles[index + 3])
            packed5.append(jnp.where(line < 4, roll(first, 4, 0), second))
        source4, density4 = split_packed(jnp.concatenate(packed4, axis=0))
        source5, density5 = split_packed(jnp.concatenate(packed5, axis=0))
        if cycle == 0:
            low_in = jnp.where(g > 0, 1.0, 0.0).astype(F32)
            high_in = jnp.where(g < ng - 1, 1.0, 0.0).astype(F32)
            for half in range(2):
                cols = slice(128 * half, 128 * half + 128)
                dens3[0:8, cols] = phase.low[2 + half] * low_in
                dens3[8:16, cols] = phase.group[2 + half]
                dens3[16:24, cols] = phase.high[2 + half] * high_in
            for index, (dens, ny) in enumerate(
                ((dens3[...], 16), (density4, 8), (density5, 4))
            ):
                values = packed_coefficients(dens, ny, ny, 0.25 ** (3 + index))
                for ref, value in zip(coarse_coef[index], values):
                    ref[...] = value
        coef3, coef4, coef5 = ([ref[...] for ref in refs5] for refs5 in coarse_coef)
        total = jnp.sum(jnp.sum(source5, axis=0, keepdims=True), axis=1, keepdims=True)
        weight = jnp.sum(jnp.sum(coef5[3], axis=0, keepdims=True), axis=1, keepdims=True)
        n4, n5 = 4 * ng, 2 * ng
        keep5[8 : 8 + n5, :] = packed_smooth(source5, coef5, 4, 0.05) + total / weight
        keep4[8 : 8 + n4, :] = packed_smooth(source4, coef4, 8, 0.5)

        source3 = jnp.concatenate(
            [
                jnp.concatenate([phase.low[0], phase.low[1]], axis=1),
                jnp.concatenate([phase.group[0], phase.group[1]], axis=1),
                jnp.concatenate([phase.high[0], phase.high[1]], axis=1),
            ],
            axis=0,
        )
        keep3[...] = packed_smooth(source3, coef3, 16, 0.5)

        row = iota((16, 512), 0)
        lane = iota((16, 512), 1)
        x3 = row // 2 + jnp.where(row < 12, 0, -8) + (4 * s + 4)
        inside = (x3 >= 4) & (x3 < 20)
        x_lane = jnp.where(
            lane < 256, lane // 16, jnp.where(lane < 384, (lane - 256) // 8, (lane - 384) // 4)
        )
        x_row = jnp.where(lane < 256, x3 - 4, jnp.where(lane < 384, x3 // 2 - 2, x3 // 4 - 1))
        chosen = (x_lane == x_row) & inside
        picked = []
        for t in range(3):
            parts = jnp.concatenate(
                [
                    keep3[pl.ds(7 + i + t, 1), :],
                    keep4[pl.ds((k + 1 + t) // 2 + 7, 1), :],
                    keep5[pl.ds((k + 3 + t) // 4 + 7, 1), :],
                ],
                axis=1,
            )
            picked.append(jnp.where(chosen, parts, 0.0))
        spread[0:3, 0:16, :] = one_hot_matmul(
            jnp.concatenate(picked, axis=0), fan[...]
        ).reshape(3, 16, 128)

        for level in (2, 1):
            rows = ROWS[level]
            answer = answers[level]
            planes = PLANES[level] + 2
            coarse = jnp.concatenate(
                [spread[(p + 1) // 2 : (p + 1) // 2 + 1, 0 : rows + 8, :] for p in range(planes)],
                axis=0,
            )
            value = answer[3 : 3 + planes] + coarse
            own, ends = value[:, 0:rows, :], value[:, rows : rows + 8, :]
            spread[0:planes, pl.ds(0, rows, stride=2), :] = own
            spread[0:planes, pl.ds(1, rows, stride=2), :] = own
            spread[0:planes, 2 * rows : 2 * rows + 8, :] = jnp.where(
                upper_rows(planes), ends[:, 0:1, :], ends[:, 7:8, :]
            )

        phase.unpack_z("large")
        smooth(0, cycle)

        def advance(p, carry, cycle=cycle):
            step = 0.4 * (answers[0][p + 3] + spread[(p + 1) // 2])
            sol[p] = step if cycle == 0 else sol[p] + step
            return carry

        lax.fori_loop(0, PLANES[0] + 2, advance, 0, unroll=True)

        def defect(p, carry, cycle=cycle):
            applied = fine_apply(sol, p + 1, fine_coef[0], p + 4, 1)
            left = rhs[p] - applied[0:32, :]
            if cycle == 0:
                refs["R0"][p + 4, 0:32, :] = left
            else:
                residual[p] = left
                solution[p] = sol[p + 1, 0:32, :]
            return carry

        lax.fori_loop(0, PLANES[0], defect, 0, unroll=True)

    phases[1].finish(-(ng + 1), None)


def scratch_shapes(ng):
    shapes = []
    for level in range(3):
        shapes.append(pltpu.VMEM((PLANES[level] + 10, ROWS[level] + 16, 128), F32))
    extents = [(PLANES[level] + 8, ROWS[level] + 8, 128) for level in range(3)]
    shapes += [pltpu.VMEM(extent, F32) for extent in extents]
    for extent in extents:
        shapes += [pltpu.VMEM(extent, F32)] * 5
    shapes += [pltpu.VMEM(extent, F32) for extent in extents]
    for extent in extents:
        shapes += [pltpu.VMEM(extent, F32)] * 3
    shapes += [pltpu.VMEM(extent, F32) for extent in extents]
    shapes += [
        pltpu.VMEM((8, 32, 128), F32),
        pltpu.SemaphoreType.DMA((3,)),
        pltpu.VMEM((4, 32, 128), F32),
        pltpu.VMEM((8, 128), F32),
        pltpu.VMEM((16, 128), F32),
        pltpu.VMEM((10, 40, 128), F32),
        pltpu.VMEM((6, 40, 128), F32),
        pltpu.VMEM((128, 128), BF16),
        pltpu.VMEM((512, 256), BF16),
        pltpu.VMEM((512, 128), BF16),
        pltpu.VMEM((24, 256), F32),
        pltpu.VMEM((4 * ng + 16, 128), F32),
        pltpu.VMEM((2 * ng + 16, 128), F32),
        pltpu.VMEM((24, 256), F32),
    ]
    for extent in ((24, 256), (4 * ng, 128), (2 * ng, 128)):
        shapes += [pltpu.VMEM(extent, F32)] * 5
    for with_density in (True, False):
        halo = buffer_shapes(with_density)
        shapes += halo + halo
        tiles = 4 if with_density else 2
        shapes += [
            pltpu.VMEM((1, 128), F32),
            pltpu.VMEM((ROW, 1, 128), F32),
            pltpu.VMEM((4, 8, 128), F32),
            pltpu.VMEM((tiles, 8, 128), F32),
            pltpu.VMEM((tiles, 8, 128), F32),
            pltpu.VMEM((tiles, 8, 128), F32),
            pltpu.VMEM((ng, 8, 128), F32),
        ]
        copies = n_halo(with_density) + (ROW - 1) + 3 + 2 + (ng - 1)
        shapes += [pltpu.SemaphoreType.DMA((copies,)), pltpu.SemaphoreType.DMA((copies,))]
    return shapes


def solution(mesh):
    nf, ns = mesh.shape["fine"], mesh.shape["sub"]

    def body(rhs, density):
        return pl.pallas_call(
            functools.partial(kernel, nf, ns),
            out_shape=(
                jax.ShapeDtypeStruct(rhs.shape, F32),
                jax.ShapeDtypeStruct(rhs.shape, F32),
            ),
            in_specs=[pl.BlockSpec(memory_space=pltpu.HBM)] * 2,
            out_specs=[pl.BlockSpec(memory_space=pltpu.VMEM)] * 2,
            scratch_shapes=scratch_shapes(nf // ROW),
            compiler_params=pltpu.CompilerParams(
                collective_id=0, has_side_effects=True, vmem_limit_bytes=32 * 1024 * 1024
            ),
        )(rhs, density)

    return jax.shard_map(
        body,
        mesh=mesh,
        in_specs=(P("fine", "sub", None), P("fine", "sub", None)),
        out_specs=(P("fine", "sub", None), P("fine", "sub", None)),
        check_vma=False,
    )
```

```python
import functools

import jax
import jax.numpy as jnp
from jax import lax
from jax.experimental import pallas as pl
from jax.experimental.pallas import tpu as pltpu
from jax.sharding import PartitionSpec as P

DEGREE = 4
CYCLES = 2
MESH = pl.DeviceIdType.MESH
F32 = jnp.float32
BF16 = jnp.bfloat16
ROW = 8
PLANES = (8, 4, 2)
ROWS = (32, 16, 8)


def chebyshev_constants(lower):
    upper = 2.0
    theta = 0.5 * (upper + lower)
    delta = 0.5 * (upper - lower)
    sigma = theta / delta
    ratio = 1.0 / sigma
    steps = []
    for _ in range(DEGREE - 1):
        next_ratio = 1.0 / (2.0 * sigma - ratio)
        steps.append((next_ratio * ratio, 2.0 * next_ratio / delta))
        ratio = next_ratio
    return 1.0 / theta, steps


def iota(shape, dim):
    return lax.broadcasted_iota(jnp.int32, shape, dim)


def roll(value, shift, axis):
    return pltpu.roll(value, shift % value.shape[axis], axis)


def invert(value):
    return pltpu.reciprocal(value, full_range=False)


def one_hot(condition):
    return jnp.where(condition, 1.0, 0.0).astype(F32)


def one_hot_matmul(value, matrix):
    count = value.shape[0]
    first = value.astype(BF16).astype(F32)
    rest = value - first
    second = rest.astype(BF16).astype(F32)
    parts = jnp.concatenate([first, second, rest - second], axis=0).astype(BF16)
    product = jnp.dot(parts, matrix, preferred_element_type=F32)
    return product[0:count] + product[count : 2 * count] + product[2 * count :]


def restrict_block(source, first, planes, rows, stride, work):
    field = source[first : first + planes, 0:rows, :]
    field = field.reshape(planes // 2, 2, rows, 128)
    work[0 : planes // 2, 0:rows, :] = field[:, 0] + field[:, 1]
    half = rows // 2
    both = (
        work[0 : planes // 2, pl.ds(0, half, stride=2), :]
        + work[0 : planes // 2, pl.ds(1, half, stride=2), :]
    )
    lane = iota(both.shape, 2)
    even = (lane // stride) % 2 == 0
    other = jnp.where(even, roll(both, -stride, 2), roll(both, stride, 2))
    return (both + other) * 0.125


def fine_coefficients(level, dens, coef, low, high):
    own = ROWS[level]
    scale = 2.0 * 0.25**level
    stride = 2**level
    face_z, face_x, face_y, diagonal, inverse = coef
    shape = (own + 16, 128)

    def compress(value):
        tail = jnp.where(
            iota((8, 128), 0) < 4, value[own : own + 8], value[own + 8 : own + 16]
        )
        return jnp.concatenate([value[0:own], tail], axis=0)

    def plane(p, down):
        here = dens[p + 1]
        above = dens[p + 2]
        lane = iota(shape, 1)
        right = roll(here, -1, 0)
        up = scale * invert(jnp.maximum(here + above, 0.1))
        x_face = scale * invert(jnp.maximum(here + right, 0.1))
        ahead = jnp.where(lane >= 128 - stride, 0.0, roll(here, -stride, 1))
        behind = jnp.where(lane < stride, 0.0, roll(here, stride, 1))
        y_face = scale * invert(jnp.maximum(here + ahead, 0.1))
        y_back = scale * invert(jnp.maximum(here + behind, 0.1))
        diag = up + down + x_face + roll(x_face, 1, 0) + y_face + y_back
        inside = here > 0.0
        face_z[p] = compress(jnp.where(inside & (above > 0.0), up, 0.0))
        face_x[p] = compress(jnp.where(inside & (right > 0.0), x_face, 0.0))
        face_y[p] = compress(jnp.where(lane >= 128 - stride, 0.0, y_face))
        diagonal[p] = compress(diag)
        inverse[p] = compress(invert(diag))
        return up

    lowest = scale * invert(jnp.maximum(dens[low] + dens[low + 1], 0.1))
    lax.fori_loop(low, high, plane, lowest, unroll=True)


def fine_apply(field, p, coef, q, stride):
    face_z, face_x, face_y, diagonal, _ = coef
    here = field[p]
    x_face = face_x[q]
    y_face = face_y[q]
    result = diagonal[q] * here
    result = result - face_z[q] * field[p + 1] - face_z[q - 1] * field[p - 1]
    result = result - x_face * roll(here, -1, 0) - roll(x_face * here, 1, 0)
    result = result - y_face * roll(here, -stride, 1) - roll(y_face * here, stride, 1)
    return result


def fine_smooth(level, source, coef, remain, updates, answer):
    planes = PLANES[level] + 8
    stride = 2**level
    inverse = coef[4]
    first, steps = chebyshev_constants(0.5)
    d0, d1, d2 = updates

    def start(p, carry):
        d0[p] = source[p] * inverse[p] * first
        return carry

    lax.fori_loop(0, planes, start, 0, unroll=True)
    chain = (d0, d1, d2)
    for sweep in range(3):
        old = chain[sweep]
        keep, add = steps[sweep]

        def step(p, carry, sweep=sweep, old=old, keep=keep, add=add):
            left = source[p] if sweep == 0 else remain[p]
            left = left - fine_apply(old, p, coef, p, stride)
            new = keep * old[p] + add * (left * inverse[p])
            if sweep < 2:
                remain[p] = left
                chain[sweep + 1][p] = new
            else:
                answer[p] = d0[p] + d1[p] + d2[p] + new
            return carry

        lax.fori_loop(sweep + 1, planes - sweep - 1, step, 0, unroll=True)


def packed_coefficients(dens, ny, nx, scale):
    rows = dens.shape[0]
    z = iota(dens.shape, 0)
    lane = iota(dens.shape, 1)
    y = lane % ny
    x = lane // ny
    scale = 2.0 * scale

    def neighbour(shift, axis, outside):
        return jnp.where(outside, 0.0, roll(dens, shift, axis))

    above = neighbour(-1, 0, z == rows - 1)
    below = neighbour(1, 0, z == 0)
    right = neighbour(-ny, 1, x >= nx - 1)
    left = neighbour(ny, 1, x == 0)
    ahead = neighbour(-1, 1, y == ny - 1)
    behind = neighbour(1, 1, y == 0)

    def face(other):
        return scale * invert(jnp.maximum(dens + other, 0.1))

    up, x_face, y_face = face(above), face(right), face(ahead)
    diagonal = up + face(below) + x_face + face(left) + y_face + face(behind)
    inside = dens > 0.0

    def inner(value, other):
        return jnp.where(inside & (other > 0.0), value, 0.0)

    return (
        inner(up, above),
        inner(x_face, right),
        inner(y_face, ahead),
        jnp.where(inside, diagonal, 0.0),
        jnp.where(inside, invert(diagonal), 0.0),
    )


def packed_apply(field, coef, ny):
    face_z, face_x, face_y, diagonal, _ = coef
    result = diagonal * field
    result = result - face_z * roll(field, -1, 0) - roll(face_z * field, 1, 0)
    result = result - face_x * roll(field, -ny, 1) - roll(face_x * field, ny, 1)
    result = result - face_y * roll(field, -1, 1) - roll(face_y * field, 1, 1)
    return result


def packed_smooth(source, coef, ny, lower):
    first, steps = chebyshev_constants(lower)
    inverse = coef[4]
    update = source * inverse * first
    answer = update
    for keep, add in steps:
        source = source - packed_apply(update, coef, ny)
        update = keep * update + add * (source * inverse)
        answer = answer + update
    return answer


SMALL = {
    ("a", 1): ((("D1", 5, 1, 4), ("D2", 5, 3, 2)), (("R1", 4, 0, 4), ("R2", 4, 2, 2))),
    ("a", -1): ((("D1", 5, 9, 4), ("D2", 5, 7, 2)), (("R1", 4, 8, 4), ("R2", 4, 6, 2))),
    ("a", 2): ((("D1", 8, 0, 1), ("D2", 5, 1, 2)), (("R2", 4, 0, 2),)),
    ("a", -2): ((("D1", 5, 13, 1), ("D2", 5, 9, 2)), (("R2", 4, 8, 2),)),
    ("a", 3): ((("D2", 6, 0, 1),), ()),
    ("a", -3): ((("D2", 5, 11, 1),), ()),
    ("b", 1): ((("D1", 5, 1, 4), ("D2", 5, 3, 2)), (("R1", 4, 0, 4), ("R2", 4, 2, 2))),
    ("b", -1): ((("D1", 5, 9, 4), ("D2", 5, 7, 2)), (("R1", 4, 8, 4), ("R2", 4, 6, 2))),
    ("b", 2): ((("D2", 5, 1, 2),), (("R2", 4, 0, 2),)),
    ("b", -2): ((("D2", 5, 9, 2),), (("R2", 4, 8, 2),)),
}
LARGE = {
    ("b", 1): ((("D0", 9, 1, 4),), (("R0", 9, 1, 3),)),
    ("b", -1): ((("D0", 5, 13, 4),), (("R0", 4, 12, 3),)),
}


WHOLE = (("D0", 1, 3, 0, 5), ("D0", -1, 0, 13, 5), ("R0", 1, 4, 0, 4), ("R0", -1, 0, 12, 4))


def whole_messages(with_density):
    return WHOLE if with_density else WHOLE[2:]


def z_messages(with_density):
    result = []
    for which, table in (("small", SMALL), ("large", LARGE)):
        for (part, shift), (density, field) in table.items():
            pieces = (density if with_density else ()) + field
            if pieces:
                result.append((which, part, shift, pieces))
    return result


def paired(name, tiles):
    return name[1] != "0" and tiles % 2 == 0


def piece_tiles(part, piece):
    name, _, _, count = piece
    tiles = count * (ROWS[int(name[1])] // 8 if part == "a" else 1)
    return tiles // 2 if paired(name, tiles) else tiles


def x_pieces(with_density):
    result = []
    for level in range(3):
        count = PLANES[level]
        if with_density:
            result.append(("D%d" % level, count, count // 2 if level else count))
        result.append(("R%d" % level, count, (4, 1, 1)[level]))
    return result


def buffer_shapes(with_density):
    tiles = [sum(sent for _, _, sent in x_pieces(with_density))] * 2
    for _, part, _, pieces in z_messages(with_density):
        tiles.append(sum(piece_tiles(part, piece) for piece in pieces))
    return [pltpu.VMEM((count, 8, 128), F32) for count in tiles]


def whole_shapes(with_density):
    return [pltpu.VMEM((count, 32, 128), F32) for _, _, _, _, count in whole_messages(with_density)]


def n_halo(with_density):
    return 2 + len(z_messages(with_density))


def even_lanes(tiles):
    return iota((tiles, 8, 128), 2) % 2 == 0


def upper_rows(tiles):
    return iota((tiles, 8, 128), 1) < 4


def pack_lanes(block):
    half = block.shape[0] // 2
    return jnp.where(even_lanes(half), block[0:half], block[half:])


def unpack_lanes(block):
    even = even_lanes(block.shape[0])
    return jnp.concatenate(
        [jnp.where(even, block, roll(block, 1, 2)), jnp.where(even, roll(block, -1, 2), block)],
        axis=0,
    )


class Phase:
    def __init__(self, refs, place, with_density, buffers, coarse, send_sem, recv_sem):
        send, recv, whole = buffers
        self.whole_in = whole
        self.whole = whole_messages(with_density)
        self.refs = refs
        self.k, self.s, self.nf, self.ns = place
        self.dense = with_density
        self.send, self.recv = send, recv
        self.row, self.row_in, self.sub_in, self.group, self.low, self.high, self.quad_in = coarse
        self.send_sem, self.recv_sem = send_sem, recv_sem
        self.started = []
        self.count = 0
        self.z = z_messages(with_density)
        self.copies = {}
        self.i = self.k % ROW
        self.g = self.k // ROW
        self.ng = self.nf // ROW

    def start(self, source, target, k, s, shift=0):
        index = self.count
        self.count += 1
        copy = pltpu.make_async_remote_copy(
            src_ref=source,
            dst_ref=target,
            send_sem=self.send_sem.at[index],
            recv_sem=self.recv_sem.at[index],
            device_id=(k, s),
            device_id_type=MESH,
        )
        self.when(self.has_target(shift), copy.start)
        self.started.append((copy, shift))
        return copy

    def has_target(self, shift):
        if shift == 0:
            return None
        return self.k < self.nf - shift if shift > 0 else self.k >= -shift

    def has_source(self, shift):
        return self.has_target(-shift)

    def when(self, condition, action):
        if condition is None:
            action()
        else:
            pl.when(condition)(action)

    def start_whole(self, fields):
        self.whole_copies = []
        for index, (name, shift, first, _, count) in enumerate(self.whole):
            target = (self.k + shift + self.nf) % self.nf
            ref, lead = fields[name]
            source = ref.at[lead + first : lead + first + count, 0:32, :]
            self.whole_copies.append(
                self.start(source, self.whole_in[index], target, self.s, shift)
            )

    def unpack_whole(self):
        for index, (name, shift, _, target, count) in enumerate(self.whole):
            self.when(self.has_source(shift), self.whole_copies[index].wait_recv)
        for index, (name, shift, _, target, count) in enumerate(self.whole):
            block = jnp.where(self.has_source(shift), self.whole_in[index][...], 0.0)
            self.refs[name][target : target + count, 0:32, :] = block

    def pack_x(self):
        for which in (0, 1):
            at = 0
            for name, count, sent in x_pieces(self.dense):
                level = int(name[1])
                lead = 5 if name[0] == "D" else 4
                row = ROWS[level] - 8 if which == 0 else 0
                block = self.refs[name][lead : lead + count, row : row + 8, :]
                if level:
                    block = pack_lanes(block)
                if block.shape[0] > sent:
                    near, far = block[0:sent], roll(block[sent:], 4, 1)
                    upper = upper_rows(sent)
                    if which == 0:
                        block = jnp.where(upper, far, near)
                    else:
                        block = jnp.where(upper, near, far)
                self.send[which][at : at + sent] = block
                at += sent

    def start_x(self):
        up, down = (self.s + 1) % self.ns, (self.s + self.ns - 1) % self.ns
        self.x_copies = [
            self.start(self.send[0], self.recv[0], self.k, up),
            self.start(self.send[1], self.recv[1], self.k, down),
        ]

    def unpack_x(self):
        for copy in self.x_copies:
            copy.wait_recv()
        low_in = jnp.where(self.s > 0, 1.0, 0.0).astype(F32)
        high_in = jnp.where(self.s < self.ns - 1, 1.0, 0.0).astype(F32)
        at = 0
        for name, count, sent in x_pieces(self.dense):
            level = int(name[1])
            own = ROWS[level]
            lead = 5 if name[0] == "D" else 4
            low, high = self.recv[0][at : at + sent], self.recv[1][at : at + sent]
            at += sent
            ref = self.refs[name]
            if name[0] == "D":
                if level:
                    low, high = unpack_lanes(low), unpack_lanes(high)
                ref[lead : lead + count, own : own + 8, :] = high * high_in
                ref[lead : lead + count, own + 8 : own + 16, :] = low * low_in
                continue
            upper = upper_rows(sent)
            block = jnp.where(upper, high, low)
            if sent < (count // 2 if level else count):
                far = roll(jnp.where(upper, low, high), 4, 1)
                block = jnp.concatenate([block, far], axis=0)
            if level:
                block = unpack_lanes(block)
            ref[lead : lead + count, own : own + 8, :] = block

    def pack_z(self, part):
        for index, (_, kind, _, pieces) in enumerate(self.z):
            if kind != part:
                continue
            at = 0
            for piece in pieces:
                name, source, _, count = piece
                ref, own = self.refs[name], ROWS[int(name[1])]
                if part == "a":
                    block = ref[source : source + count, 0:own, :]
                    block = block.reshape(count * own // 8, 8, 128)
                else:
                    block = ref[source : source + count, own : own + 8, :]
                    if name[0] == "D":
                        low = ref[source : source + count, own + 8 : own + 16, :]
                        block = jnp.where(upper_rows(count), block, low)
                if paired(name, block.shape[0]):
                    block = pack_lanes(block)
                self.send[2 + index][at : at + block.shape[0]] = block
                at += block.shape[0]

    def start_z(self, which, part):
        for index, (size, kind, shift, _) in enumerate(self.z):
            if (size, kind) == (which, part):
                target = (self.k + shift + self.nf) % self.nf
                self.copies[index] = self.start(
                    self.send[2 + index], self.recv[2 + index], target, self.s, shift
                )

    def unpack_z(self, which):
        for index, (size, _, shift, _) in enumerate(self.z):
            if size == which:
                self.when(self.has_source(shift), self.copies[index].wait_recv)
        for index, (size, part, shift, pieces) in enumerate(self.z):
            if size != which:
                continue
            inside = self.has_source(shift)
            at = 0
            for piece in pieces:
                name, _, target, count = piece
                ref, own = self.refs[name], ROWS[int(name[1])]
                sent = piece_tiles(part, piece)
                block = jnp.where(inside, self.recv[2 + index][at : at + sent], 0.0)
                at += sent
                if sent < (count * own // 8 if part == "a" else count):
                    block = unpack_lanes(block)
                if part == "a":
                    ref[target : target + count, 0:own, :] = block.reshape(count, own, 128)
                else:
                    ref[target : target + count, own : own + 8, :] = block
                    if name[0] == "D":
                        ref[target : target + count, own + 8 : own + 16, :] = block

    def pack_row(self, fields, pair, spread_row):
        for index, field in enumerate(fields):
            pillar = jnp.sum(field, axis=0).reshape(4, 8, 128)
            pair[4 * index : 4 * index + 4, :] = jnp.sum(pillar, axis=1) * 0.125**3
        spread = one_hot_matmul(pair[...], spread_row[...])[0:8]
        mine = iota((8, 128), 1) // 16 == iota((8, 128), 0)
        row = jnp.sum(jnp.where(mine, spread, 0.0), axis=0, keepdims=True)
        self.row[...] = row
        self.row_in[self.i] = row

    def start_rows(self):
        self.row_copies = []
        for delta in range(1, ROW):
            target = self.g * ROW + (self.i + delta) % ROW
            self.row_copies.append(
                self.start(self.row, self.row_in.at[self.i], target, self.s)
            )

    def start_subs(self):
        for copy in self.row_copies:
            copy.wait_recv()
        line = iota((8, 128), 0)
        tile = jnp.zeros((8, 128), F32)
        for index in range(ROW):
            tile = jnp.where(line == index, self.row_in[index], tile)
        self.sub_in[self.s] = tile
        self.sub_copies = []
        for delta in range(1, 4):
            self.sub_copies.append(
                self.start(
                    self.sub_in.at[self.s],
                    self.sub_in.at[self.s],
                    self.k,
                    (self.s + delta) % self.ns,
                )
            )

    def start_groups(self, work, pool):
        for copy in self.sub_copies:
            copy.wait_recv()
        tiles = [self.sub_in[index] for index in range(4)]
        turned = [roll(tile, 64, 1) for tile in tiles]
        left = iota((8, 128), 1) < 64
        fields = []
        for half in range(2):
            a, b = 2 * half, 2 * half + 1
            fields.append(jnp.where(left, tiles[a], turned[b]))
        if self.dense:
            for half in range(2):
                a, b = 2 * half, 2 * half + 1
                fields.append(jnp.where(left, turned[a], tiles[b]))
        for index, field in enumerate(fields):
            self.group[index] = field
        up = ((self.g + 1) % self.ng) * ROW + self.i
        down = ((self.g + self.ng - 1) % self.ng) * ROW + self.i
        self.group_copies = [
            self.start(self.group, self.low, up, self.s),
            self.start(self.group, self.high, down, self.s),
        ]
        wide = jnp.concatenate(fields, axis=1)
        wide = jnp.concatenate([wide, jnp.zeros(wide.shape, F32)], axis=0)
        sums = one_hot_matmul(wide, pool[0 : wide.shape[1], :])[0:8]
        work[...] = sums[:, 0:128]
        four = (work[pl.ds(0, 4, stride=2), :] + work[pl.ds(1, 4, stride=2), :]) * 0.125
        self.quad_in[self.g, 0:4, :] = four
        five = sums[:, 128:256]
        five = five + roll(five, -1, 0)
        five = (five + roll(five, -2, 0)) * (0.125 * 0.125)
        line = iota((8, 128), 0)
        five = jnp.where(line % 2 == 0, five[0:1], five[4:5])
        self.quad_in[self.g, 4:8, :] = five[4:8]
        half = self.ng // 4
        for delta in sorted(range(1, self.ng), key=lambda delta: abs(delta % (2 * half) - half)):
            target = ((self.g + delta) % self.ng) * ROW + self.i
            self.group_copies.append(
                self.start(
                    self.quad_in.at[self.g], self.quad_in.at[self.g], target, self.s
                )
            )

    def wait_groups(self):
        for copy in self.group_copies:
            copy.wait_recv()

    def finish(self, first, last):
        for copy, shift in self.started[first:last]:
            self.when(self.has_target(shift), copy.wait_send)


def split_packed(value):
    left = iota(value.shape, 1) < 64
    return jnp.where(left, value, 0.0), jnp.where(left, roll(value, 64, 1), 0.0)


def build_matrices(pool, fan):
    line, lane = iota((128, 128), 0), iota((128, 128), 1)
    for half in range(4):
        x, y = line // 16 + 8 * (half % 2), line % 16
        rows = slice(128 * half, 128 * half + 128)
        home4 = (x // 2) * 8 + y // 2 + 64 * (half // 2)
        home5 = (x // 4) * 4 + y // 4 + 64 * (half // 2)
        pool[rows, 0:128] = one_hot(home4 == lane).astype(BF16)
        pool[rows, 128:256] = one_hot(home5 == lane).astype(BF16)
    three = one_hot(line % 16 == lane // 8).astype(BF16)
    fan[0:128, :] = three
    fan[128:256, :] = three
    fan[256:384, :] = one_hot(line % 8 == lane // 16).astype(BF16)
    fan[384:512, :] = one_hot(line % 4 == lane // 32).astype(BF16)


def kernel(nf, ns, rhs, dens, solution, residual, *scratch):
    scratch = list(scratch)

    def take(count):
        taken = scratch[:count]
        del scratch[:count]
        return taken

    refs = {}
    for name in ("D0", "D1", "D2", "R0", "R1", "R2"):
        (refs[name],) = take(1)
    fine_coef = [take(5) for _ in range(3)]
    remains = take(3)
    updates = [take(3) for _ in range(3)]
    answers = take(3)
    (work, tile_work, pair, sol, spread) = take(5)
    (spread_row, pool, fan, keep3, keep4, keep5, dens3) = take(7)
    coarse_coef = [take(5) for _ in range(3)]
    phases = []
    k, s = lax.axis_index("fine"), lax.axis_index("sub")
    for with_density in (True, False):
        count = n_halo(with_density)
        buffers = take(count), take(count), take(len(whole_messages(with_density)))
        coarse = take(7)
        send_sem, recv_sem = take(2)
        phases.append(
            Phase(refs, (k, s, nf, ns), with_density, buffers, coarse, send_sem, recv_sem)
        )
    ng = nf // ROW
    i, g = k % ROW, k // ROW

    barrier = pltpu.get_barrier_semaphore()
    partners = []
    for shift in (1, 2, 3):
        partners += [((k + shift) % nf, s), ((k + nf - shift) % nf, s)]
    partners += [(k, (s + delta) % ns) for delta in range(1, ns)]
    partners += [(g * ROW + (i + delta) % ROW, s) for delta in range(1, ROW)]
    partners += [(((g + delta) % ng) * ROW + i, s) for delta in range(1, ng)]
    for partner in partners:
        pl.semaphore_signal(barrier, inc=1, device_id=partner, device_id_type=MESH)

    for level in range(3):
        for name, lead in (("D", 5), ("R", 4)):
            ref = refs[name + str(level)]
            planes, rows, _ = ref.shape
            blank = jnp.zeros((lead, rows, 128), F32)
            ref[0:lead] = blank
            ref[planes - lead : planes] = blank
    for ref in (keep4, keep5):
        rows = ref.shape[0]
        ref[0:8, :] = jnp.zeros((8, 128), F32)
        ref[rows - 8 : rows, :] = jnp.zeros((8, 128), F32)
    pair[...] = jnp.zeros((16, 128), F32)

    def restrict_all(name, lead):
        for level in range(2):
            refs[name + str(level + 1)][
                lead : lead + PLANES[level + 1], 0 : ROWS[level + 1], :
            ] = restrict_block(
                refs[name + str(level)], lead, PLANES[level], ROWS[level], 2**level, work
            )

    def coefficients(level, low, high):
        fine_coefficients(level, refs["D" + str(level)], fine_coef[level], low, high)

    def smooth(level):
        fine_smooth(
            level,
            refs["R" + str(level)],
            fine_coef[level],
            remains[level],
            updates[level],
            answers[level],
        )

    line, lane = iota((128, 128), 0), iota((128, 128), 1)
    spread_row[...] = one_hot(line // 8 == lane % 16).astype(BF16)
    refs["R0"][4:12, 0:32, :] = rhs[...]
    refs["D0"][5:13, 0:32, :] = dens[...]

    for cycle in range(CYCLES):
        phase = phases[cycle]
        if cycle == 0:
            phase.pack_row((rhs[...], dens[...]), pair, spread_row)
            pl.semaphore_wait(barrier, len(partners))
        else:
            phase.pack_row((refs["R0"][4:12, 0:32, :],), pair, spread_row)
        phase.start_rows()
        if cycle == 0:
            phase.start_whole({"D0": (dens, 0), "R0": (rhs, 0)})
        else:
            phase.start_whole({"R0": (refs["R0"], 4)})
        restrict_all("R", 4)
        if cycle == 0:
            restrict_all("D", 5)
        phase.pack_x()
        phase.start_x()
        phase.pack_z("a")
        phase.start_z("small", "a")
        if cycle == 0:
            build_matrices(pool, fan)
        phase.start_subs()
        phase.unpack_x()
        phase.pack_z("b")
        phase.start_z("small", "b")
        phase.start_z("large", "b")
        phase.start_groups(tile_work, pool)
        if cycle == 1:
            phases[0].finish(0, None)
        if cycle == 0:
            coefficients(0, 5, 11)
        phase.unpack_z("small")
        for level in (2, 1):
            if cycle == 0:
                coefficients(level, 0, PLANES[level] + 8)
            smooth(level)
        if cycle == 1:
            phase.finish(0, -(ng + 1))
        phase.wait_groups()

        tiles = [phase.quad_in[index] for index in range(ng)]
        line = iota((8, 128), 0)
        packed4, packed5 = [], []
        for index in range(0, ng, 2):
            packed4.append(jnp.where(line < 4, tiles[index], roll(tiles[index + 1], 4, 0)))
        for index in range(0, ng, 4):
            first = jnp.where(line < 6, tiles[index], tiles[index + 1])
            second = jnp.where(line < 6, tiles[index + 2], tiles[index + 3])
            packed5.append(jnp.where(line < 4, roll(first, 4, 0), second))
        source4, density4 = split_packed(jnp.concatenate(packed4, axis=0))
        source5, density5 = split_packed(jnp.concatenate(packed5, axis=0))
        if cycle == 0:
            low_in = jnp.where(g > 0, 1.0, 0.0).astype(F32)
            high_in = jnp.where(g < ng - 1, 1.0, 0.0).astype(F32)
            for half in range(2):
                cols = slice(128 * half, 128 * half + 128)
                dens3[0:8, cols] = phase.low[2 + half] * low_in
                dens3[8:16, cols] = phase.group[2 + half]
                dens3[16:24, cols] = phase.high[2 + half] * high_in
            for index, (dens, ny) in enumerate(
                ((dens3[...], 16), (density4, 8), (density5, 4))
            ):
                values = packed_coefficients(dens, ny, ny, 0.25 ** (3 + index))
                for ref, value in zip(coarse_coef[index], values):
                    ref[...] = value
        coef3, coef4, coef5 = ([ref[...] for ref in refs5] for refs5 in coarse_coef)
        total = jnp.sum(jnp.sum(source5, axis=0, keepdims=True), axis=1, keepdims=True)
        weight = jnp.sum(jnp.sum(coef5[3], axis=0, keepdims=True), axis=1, keepdims=True)
        n4, n5 = 4 * ng, 2 * ng
        keep5[8 : 8 + n5, :] = packed_smooth(source5, coef5, 4, 0.05) + total / weight
        keep4[8 : 8 + n4, :] = packed_smooth(source4, coef4, 8, 0.5)

        source3 = jnp.concatenate(
            [
                jnp.concatenate([phase.low[0], phase.low[1]], axis=1),
                jnp.concatenate([phase.group[0], phase.group[1]], axis=1),
                jnp.concatenate([phase.high[0], phase.high[1]], axis=1),
            ],
            axis=0,
        )
        keep3[...] = packed_smooth(source3, coef3, 16, 0.5)

        row = iota((16, 512), 0)
        lane = iota((16, 512), 1)
        x3 = row // 2 + jnp.where(row < 12, 0, -8) + (4 * s + 4)
        inside = (x3 >= 4) & (x3 < 20)
        x_lane = jnp.where(
            lane < 256, lane // 16, jnp.where(lane < 384, (lane - 256) // 8, (lane - 384) // 4)
        )
        x_row = jnp.where(lane < 256, x3 - 4, jnp.where(lane < 384, x3 // 2 - 2, x3 // 4 - 1))
        chosen = (x_lane == x_row) & inside
        picked = []
        for t in range(3):
            parts = jnp.concatenate(
                [
                    keep3[pl.ds(7 + i + t, 1), :],
                    keep4[pl.ds((k + 1 + t) // 2 + 7, 1), :],
                    keep5[pl.ds((k + 3 + t) // 4 + 7, 1), :],
                ],
                axis=1,
            )
            picked.append(jnp.where(chosen, parts, 0.0))
        spread[0:3, 0:16, :] = one_hot_matmul(
            jnp.concatenate(picked, axis=0), fan[...]
        ).reshape(3, 16, 128)

        for level in (2, 1):
            rows = ROWS[level]
            answer = answers[level]
            planes = PLANES[level] + 2
            coarse = jnp.concatenate(
                [spread[(p + 1) // 2 : (p + 1) // 2 + 1, 0 : rows + 8, :] for p in range(planes)],
                axis=0,
            )
            value = answer[3 : 3 + planes] + coarse
            own, ends = value[:, 0:rows, :], value[:, rows : rows + 8, :]
            spread[0:planes, pl.ds(0, rows, stride=2), :] = own
            spread[0:planes, pl.ds(1, rows, stride=2), :] = own
            spread[0:planes, 2 * rows : 2 * rows + 8, :] = jnp.where(
                upper_rows(planes), ends[:, 0:1, :], ends[:, 7:8, :]
            )

        phase.unpack_whole()
        phase.unpack_z("large")
        if cycle == 0:
            coefficients(0, 0, 5)
            coefficients(0, 11, 16)
        smooth(0)

        def advance(p, carry, cycle=cycle):
            step = 0.4 * (answers[0][p + 3] + spread[(p + 1) // 2])
            sol[p] = step if cycle == 0 else sol[p] + step
            return carry

        lax.fori_loop(0, PLANES[0] + 2, advance, 0, unroll=True)

        def defect(p, carry, cycle=cycle):
            applied = fine_apply(sol, p + 1, fine_coef[0], p + 4, 1)
            left = rhs[p] - applied[0:32, :]
            if cycle == 0:
                refs["R0"][p + 4, 0:32, :] = left
            else:
                residual[p] = left
                solution[p] = sol[p + 1, 0:32, :]
            return carry

        lax.fori_loop(0, PLANES[0], defect, 0, unroll=True)

    phases[1].finish(-(ng + 1), None)


def scratch_shapes(ng):
    shapes = []
    for level in range(3):
        shapes.append(pltpu.VMEM((PLANES[level] + 10, ROWS[level] + 16, 128), F32))
    extents = [(PLANES[level] + 8, ROWS[level] + 8, 128) for level in range(3)]
    shapes += [pltpu.VMEM(extent, F32) for extent in extents]
    for extent in extents:
        shapes += [pltpu.VMEM(extent, F32)] * 5
    shapes += [pltpu.VMEM(extent, F32) for extent in extents]
    for extent in extents:
        shapes += [pltpu.VMEM(extent, F32)] * 3
    shapes += [pltpu.VMEM(extent, F32) for extent in extents]
    shapes += [
        pltpu.VMEM((4, 32, 128), F32),
        pltpu.VMEM((8, 128), F32),
        pltpu.VMEM((16, 128), F32),
        pltpu.VMEM((10, 40, 128), F32),
        pltpu.VMEM((6, 40, 128), F32),
        pltpu.VMEM((128, 128), BF16),
        pltpu.VMEM((512, 256), BF16),
        pltpu.VMEM((512, 128), BF16),
        pltpu.VMEM((24, 256), F32),
        pltpu.VMEM((4 * ng + 16, 128), F32),
        pltpu.VMEM((2 * ng + 16, 128), F32),
        pltpu.VMEM((24, 256), F32),
    ]
    for extent in ((24, 256), (4 * ng, 128), (2 * ng, 128)):
        shapes += [pltpu.VMEM(extent, F32)] * 5
    for with_density in (True, False):
        halo = buffer_shapes(with_density)
        shapes += halo + halo + whole_shapes(with_density)
        tiles = 4 if with_density else 2
        shapes += [
            pltpu.VMEM((1, 128), F32),
            pltpu.VMEM((ROW, 1, 128), F32),
            pltpu.VMEM((4, 8, 128), F32),
            pltpu.VMEM((tiles, 8, 128), F32),
            pltpu.VMEM((tiles, 8, 128), F32),
            pltpu.VMEM((tiles, 8, 128), F32),
            pltpu.VMEM((ng, 8, 128), F32),
        ]
        copies = n_halo(with_density) + len(whole_messages(with_density))
        copies += (ROW - 1) + 3 + 2 + (ng - 1)
        shapes += [pltpu.SemaphoreType.DMA((copies,)), pltpu.SemaphoreType.DMA((copies,))]
    return shapes


def solution(mesh):
    nf, ns = mesh.shape["fine"], mesh.shape["sub"]

    def body(rhs, density):
        return pl.pallas_call(
            functools.partial(kernel, nf, ns),
            out_shape=(
                jax.ShapeDtypeStruct(rhs.shape, F32),
                jax.ShapeDtypeStruct(rhs.shape, F32),
            ),
            in_specs=[pl.BlockSpec(memory_space=pltpu.VMEM)] * 2,
            out_specs=[pl.BlockSpec(memory_space=pltpu.VMEM)] * 2,
            scratch_shapes=scratch_shapes(nf // ROW),
            compiler_params=pltpu.CompilerParams(
                collective_id=0, has_side_effects=True, vmem_limit_bytes=32 * 1024 * 1024
            ),
        )(rhs, density)

    return jax.shard_map(
        body,
        mesh=mesh,
        in_specs=(P("fine", "sub", None), P("fine", "sub", None)),
        out_specs=(P("fine", "sub", None), P("fine", "sub", None)),
        check_vma=False,
    )
```

```python
import functools

import jax
import jax.numpy as jnp
from jax import lax
from jax.experimental import pallas as pl
from jax.experimental.pallas import tpu as pltpu
from jax.sharding import PartitionSpec as P

DEGREE = 4
CYCLES = 2
MESH = pl.DeviceIdType.MESH
F32 = jnp.float32
BF16 = jnp.bfloat16
ROW = 8
PLANES = (8, 4, 2)
ROWS = (32, 16, 8)


def chebyshev_constants(lower):
    upper = 2.0
    theta = 0.5 * (upper + lower)
    delta = 0.5 * (upper - lower)
    sigma = theta / delta
    ratio = 1.0 / sigma
    steps = []
    for _ in range(DEGREE - 1):
        next_ratio = 1.0 / (2.0 * sigma - ratio)
        steps.append((next_ratio * ratio, 2.0 * next_ratio / delta))
        ratio = next_ratio
    return 1.0 / theta, steps


def iota(shape, dim):
    return lax.broadcasted_iota(jnp.int32, shape, dim)


def roll(value, shift, axis):
    return pltpu.roll(value, shift % value.shape[axis], axis)


def invert(value):
    return pltpu.reciprocal(value, full_range=False)


def one_hot(condition):
    return jnp.where(condition, 1.0, 0.0).astype(F32)


def one_hot_matmul(value, matrix):
    count = value.shape[0]
    first = value.astype(BF16).astype(F32)
    rest = value - first
    second = rest.astype(BF16).astype(F32)
    parts = jnp.concatenate([first, second, rest - second], axis=0).astype(BF16)
    product = jnp.dot(parts, matrix, preferred_element_type=F32)
    return product[0:count] + product[count : 2 * count] + product[2 * count :]


def restrict_block(source, first, planes, rows, stride, work):
    field = source[first : first + planes, 0:rows, :]
    field = field.reshape(planes // 2, 2, rows, 128)
    work[0 : planes // 2, 0:rows, :] = field[:, 0] + field[:, 1]
    half = rows // 2
    both = (
        work[0 : planes // 2, pl.ds(0, half, stride=2), :]
        + work[0 : planes // 2, pl.ds(1, half, stride=2), :]
    )
    lane = iota(both.shape, 2)
    even = (lane // stride) % 2 == 0
    other = jnp.where(even, roll(both, -stride, 2), roll(both, stride, 2))
    return (both + other) * 0.125


def fine_coefficients(level, dens, coef, low, high):
    own = ROWS[level]
    scale = 2.0 * 0.25**level
    stride = 2**level
    face_z, face_x, face_y, diagonal, inverse = coef
    shape = (own + 16, 128)

    def compress(value):
        tail = jnp.where(
            iota((8, 128), 0) < 4, value[own : own + 8], value[own + 8 : own + 16]
        )
        return jnp.concatenate([value[0:own], tail], axis=0)

    def plane(p, down):
        here = dens[p + 1]
        above = dens[p + 2]
        lane = iota(shape, 1)
        right = roll(here, -1, 0)
        up = scale * invert(jnp.maximum(here + above, 0.1))
        x_face = scale * invert(jnp.maximum(here + right, 0.1))
        ahead = jnp.where(lane >= 128 - stride, 0.0, roll(here, -stride, 1))
        behind = jnp.where(lane < stride, 0.0, roll(here, stride, 1))
        y_face = scale * invert(jnp.maximum(here + ahead, 0.1))
        y_back = scale * invert(jnp.maximum(here + behind, 0.1))
        diag = up + down + x_face + roll(x_face, 1, 0) + y_face + y_back
        inside = here > 0.0
        face_z[p] = compress(jnp.where(inside & (above > 0.0), up, 0.0))
        face_x[p] = compress(jnp.where(inside & (right > 0.0), x_face, 0.0))
        face_y[p] = compress(jnp.where(lane >= 128 - stride, 0.0, y_face))
        diagonal[p] = compress(diag)
        inverse[p] = compress(invert(diag))
        return up

    lowest = scale * invert(jnp.maximum(dens[low] + dens[low + 1], 0.1))
    lax.fori_loop(low, high, plane, lowest, unroll=True)


def fine_apply(field, p, coef, q, stride):
    face_z, face_x, face_y, diagonal, _ = coef
    here = field[p]
    x_face = face_x[q]
    y_face = face_y[q]
    result = diagonal[q] * here
    result = result - face_z[q] * field[p + 1] - face_z[q - 1] * field[p - 1]
    result = result - x_face * roll(here, -1, 0) - roll(x_face * here, 1, 0)
    result = result - y_face * roll(here, -stride, 1) - roll(y_face * here, stride, 1)
    return result


def fine_smooth(level, source, coef, remain, updates, answer):
    planes = PLANES[level] + 8
    stride = 2**level
    inverse = coef[4]
    first, steps = chebyshev_constants(0.5)
    d0, d1, d2 = updates

    def start(p, carry):
        d0[p] = source[p] * inverse[p] * first
        return carry

    lax.fori_loop(0, planes, start, 0, unroll=True)
    chain = (d0, d1, d2)
    for sweep in range(3):
        old = chain[sweep]
        keep, add = steps[sweep]

        def step(p, carry, sweep=sweep, old=old, keep=keep, add=add):
            left = source[p] if sweep == 0 else remain[p]
            left = left - fine_apply(old, p, coef, p, stride)
            new = keep * old[p] + add * (left * inverse[p])
            if sweep < 2:
                remain[p] = left
                chain[sweep + 1][p] = new
            else:
                answer[p] = d0[p] + d1[p] + d2[p] + new
            return carry

        lax.fori_loop(sweep + 1, planes - sweep - 1, step, 0, unroll=True)


def packed_coefficients(dens, ny, nx, scale):
    rows = dens.shape[0]
    z = iota(dens.shape, 0)
    lane = iota(dens.shape, 1)
    y = lane % ny
    x = lane // ny
    scale = 2.0 * scale

    def neighbour(shift, axis, outside):
        return jnp.where(outside, 0.0, roll(dens, shift, axis))

    above = neighbour(-1, 0, z == rows - 1)
    below = neighbour(1, 0, z == 0)
    right = neighbour(-ny, 1, x >= nx - 1)
    left = neighbour(ny, 1, x == 0)
    ahead = neighbour(-1, 1, y == ny - 1)
    behind = neighbour(1, 1, y == 0)

    def face(other):
        return scale * invert(jnp.maximum(dens + other, 0.1))

    up, x_face, y_face = face(above), face(right), face(ahead)
    diagonal = up + face(below) + x_face + face(left) + y_face + face(behind)
    inside = dens > 0.0

    def inner(value, other):
        return jnp.where(inside & (other > 0.0), value, 0.0)

    return (
        inner(up, above),
        inner(x_face, right),
        inner(y_face, ahead),
        jnp.where(inside, diagonal, 0.0),
        jnp.where(inside, invert(diagonal), 0.0),
    )


def packed_apply(field, coef, ny):
    face_z, face_x, face_y, diagonal, _ = coef
    result = diagonal * field
    result = result - face_z * roll(field, -1, 0) - roll(face_z * field, 1, 0)
    result = result - face_x * roll(field, -ny, 1) - roll(face_x * field, ny, 1)
    result = result - face_y * roll(field, -1, 1) - roll(face_y * field, 1, 1)
    return result


def packed_smooth(source, coef, ny, lower):
    first, steps = chebyshev_constants(lower)
    inverse = coef[4]
    update = source * inverse * first
    answer = update
    for keep, add in steps:
        source = source - packed_apply(update, coef, ny)
        update = keep * update + add * (source * inverse)
        answer = answer + update
    return answer


PIECES = {
    ("a", 1): ((("D1", 5, 1, 4), ("D2", 5, 3, 2)), (("R1", 4, 0, 4), ("R2", 4, 2, 2))),
    ("a", -1): ((("D1", 5, 9, 4), ("D2", 5, 7, 2)), (("R1", 4, 8, 4), ("R2", 4, 6, 2))),
    ("a", 2): ((("D1", 8, 0, 1), ("D2", 5, 1, 2)), (("R2", 4, 0, 2),)),
    ("a", -2): ((("D1", 5, 13, 1), ("D2", 5, 9, 2)), (("R2", 4, 8, 2),)),
    ("a", 3): ((("D2", 6, 0, 1),), ()),
    ("a", -3): ((("D2", 5, 11, 1),), ()),
    ("b", 1): (
        (("D0", 9, 1, 4), ("D1", 5, 1, 4), ("D2", 5, 3, 2)),
        (("R0", 9, 1, 3), ("R1", 4, 0, 4), ("R2", 4, 2, 2)),
    ),
    ("b", -1): (
        (("D0", 5, 13, 4), ("D1", 5, 9, 4), ("D2", 5, 7, 2)),
        (("R0", 4, 12, 3), ("R1", 4, 8, 4), ("R2", 4, 6, 2)),
    ),
    ("b", 2): ((("D2", 5, 1, 2),), (("R2", 4, 0, 2),)),
    ("b", -2): ((("D2", 5, 9, 2),), (("R2", 4, 8, 2),)),
}
WHOLE = (("D0", 1, 3, 0, 5), ("D0", -1, 0, 13, 5), ("R0", 1, 4, 0, 4), ("R0", -1, 0, 12, 4))


def whole_messages(with_density):
    return WHOLE if with_density else WHOLE[2:]


def z_messages(with_density):
    result = []
    for (part, shift), (density, field) in PIECES.items():
        pieces = (density if with_density else ()) + field
        if pieces:
            result.append((part, shift, pieces))
    return result


def paired(name, tiles):
    return name[1] != "0" and tiles % 2 == 0


def piece_tiles(part, piece):
    name, _, _, count = piece
    tiles = count * (ROWS[int(name[1])] // 8 if part == "a" else 1)
    return tiles // 2 if paired(name, tiles) else tiles


def x_pieces(with_density):
    result = []
    for level in range(3):
        count = PLANES[level]
        if with_density:
            result.append(("D%d" % level, count, count // 2 if level else count))
        result.append(("R%d" % level, count, (4, 1, 1)[level]))
    return result


def buffer_shapes(with_density):
    tiles = [sum(sent for _, _, sent in x_pieces(with_density))] * 2
    for part, _, pieces in z_messages(with_density):
        tiles.append(sum(piece_tiles(part, piece) for piece in pieces))
    return [pltpu.VMEM((count, 8, 128), F32) for count in tiles]


def whole_shapes(with_density):
    return [pltpu.VMEM((count, 32, 128), F32) for _, _, _, _, count in whole_messages(with_density)]


def n_halo(with_density):
    return 2 + len(z_messages(with_density))


def even_lanes(tiles):
    return iota((tiles, 8, 128), 2) % 2 == 0


def upper_rows(tiles):
    return iota((tiles, 8, 128), 1) < 4


def pack_lanes(block):
    half = block.shape[0] // 2
    return jnp.where(even_lanes(half), block[0:half], block[half:])


def unpack_lanes(block):
    even = even_lanes(block.shape[0])
    return jnp.concatenate(
        [jnp.where(even, block, roll(block, 1, 2)), jnp.where(even, roll(block, -1, 2), block)],
        axis=0,
    )


def partners_of(place):
    k, s, _, ns = place
    i, y, half = k % ROW, k // ROW % 8, k // (8 * ROW)
    depth, side = [], []
    for delta in (4, 3, 5, 2, 6, 1, 7):
        z = (half * ns + s + delta) % (2 * ns)
        depth.append((((z // ns) * 8 + y) * ROW + i, z % ns))
        side.append((delta, ((half * 8 + (y + delta) % 8) * ROW + i, s)))
    return depth, side


class Phase:
    def __init__(self, refs, place, with_density, buffers, coarse, send_sem, recv_sem):
        send, recv, whole = buffers
        self.whole_in = whole
        self.whole = whole_messages(with_density)
        self.refs = refs
        self.k, self.s, self.nf, self.ns = place
        self.dense = with_density
        self.send, self.recv = send, recv
        self.row, self.row_in, self.depth_in, self.side_in = coarse
        self.send_sem, self.recv_sem = send_sem, recv_sem
        self.started = []
        self.count = 0
        self.z = z_messages(with_density)
        self.copies = {}
        self.i = self.k % ROW
        self.g = self.k // ROW
        self.ng = self.nf // ROW
        self.y = self.g % 8
        self.z_at = self.g // 8 * self.ns + self.s
        self.depth_partners, self.side_partners = partners_of(place)

    def start(self, source, target, k, s, shift=0):
        index = self.count
        self.count += 1
        copy = pltpu.make_async_remote_copy(
            src_ref=source,
            dst_ref=target,
            send_sem=self.send_sem.at[index],
            recv_sem=self.recv_sem.at[index],
            device_id=(k, s),
            device_id_type=MESH,
        )
        self.when(self.has_target(shift), copy.start)
        self.started.append((copy, shift))
        return copy

    def has_target(self, shift):
        if shift == 0:
            return None
        return self.k < self.nf - shift if shift > 0 else self.k >= -shift

    def has_source(self, shift):
        return self.has_target(-shift)

    def when(self, condition, action):
        if condition is None:
            action()
        else:
            pl.when(condition)(action)

    def start_whole(self, fields):
        self.whole_copies = []
        for index, (name, shift, first, _, count) in enumerate(self.whole):
            target = (self.k + shift + self.nf) % self.nf
            ref, lead = fields[name]
            source = ref.at[lead + first : lead + first + count, 0:32, :]
            self.whole_copies.append(
                self.start(source, self.whole_in[index], target, self.s, shift)
            )

    def unpack_whole(self):
        for index, (name, shift, _, target, count) in enumerate(self.whole):
            self.when(self.has_source(shift), self.whole_copies[index].wait_recv)
        for index, (name, shift, _, target, count) in enumerate(self.whole):
            block = jnp.where(self.has_source(shift), self.whole_in[index][...], 0.0)
            self.refs[name][target : target + count, 0:32, :] = block

    def pack_x(self):
        for which in (0, 1):
            at = 0
            for name, count, sent in x_pieces(self.dense):
                level = int(name[1])
                lead = 5 if name[0] == "D" else 4
                row = ROWS[level] - 8 if which == 0 else 0
                block = self.refs[name][lead : lead + count, row : row + 8, :]
                if level:
                    block = pack_lanes(block)
                if block.shape[0] > sent:
                    near, far = block[0:sent], roll(block[sent:], 4, 1)
                    upper = upper_rows(sent)
                    if which == 0:
                        block = jnp.where(upper, far, near)
                    else:
                        block = jnp.where(upper, near, far)
                self.send[which][at : at + sent] = block
                at += sent

    def start_x(self):
        up, down = (self.s + 1) % self.ns, (self.s + self.ns - 1) % self.ns
        self.x_copies = [
            self.start(self.send[0], self.recv[0], self.k, up),
            self.start(self.send[1], self.recv[1], self.k, down),
        ]

    def unpack_x(self):
        for copy in self.x_copies:
            copy.wait_recv()
        low_in = jnp.where(self.s > 0, 1.0, 0.0).astype(F32)
        high_in = jnp.where(self.s < self.ns - 1, 1.0, 0.0).astype(F32)
        at = 0
        for name, count, sent in x_pieces(self.dense):
            level = int(name[1])
            own = ROWS[level]
            lead = 5 if name[0] == "D" else 4
            low, high = self.recv[0][at : at + sent], self.recv[1][at : at + sent]
            at += sent
            ref = self.refs[name]
            if name[0] == "D":
                if level:
                    low, high = unpack_lanes(low), unpack_lanes(high)
                ref[lead : lead + count, own : own + 8, :] = high * high_in
                ref[lead : lead + count, own + 8 : own + 16, :] = low * low_in
                continue
            upper = upper_rows(sent)
            block = jnp.where(upper, high, low)
            if sent < (count // 2 if level else count):
                far = roll(jnp.where(upper, low, high), 4, 1)
                block = jnp.concatenate([block, far], axis=0)
            if level:
                block = unpack_lanes(block)
            ref[lead : lead + count, own : own + 8, :] = block

    def pack_z(self, part):
        for index, (kind, _, pieces) in enumerate(self.z):
            if kind != part:
                continue
            at = 0
            for piece in pieces:
                name, source, _, count = piece
                ref, own = self.refs[name], ROWS[int(name[1])]
                if part == "a":
                    block = ref[source : source + count, 0:own, :]
                    block = block.reshape(count * own // 8, 8, 128)
                else:
                    block = ref[source : source + count, own : own + 8, :]
                    if name[0] == "D":
                        low = ref[source : source + count, own + 8 : own + 16, :]
                        block = jnp.where(upper_rows(count), block, low)
                if paired(name, block.shape[0]):
                    block = pack_lanes(block)
                self.send[2 + index][at : at + block.shape[0]] = block
                at += block.shape[0]

    def start_z(self, part):
        for index, (kind, shift, _) in enumerate(self.z):
            if kind == part:
                target = (self.k + shift + self.nf) % self.nf
                self.copies[index] = self.start(
                    self.send[2 + index], self.recv[2 + index], target, self.s, shift
                )

    def unpack_z(self):
        for index, (_, shift, _) in enumerate(self.z):
            self.when(self.has_source(shift), self.copies[index].wait_recv)
        for index, (part, shift, pieces) in enumerate(self.z):
            inside = self.has_source(shift)
            at = 0
            for piece in pieces:
                name, _, target, count = piece
                ref, own = self.refs[name], ROWS[int(name[1])]
                sent = piece_tiles(part, piece)
                block = jnp.where(inside, self.recv[2 + index][at : at + sent], 0.0)
                at += sent
                if sent < (count * own // 8 if part == "a" else count):
                    block = unpack_lanes(block)
                if part == "a":
                    ref[target : target + count, 0:own, :] = block.reshape(count, own, 128)
                else:
                    ref[target : target + count, own : own + 8, :] = block
                    if name[0] == "D":
                        ref[target : target + count, own + 8 : own + 16, :] = block

    def pack_row(self, fields, pair, spread_row):
        for index, field in enumerate(fields):
            pillar = jnp.sum(field, axis=0).reshape(4, 8, 128)
            pair[4 * index : 4 * index + 4, :] = jnp.sum(pillar, axis=1) * 0.125**3
        spread = one_hot_matmul(pair[...], spread_row[...])[0:8]
        mine = iota((8, 128), 1) // 16 == iota((8, 128), 0)
        row = jnp.sum(jnp.where(mine, spread, 0.0), axis=0, keepdims=True)
        self.row[...] = row
        self.row_in[self.i] = row

    def start_rows(self):
        self.row_copies = []
        for delta in range(1, ROW):
            target = self.g * ROW + (self.i + delta) % ROW
            self.row_copies.append(
                self.start(self.row, self.row_in.at[self.i], target, self.s)
            )

    def start_depth(self):
        for copy in self.row_copies:
            copy.wait_recv()
        line = iota((8, 128), 0)
        tile = jnp.zeros((8, 128), F32)
        for index in range(ROW):
            tile = jnp.where(line == index, self.row_in[index], tile)
        self.depth_in[self.z_at] = tile
        self.depth_copies = []
        for k, s in self.depth_partners:
            slot = self.depth_in.at[self.z_at]
            self.depth_copies.append(self.start(slot, slot, k, s))

    def start_sides(self, work, pool):
        for copy in self.depth_copies:
            copy.wait_recv()
        left = iota((8, 128), 1) < 64
        slot = self.side_in.at[self.y]
        wide = []
        for half in range(2):
            tiles = [self.depth_in[4 * half + index] for index in range(4)]
            turned = [roll(tile, 64, 1) for tile in tiles]
            fields = [jnp.where(left, tiles[a], turned[a + 1]) for a in (0, 2)]
            if self.dense:
                fields += [jnp.where(left, turned[a], tiles[a + 1]) for a in (0, 2)]
            for index, field in enumerate(fields):
                slot[2 + len(fields) * half + index] = field
            wide.append(jnp.concatenate(fields, axis=1))
        wide = jnp.concatenate(wide, axis=0)
        sums = one_hot_matmul(wide, pool[0 : wide.shape[1], :])
        work[...] = sums[:, 0:128]
        line = iota((8, 128), 0)
        for half in range(2):
            four = work[pl.ds(8 * half, 4, stride=2), :] + work[pl.ds(8 * half + 1, 4, stride=2), :]
            slot[half, 0:4, :] = four * 0.125
            five = sums[8 * half : 8 * half + 8, 128:256]
            five = five + roll(five, -1, 0)
            five = (five + roll(five, -2, 0)) * (0.125 * 0.125)
            five = jnp.where(line % 2 == 0, five[0:1], five[4:5])
            slot[half, 4:8, :] = five[4:8]
        self.side_copies = []
        for delta, (k, s) in self.side_partners:
            if delta in (1, 7):
                self.side_copies.append(self.start(slot, slot, k, s))
            else:
                part = slot.at[0:2]
                self.side_copies.append(self.start(part, part, k, s))

    def wait_sides(self):
        for copy in self.side_copies:
            copy.wait_recv()

    def group_fields(self, group):
        wrapped = (group + self.ng) % self.ng
        y, half = wrapped % 8, wrapped // 8
        count = 4 if self.dense else 2
        tiles = [self.side_in[y, 2 + half * count + index] for index in range(count)]
        return [
            jnp.concatenate(tiles[at : at + 2], axis=1) for at in range(0, count, 2)
        ]

    def finish(self, first, last):
        for copy, shift in self.started[first:last]:
            self.when(self.has_target(shift), copy.wait_send)


def split_packed(value):
    left = iota(value.shape, 1) < 64
    return jnp.where(left, value, 0.0), jnp.where(left, roll(value, 64, 1), 0.0)


def build_matrices(pool, fan):
    line, lane = iota((128, 128), 0), iota((128, 128), 1)
    for half in range(4):
        x, y = line // 16 + 8 * (half % 2), line % 16
        rows = slice(128 * half, 128 * half + 128)
        home4 = (x // 2) * 8 + y // 2 + 64 * (half // 2)
        home5 = (x // 4) * 4 + y // 4 + 64 * (half // 2)
        pool[rows, 0:128] = one_hot(home4 == lane).astype(BF16)
        pool[rows, 128:256] = one_hot(home5 == lane).astype(BF16)
    three = one_hot(line % 16 == lane // 8).astype(BF16)
    fan[0:128, :] = three
    fan[128:256, :] = three
    fan[256:384, :] = one_hot(line % 8 == lane // 16).astype(BF16)
    fan[384:512, :] = one_hot(line % 4 == lane // 32).astype(BF16)


def kernel(nf, ns, rhs, dens, solution, residual, *scratch):
    scratch = list(scratch)

    def take(count):
        taken = scratch[:count]
        del scratch[:count]
        return taken

    refs = {}
    for name in ("D0", "D1", "D2", "R0", "R1", "R2"):
        (refs[name],) = take(1)
    fine_coef = [take(5) for _ in range(3)]
    remains = take(3)
    updates = [take(3) for _ in range(3)]
    answers = take(3)
    (work, tile_work, pair, sol, spread) = take(5)
    (spread_row, pool, fan, keep3, keep4, keep5) = take(6)
    coarse_coef = [take(5) for _ in range(3)]
    phases = []
    k, s = lax.axis_index("fine"), lax.axis_index("sub")
    for with_density in (True, False):
        count = n_halo(with_density)
        buffers = take(count), take(count), take(len(whole_messages(with_density)))
        coarse = take(4)
        send_sem, recv_sem = take(2)
        phases.append(
            Phase(refs, (k, s, nf, ns), with_density, buffers, coarse, send_sem, recv_sem)
        )
    ng = nf // ROW
    i, g = k % ROW, k // ROW

    barrier = pltpu.get_barrier_semaphore()
    partners = []
    for shift in (1, 2, 3):
        partners += [((k + shift) % nf, s), ((k + nf - shift) % nf, s)]
    partners += [(g * ROW + (i + delta) % ROW, s) for delta in range(1, ROW)]
    depth, side = partners_of((k, s, nf, ns))
    partners += depth + [device for _, device in side]
    for partner in partners:
        pl.semaphore_signal(barrier, inc=1, device_id=partner, device_id_type=MESH)

    for level in range(3):
        for name, lead in (("D", 5), ("R", 4)):
            ref = refs[name + str(level)]
            planes, rows, _ = ref.shape
            blank = jnp.zeros((lead, rows, 128), F32)
            ref[0:lead] = blank
            ref[planes - lead : planes] = blank
    for ref in (keep4, keep5):
        rows = ref.shape[0]
        ref[0:8, :] = jnp.zeros((8, 128), F32)
        ref[rows - 8 : rows, :] = jnp.zeros((8, 128), F32)
    pair[...] = jnp.zeros((16, 128), F32)

    def restrict_all(name, lead):
        for level in range(2):
            refs[name + str(level + 1)][
                lead : lead + PLANES[level + 1], 0 : ROWS[level + 1], :
            ] = restrict_block(
                refs[name + str(level)], lead, PLANES[level], ROWS[level], 2**level, work
            )

    def coefficients(level, low, high):
        fine_coefficients(level, refs["D" + str(level)], fine_coef[level], low, high)

    def smooth(level):
        fine_smooth(
            level,
            refs["R" + str(level)],
            fine_coef[level],
            remains[level],
            updates[level],
            answers[level],
        )

    line, lane = iota((128, 128), 0), iota((128, 128), 1)
    spread_row[...] = one_hot(line // 8 == lane % 16).astype(BF16)
    refs["R0"][4:12, 0:32, :] = rhs[...]
    refs["D0"][5:13, 0:32, :] = dens[...]

    for cycle in range(CYCLES):
        phase = phases[cycle]
        if cycle == 0:
            phase.pack_row((rhs[...], dens[...]), pair, spread_row)
            pl.semaphore_wait(barrier, len(partners))
        else:
            phase.pack_row((refs["R0"][4:12, 0:32, :],), pair, spread_row)
        phase.start_rows()
        if cycle == 0:
            phase.start_whole({"D0": (dens, 0), "R0": (rhs, 0)})
        else:
            phase.start_whole({"R0": (refs["R0"], 4)})
        restrict_all("R", 4)
        if cycle == 0:
            restrict_all("D", 5)
        phase.pack_x()
        phase.start_x()
        phase.pack_z("a")
        phase.start_z("a")
        if cycle == 0:
            build_matrices(pool, fan)
        phase.start_depth()
        phase.unpack_x()
        phase.pack_z("b")
        phase.start_z("b")
        phase.start_sides(tile_work, pool)
        if cycle == 0:
            coefficients(0, 5, 11)
        else:
            phases[0].finish(0, None)
        phase.unpack_z()
        for level in (2, 1):
            if cycle == 0:
                coefficients(level, 0, PLANES[level] + 8)
            smooth(level)
        if cycle == 1:
            phase.unpack_whole()
            smooth(0)
            phase.finish(0, -7)
        phase.wait_sides()

        tiles = [phase.side_in[index % 8, index // 8] for index in range(ng)]
        line = iota((8, 128), 0)
        packed4, packed5 = [], []
        for index in range(0, ng, 2):
            packed4.append(jnp.where(line < 4, tiles[index], roll(tiles[index + 1], 4, 0)))
        for index in range(0, ng, 4):
            first = jnp.where(line < 6, tiles[index], tiles[index + 1])
            second = jnp.where(line < 6, tiles[index + 2], tiles[index + 3])
            packed5.append(jnp.where(line < 4, roll(first, 4, 0), second))
        source4, density4 = split_packed(jnp.concatenate(packed4, axis=0))
        source5, density5 = split_packed(jnp.concatenate(packed5, axis=0))
        if cycle == 0:
            low_in = jnp.where(g > 0, 1.0, 0.0).astype(F32)
            high_in = jnp.where(g < ng - 1, 1.0, 0.0).astype(F32)
            density3 = jnp.concatenate(
                [
                    phase.group_fields(g - 1)[1] * low_in,
                    phase.group_fields(g)[1],
                    phase.group_fields(g + 1)[1] * high_in,
                ],
                axis=0,
            )
            for index, (field, ny) in enumerate(
                ((density3, 16), (density4, 8), (density5, 4))
            ):
                values = packed_coefficients(field, ny, ny, 0.25 ** (3 + index))
                for ref, value in zip(coarse_coef[index], values):
                    ref[...] = value
        coef3, coef4, coef5 = ([ref[...] for ref in refs5] for refs5 in coarse_coef)
        total = jnp.sum(jnp.sum(source5, axis=0, keepdims=True), axis=1, keepdims=True)
        weight = jnp.sum(jnp.sum(coef5[3], axis=0, keepdims=True), axis=1, keepdims=True)
        n4, n5 = 4 * ng, 2 * ng
        keep5[8 : 8 + n5, :] = packed_smooth(source5, coef5, 4, 0.05) + total / weight
        keep4[8 : 8 + n4, :] = packed_smooth(source4, coef4, 8, 0.5)

        source3 = jnp.concatenate(
            [phase.group_fields(g + shift)[0] for shift in (-1, 0, 1)], axis=0
        )
        keep3[...] = packed_smooth(source3, coef3, 16, 0.5)

        row = iota((16, 512), 0)
        lane = iota((16, 512), 1)
        x3 = row // 2 + jnp.where(row < 12, 0, -8) + (4 * s + 4)
        inside = (x3 >= 4) & (x3 < 20)
        x_lane = jnp.where(
            lane < 256, lane // 16, jnp.where(lane < 384, (lane - 256) // 8, (lane - 384) // 4)
        )
        x_row = jnp.where(lane < 256, x3 - 4, jnp.where(lane < 384, x3 // 2 - 2, x3 // 4 - 1))
        chosen = (x_lane == x_row) & inside
        picked = []
        for t in range(3):
            parts = jnp.concatenate(
                [
                    keep3[pl.ds(7 + i + t, 1), :],
                    keep4[pl.ds((k + 1 + t) // 2 + 7, 1), :],
                    keep5[pl.ds((k + 3 + t) // 4 + 7, 1), :],
                ],
                axis=1,
            )
            picked.append(jnp.where(chosen, parts, 0.0))
        spread[0:3, 0:16, :] = one_hot_matmul(
            jnp.concatenate(picked, axis=0), fan[...]
        ).reshape(3, 16, 128)

        for level in (2, 1):
            rows = ROWS[level]
            answer = answers[level]
            planes = PLANES[level] + 2
            coarse = jnp.concatenate(
                [spread[(p + 1) // 2 : (p + 1) // 2 + 1, 0 : rows + 8, :] for p in range(planes)],
                axis=0,
            )
            value = answer[3 : 3 + planes] + coarse
            own, ends = value[:, 0:rows, :], value[:, rows : rows + 8, :]
            spread[0:planes, pl.ds(0, rows, stride=2), :] = own
            spread[0:planes, pl.ds(1, rows, stride=2), :] = own
            spread[0:planes, 2 * rows : 2 * rows + 8, :] = jnp.where(
                upper_rows(planes), ends[:, 0:1, :], ends[:, 7:8, :]
            )

        if cycle == 0:
            phase.unpack_whole()
            coefficients(0, 0, 5)
            coefficients(0, 11, 16)
            smooth(0)

        def advance(p, carry, cycle=cycle):
            step = 0.4 * (answers[0][p + 3] + spread[(p + 1) // 2])
            sol[p] = step if cycle == 0 else sol[p] + step
            return carry

        lax.fori_loop(0, PLANES[0] + 2, advance, 0, unroll=True)

        def defect(p, carry, cycle=cycle):
            applied = fine_apply(sol, p + 1, fine_coef[0], p + 4, 1)
            left = rhs[p] - applied[0:32, :]
            if cycle == 0:
                refs["R0"][p + 4, 0:32, :] = left
            else:
                residual[p] = left
                solution[p] = sol[p + 1, 0:32, :]
            return carry

        lax.fori_loop(0, PLANES[0], defect, 0, unroll=True)

    phases[1].finish(-7, None)


def scratch_shapes(ng):
    shapes = []
    for level in range(3):
        shapes.append(pltpu.VMEM((PLANES[level] + 10, ROWS[level] + 16, 128), F32))
    extents = [(PLANES[level] + 8, ROWS[level] + 8, 128) for level in range(3)]
    shapes += [pltpu.VMEM(extent, F32) for extent in extents]
    for extent in extents:
        shapes += [pltpu.VMEM(extent, F32)] * 5
    shapes += [pltpu.VMEM(extent, F32) for extent in extents]
    for extent in extents:
        shapes += [pltpu.VMEM(extent, F32)] * 3
    shapes += [pltpu.VMEM(extent, F32) for extent in extents]
    shapes += [
        pltpu.VMEM((4, 32, 128), F32),
        pltpu.VMEM((16, 128), F32),
        pltpu.VMEM((16, 128), F32),
        pltpu.VMEM((10, 40, 128), F32),
        pltpu.VMEM((6, 40, 128), F32),
        pltpu.VMEM((128, 128), BF16),
        pltpu.VMEM((512, 256), BF16),
        pltpu.VMEM((512, 128), BF16),
        pltpu.VMEM((24, 256), F32),
        pltpu.VMEM((4 * ng + 16, 128), F32),
        pltpu.VMEM((2 * ng + 16, 128), F32),
    ]
    for extent in ((24, 256), (4 * ng, 128), (2 * ng, 128)):
        shapes += [pltpu.VMEM(extent, F32)] * 5
    for with_density in (True, False):
        halo = buffer_shapes(with_density)
        shapes += halo + halo + whole_shapes(with_density)
        tiles = 10 if with_density else 6
        shapes += [
            pltpu.VMEM((1, 128), F32),
            pltpu.VMEM((ROW, 1, 128), F32),
            pltpu.VMEM((8, 8, 128), F32),
            pltpu.VMEM((8, tiles, 8, 128), F32),
        ]
        copies = n_halo(with_density) + len(whole_messages(with_density))
        copies += (ROW - 1) + 7 + 7
        shapes += [pltpu.SemaphoreType.DMA((copies,)), pltpu.SemaphoreType.DMA((copies,))]
    return shapes


def solution(mesh):
    nf, ns = mesh.shape["fine"], mesh.shape["sub"]

    def body(rhs, density):
        return pl.pallas_call(
            functools.partial(kernel, nf, ns),
            out_shape=(
                jax.ShapeDtypeStruct(rhs.shape, F32),
                jax.ShapeDtypeStruct(rhs.shape, F32),
            ),
            in_specs=[pl.BlockSpec(memory_space=pltpu.VMEM)] * 2,
            out_specs=[pl.BlockSpec(memory_space=pltpu.VMEM)] * 2,
            scratch_shapes=scratch_shapes(nf // ROW),
            compiler_params=pltpu.CompilerParams(
                collective_id=0, has_side_effects=True, vmem_limit_bytes=32 * 1024 * 1024
            ),
        )(rhs, density)

    return jax.shard_map(
        body,
        mesh=mesh,
        in_specs=(P("fine", "sub", None), P("fine", "sub", None)),
        out_specs=(P("fine", "sub", None), P("fine", "sub", None)),
        check_vma=False,
    )
```

```python
import functools

import jax
import jax.numpy as jnp
from jax import lax
from jax.experimental import pallas as pl
from jax.experimental.pallas import tpu as pltpu
from jax.sharding import PartitionSpec as P

DEGREE = 4
CYCLES = 2
MESH = pl.DeviceIdType.MESH
F32 = jnp.float32
BF16 = jnp.bfloat16
ROW = 8
PLANES = (8, 4, 2)
ROWS = (32, 16, 8)


def chebyshev_constants(lower):
    upper = 2.0
    theta = 0.5 * (upper + lower)
    delta = 0.5 * (upper - lower)
    sigma = theta / delta
    ratio = 1.0 / sigma
    steps = []
    for _ in range(DEGREE - 1):
        next_ratio = 1.0 / (2.0 * sigma - ratio)
        steps.append((next_ratio * ratio, 2.0 * next_ratio / delta))
        ratio = next_ratio
    return 1.0 / theta, steps


def iota(shape, dim):
    return lax.broadcasted_iota(jnp.int32, shape, dim)


def roll(value, shift, axis):
    return pltpu.roll(value, shift % value.shape[axis], axis)


def invert(value):
    return pltpu.reciprocal(value, full_range=False)


def one_hot(condition):
    return jnp.where(condition, 1.0, 0.0).astype(F32)


def one_hot_matmul(value, matrix):
    count = value.shape[0]
    first = value.astype(BF16).astype(F32)
    rest = value - first
    second = rest.astype(BF16).astype(F32)
    parts = jnp.concatenate([first, second, rest - second], axis=0).astype(BF16)
    product = jnp.dot(parts, matrix, preferred_element_type=F32)
    return product[0:count] + product[count : 2 * count] + product[2 * count :]


def restrict_block(source, first, planes, rows, stride, work):
    field = source[first : first + planes, 0:rows, :]
    field = field.reshape(planes // 2, 2, rows, 128)
    work[0 : planes // 2, 0:rows, :] = field[:, 0] + field[:, 1]
    half = rows // 2
    both = (
        work[0 : planes // 2, pl.ds(0, half, stride=2), :]
        + work[0 : planes // 2, pl.ds(1, half, stride=2), :]
    )
    lane = iota(both.shape, 2)
    even = (lane // stride) % 2 == 0
    other = jnp.where(even, roll(both, -stride, 2), roll(both, stride, 2))
    return (both + other) * 0.125


def fine_coefficients(level, dens, coef, low, high):
    own = ROWS[level]
    scale = 2.0 * 0.25**level
    stride = 2**level
    face_z, face_x, face_y, diagonal, inverse = coef
    shape = (own + 16, 128)

    def compress(value):
        tail = jnp.where(
            iota((8, 128), 0) < 4, value[own : own + 8], value[own + 8 : own + 16]
        )
        return jnp.concatenate([value[0:own], tail], axis=0)

    def plane(p, down):
        here = dens[p + 1]
        above = dens[p + 2]
        lane = iota(shape, 1)
        right = roll(here, -1, 0)
        up = scale * invert(jnp.maximum(here + above, 0.1))
        x_face = scale * invert(jnp.maximum(here + right, 0.1))
        ahead = jnp.where(lane >= 128 - stride, 0.0, roll(here, -stride, 1))
        behind = jnp.where(lane < stride, 0.0, roll(here, stride, 1))
        y_face = scale * invert(jnp.maximum(here + ahead, 0.1))
        y_back = scale * invert(jnp.maximum(here + behind, 0.1))
        diag = up + down + x_face + roll(x_face, 1, 0) + y_face + y_back
        inside = here > 0.0
        face_z[p] = compress(jnp.where(inside & (above > 0.0), up, 0.0))
        face_x[p] = compress(jnp.where(inside & (right > 0.0), x_face, 0.0))
        face_y[p] = compress(jnp.where(lane >= 128 - stride, 0.0, y_face))
        diagonal[p] = compress(diag)
        inverse[p] = compress(invert(diag))
        return up

    lowest = scale * invert(jnp.maximum(dens[low] + dens[low + 1], 0.1))
    lax.fori_loop(low, high, plane, lowest, unroll=True)


def fine_apply(field, p, coef, q, stride):
    face_z, face_x, face_y, diagonal, _ = coef
    here = field[p]
    x_face = face_x[q]
    y_face = face_y[q]
    result = diagonal[q] * here
    result = result - face_z[q] * field[p + 1] - face_z[q - 1] * field[p - 1]
    result = result - x_face * roll(here, -1, 0) - roll(x_face * here, 1, 0)
    result = result - y_face * roll(here, -stride, 1) - roll(y_face * here, stride, 1)
    return result


def fine_smooth(level, source, coef, remain, updates, answer):
    planes = PLANES[level] + 8
    stride = 2**level
    inverse = coef[4]
    first, steps = chebyshev_constants(0.5)
    d0, d1, d2 = updates

    def start(p, carry):
        d0[p] = source[p] * inverse[p] * first
        return carry

    lax.fori_loop(0, planes, start, 0, unroll=True)
    chain = (d0, d1, d2)
    for sweep in range(3):
        old = chain[sweep]
        keep, add = steps[sweep]

        def step(p, carry, sweep=sweep, old=old, keep=keep, add=add):
            left = source[p] if sweep == 0 else remain[p]
            left = left - fine_apply(old, p, coef, p, stride)
            new = keep * old[p] + add * (left * inverse[p])
            if sweep < 2:
                remain[p] = left
                chain[sweep + 1][p] = new
            else:
                answer[p] = d0[p] + d1[p] + d2[p] + new
            return carry

        lax.fori_loop(sweep + 1, planes - sweep - 1, step, 0, unroll=True)


def packed_coefficients(dens, ny, nx, scale):
    rows = dens.shape[0]
    z = iota(dens.shape, 0)
    lane = iota(dens.shape, 1)
    y = lane % ny
    x = lane // ny
    scale = 2.0 * scale

    def neighbour(shift, axis, outside):
        return jnp.where(outside, 0.0, roll(dens, shift, axis))

    above = neighbour(-1, 0, z == rows - 1)
    below = neighbour(1, 0, z == 0)
    right = neighbour(-ny, 1, x >= nx - 1)
    left = neighbour(ny, 1, x == 0)
    ahead = neighbour(-1, 1, y == ny - 1)
    behind = neighbour(1, 1, y == 0)

    def face(other):
        return scale * invert(jnp.maximum(dens + other, 0.1))

    up, x_face, y_face = face(above), face(right), face(ahead)
    diagonal = up + face(below) + x_face + face(left) + y_face + face(behind)
    inside = dens > 0.0

    def inner(value, other):
        return jnp.where(inside & (other > 0.0), value, 0.0)

    return (
        inner(up, above),
        inner(x_face, right),
        inner(y_face, ahead),
        jnp.where(inside, diagonal, 0.0),
        jnp.where(inside, invert(diagonal), 0.0),
    )


def packed_apply(field, coef, ny):
    face_z, face_x, face_y, diagonal, _ = coef
    result = diagonal * field
    result = result - face_z * roll(field, -1, 0) - roll(face_z * field, 1, 0)
    result = result - face_x * roll(field, -ny, 1) - roll(face_x * field, ny, 1)
    result = result - face_y * roll(field, -1, 1) - roll(face_y * field, 1, 1)
    return result


def packed_smooth(source, coef, ny, lower):
    first, steps = chebyshev_constants(lower)
    inverse = coef[4]
    update = source * inverse * first
    answer = update
    for keep, add in steps:
        source = source - packed_apply(update, coef, ny)
        update = keep * update + add * (source * inverse)
        answer = answer + update
    return answer


PIECES = {
    ("a", 1): ((("D1", 5, 1, 4), ("D2", 5, 3, 2)), (("R1", 4, 0, 4), ("R2", 4, 2, 2))),
    ("a", -1): ((("D1", 5, 9, 4), ("D2", 5, 7, 2)), (("R1", 4, 8, 4), ("R2", 4, 6, 2))),
    ("a", 2): ((("D1", 8, 0, 1), ("D2", 5, 1, 2)), (("R2", 4, 0, 2),)),
    ("a", -2): ((("D1", 5, 13, 1), ("D2", 5, 9, 2)), (("R2", 4, 8, 2),)),
    ("a", 3): ((("D2", 6, 0, 1),), ()),
    ("a", -3): ((("D2", 5, 11, 1),), ()),
    ("b", 1): (
        (("D0", 9, 1, 4), ("D1", 5, 1, 4), ("D2", 5, 3, 2)),
        (("R0", 9, 1, 3), ("R1", 4, 0, 4), ("R2", 4, 2, 2)),
    ),
    ("b", -1): (
        (("D0", 5, 13, 4), ("D1", 5, 9, 4), ("D2", 5, 7, 2)),
        (("R0", 4, 12, 3), ("R1", 4, 8, 4), ("R2", 4, 6, 2)),
    ),
    ("b", 2): ((("D2", 5, 1, 2),), (("R2", 4, 0, 2),)),
    ("b", -2): ((("D2", 5, 9, 2),), (("R2", 4, 8, 2),)),
}
WHOLE = (("D0", 1, 3, 0, 5), ("D0", -1, 0, 13, 5), ("R0", 1, 4, 0, 4), ("R0", -1, 0, 12, 4))


def whole_messages(with_density):
    return WHOLE if with_density else WHOLE[2:]


def z_messages(with_density):
    result = []
    for (part, shift), (density, field) in PIECES.items():
        pieces = (density if with_density else ()) + field
        if pieces:
            result.append((part, shift, pieces))
    return result


def paired(name, tiles):
    return name[1] != "0" and tiles % 2 == 0


def piece_tiles(part, piece):
    name, _, _, count = piece
    tiles = count * (ROWS[int(name[1])] // 8 if part == "a" else 1)
    return tiles // 2 if paired(name, tiles) else tiles


def x_pieces(with_density):
    result = []
    for level in range(3):
        count = PLANES[level]
        if with_density:
            result.append(("D%d" % level, count, count // 2 if level else count))
        result.append(("R%d" % level, count, (4, 1, 1)[level]))
    return result


def buffer_shapes(with_density):
    tiles = [sum(sent for _, _, sent in x_pieces(with_density))] * 2
    for part, _, pieces in z_messages(with_density):
        tiles.append(sum(piece_tiles(part, piece) for piece in pieces))
    return [pltpu.VMEM((count, 8, 128), F32) for count in tiles]


def whole_shapes(with_density):
    return [pltpu.VMEM((count, 32, 128), F32) for _, _, _, _, count in whole_messages(with_density)]


def n_halo(with_density):
    return 2 + len(z_messages(with_density))


def even_lanes(tiles):
    return iota((tiles, 8, 128), 2) % 2 == 0


def upper_rows(tiles):
    return iota((tiles, 8, 128), 1) < 4


def pack_lanes(block):
    half = block.shape[0] // 2
    return jnp.where(even_lanes(half), block[0:half], block[half:])


def unpack_lanes(block):
    even = even_lanes(block.shape[0])
    return jnp.concatenate(
        [jnp.where(even, block, roll(block, 1, 2)), jnp.where(even, roll(block, -1, 2), block)],
        axis=0,
    )


def partners_of(place):
    k, s, _, ns = place
    i, y, half = k % ROW, k // ROW % 8, k // (8 * ROW)
    depth, side = [], []
    for delta in (4, 3, 5, 2, 6, 1, 7):
        z = (half * ns + s + delta) % (2 * ns)
        depth.append((((z // ns) * 8 + y) * ROW + i, z % ns))
        side.append((delta, ((half * 8 + (y + delta) % 8) * ROW + i, s)))
    return depth, side


class Phase:
    def __init__(self, refs, place, with_density, buffers, coarse, send_sem, recv_sem):
        send, recv, whole = buffers
        self.whole_in = whole
        self.whole = whole_messages(with_density)
        self.refs = refs
        self.k, self.s, self.nf, self.ns = place
        self.dense = with_density
        self.send, self.recv = send, recv
        self.row, self.row_in, self.depth_in, self.side_in = coarse
        self.send_sem, self.recv_sem = send_sem, recv_sem
        self.started = []
        self.count = 0
        self.z = z_messages(with_density)
        self.copies = {}
        self.i = self.k % ROW
        self.g = self.k // ROW
        self.ng = self.nf // ROW
        self.y = self.g % 8
        self.z_at = self.g // 8 * self.ns + self.s
        self.depth_partners, self.side_partners = partners_of(place)

    def start(self, source, target, k, s, shift=0):
        index = self.count
        self.count += 1
        copy = pltpu.make_async_remote_copy(
            src_ref=source,
            dst_ref=target,
            send_sem=self.send_sem.at[index],
            recv_sem=self.recv_sem.at[index],
            device_id=(k, s),
            device_id_type=MESH,
        )
        self.when(self.has_target(shift), copy.start)
        self.started.append((copy, shift))
        return copy

    def has_target(self, shift):
        if shift == 0:
            return None
        return self.k < self.nf - shift if shift > 0 else self.k >= -shift

    def has_source(self, shift):
        return self.has_target(-shift)

    def when(self, condition, action):
        if condition is None:
            action()
        else:
            pl.when(condition)(action)

    def start_whole(self, fields):
        self.whole_copies = []
        for index, (name, shift, first, _, count) in enumerate(self.whole):
            target = (self.k + shift + self.nf) % self.nf
            ref, lead = fields[name]
            source = ref.at[lead + first : lead + first + count, 0:32, :]
            self.whole_copies.append(
                self.start(source, self.whole_in[index], target, self.s, shift)
            )

    def unpack_whole(self):
        for index, (name, shift, _, target, count) in enumerate(self.whole):
            self.when(self.has_source(shift), self.whole_copies[index].wait_recv)
        for index, (name, shift, _, target, count) in enumerate(self.whole):
            block = jnp.where(self.has_source(shift), self.whole_in[index][...], 0.0)
            self.refs[name][target : target + count, 0:32, :] = block

    def pack_x(self):
        for which in (0, 1):
            at = 0
            for name, count, sent in x_pieces(self.dense):
                level = int(name[1])
                lead = 5 if name[0] == "D" else 4
                row = ROWS[level] - 8 if which == 0 else 0
                block = self.refs[name][lead : lead + count, row : row + 8, :]
                if level:
                    block = pack_lanes(block)
                if block.shape[0] > sent:
                    near, far = block[0:sent], roll(block[sent:], 4, 1)
                    upper = upper_rows(sent)
                    if which == 0:
                        block = jnp.where(upper, far, near)
                    else:
                        block = jnp.where(upper, near, far)
                self.send[which][at : at + sent] = block
                at += sent

    def start_x(self):
        up, down = (self.s + 1) % self.ns, (self.s + self.ns - 1) % self.ns
        self.x_copies = [
            self.start(self.send[0], self.recv[0], self.k, up),
            self.start(self.send[1], self.recv[1], self.k, down),
        ]

    def unpack_x(self):
        for copy in self.x_copies:
            copy.wait_recv()
        low_in = jnp.where(self.s > 0, 1.0, 0.0).astype(F32)
        high_in = jnp.where(self.s < self.ns - 1, 1.0, 0.0).astype(F32)
        at = 0
        for name, count, sent in x_pieces(self.dense):
            level = int(name[1])
            own = ROWS[level]
            lead = 5 if name[0] == "D" else 4
            low, high = self.recv[0][at : at + sent], self.recv[1][at : at + sent]
            at += sent
            ref = self.refs[name]
            if name[0] == "D":
                if level:
                    low, high = unpack_lanes(low), unpack_lanes(high)
                ref[lead : lead + count, own : own + 8, :] = high * high_in
                ref[lead : lead + count, own + 8 : own + 16, :] = low * low_in
                continue
            upper = upper_rows(sent)
            block = jnp.where(upper, high, low)
            if sent < (count // 2 if level else count):
                far = roll(jnp.where(upper, low, high), 4, 1)
                block = jnp.concatenate([block, far], axis=0)
            if level:
                block = unpack_lanes(block)
            ref[lead : lead + count, own : own + 8, :] = block

    def pack_z(self, part):
        for index, (kind, _, pieces) in enumerate(self.z):
            if kind != part:
                continue
            at = 0
            for piece in pieces:
                name, source, _, count = piece
                ref, own = self.refs[name], ROWS[int(name[1])]
                if part == "a":
                    block = ref[source : source + count, 0:own, :]
                    block = block.reshape(count * own // 8, 8, 128)
                else:
                    block = ref[source : source + count, own : own + 8, :]
                    if name[0] == "D":
                        low = ref[source : source + count, own + 8 : own + 16, :]
                        block = jnp.where(upper_rows(count), block, low)
                if paired(name, block.shape[0]):
                    block = pack_lanes(block)
                self.send[2 + index][at : at + block.shape[0]] = block
                at += block.shape[0]

    def start_z(self, part):
        for index, (kind, shift, _) in enumerate(self.z):
            if kind == part:
                target = (self.k + shift + self.nf) % self.nf
                self.copies[index] = self.start(
                    self.send[2 + index], self.recv[2 + index], target, self.s, shift
                )

    def unpack_z(self):
        for index, (_, shift, _) in enumerate(self.z):
            self.when(self.has_source(shift), self.copies[index].wait_recv)
        for index, (part, shift, pieces) in enumerate(self.z):
            inside = self.has_source(shift)
            at = 0
            for piece in pieces:
                name, _, target, count = piece
                ref, own = self.refs[name], ROWS[int(name[1])]
                sent = piece_tiles(part, piece)
                block = jnp.where(inside, self.recv[2 + index][at : at + sent], 0.0)
                at += sent
                if sent < (count * own // 8 if part == "a" else count):
                    block = unpack_lanes(block)
                if part == "a":
                    ref[target : target + count, 0:own, :] = block.reshape(count, own, 128)
                else:
                    ref[target : target + count, own : own + 8, :] = block
                    if name[0] == "D":
                        ref[target : target + count, own + 8 : own + 16, :] = block

    def pack_row(self, fields, pair, spread_row):
        for index, field in enumerate(fields):
            pillar = jnp.sum(field, axis=0).reshape(4, 8, 128)
            pair[4 * index : 4 * index + 4, :] = jnp.sum(pillar, axis=1) * 0.125**3
        spread = one_hot_matmul(pair[...], spread_row[...])[0:8]
        mine = iota((8, 128), 1) // 16 == iota((8, 128), 0)
        row = jnp.sum(jnp.where(mine, spread, 0.0), axis=0, keepdims=True)
        self.row[...] = row
        self.row_in[self.i] = row

    def start_rows(self):
        self.row_copies = []
        for delta in range(1, ROW):
            target = self.g * ROW + (self.i + delta) % ROW
            self.row_copies.append(
                self.start(self.row, self.row_in.at[self.i], target, self.s)
            )

    def start_depth(self):
        for copy in self.row_copies:
            copy.wait_recv()
        line = iota((8, 128), 0)
        tile = jnp.zeros((8, 128), F32)
        for index in range(ROW):
            tile = jnp.where(line == index, self.row_in[index], tile)
        self.depth_in[self.z_at] = tile
        self.depth_copies = []
        for k, s in self.depth_partners:
            slot = self.depth_in.at[self.z_at]
            self.depth_copies.append(self.start(slot, slot, k, s))

    def start_sides(self, work, pool):
        for copy in self.depth_copies:
            copy.wait_recv()
        left = iota((8, 128), 1) < 64
        slot = self.side_in.at[self.y]
        wide = []
        for half in range(2):
            tiles = [self.depth_in[4 * half + index] for index in range(4)]
            turned = [roll(tile, 64, 1) for tile in tiles]
            fields = [jnp.where(left, tiles[a], turned[a + 1]) for a in (0, 2)]
            if self.dense:
                fields += [jnp.where(left, turned[a], tiles[a + 1]) for a in (0, 2)]
            for index, field in enumerate(fields):
                slot[2 + len(fields) * half + index] = field
            wide.append(jnp.concatenate(fields, axis=1))
        wide = jnp.concatenate(wide, axis=0)
        sums = one_hot_matmul(wide, pool[0 : wide.shape[1], :])
        work[...] = sums[:, 0:128]
        line = iota((8, 128), 0)
        for half in range(2):
            four = work[pl.ds(8 * half, 4, stride=2), :] + work[pl.ds(8 * half + 1, 4, stride=2), :]
            slot[half, 0:4, :] = four * 0.125
            five = sums[8 * half : 8 * half + 8, 128:256]
            five = five + roll(five, -1, 0)
            five = (five + roll(five, -2, 0)) * (0.125 * 0.125)
            five = jnp.where(line % 2 == 0, five[0:1], five[4:5])
            slot[half, 4:8, :] = five[4:8]
        self.side_copies = []
        for delta, (k, s) in self.side_partners:
            if delta in (1, 7):
                self.side_copies.append(self.start(slot, slot, k, s))
            else:
                part = slot.at[0:2]
                self.side_copies.append(self.start(part, part, k, s))

    def wait_sides(self):
        for copy in self.side_copies:
            copy.wait_recv()

    def group_fields(self, group):
        wrapped = (group + self.ng) % self.ng
        y, half = wrapped % 8, wrapped // 8
        count = 4 if self.dense else 2
        tiles = [self.side_in[y, 2 + half * count + index] for index in range(count)]
        return [
            jnp.concatenate(tiles[at : at + 2], axis=1) for at in range(0, count, 2)
        ]

    def finish(self, first, last):
        for copy, shift in self.started[first:last]:
            self.when(self.has_target(shift), copy.wait_send)


def split_packed(value):
    left = iota(value.shape, 1) < 64
    return jnp.where(left, value, 0.0), jnp.where(left, roll(value, 64, 1), 0.0)


def build_matrices(pool, fan):
    line, lane = iota((128, 128), 0), iota((128, 128), 1)
    for half in range(4):
        x, y = line // 16 + 8 * (half % 2), line % 16
        rows = slice(128 * half, 128 * half + 128)
        home4 = (x // 2) * 8 + y // 2 + 64 * (half // 2)
        home5 = (x // 4) * 4 + y // 4 + 64 * (half // 2)
        pool[rows, 0:128] = one_hot(home4 == lane).astype(BF16)
        pool[rows, 128:256] = one_hot(home5 == lane).astype(BF16)
    three = one_hot(line % 16 == lane // 8).astype(BF16)
    fan[0:128, :] = three
    fan[128:256, :] = three
    fan[256:384, :] = one_hot(line % 8 == lane // 16).astype(BF16)
    fan[384:512, :] = one_hot(line % 4 == lane // 32).astype(BF16)


def kernel(nf, ns, rhs, dens, solution, residual, *scratch):
    scratch = list(scratch)

    def take(count):
        taken = scratch[:count]
        del scratch[:count]
        return taken

    refs = {}
    for name in ("D0", "D1", "D2", "R0", "R1", "R2"):
        (refs[name],) = take(1)
    fine_coef = [take(5) for _ in range(3)]
    remains = take(3)
    updates = [take(3) for _ in range(3)]
    answers = take(3)
    (work, tile_work, pair, sol, spread) = take(5)
    (spread_row, pool, fan, keep3, keep4, keep5) = take(6)
    coarse_coef = [take(5) for _ in range(3)]
    phases = []
    k, s = lax.axis_index("fine"), lax.axis_index("sub")
    for with_density in (True, False):
        count = n_halo(with_density)
        buffers = take(count), take(count), take(len(whole_messages(with_density)))
        coarse = take(4)
        send_sem, recv_sem = take(2)
        phases.append(
            Phase(refs, (k, s, nf, ns), with_density, buffers, coarse, send_sem, recv_sem)
        )
    ng = nf // ROW
    i, g = k % ROW, k // ROW

    barrier = pltpu.get_barrier_semaphore()
    partners = []
    for shift in (1, 2, 3):
        partners += [((k + shift) % nf, s), ((k + nf - shift) % nf, s)]
    partners += [(g * ROW + (i + delta) % ROW, s) for delta in range(1, ROW)]
    depth, side = partners_of((k, s, nf, ns))
    partners += depth + [device for _, device in side]
    for partner in partners:
        pl.semaphore_signal(barrier, inc=1, device_id=partner, device_id_type=MESH)

    pair[...] = jnp.zeros((16, 128), F32)

    def restrict_all(name, lead):
        for level in range(2):
            refs[name + str(level + 1)][
                lead : lead + PLANES[level + 1], 0 : ROWS[level + 1], :
            ] = restrict_block(
                refs[name + str(level)], lead, PLANES[level], ROWS[level], 2**level, work
            )

    def coefficients(level, low, high):
        fine_coefficients(level, refs["D" + str(level)], fine_coef[level], low, high)

    def smooth(level):
        fine_smooth(
            level,
            refs["R" + str(level)],
            fine_coef[level],
            remains[level],
            updates[level],
            answers[level],
        )

    line, lane = iota((128, 128), 0), iota((128, 128), 1)
    spread_row[...] = one_hot(line // 8 == lane % 16).astype(BF16)

    for cycle in range(CYCLES):
        phase = phases[cycle]
        if cycle == 0:
            phase.pack_row((rhs[...], dens[...]), pair, spread_row)
            pl.semaphore_wait(barrier, len(partners))
        else:
            phase.pack_row((refs["R0"][4:12, 0:32, :],), pair, spread_row)
        phase.start_rows()
        if cycle == 0:
            refs["R0"][4:12, 0:32, :] = rhs[...]
            refs["D0"][5:13, 0:32, :] = dens[...]
            restrict_all("D", 5)
        restrict_all("R", 4)
        phase.pack_x()
        phase.start_x()
        if cycle == 0:
            phase.start_whole({"D0": (dens, 0), "R0": (rhs, 0)})
        else:
            phase.start_whole({"R0": (refs["R0"], 4)})
        phase.pack_z("a")
        phase.start_z("a")
        if cycle == 0:
            build_matrices(pool, fan)
            for level in range(3):
                for name, lead in (("D", 5), ("R", 4)):
                    ref = refs[name + str(level)]
                    planes, rows, _ = ref.shape
                    blank = jnp.zeros((lead, rows, 128), F32)
                    ref[0:lead] = blank
                    ref[planes - lead : planes] = blank
            for ref in (keep4, keep5):
                rows = ref.shape[0]
                ref[0:8, :] = jnp.zeros((8, 128), F32)
                ref[rows - 8 : rows, :] = jnp.zeros((8, 128), F32)
        phase.start_depth()
        phase.unpack_x()
        phase.pack_z("b")
        phase.start_z("b")
        phase.start_sides(tile_work, pool)
        if cycle == 0:
            coefficients(0, 5, 11)
        else:
            phases[0].finish(0, None)
        phase.unpack_z()
        for level in (2, 1):
            if cycle == 0:
                coefficients(level, 0, PLANES[level] + 8)
            smooth(level)
        if cycle == 1:
            phase.unpack_whole()
            smooth(0)
            phase.finish(0, -7)
        phase.wait_sides()

        tiles = [phase.side_in[index % 8, index // 8] for index in range(ng)]
        line = iota((8, 128), 0)
        packed4, packed5 = [], []
        for index in range(0, ng, 2):
            packed4.append(jnp.where(line < 4, tiles[index], roll(tiles[index + 1], 4, 0)))
        for index in range(0, ng, 4):
            first = jnp.where(line < 6, tiles[index], tiles[index + 1])
            second = jnp.where(line < 6, tiles[index + 2], tiles[index + 3])
            packed5.append(jnp.where(line < 4, roll(first, 4, 0), second))
        source4, density4 = split_packed(jnp.concatenate(packed4, axis=0))
        source5, density5 = split_packed(jnp.concatenate(packed5, axis=0))
        if cycle == 0:
            low_in = jnp.where(g > 0, 1.0, 0.0).astype(F32)
            high_in = jnp.where(g < ng - 1, 1.0, 0.0).astype(F32)
            density3 = jnp.concatenate(
                [
                    phase.group_fields(g - 1)[1] * low_in,
                    phase.group_fields(g)[1],
                    phase.group_fields(g + 1)[1] * high_in,
                ],
                axis=0,
            )
            for index, (field, ny) in enumerate(
                ((density3, 16), (density4, 8), (density5, 4))
            ):
                values = packed_coefficients(field, ny, ny, 0.25 ** (3 + index))
                for ref, value in zip(coarse_coef[index], values):
                    ref[...] = value
        coef3, coef4, coef5 = ([ref[...] for ref in refs5] for refs5 in coarse_coef)
        total = jnp.sum(jnp.sum(source5, axis=0, keepdims=True), axis=1, keepdims=True)
        weight = jnp.sum(jnp.sum(coef5[3], axis=0, keepdims=True), axis=1, keepdims=True)
        n4, n5 = 4 * ng, 2 * ng
        keep5[8 : 8 + n5, :] = packed_smooth(source5, coef5, 4, 0.05) + total / weight
        keep4[8 : 8 + n4, :] = packed_smooth(source4, coef4, 8, 0.5)

        source3 = jnp.concatenate(
            [phase.group_fields(g + shift)[0] for shift in (-1, 0, 1)], axis=0
        )
        keep3[...] = packed_smooth(source3, coef3, 16, 0.5)

        row = iota((16, 512), 0)
        lane = iota((16, 512), 1)
        x3 = row // 2 + jnp.where(row < 12, 0, -8) + (4 * s + 4)
        inside = (x3 >= 4) & (x3 < 20)
        x_lane = jnp.where(
            lane < 256, lane // 16, jnp.where(lane < 384, (lane - 256) // 8, (lane - 384) // 4)
        )
        x_row = jnp.where(lane < 256, x3 - 4, jnp.where(lane < 384, x3 // 2 - 2, x3 // 4 - 1))
        chosen = (x_lane == x_row) & inside
        picked = []
        for t in range(3):
            parts = jnp.concatenate(
                [
                    keep3[pl.ds(7 + i + t, 1), :],
                    keep4[pl.ds((k + 1 + t) // 2 + 7, 1), :],
                    keep5[pl.ds((k + 3 + t) // 4 + 7, 1), :],
                ],
                axis=1,
            )
            picked.append(jnp.where(chosen, parts, 0.0))
        spread[0:3, 0:16, :] = one_hot_matmul(
            jnp.concatenate(picked, axis=0), fan[...]
        ).reshape(3, 16, 128)

        for level in (2, 1):
            rows = ROWS[level]
            answer = answers[level]
            planes = PLANES[level] + 2
            coarse = jnp.concatenate(
                [spread[(p + 1) // 2 : (p + 1) // 2 + 1, 0 : rows + 8, :] for p in range(planes)],
                axis=0,
            )
            value = answer[3 : 3 + planes] + coarse
            own, ends = value[:, 0:rows, :], value[:, rows : rows + 8, :]
            spread[0:planes, pl.ds(0, rows, stride=2), :] = own
            spread[0:planes, pl.ds(1, rows, stride=2), :] = own
            spread[0:planes, 2 * rows : 2 * rows + 8, :] = jnp.where(
                upper_rows(planes), ends[:, 0:1, :], ends[:, 7:8, :]
            )

        if cycle == 0:
            phase.unpack_whole()
            coefficients(0, 0, 5)
            coefficients(0, 11, 16)
            smooth(0)

        def advance(p, carry, cycle=cycle):
            step = 0.4 * (answers[0][p + 3] + spread[(p + 1) // 2])
            sol[p] = step if cycle == 0 else sol[p] + step
            return carry

        lax.fori_loop(0, PLANES[0] + 2, advance, 0, unroll=True)

        def defect(p, carry, cycle=cycle):
            applied = fine_apply(sol, p + 1, fine_coef[0], p + 4, 1)
            left = rhs[p] - applied[0:32, :]
            if cycle == 0:
                refs["R0"][p + 4, 0:32, :] = left
            else:
                residual[p] = left
                solution[p] = sol[p + 1, 0:32, :]
            return carry

        lax.fori_loop(0, PLANES[0], defect, 0, unroll=True)

    phases[1].finish(-7, None)


def scratch_shapes(ng):
    shapes = []
    for level in range(3):
        shapes.append(pltpu.VMEM((PLANES[level] + 10, ROWS[level] + 16, 128), F32))
    extents = [(PLANES[level] + 8, ROWS[level] + 8, 128) for level in range(3)]
    shapes += [pltpu.VMEM(extent, F32) for extent in extents]
    for extent in extents:
        shapes += [pltpu.VMEM(extent, F32)] * 5
    shapes += [pltpu.VMEM(extent, F32) for extent in extents]
    for extent in extents:
        shapes += [pltpu.VMEM(extent, F32)] * 3
    shapes += [pltpu.VMEM(extent, F32) for extent in extents]
    shapes += [
        pltpu.VMEM((4, 32, 128), F32),
        pltpu.VMEM((16, 128), F32),
        pltpu.VMEM((16, 128), F32),
        pltpu.VMEM((10, 40, 128), F32),
        pltpu.VMEM((6, 40, 128), F32),
        pltpu.VMEM((128, 128), BF16),
        pltpu.VMEM((512, 256), BF16),
        pltpu.VMEM((512, 128), BF16),
        pltpu.VMEM((24, 256), F32),
        pltpu.VMEM((4 * ng + 16, 128), F32),
        pltpu.VMEM((2 * ng + 16, 128), F32),
    ]
    for extent in ((24, 256), (4 * ng, 128), (2 * ng, 128)):
        shapes += [pltpu.VMEM(extent, F32)] * 5
    for with_density in (True, False):
        halo = buffer_shapes(with_density)
        shapes += halo + halo + whole_shapes(with_density)
        tiles = 10 if with_density else 6
        shapes += [
            pltpu.VMEM((1, 128), F32),
            pltpu.VMEM((ROW, 1, 128), F32),
            pltpu.VMEM((8, 8, 128), F32),
            pltpu.VMEM((8, tiles, 8, 128), F32),
        ]
        copies = n_halo(with_density) + len(whole_messages(with_density))
        copies += (ROW - 1) + 7 + 7
        shapes += [pltpu.SemaphoreType.DMA((copies,)), pltpu.SemaphoreType.DMA((copies,))]
    return shapes


def solution(mesh):
    nf, ns = mesh.shape["fine"], mesh.shape["sub"]

    def body(rhs, density):
        return pl.pallas_call(
            functools.partial(kernel, nf, ns),
            out_shape=(
                jax.ShapeDtypeStruct(rhs.shape, F32),
                jax.ShapeDtypeStruct(rhs.shape, F32),
            ),
            in_specs=[pl.BlockSpec(memory_space=pltpu.VMEM)] * 2,
            out_specs=[pl.BlockSpec(memory_space=pltpu.VMEM)] * 2,
            scratch_shapes=scratch_shapes(nf // ROW),
            compiler_params=pltpu.CompilerParams(
                collective_id=0, has_side_effects=True, vmem_limit_bytes=32 * 1024 * 1024
            ),
        )(rhs, density)

    return jax.shard_map(
        body,
        mesh=mesh,
        in_specs=(P("fine", "sub", None), P("fine", "sub", None)),
        out_specs=(P("fine", "sub", None), P("fine", "sub", None)),
        check_vma=False,
    )
```

```python
import functools

import jax
import jax.numpy as jnp
from jax import lax
from jax.experimental import pallas as pl
from jax.experimental.pallas import tpu as pltpu
from jax.sharding import PartitionSpec as P

DEGREE = 4
CYCLES = 2
MESH = pl.DeviceIdType.MESH
F32 = jnp.float32
BF16 = jnp.bfloat16
ROW = 8
PLANES = (8, 4, 2)
ROWS = (32, 16, 8)


def chebyshev_constants(lower):
    upper = 2.0
    theta = 0.5 * (upper + lower)
    delta = 0.5 * (upper - lower)
    sigma = theta / delta
    ratio = 1.0 / sigma
    steps = []
    for _ in range(DEGREE - 1):
        next_ratio = 1.0 / (2.0 * sigma - ratio)
        steps.append((next_ratio * ratio, 2.0 * next_ratio / delta))
        ratio = next_ratio
    return 1.0 / theta, steps


def iota(shape, dim):
    return lax.broadcasted_iota(jnp.int32, shape, dim)


def roll(value, shift, axis):
    return pltpu.roll(value, shift % value.shape[axis], axis)


def invert(value):
    return pltpu.reciprocal(value, full_range=False)


def one_hot(condition):
    return jnp.where(condition, 1.0, 0.0).astype(F32)


def one_hot_matmul(value, matrix):
    count = value.shape[0]
    first = value.astype(BF16).astype(F32)
    rest = value - first
    second = rest.astype(BF16).astype(F32)
    parts = jnp.concatenate([first, second, rest - second], axis=0).astype(BF16)
    product = jnp.dot(parts, matrix, preferred_element_type=F32)
    return product[0:count] + product[count : 2 * count] + product[2 * count :]


def restrict_block(source, first, planes, rows, stride, work):
    field = source[first : first + planes, 0:rows, :]
    field = field.reshape(planes // 2, 2, rows, 128)
    work[0 : planes // 2, 0:rows, :] = field[:, 0] + field[:, 1]
    half = rows // 2
    both = (
        work[0 : planes // 2, pl.ds(0, half, stride=2), :]
        + work[0 : planes // 2, pl.ds(1, half, stride=2), :]
    )
    lane = iota(both.shape, 2)
    even = (lane // stride) % 2 == 0
    other = jnp.where(even, roll(both, -stride, 2), roll(both, stride, 2))
    return (both + other) * 0.125


def fine_coefficients(level, dens, coef, low, high):
    own = ROWS[level]
    scale = 2.0 * 0.25**level
    stride = 2**level
    face_z, face_x, face_y, diagonal, inverse = coef
    shape = (own + 16, 128)

    def compress(value):
        tail = jnp.where(
            iota((8, 128), 0) < 4, value[own : own + 8], value[own + 8 : own + 16]
        )
        return jnp.concatenate([value[0:own], tail], axis=0)

    def plane(p, down):
        here = dens[p + 1]
        above = dens[p + 2]
        lane = iota(shape, 1)
        right = roll(here, -1, 0)
        up = scale * invert(jnp.maximum(here + above, 0.1))
        x_face = scale * invert(jnp.maximum(here + right, 0.1))
        ahead = jnp.where(lane >= 128 - stride, 0.0, roll(here, -stride, 1))
        behind = jnp.where(lane < stride, 0.0, roll(here, stride, 1))
        y_face = scale * invert(jnp.maximum(here + ahead, 0.1))
        y_back = scale * invert(jnp.maximum(here + behind, 0.1))
        diag = up + down + x_face + roll(x_face, 1, 0) + y_face + y_back
        inside = here > 0.0
        face_z[p] = compress(jnp.where(inside & (above > 0.0), up, 0.0))
        face_x[p] = compress(jnp.where(inside & (right > 0.0), x_face, 0.0))
        face_y[p] = compress(jnp.where(lane >= 128 - stride, 0.0, y_face))
        diagonal[p] = compress(diag)
        inverse[p] = compress(invert(diag))
        return up

    lowest = scale * invert(jnp.maximum(dens[low] + dens[low + 1], 0.1))
    lax.fori_loop(low, high, plane, lowest, unroll=True)


def fine_apply(field, p, coef, q, stride):
    face_z, face_x, face_y, diagonal, _ = coef
    here = field[p]
    x_face = face_x[q]
    y_face = face_y[q]
    result = diagonal[q] * here
    result = result - face_z[q] * field[p + 1] - face_z[q - 1] * field[p - 1]
    result = result - x_face * roll(here, -1, 0) - roll(x_face * here, 1, 0)
    result = result - y_face * roll(here, -stride, 1) - roll(y_face * here, stride, 1)
    return result


def fine_smooth(level, source, coef, remain, updates, answer):
    planes = PLANES[level] + 8
    stride = 2**level
    inverse = coef[4]
    first, steps = chebyshev_constants(0.5)
    d0, d1, d2 = updates

    def start(p, carry):
        d0[p] = source[p] * inverse[p] * first
        return carry

    lax.fori_loop(0, planes, start, 0, unroll=True)
    chain = (d0, d1, d2)
    for sweep in range(3):
        old = chain[sweep]
        keep, add = steps[sweep]

        def step(p, carry, sweep=sweep, old=old, keep=keep, add=add):
            left = source[p] if sweep == 0 else remain[p]
            left = left - fine_apply(old, p, coef, p, stride)
            new = keep * old[p] + add * (left * inverse[p])
            if sweep < 2:
                remain[p] = left
                chain[sweep + 1][p] = new
            else:
                answer[p] = d0[p] + d1[p] + d2[p] + new
            return carry

        lax.fori_loop(sweep + 1, planes - sweep - 1, step, 0, unroll=True)


def packed_coefficients(dens, ny, nx, scale):
    rows = dens.shape[0]
    z = iota(dens.shape, 0)
    lane = iota(dens.shape, 1)
    y = lane % ny
    x = lane // ny
    scale = 2.0 * scale

    def neighbour(shift, axis, outside):
        return jnp.where(outside, 0.0, roll(dens, shift, axis))

    above = neighbour(-1, 0, z == rows - 1)
    below = neighbour(1, 0, z == 0)
    right = neighbour(-ny, 1, x >= nx - 1)
    left = neighbour(ny, 1, x == 0)
    ahead = neighbour(-1, 1, y == ny - 1)
    behind = neighbour(1, 1, y == 0)

    def face(other):
        return scale * invert(jnp.maximum(dens + other, 0.1))

    up, x_face, y_face = face(above), face(right), face(ahead)
    diagonal = up + face(below) + x_face + face(left) + y_face + face(behind)
    inside = dens > 0.0

    def inner(value, other):
        return jnp.where(inside & (other > 0.0), value, 0.0)

    return (
        inner(up, above),
        inner(x_face, right),
        inner(y_face, ahead),
        jnp.where(inside, diagonal, 0.0),
        jnp.where(inside, invert(diagonal), 0.0),
    )


def packed_apply(field, coef, ny):
    face_z, face_x, face_y, diagonal, _ = coef
    result = diagonal * field
    result = result - face_z * roll(field, -1, 0) - roll(face_z * field, 1, 0)
    result = result - face_x * roll(field, -ny, 1) - roll(face_x * field, ny, 1)
    result = result - face_y * roll(field, -1, 1) - roll(face_y * field, 1, 1)
    return result


def packed_smooth(source, coef, ny, lower):
    first, steps = chebyshev_constants(lower)
    inverse = coef[4]
    update = source * inverse * first
    answer = update
    for keep, add in steps:
        source = source - packed_apply(update, coef, ny)
        update = keep * update + add * (source * inverse)
        answer = answer + update
    return answer


PIECES = {
    ("a", 1): ((("D1", 5, 1, 4), ("D2", 5, 3, 2)), (("R1", 4, 0, 4), ("R2", 4, 2, 2))),
    ("a", -1): ((("D1", 5, 9, 4), ("D2", 5, 7, 2)), (("R1", 4, 8, 4), ("R2", 4, 6, 2))),
    ("a", 2): ((("D1", 8, 0, 1), ("D2", 5, 1, 2)), (("R2", 4, 0, 2),)),
    ("a", -2): ((("D1", 5, 13, 1), ("D2", 5, 9, 2)), (("R2", 4, 8, 2),)),
    ("a", 3): ((("D2", 6, 0, 1),), ()),
    ("a", -3): ((("D2", 5, 11, 1),), ()),
    ("b", 1): (
        (("D0", 9, 1, 4), ("D1", 5, 1, 4), ("D2", 5, 3, 2)),
        (("R0", 9, 1, 3), ("R1", 4, 0, 4), ("R2", 4, 2, 2)),
    ),
    ("b", -1): (
        (("D0", 5, 13, 4), ("D1", 5, 9, 4), ("D2", 5, 7, 2)),
        (("R0", 4, 12, 3), ("R1", 4, 8, 4), ("R2", 4, 6, 2)),
    ),
    ("b", 2): ((("D2", 5, 1, 2),), (("R2", 4, 0, 2),)),
    ("b", -2): ((("D2", 5, 9, 2),), (("R2", 4, 8, 2),)),
}
WHOLE = (("D0", 1, 3, 0, 5), ("D0", -1, 0, 13, 5), ("R0", 1, 4, 0, 4), ("R0", -1, 0, 12, 4))


def whole_messages(with_density):
    return WHOLE if with_density else WHOLE[2:]


def z_messages(with_density):
    result = []
    for (part, shift), (density, field) in PIECES.items():
        pieces = (density if with_density else ()) + field
        if pieces:
            result.append((part, shift, pieces))
    return result


def paired(name, tiles):
    return name[1] != "0" and tiles % 2 == 0


def piece_tiles(part, piece):
    name, _, _, count = piece
    tiles = count * (ROWS[int(name[1])] // 8 if part == "a" else 1)
    return tiles // 2 if paired(name, tiles) else tiles


def x_pieces(with_density):
    result = []
    for level in range(3):
        count = PLANES[level]
        if with_density:
            result.append(("D%d" % level, count, count // 2 if level else count))
        result.append(("R%d" % level, count, (4, 1, 1)[level]))
    return result


def buffer_shapes(with_density):
    tiles = [sum(sent for _, _, sent in x_pieces(with_density))] * 2
    for part, _, pieces in z_messages(with_density):
        tiles.append(sum(piece_tiles(part, piece) for piece in pieces))
    return [pltpu.VMEM((count, 8, 128), F32) for count in tiles]


def whole_shapes(with_density):
    return [pltpu.VMEM((count, 32, 128), F32) for _, _, _, _, count in whole_messages(with_density)]


def n_halo(with_density):
    return 2 + len(z_messages(with_density))


def even_lanes(tiles):
    return iota((tiles, 8, 128), 2) % 2 == 0


def upper_rows(tiles):
    return iota((tiles, 8, 128), 1) < 4


def pack_lanes(block):
    half = block.shape[0] // 2
    return jnp.where(even_lanes(half), block[0:half], block[half:])


def unpack_lanes(block):
    even = even_lanes(block.shape[0])
    return jnp.concatenate(
        [jnp.where(even, block, roll(block, 1, 2)), jnp.where(even, roll(block, -1, 2), block)],
        axis=0,
    )


def partners_of(place):
    k, s, _, ns = place
    i, y, half = k % ROW, k // ROW % 8, k // (8 * ROW)
    depth, side = [], []
    for delta in (4, 3, 5, 2, 6, 1, 7):
        z = (half * ns + s + delta) % (2 * ns)
        depth.append((((z // ns) * 8 + y) * ROW + i, z % ns))
        side.append((delta, ((half * 8 + (y + delta) % 8) * ROW + i, s)))
    return depth, side


class Phase:
    def __init__(self, refs, place, with_density, buffers, coarse, send_sem, recv_sem):
        send, recv, whole = buffers
        self.whole_in = whole
        self.whole = whole_messages(with_density)
        self.refs = refs
        self.k, self.s, self.nf, self.ns = place
        self.dense = with_density
        self.send, self.recv = send, recv
        self.row, self.row_in, self.depth_in, self.side_in = coarse
        self.send_sem, self.recv_sem = send_sem, recv_sem
        self.started = []
        self.count = 0
        self.z = z_messages(with_density)
        self.copies = {}
        self.i = self.k % ROW
        self.g = self.k // ROW
        self.ng = self.nf // ROW
        self.y = self.g % 8
        self.z_at = self.g // 8 * self.ns + self.s
        self.depth_partners, self.side_partners = partners_of(place)

    def start(self, source, target, k, s, shift=0):
        index = self.count
        self.count += 1
        copy = pltpu.make_async_remote_copy(
            src_ref=source,
            dst_ref=target,
            send_sem=self.send_sem.at[index],
            recv_sem=self.recv_sem.at[index],
            device_id=(k, s),
            device_id_type=MESH,
        )
        self.when(self.has_target(shift), copy.start)
        self.started.append((copy, shift))
        return copy

    def has_target(self, shift):
        if shift == 0:
            return None
        return self.k < self.nf - shift if shift > 0 else self.k >= -shift

    def has_source(self, shift):
        return self.has_target(-shift)

    def when(self, condition, action):
        if condition is None:
            action()
        else:
            pl.when(condition)(action)

    def start_whole(self, fields):
        self.whole_copies = []
        for index, (name, shift, first, _, count) in enumerate(self.whole):
            target = (self.k + shift + self.nf) % self.nf
            ref, lead = fields[name]
            source = ref.at[lead + first : lead + first + count, 0:32, :]
            self.whole_copies.append(
                self.start(source, self.whole_in[index], target, self.s, shift)
            )

    def unpack_whole(self):
        for index, (name, shift, _, target, count) in enumerate(self.whole):
            self.when(self.has_source(shift), self.whole_copies[index].wait_recv)
        for index, (name, shift, _, target, count) in enumerate(self.whole):
            block = jnp.where(self.has_source(shift), self.whole_in[index][...], 0.0)
            self.refs[name][target : target + count, 0:32, :] = block

    def pack_x(self):
        for which in (0, 1):
            at = 0
            for name, count, sent in x_pieces(self.dense):
                level = int(name[1])
                lead = 5 if name[0] == "D" else 4
                row = ROWS[level] - 8 if which == 0 else 0
                block = self.refs[name][lead : lead + count, row : row + 8, :]
                if level:
                    block = pack_lanes(block)
                if block.shape[0] > sent:
                    near, far = block[0:sent], roll(block[sent:], 4, 1)
                    upper = upper_rows(sent)
                    if which == 0:
                        block = jnp.where(upper, far, near)
                    else:
                        block = jnp.where(upper, near, far)
                self.send[which][at : at + sent] = block
                at += sent

    def start_x(self):
        up, down = (self.s + 1) % self.ns, (self.s + self.ns - 1) % self.ns
        self.x_copies = [
            self.start(self.send[0], self.recv[0], self.k, up),
            self.start(self.send[1], self.recv[1], self.k, down),
        ]

    def unpack_x(self):
        for copy in self.x_copies:
            copy.wait_recv()
        low_in = jnp.where(self.s > 0, 1.0, 0.0).astype(F32)
        high_in = jnp.where(self.s < self.ns - 1, 1.0, 0.0).astype(F32)
        at = 0
        for name, count, sent in x_pieces(self.dense):
            level = int(name[1])
            own = ROWS[level]
            lead = 5 if name[0] == "D" else 4
            low, high = self.recv[0][at : at + sent], self.recv[1][at : at + sent]
            at += sent
            ref = self.refs[name]
            if name[0] == "D":
                if level:
                    low, high = unpack_lanes(low), unpack_lanes(high)
                ref[lead : lead + count, own : own + 8, :] = high * high_in
                ref[lead : lead + count, own + 8 : own + 16, :] = low * low_in
                continue
            upper = upper_rows(sent)
            block = jnp.where(upper, high, low)
            if sent < (count // 2 if level else count):
                far = roll(jnp.where(upper, low, high), 4, 1)
                block = jnp.concatenate([block, far], axis=0)
            if level:
                block = unpack_lanes(block)
            ref[lead : lead + count, own : own + 8, :] = block

    def pack_z(self, part):
        for index, (kind, _, pieces) in enumerate(self.z):
            if kind != part:
                continue
            at = 0
            for piece in pieces:
                name, source, _, count = piece
                ref, own = self.refs[name], ROWS[int(name[1])]
                if part == "a":
                    block = ref[source : source + count, 0:own, :]
                    block = block.reshape(count * own // 8, 8, 128)
                else:
                    block = ref[source : source + count, own : own + 8, :]
                    if name[0] == "D":
                        low = ref[source : source + count, own + 8 : own + 16, :]
                        block = jnp.where(upper_rows(count), block, low)
                if paired(name, block.shape[0]):
                    block = pack_lanes(block)
                self.send[2 + index][at : at + block.shape[0]] = block
                at += block.shape[0]

    def start_z(self, part):
        for index, (kind, shift, _) in enumerate(self.z):
            if kind == part:
                target = (self.k + shift + self.nf) % self.nf
                self.copies[index] = self.start(
                    self.send[2 + index], self.recv[2 + index], target, self.s, shift
                )

    def unpack_z(self):
        for index, (_, shift, _) in enumerate(self.z):
            self.when(self.has_source(shift), self.copies[index].wait_recv)
        for index, (part, shift, pieces) in enumerate(self.z):
            inside = self.has_source(shift)
            at = 0
            for piece in pieces:
                name, _, target, count = piece
                ref, own = self.refs[name], ROWS[int(name[1])]
                sent = piece_tiles(part, piece)
                block = jnp.where(inside, self.recv[2 + index][at : at + sent], 0.0)
                at += sent
                if sent < (count * own // 8 if part == "a" else count):
                    block = unpack_lanes(block)
                if part == "a":
                    ref[target : target + count, 0:own, :] = block.reshape(count, own, 128)
                else:
                    ref[target : target + count, own : own + 8, :] = block
                    if name[0] == "D":
                        ref[target : target + count, own + 8 : own + 16, :] = block

    def pack_row(self, fields, pair, spread_row):
        for index, field in enumerate(fields):
            pillar = jnp.sum(field, axis=0).reshape(4, 8, 128)
            pair[4 * index : 4 * index + 4, :] = jnp.sum(pillar, axis=1) * 0.125**3
        spread = one_hot_matmul(pair[...], spread_row[...])[0:8]
        mine = iota((8, 128), 1) // 16 == iota((8, 128), 0)
        row = jnp.sum(jnp.where(mine, spread, 0.0), axis=0, keepdims=True)
        self.row[...] = row
        self.row_in[self.i] = row

    def start_rows(self):
        self.row_copies = []
        for delta in range(1, ROW):
            target = self.g * ROW + (self.i + delta) % ROW
            self.row_copies.append(
                self.start(self.row, self.row_in.at[self.i], target, self.s)
            )

    def start_depth(self):
        for copy in self.row_copies:
            copy.wait_recv()
        line = iota((8, 128), 0)
        tile = jnp.zeros((8, 128), F32)
        for index in range(ROW):
            tile = jnp.where(line == index, self.row_in[index], tile)
        self.depth_in[self.z_at] = tile
        self.depth_copies = []
        for k, s in self.depth_partners:
            slot = self.depth_in.at[self.z_at]
            self.depth_copies.append(self.start(slot, slot, k, s))

    def start_sides(self, work, pool):
        for copy in self.depth_copies:
            copy.wait_recv()
        left = iota((8, 128), 1) < 64
        slot = self.side_in.at[self.y]
        wide = []
        for half in range(2):
            tiles = [self.depth_in[4 * half + index] for index in range(4)]
            turned = [roll(tile, 64, 1) for tile in tiles]
            fields = [jnp.where(left, tiles[a], turned[a + 1]) for a in (0, 2)]
            if self.dense:
                fields += [jnp.where(left, turned[a], tiles[a + 1]) for a in (0, 2)]
            for index, field in enumerate(fields):
                slot[2 + len(fields) * half + index] = field
            wide.append(jnp.concatenate(fields, axis=1))
        wide = jnp.concatenate(wide, axis=0)
        sums = one_hot_matmul(wide, pool[0 : wide.shape[1], :])
        work[...] = sums[:, 0:128]
        line = iota((8, 128), 0)
        for half in range(2):
            four = work[pl.ds(8 * half, 4, stride=2), :] + work[pl.ds(8 * half + 1, 4, stride=2), :]
            slot[half, 0:4, :] = four * 0.125
            five = sums[8 * half : 8 * half + 8, 128:256]
            five = five + roll(five, -1, 0)
            five = (five + roll(five, -2, 0)) * (0.125 * 0.125)
            five = jnp.where(line % 2 == 0, five[0:1], five[4:5])
            slot[half, 4:8, :] = five[4:8]
        self.side_copies = []
        for delta, (k, s) in self.side_partners:
            if delta in (1, 7):
                self.side_copies.append(self.start(slot, slot, k, s))
            else:
                part = slot.at[0:2]
                self.side_copies.append(self.start(part, part, k, s))

    def wait_sides(self):
        for copy in self.side_copies:
            copy.wait_recv()

    def group_fields(self, group):
        wrapped = (group + self.ng) % self.ng
        y, half = wrapped % 8, wrapped // 8
        count = 4 if self.dense else 2
        tiles = [self.side_in[y, 2 + half * count + index] for index in range(count)]
        return [
            jnp.concatenate(tiles[at : at + 2], axis=1) for at in range(0, count, 2)
        ]

    def finish(self, first, last):
        for copy, shift in self.started[first:last]:
            self.when(self.has_target(shift), copy.wait_send)


def split_packed(value):
    left = iota(value.shape, 1) < 64
    return jnp.where(left, value, 0.0), jnp.where(left, roll(value, 64, 1), 0.0)


def build_matrices(pool, fan):
    line, lane = iota((128, 128), 0), iota((128, 128), 1)
    for half in range(4):
        x, y = line // 16 + 8 * (half % 2), line % 16
        rows = slice(128 * half, 128 * half + 128)
        home4 = (x // 2) * 8 + y // 2 + 64 * (half // 2)
        home5 = (x // 4) * 4 + y // 4 + 64 * (half // 2)
        pool[rows, 0:128] = one_hot(home4 == lane).astype(BF16)
        pool[rows, 128:256] = one_hot(home5 == lane).astype(BF16)
    three = one_hot(line % 16 == lane // 8).astype(BF16)
    fan[0:128, :] = three
    fan[128:256, :] = three
    fan[256:384, :] = one_hot(line % 8 == lane // 16).astype(BF16)
    fan[384:512, :] = one_hot(line % 4 == lane // 32).astype(BF16)


def kernel(nf, ns, rhs, dens, solution, residual, *scratch):
    scratch = list(scratch)

    def take(count):
        taken = scratch[:count]
        del scratch[:count]
        return taken

    refs = {}
    for name in ("D0", "D1", "D2", "R0", "R1", "R2"):
        (refs[name],) = take(1)
    fine_coef = [take(5) for _ in range(3)]
    remains = take(3)
    updates = [take(3) for _ in range(3)]
    answers = take(3)
    (work, tile_work, pair, sol, spread) = take(5)
    (spread_row, pool, fan, keep3, keep4, keep5) = take(6)
    coarse_coef = [take(5) for _ in range(3)]
    phases = []
    k, s = lax.axis_index("fine"), lax.axis_index("sub")
    for with_density in (True, False):
        count = n_halo(with_density)
        buffers = take(count), take(count), take(len(whole_messages(with_density)))
        coarse = take(4)
        send_sem, recv_sem = take(2)
        phases.append(
            Phase(refs, (k, s, nf, ns), with_density, buffers, coarse, send_sem, recv_sem)
        )
    ng = nf // ROW
    i, g = k % ROW, k // ROW

    barrier = pltpu.get_barrier_semaphore()
    partners = []
    for shift in (1, 2, 3):
        partners += [((k + shift) % nf, s), ((k + nf - shift) % nf, s)]
    partners += [(g * ROW + (i + delta) % ROW, s) for delta in range(1, ROW)]
    depth, side = partners_of((k, s, nf, ns))
    partners += depth + [device for _, device in side]
    for partner in partners:
        pl.semaphore_signal(barrier, inc=1, device_id=partner, device_id_type=MESH)

    pair[...] = jnp.zeros((16, 128), F32)

    def restrict_all(name, lead):
        for level in range(2):
            refs[name + str(level + 1)][
                lead : lead + PLANES[level + 1], 0 : ROWS[level + 1], :
            ] = restrict_block(
                refs[name + str(level)], lead, PLANES[level], ROWS[level], 2**level, work
            )

    def coefficients(level, low, high):
        fine_coefficients(level, refs["D" + str(level)], fine_coef[level], low, high)

    def smooth(level):
        fine_smooth(
            level,
            refs["R" + str(level)],
            fine_coef[level],
            remains[level],
            updates[level],
            answers[level],
        )

    line, lane = iota((128, 128), 0), iota((128, 128), 1)
    spread_row[...] = one_hot(line // 8 == lane % 16).astype(BF16)

    for cycle in range(CYCLES):
        phase = phases[cycle]
        if cycle == 0:
            phase.pack_row((rhs[...], dens[...]), pair, spread_row)
            pl.semaphore_wait(barrier, len(partners))
        else:
            phase.pack_row((refs["R0"][4:12, 0:32, :],), pair, spread_row)
        phase.start_rows()
        if cycle == 0:
            refs["R0"][4:12, 0:32, :] = rhs[...]
            refs["D0"][5:13, 0:32, :] = dens[...]
            restrict_all("D", 5)
        restrict_all("R", 4)
        phase.pack_x()
        phase.start_x()
        if cycle == 0:
            phase.start_whole({"D0": (dens, 0), "R0": (rhs, 0)})
        else:
            phase.start_whole({"R0": (refs["R0"], 4)})
        phase.pack_z("a")
        phase.start_z("a")
        if cycle == 0:
            build_matrices(pool, fan)
            for level in range(3):
                for name, lead in (("D", 5), ("R", 4)):
                    ref = refs[name + str(level)]
                    planes, rows, _ = ref.shape
                    blank = jnp.zeros((lead, rows, 128), F32)
                    ref[0:lead] = blank
                    ref[planes - lead : planes] = blank
            for ref in (keep4, keep5):
                rows = ref.shape[0]
                ref[0:8, :] = jnp.zeros((8, 128), F32)
                ref[rows - 8 : rows, :] = jnp.zeros((8, 128), F32)
        phase.start_depth()
        phase.unpack_x()
        phase.pack_z("b")
        phase.start_z("b")
        phase.start_sides(tile_work, pool)
        if cycle == 0:
            coefficients(0, 5, 11)
        else:
            phases[0].finish(0, None)
        phase.unpack_z()
        for level in (2, 1):
            if cycle == 0:
                coefficients(level, 0, PLANES[level] + 8)
            smooth(level)
        phase.unpack_whole()
        if cycle == 0:
            coefficients(0, 0, 5)
            coefficients(0, 11, 16)
        smooth(0)
        if cycle == 1:
            phase.finish(0, -7)
        phase.wait_sides()

        tiles = [phase.side_in[index % 8, index // 8] for index in range(ng)]
        line = iota((8, 128), 0)
        packed4, packed5 = [], []
        for index in range(0, ng, 2):
            packed4.append(jnp.where(line < 4, tiles[index], roll(tiles[index + 1], 4, 0)))
        for index in range(0, ng, 4):
            first = jnp.where(line < 6, tiles[index], tiles[index + 1])
            second = jnp.where(line < 6, tiles[index + 2], tiles[index + 3])
            packed5.append(jnp.where(line < 4, roll(first, 4, 0), second))
        source4, density4 = split_packed(jnp.concatenate(packed4, axis=0))
        source5, density5 = split_packed(jnp.concatenate(packed5, axis=0))
        if cycle == 0:
            low_in = jnp.where(g > 0, 1.0, 0.0).astype(F32)
            high_in = jnp.where(g < ng - 1, 1.0, 0.0).astype(F32)
            density3 = jnp.concatenate(
                [
                    phase.group_fields(g - 1)[1] * low_in,
                    phase.group_fields(g)[1],
                    phase.group_fields(g + 1)[1] * high_in,
                ],
                axis=0,
            )
            for index, (field, ny) in enumerate(
                ((density3, 16), (density4, 8), (density5, 4))
            ):
                values = packed_coefficients(field, ny, ny, 0.25 ** (3 + index))
                for ref, value in zip(coarse_coef[index], values):
                    ref[...] = value
        coef3, coef4, coef5 = ([ref[...] for ref in refs5] for refs5 in coarse_coef)
        total = jnp.sum(jnp.sum(source5, axis=0, keepdims=True), axis=1, keepdims=True)
        weight = jnp.sum(jnp.sum(coef5[3], axis=0, keepdims=True), axis=1, keepdims=True)
        n4, n5 = 4 * ng, 2 * ng
        keep5[8 : 8 + n5, :] = packed_smooth(source5, coef5, 4, 0.05) + total / weight
        keep4[8 : 8 + n4, :] = packed_smooth(source4, coef4, 8, 0.5)

        source3 = jnp.concatenate(
            [phase.group_fields(g + shift)[0] for shift in (-1, 0, 1)], axis=0
        )
        keep3[...] = packed_smooth(source3, coef3, 16, 0.5)

        row = iota((16, 512), 0)
        lane = iota((16, 512), 1)
        x3 = row // 2 + jnp.where(row < 12, 0, -8) + (4 * s + 4)
        inside = (x3 >= 4) & (x3 < 20)
        x_lane = jnp.where(
            lane < 256, lane // 16, jnp.where(lane < 384, (lane - 256) // 8, (lane - 384) // 4)
        )
        x_row = jnp.where(lane < 256, x3 - 4, jnp.where(lane < 384, x3 // 2 - 2, x3 // 4 - 1))
        chosen = (x_lane == x_row) & inside
        picked = []
        for t in range(3):
            parts = jnp.concatenate(
                [
                    keep3[pl.ds(7 + i + t, 1), :],
                    keep4[pl.ds((k + 1 + t) // 2 + 7, 1), :],
                    keep5[pl.ds((k + 3 + t) // 4 + 7, 1), :],
                ],
                axis=1,
            )
            picked.append(jnp.where(chosen, parts, 0.0))
        spread[0:3, 0:16, :] = one_hot_matmul(
            jnp.concatenate(picked, axis=0), fan[...]
        ).reshape(3, 16, 128)

        for level in (2, 1):
            rows = ROWS[level]
            answer = answers[level]
            planes = PLANES[level] + 2
            coarse = jnp.concatenate(
                [spread[(p + 1) // 2 : (p + 1) // 2 + 1, 0 : rows + 8, :] for p in range(planes)],
                axis=0,
            )
            value = answer[3 : 3 + planes] + coarse
            own, ends = value[:, 0:rows, :], value[:, rows : rows + 8, :]
            spread[0:planes, pl.ds(0, rows, stride=2), :] = own
            spread[0:planes, pl.ds(1, rows, stride=2), :] = own
            spread[0:planes, 2 * rows : 2 * rows + 8, :] = jnp.where(
                upper_rows(planes), ends[:, 0:1, :], ends[:, 7:8, :]
            )


        def advance(p, carry, cycle=cycle):
            step = 0.4 * (answers[0][p + 3] + spread[(p + 1) // 2])
            sol[p] = step if cycle == 0 else sol[p] + step
            return carry

        lax.fori_loop(0, PLANES[0] + 2, advance, 0, unroll=True)

        def defect(p, carry, cycle=cycle):
            applied = fine_apply(sol, p + 1, fine_coef[0], p + 4, 1)
            left = rhs[p] - applied[0:32, :]
            if cycle == 0:
                refs["R0"][p + 4, 0:32, :] = left
            else:
                residual[p] = left
                solution[p] = sol[p + 1, 0:32, :]
            return carry

        lax.fori_loop(0, PLANES[0], defect, 0, unroll=True)

    phases[1].finish(-7, None)


def scratch_shapes(ng):
    shapes = []
    for level in range(3):
        shapes.append(pltpu.VMEM((PLANES[level] + 10, ROWS[level] + 16, 128), F32))
    extents = [(PLANES[level] + 8, ROWS[level] + 8, 128) for level in range(3)]
    shapes += [pltpu.VMEM(extent, F32) for extent in extents]
    for extent in extents:
        shapes += [pltpu.VMEM(extent, F32)] * 5
    shapes += [pltpu.VMEM(extent, F32) for extent in extents]
    for extent in extents:
        shapes += [pltpu.VMEM(extent, F32)] * 3
    shapes += [pltpu.VMEM(extent, F32) for extent in extents]
    shapes += [
        pltpu.VMEM((4, 32, 128), F32),
        pltpu.VMEM((16, 128), F32),
        pltpu.VMEM((16, 128), F32),
        pltpu.VMEM((10, 40, 128), F32),
        pltpu.VMEM((6, 40, 128), F32),
        pltpu.VMEM((128, 128), BF16),
        pltpu.VMEM((512, 256), BF16),
        pltpu.VMEM((512, 128), BF16),
        pltpu.VMEM((24, 256), F32),
        pltpu.VMEM((4 * ng + 16, 128), F32),
        pltpu.VMEM((2 * ng + 16, 128), F32),
    ]
    for extent in ((24, 256), (4 * ng, 128), (2 * ng, 128)):
        shapes += [pltpu.VMEM(extent, F32)] * 5
    for with_density in (True, False):
        halo = buffer_shapes(with_density)
        shapes += halo + halo + whole_shapes(with_density)
        tiles = 10 if with_density else 6
        shapes += [
            pltpu.VMEM((1, 128), F32),
            pltpu.VMEM((ROW, 1, 128), F32),
            pltpu.VMEM((8, 8, 128), F32),
            pltpu.VMEM((8, tiles, 8, 128), F32),
        ]
        copies = n_halo(with_density) + len(whole_messages(with_density))
        copies += (ROW - 1) + 7 + 7
        shapes += [pltpu.SemaphoreType.DMA((copies,)), pltpu.SemaphoreType.DMA((copies,))]
    return shapes


def solution(mesh):
    nf, ns = mesh.shape["fine"], mesh.shape["sub"]

    def body(rhs, density):
        return pl.pallas_call(
            functools.partial(kernel, nf, ns),
            out_shape=(
                jax.ShapeDtypeStruct(rhs.shape, F32),
                jax.ShapeDtypeStruct(rhs.shape, F32),
            ),
            in_specs=[pl.BlockSpec(memory_space=pltpu.VMEM)] * 2,
            out_specs=[pl.BlockSpec(memory_space=pltpu.VMEM)] * 2,
            scratch_shapes=scratch_shapes(nf // ROW),
            compiler_params=pltpu.CompilerParams(
                collective_id=0, has_side_effects=True, vmem_limit_bytes=32 * 1024 * 1024
            ),
        )(rhs, density)

    return jax.shard_map(
        body,
        mesh=mesh,
        in_specs=(P("fine", "sub", None), P("fine", "sub", None)),
        out_specs=(P("fine", "sub", None), P("fine", "sub", None)),
        check_vma=False,
    )
```

```python
import functools

import jax
import jax.numpy as jnp
from jax import lax
from jax.experimental import pallas as pl
from jax.experimental.pallas import tpu as pltpu
from jax.sharding import PartitionSpec as P

DEGREE = 4
CYCLES = 2
MESH = pl.DeviceIdType.MESH
F32 = jnp.float32
BF16 = jnp.bfloat16
ROW = 8
PLANES = (8, 4, 2)
ROWS = (32, 16, 8)


def chebyshev_constants(lower):
    upper = 2.0
    theta = 0.5 * (upper + lower)
    delta = 0.5 * (upper - lower)
    sigma = theta / delta
    ratio = 1.0 / sigma
    steps = []
    for _ in range(DEGREE - 1):
        next_ratio = 1.0 / (2.0 * sigma - ratio)
        steps.append((next_ratio * ratio, 2.0 * next_ratio / delta))
        ratio = next_ratio
    return 1.0 / theta, steps


def iota(shape, dim):
    return lax.broadcasted_iota(jnp.int32, shape, dim)


def roll(value, shift, axis):
    return pltpu.roll(value, shift % value.shape[axis], axis)


def invert(value):
    return pltpu.reciprocal(value, full_range=False)


def one_hot(condition):
    return jnp.where(condition, 1.0, 0.0).astype(F32)


def one_hot_matmul(value, matrix):
    count = value.shape[0]
    first = value.astype(BF16).astype(F32)
    rest = value - first
    second = rest.astype(BF16).astype(F32)
    parts = jnp.concatenate([first, second, rest - second], axis=0).astype(BF16)
    product = jnp.dot(parts, matrix, preferred_element_type=F32)
    return product[0:count] + product[count : 2 * count] + product[2 * count :]


def restrict_block(source, first, planes, rows, stride, work):
    field = source[first : first + planes, 0:rows, :]
    field = field.reshape(planes // 2, 2, rows, 128)
    work[0 : planes // 2, 0:rows, :] = field[:, 0] + field[:, 1]
    half = rows // 2
    both = (
        work[0 : planes // 2, pl.ds(0, half, stride=2), :]
        + work[0 : planes // 2, pl.ds(1, half, stride=2), :]
    )
    lane = iota(both.shape, 2)
    even = (lane // stride) % 2 == 0
    other = jnp.where(even, roll(both, -stride, 2), roll(both, stride, 2))
    return (both + other) * 0.125


def fine_coefficients(level, dens, coef, low, high):
    own = ROWS[level]
    scale = 2.0 * 0.25**level
    stride = 2**level
    face_z, face_x, face_y, diagonal, inverse = coef
    shape = (own + 16, 128)

    def compress(value):
        tail = jnp.where(
            iota((8, 128), 0) < 4, value[own : own + 8], value[own + 8 : own + 16]
        )
        return jnp.concatenate([value[0:own], tail], axis=0)

    def plane(p, down):
        here = dens[p + 1]
        above = dens[p + 2]
        lane = iota(shape, 1)
        right = roll(here, -1, 0)
        up = scale * invert(jnp.maximum(here + above, 0.1))
        x_face = scale * invert(jnp.maximum(here + right, 0.1))
        ahead = jnp.where(lane >= 128 - stride, 0.0, roll(here, -stride, 1))
        behind = jnp.where(lane < stride, 0.0, roll(here, stride, 1))
        y_face = scale * invert(jnp.maximum(here + ahead, 0.1))
        y_back = scale * invert(jnp.maximum(here + behind, 0.1))
        diag = up + down + x_face + roll(x_face, 1, 0) + y_face + y_back
        inside = here > 0.0
        face_z[p] = compress(jnp.where(inside & (above > 0.0), up, 0.0))
        face_x[p] = compress(jnp.where(inside & (right > 0.0), x_face, 0.0))
        face_y[p] = compress(jnp.where(lane >= 128 - stride, 0.0, y_face))
        diagonal[p] = compress(diag)
        inverse[p] = compress(invert(diag))
        return up

    lowest = scale * invert(jnp.maximum(dens[low] + dens[low + 1], 0.1))
    lax.fori_loop(low, high, plane, lowest, unroll=True)


def fine_apply(field, p, coef, q, stride):
    face_z, face_x, face_y, diagonal, _ = coef
    here = field[p]
    x_face = face_x[q]
    y_face = face_y[q]
    result = diagonal[q] * here
    result = result - face_z[q] * field[p + 1] - face_z[q - 1] * field[p - 1]
    result = result - x_face * roll(here, -1, 0) - roll(x_face * here, 1, 0)
    result = result - y_face * roll(here, -stride, 1) - roll(y_face * here, stride, 1)
    return result


def fine_smooth(level, source, coef, remain, updates, answer):
    planes = PLANES[level] + 8
    stride = 2**level
    inverse = coef[4]
    first, steps = chebyshev_constants(0.5)
    d0, d1, d2 = updates

    def start(p, carry):
        d0[p] = source[p] * inverse[p] * first
        return carry

    lax.fori_loop(0, planes, start, 0, unroll=True)
    chain = (d0, d1, d2)
    for sweep in range(3):
        old = chain[sweep]
        keep, add = steps[sweep]

        def step(p, carry, sweep=sweep, old=old, keep=keep, add=add):
            left = source[p] if sweep == 0 else remain[p]
            left = left - fine_apply(old, p, coef, p, stride)
            new = keep * old[p] + add * (left * inverse[p])
            if sweep < 2:
                remain[p] = left
                chain[sweep + 1][p] = new
            else:
                answer[p] = d0[p] + d1[p] + d2[p] + new
            return carry

        lax.fori_loop(sweep + 1, planes - sweep - 1, step, 0, unroll=True)


def packed_coefficients(dens, ny, nx, scale):
    rows = dens.shape[0]
    z = iota(dens.shape, 0)
    lane = iota(dens.shape, 1)
    y = lane % ny
    x = lane // ny
    scale = 2.0 * scale

    def neighbour(shift, axis, outside):
        return jnp.where(outside, 0.0, roll(dens, shift, axis))

    above = neighbour(-1, 0, z == rows - 1)
    below = neighbour(1, 0, z == 0)
    right = neighbour(-ny, 1, x >= nx - 1)
    left = neighbour(ny, 1, x == 0)
    ahead = neighbour(-1, 1, y == ny - 1)
    behind = neighbour(1, 1, y == 0)

    def face(other):
        return scale * invert(jnp.maximum(dens + other, 0.1))

    up, x_face, y_face = face(above), face(right), face(ahead)
    diagonal = up + face(below) + x_face + face(left) + y_face + face(behind)
    inside = dens > 0.0

    def inner(value, other):
        return jnp.where(inside & (other > 0.0), value, 0.0)

    return (
        inner(up, above),
        inner(x_face, right),
        inner(y_face, ahead),
        jnp.where(inside, diagonal, 0.0),
        jnp.where(inside, invert(diagonal), 0.0),
    )


def packed_apply(field, coef, ny):
    face_z, face_x, face_y, diagonal, _ = coef
    result = diagonal * field
    result = result - face_z * roll(field, -1, 0) - roll(face_z * field, 1, 0)
    result = result - face_x * roll(field, -ny, 1) - roll(face_x * field, ny, 1)
    result = result - face_y * roll(field, -1, 1) - roll(face_y * field, 1, 1)
    return result


def packed_smooth(source, coef, ny, lower):
    first, steps = chebyshev_constants(lower)
    inverse = coef[4]
    update = source * inverse * first
    answer = update
    for keep, add in steps:
        source = source - packed_apply(update, coef, ny)
        update = keep * update + add * (source * inverse)
        answer = answer + update
    return answer


PIECES = {
    ("first", 1): {
        "a": (("D0", 8, 0, 5), ("R0", 8, 0, 4), ("D1", 5, 1, 4), ("D2", 5, 3, 2))
        + (("R1", 4, 0, 4), ("R2", 4, 2, 2)),
    },
    ("first", -1): {
        "a": (("D0", 5, 13, 5), ("R0", 4, 12, 4), ("D1", 5, 9, 4), ("D2", 5, 7, 2))
        + (("R1", 4, 8, 4), ("R2", 4, 6, 2)),
    },
    ("first", 3): {"a": (("D2", 6, 0, 1),)},
    ("first", -3): {"a": (("D2", 5, 11, 1),)},
    ("second", 2): {
        "a": (("D1", 8, 0, 1), ("D2", 5, 1, 2), ("R2", 4, 0, 2)),
        "b": (("D2", 5, 1, 2), ("R2", 4, 0, 2)),
    },
    ("second", -2): {
        "a": (("D1", 5, 13, 1), ("D2", 5, 9, 2), ("R2", 4, 8, 2)),
        "b": (("D2", 5, 9, 2), ("R2", 4, 8, 2)),
    },
    ("second", 1): {
        "b": (("D0", 9, 1, 4), ("D1", 5, 1, 4), ("D2", 5, 3, 2))
        + (("R0", 9, 1, 3), ("R1", 4, 0, 4), ("R2", 4, 2, 2)),
    },
    ("second", -1): {
        "b": (("D0", 5, 13, 4), ("D1", 5, 9, 4), ("D2", 5, 7, 2))
        + (("R0", 4, 12, 3), ("R1", 4, 8, 4), ("R2", 4, 6, 2)),
    },
}


def z_messages(with_density):
    result = []
    for (stage, shift), parts in PIECES.items():
        pieces = [
            (part, piece)
            for part, listed in parts.items()
            for piece in listed
            if with_density or piece[0][0] == "R"
        ]
        if pieces:
            result.append((stage, shift, pieces))
    return result


def paired(name, tiles):
    return name[1] != "0" and tiles % 2 == 0


def piece_tiles(part, piece):
    name, _, _, count = piece
    tiles = count * (ROWS[int(name[1])] // 8 if part == "a" else 1)
    return tiles // 2 if paired(name, tiles) else tiles


def x_pieces(with_density):
    result = []
    for level in range(3):
        count = PLANES[level]
        if with_density:
            result.append(("D%d" % level, count, count // 2 if level else count))
        result.append(("R%d" % level, count, (4, 1, 1)[level]))
    return result


def buffer_shapes(with_density):
    tiles = [sum(sent for _, _, sent in x_pieces(with_density))] * 2
    for _, _, pieces in z_messages(with_density):
        tiles.append(sum(piece_tiles(part, piece) for part, piece in pieces))
    return [pltpu.VMEM((count, 8, 128), F32) for count in tiles]


def n_halo(with_density):
    return 2 + len(z_messages(with_density))


def even_lanes(tiles):
    return iota((tiles, 8, 128), 2) % 2 == 0


def upper_rows(tiles):
    return iota((tiles, 8, 128), 1) < 4


def pack_lanes(block):
    half = block.shape[0] // 2
    return jnp.where(even_lanes(half), block[0:half], block[half:])


def unpack_lanes(block):
    even = even_lanes(block.shape[0])
    return jnp.concatenate(
        [jnp.where(even, block, roll(block, 1, 2)), jnp.where(even, roll(block, -1, 2), block)],
        axis=0,
    )


def partners_of(place):
    k, s, _, ns = place
    i, y, half = k % ROW, k // ROW % 8, k // (8 * ROW)
    depth, side = [], []
    for delta in (4, 3, 5, 2, 6, 1, 7):
        z = (half * ns + s + delta) % (2 * ns)
        depth.append((((z // ns) * 8 + y) * ROW + i, z % ns))
        side.append((delta, ((half * 8 + (y + delta) % 8) * ROW + i, s)))
    return depth, side


class Phase:
    def __init__(self, refs, place, with_density, buffers, coarse, send_sem, recv_sem):
        send, recv = buffers
        self.refs = refs
        self.k, self.s, self.nf, self.ns = place
        self.dense = with_density
        self.send, self.recv = send, recv
        self.row, self.row_in, self.depth_in, self.side_in = coarse
        self.send_sem, self.recv_sem = send_sem, recv_sem
        self.started = []
        self.count = 0
        self.z = z_messages(with_density)
        self.copies = {}
        self.i = self.k % ROW
        self.g = self.k // ROW
        self.ng = self.nf // ROW
        self.y = self.g % 8
        self.z_at = self.g // 8 * self.ns + self.s
        self.depth_partners, self.side_partners = partners_of(place)

    def start(self, source, target, k, s, shift=0):
        index = self.count
        self.count += 1
        copy = pltpu.make_async_remote_copy(
            src_ref=source,
            dst_ref=target,
            send_sem=self.send_sem.at[index],
            recv_sem=self.recv_sem.at[index],
            device_id=(k, s),
            device_id_type=MESH,
        )
        self.when(self.has_target(shift), copy.start)
        self.started.append((copy, shift))
        return copy

    def has_target(self, shift):
        if shift == 0:
            return None
        return self.k < self.nf - shift if shift > 0 else self.k >= -shift

    def has_source(self, shift):
        return self.has_target(-shift)

    def when(self, condition, action):
        if condition is None:
            action()
        else:
            pl.when(condition)(action)

    def start_all(self, pairs, total):
        index = self.count
        self.count += 1
        sems = {"send_sem": self.send_sem.at[index], "recv_sem": self.recv_sem.at[index]}
        for source, target, device in pairs:
            pltpu.make_async_remote_copy(
                src_ref=source,
                dst_ref=target,
                device_id=device,
                device_id_type=MESH,
                **sems,
            ).start()
        whole = pltpu.make_async_remote_copy(
            src_ref=total,
            dst_ref=total,
            device_id=pairs[0][2],
            device_id_type=MESH,
            **sems,
        )
        self.started.append((whole, 0))
        return whole

    def pack_x(self):
        for which in (0, 1):
            at = 0
            for name, count, sent in x_pieces(self.dense):
                level = int(name[1])
                lead = 5 if name[0] == "D" else 4
                row = ROWS[level] - 8 if which == 0 else 0
                block = self.refs[name][lead : lead + count, row : row + 8, :]
                if level:
                    block = pack_lanes(block)
                if block.shape[0] > sent:
                    near, far = block[0:sent], roll(block[sent:], 4, 1)
                    upper = upper_rows(sent)
                    if which == 0:
                        block = jnp.where(upper, far, near)
                    else:
                        block = jnp.where(upper, near, far)
                self.send[which][at : at + sent] = block
                at += sent

    def start_x(self):
        up, down = (self.s + 1) % self.ns, (self.s + self.ns - 1) % self.ns
        self.x_copies = [
            self.start(self.send[0], self.recv[0], self.k, up),
            self.start(self.send[1], self.recv[1], self.k, down),
        ]

    def unpack_x(self):
        for copy in self.x_copies:
            copy.wait_recv()
        low_in = jnp.where(self.s > 0, 1.0, 0.0).astype(F32)
        high_in = jnp.where(self.s < self.ns - 1, 1.0, 0.0).astype(F32)
        at = 0
        for name, count, sent in x_pieces(self.dense):
            level = int(name[1])
            own = ROWS[level]
            lead = 5 if name[0] == "D" else 4
            low, high = self.recv[0][at : at + sent], self.recv[1][at : at + sent]
            at += sent
            ref = self.refs[name]
            if name[0] == "D":
                if level:
                    low, high = unpack_lanes(low), unpack_lanes(high)
                ref[lead : lead + count, own : own + 8, :] = high * high_in
                ref[lead : lead + count, own + 8 : own + 16, :] = low * low_in
                continue
            upper = upper_rows(sent)
            block = jnp.where(upper, high, low)
            if sent < (count // 2 if level else count):
                far = roll(jnp.where(upper, low, high), 4, 1)
                block = jnp.concatenate([block, far], axis=0)
            if level:
                block = unpack_lanes(block)
            ref[lead : lead + count, own : own + 8, :] = block

    def pack_z(self, stage):
        for index, (when, _, pieces) in enumerate(self.z):
            if when != stage:
                continue
            at = 0
            for part, piece in pieces:
                name, source, _, count = piece
                ref, own = self.refs[name], ROWS[int(name[1])]
                if part == "a":
                    block = ref[source : source + count, 0:own, :]
                    block = block.reshape(count * own // 8, 8, 128)
                else:
                    block = ref[source : source + count, own : own + 8, :]
                    if name[0] == "D":
                        low = ref[source : source + count, own + 8 : own + 16, :]
                        block = jnp.where(upper_rows(count), block, low)
                if paired(name, block.shape[0]):
                    block = pack_lanes(block)
                self.send[2 + index][at : at + block.shape[0]] = block
                at += block.shape[0]

    def start_z(self, stage):
        for index, (when, shift, _) in enumerate(self.z):
            if when == stage:
                target = (self.k + shift + self.nf) % self.nf
                self.copies[index] = self.start(
                    self.send[2 + index], self.recv[2 + index], target, self.s, shift
                )

    def unpack_z(self):
        for index, (_, shift, _) in enumerate(self.z):
            self.when(self.has_source(shift), self.copies[index].wait_recv)
        for index, (_, shift, pieces) in enumerate(self.z):
            inside = self.has_source(shift)
            at = 0
            for part, piece in pieces:
                name, _, target, count = piece
                ref, own = self.refs[name], ROWS[int(name[1])]
                sent = piece_tiles(part, piece)
                block = jnp.where(inside, self.recv[2 + index][at : at + sent], 0.0)
                at += sent
                if sent < (count * own // 8 if part == "a" else count):
                    block = unpack_lanes(block)
                if part == "a":
                    ref[target : target + count, 0:own, :] = block.reshape(count, own, 128)
                else:
                    ref[target : target + count, own : own + 8, :] = block
                    if name[0] == "D":
                        ref[target : target + count, own + 8 : own + 16, :] = block

    def pack_row(self, fields, pair, spread_row):
        for index, field in enumerate(fields):
            pillar = jnp.sum(field, axis=0).reshape(4, 8, 128)
            pair[4 * index : 4 * index + 4, :] = jnp.sum(pillar, axis=1) * 0.125**3
        spread = one_hot_matmul(pair[...], spread_row[...])[0:8]
        mine = iota((8, 128), 1) // 16 == iota((8, 128), 0)
        row = jnp.sum(jnp.where(mine, spread, 0.0), axis=0, keepdims=True)
        self.row[...] = row
        self.row_in[self.i] = row

    def start_rows(self):
        slot = self.row_in.at[self.i]
        devices = [(self.g * ROW + (self.i + delta) % ROW, self.s) for delta in (4, 3, 5, 2, 6, 1, 7)]
        pairs = [(self.row, slot, device) for device in devices]
        self.row_copies = self.start_all(pairs, self.row_in.at[0 : ROW - 1])

    def start_depth(self):
        self.row_copies.wait_recv()
        line = iota((8, 128), 0)
        tile = jnp.zeros((8, 128), F32)
        for index in range(ROW):
            tile = jnp.where(line == index, self.row_in[index], tile)
        self.depth_in[self.z_at] = tile
        slot = self.depth_in.at[self.z_at]
        pairs = [(slot, slot, device) for device in self.depth_partners]
        self.depth_copies = self.start_all(pairs, self.depth_in.at[0:7])

    def start_sides(self, work, pool):
        self.depth_copies.wait_recv()
        left = iota((8, 128), 1) < 64
        slot = self.side_in.at[self.y]
        wide = []
        for half in range(2):
            tiles = [self.depth_in[4 * half + index] for index in range(4)]
            turned = [roll(tile, 64, 1) for tile in tiles]
            fields = [jnp.where(left, tiles[a], turned[a + 1]) for a in (0, 2)]
            if self.dense:
                fields += [jnp.where(left, turned[a], tiles[a + 1]) for a in (0, 2)]
            for index, field in enumerate(fields):
                slot[2 + len(fields) * half + index] = field
            wide.append(jnp.concatenate(fields, axis=1))
        wide = jnp.concatenate(wide, axis=0)
        sums = one_hot_matmul(wide, pool[0 : wide.shape[1], :])
        work[...] = sums[:, 0:128]
        line = iota((8, 128), 0)
        for half in range(2):
            four = work[pl.ds(8 * half, 4, stride=2), :] + work[pl.ds(8 * half + 1, 4, stride=2), :]
            slot[half, 0:4, :] = four * 0.125
            five = sums[8 * half : 8 * half + 8, 128:256]
            five = five + roll(five, -1, 0)
            five = (five + roll(five, -2, 0)) * (0.125 * 0.125)
            five = jnp.where(line % 2 == 0, five[0:1], five[4:5])
            slot[half, 4:8, :] = five[4:8]
        part = slot.at[0:2]
        far = [(part, part, device) for delta, device in self.side_partners if delta not in (1, 7)]
        self.side_copies = [self.start_all(far, self.side_in.at[0:5, 0:2])]
        near = [(slot, slot, device) for delta, device in self.side_partners if delta in (1, 7)]
        self.side_copies.append(self.start_all(near, self.side_in.at[0:2]))

    def wait_sides(self):
        for copy in self.side_copies:
            copy.wait_recv()

    def group_fields(self, group):
        wrapped = (group + self.ng) % self.ng
        y, half = wrapped % 8, wrapped // 8
        count = 4 if self.dense else 2
        tiles = [self.side_in[y, 2 + half * count + index] for index in range(count)]
        return [
            jnp.concatenate(tiles[at : at + 2], axis=1) for at in range(0, count, 2)
        ]

    def finish(self, first, last):
        for copy, shift in self.started[first:last]:
            self.when(self.has_target(shift), copy.wait_send)


def split_packed(value):
    left = iota(value.shape, 1) < 64
    return jnp.where(left, value, 0.0), jnp.where(left, roll(value, 64, 1), 0.0)


def build_matrices(pool, fan):
    line, lane = iota((128, 128), 0), iota((128, 128), 1)
    for half in range(4):
        x, y = line // 16 + 8 * (half % 2), line % 16
        rows = slice(128 * half, 128 * half + 128)
        home4 = (x // 2) * 8 + y // 2 + 64 * (half // 2)
        home5 = (x // 4) * 4 + y // 4 + 64 * (half // 2)
        pool[rows, 0:128] = one_hot(home4 == lane).astype(BF16)
        pool[rows, 128:256] = one_hot(home5 == lane).astype(BF16)
    three = one_hot(line % 16 == lane // 8).astype(BF16)
    fan[0:128, :] = three
    fan[128:256, :] = three
    fan[256:384, :] = one_hot(line % 8 == lane // 16).astype(BF16)
    fan[384:512, :] = one_hot(line % 4 == lane // 32).astype(BF16)


def kernel(nf, ns, rhs, dens, solution, residual, *scratch):
    scratch = list(scratch)

    def take(count):
        taken = scratch[:count]
        del scratch[:count]
        return taken

    refs = {}
    for name in ("D0", "D1", "D2", "R0", "R1", "R2"):
        (refs[name],) = take(1)
    fine_coef = [take(5) for _ in range(3)]
    remains = take(3)
    updates = [take(3) for _ in range(3)]
    answers = take(3)
    (work, tile_work, pair, sol, spread) = take(5)
    (spread_row, pool, fan, keep3, keep4, keep5) = take(6)
    coarse_coef = [take(5) for _ in range(3)]
    phases = []
    k, s = lax.axis_index("fine"), lax.axis_index("sub")
    for with_density in (True, False):
        count = n_halo(with_density)
        buffers = take(count), take(count)
        coarse = take(4)
        send_sem, recv_sem = take(2)
        phases.append(
            Phase(refs, (k, s, nf, ns), with_density, buffers, coarse, send_sem, recv_sem)
        )
    ng = nf // ROW
    i, g = k % ROW, k // ROW

    barrier = pltpu.get_barrier_semaphore()
    partners = []
    for shift in (1, 2, 3):
        partners += [((k + shift) % nf, s), ((k + nf - shift) % nf, s)]
    partners += [(g * ROW + (i + delta) % ROW, s) for delta in range(1, ROW)]
    depth, side = partners_of((k, s, nf, ns))
    partners += depth + [device for _, device in side]
    for partner in partners:
        pl.semaphore_signal(barrier, inc=1, device_id=partner, device_id_type=MESH)

    pair[...] = jnp.zeros((16, 128), F32)

    def restrict_all(name, lead):
        for level in range(2):
            refs[name + str(level + 1)][
                lead : lead + PLANES[level + 1], 0 : ROWS[level + 1], :
            ] = restrict_block(
                refs[name + str(level)], lead, PLANES[level], ROWS[level], 2**level, work
            )

    def coefficients(level, low, high):
        fine_coefficients(level, refs["D" + str(level)], fine_coef[level], low, high)

    def smooth(level):
        fine_smooth(
            level,
            refs["R" + str(level)],
            fine_coef[level],
            remains[level],
            updates[level],
            answers[level],
        )

    line, lane = iota((128, 128), 0), iota((128, 128), 1)
    spread_row[...] = one_hot(line // 8 == lane % 16).astype(BF16)

    for cycle in range(CYCLES):
        phase = phases[cycle]
        if cycle == 0:
            phase.pack_row((rhs[...], dens[...]), pair, spread_row)
            pl.semaphore_wait(barrier, len(partners))
        else:
            phase.pack_row((refs["R0"][4:12, 0:32, :],), pair, spread_row)
        phase.start_rows()
        if cycle == 0:
            refs["R0"][4:12, 0:32, :] = rhs[...]
            refs["D0"][5:13, 0:32, :] = dens[...]
            restrict_all("D", 5)
        restrict_all("R", 4)
        phase.pack_x()
        phase.start_x()
        phase.pack_z("first")
        phase.start_z("first")
        if cycle == 0:
            build_matrices(pool, fan)
            for level in range(3):
                for name, lead in (("D", 5), ("R", 4)):
                    ref = refs[name + str(level)]
                    planes, rows, _ = ref.shape
                    blank = jnp.zeros((lead, rows, 128), F32)
                    ref[0:lead] = blank
                    ref[planes - lead : planes] = blank
            for ref in (keep4, keep5):
                rows = ref.shape[0]
                ref[0:8, :] = jnp.zeros((8, 128), F32)
                ref[rows - 8 : rows, :] = jnp.zeros((8, 128), F32)
        phase.start_depth()
        phase.unpack_x()
        phase.pack_z("second")
        phase.start_z("second")
        phase.start_sides(tile_work, pool)
        if cycle == 0:
            coefficients(0, 5, 11)
        else:
            phases[0].finish(0, None)
        phase.unpack_z()
        for level in (2, 1):
            if cycle == 0:
                coefficients(level, 0, PLANES[level] + 8)
            smooth(level)
        if cycle == 0:
            coefficients(0, 0, 5)
            coefficients(0, 11, 16)
        smooth(0)
        if cycle == 1:
            phase.finish(0, -2)
        phase.wait_sides()

        tiles = [phase.side_in[index % 8, index // 8] for index in range(ng)]
        line = iota((8, 128), 0)
        packed4, packed5 = [], []
        for index in range(0, ng, 2):
            packed4.append(jnp.where(line < 4, tiles[index], roll(tiles[index + 1], 4, 0)))
        for index in range(0, ng, 4):
            first = jnp.where(line < 6, tiles[index], tiles[index + 1])
            second = jnp.where(line < 6, tiles[index + 2], tiles[index + 3])
            packed5.append(jnp.where(line < 4, roll(first, 4, 0), second))
        source4, density4 = split_packed(jnp.concatenate(packed4, axis=0))
        source5, density5 = split_packed(jnp.concatenate(packed5, axis=0))
        if cycle == 0:
            low_in = jnp.where(g > 0, 1.0, 0.0).astype(F32)
            high_in = jnp.where(g < ng - 1, 1.0, 0.0).astype(F32)
            density3 = jnp.concatenate(
                [
                    phase.group_fields(g - 1)[1] * low_in,
                    phase.group_fields(g)[1],
                    phase.group_fields(g + 1)[1] * high_in,
                ],
                axis=0,
            )
            for index, (field, ny) in enumerate(
                ((density3, 16), (density4, 8), (density5, 4))
            ):
                values = packed_coefficients(field, ny, ny, 0.25 ** (3 + index))
                for ref, value in zip(coarse_coef[index], values):
                    ref[...] = value
        coef3, coef4, coef5 = ([ref[...] for ref in refs5] for refs5 in coarse_coef)
        total = jnp.sum(jnp.sum(source5, axis=0, keepdims=True), axis=1, keepdims=True)
        weight = jnp.sum(jnp.sum(coef5[3], axis=0, keepdims=True), axis=1, keepdims=True)
        n4, n5 = 4 * ng, 2 * ng
        keep5[8 : 8 + n5, :] = packed_smooth(source5, coef5, 4, 0.05) + total / weight
        keep4[8 : 8 + n4, :] = packed_smooth(source4, coef4, 8, 0.5)

        source3 = jnp.concatenate(
            [phase.group_fields(g + shift)[0] for shift in (-1, 0, 1)], axis=0
        )
        keep3[...] = packed_smooth(source3, coef3, 16, 0.5)

        row = iota((16, 512), 0)
        lane = iota((16, 512), 1)
        x3 = row // 2 + jnp.where(row < 12, 0, -8) + (4 * s + 4)
        inside = (x3 >= 4) & (x3 < 20)
        x_lane = jnp.where(
            lane < 256, lane // 16, jnp.where(lane < 384, (lane - 256) // 8, (lane - 384) // 4)
        )
        x_row = jnp.where(lane < 256, x3 - 4, jnp.where(lane < 384, x3 // 2 - 2, x3 // 4 - 1))
        chosen = (x_lane == x_row) & inside
        picked = []
        for t in range(3):
            parts = jnp.concatenate(
                [
                    keep3[pl.ds(7 + i + t, 1), :],
                    keep4[pl.ds((k + 1 + t) // 2 + 7, 1), :],
                    keep5[pl.ds((k + 3 + t) // 4 + 7, 1), :],
                ],
                axis=1,
            )
            picked.append(jnp.where(chosen, parts, 0.0))
        spread[0:3, 0:16, :] = one_hot_matmul(
            jnp.concatenate(picked, axis=0), fan[...]
        ).reshape(3, 16, 128)

        for level in (2, 1):
            rows = ROWS[level]
            answer = answers[level]
            planes = PLANES[level] + 2
            coarse = jnp.concatenate(
                [spread[(p + 1) // 2 : (p + 1) // 2 + 1, 0 : rows + 8, :] for p in range(planes)],
                axis=0,
            )
            value = answer[3 : 3 + planes] + coarse
            own, ends = value[:, 0:rows, :], value[:, rows : rows + 8, :]
            spread[0:planes, pl.ds(0, rows, stride=2), :] = own
            spread[0:planes, pl.ds(1, rows, stride=2), :] = own
            spread[0:planes, 2 * rows : 2 * rows + 8, :] = jnp.where(
                upper_rows(planes), ends[:, 0:1, :], ends[:, 7:8, :]
            )


        def advance(p, carry, cycle=cycle):
            step = 0.4 * (answers[0][p + 3] + spread[(p + 1) // 2])
            sol[p] = step if cycle == 0 else sol[p] + step
            return carry

        lax.fori_loop(0, PLANES[0] + 2, advance, 0, unroll=True)

        def defect(p, carry, cycle=cycle):
            applied = fine_apply(sol, p + 1, fine_coef[0], p + 4, 1)
            left = rhs[p] - applied[0:32, :]
            if cycle == 0:
                refs["R0"][p + 4, 0:32, :] = left
            else:
                residual[p] = left
                solution[p] = sol[p + 1, 0:32, :]
            return carry

        lax.fori_loop(0, PLANES[0], defect, 0, unroll=True)

    phases[1].finish(-2, None)


def scratch_shapes(ng):
    shapes = []
    for level in range(3):
        shapes.append(pltpu.VMEM((PLANES[level] + 10, ROWS[level] + 16, 128), F32))
    extents = [(PLANES[level] + 8, ROWS[level] + 8, 128) for level in range(3)]
    shapes += [pltpu.VMEM(extent, F32) for extent in extents]
    for extent in extents:
        shapes += [pltpu.VMEM(extent, F32)] * 5
    shapes += [pltpu.VMEM(extent, F32) for extent in extents]
    for extent in extents:
        shapes += [pltpu.VMEM(extent, F32)] * 3
    shapes += [pltpu.VMEM(extent, F32) for extent in extents]
    shapes += [
        pltpu.VMEM((4, 32, 128), F32),
        pltpu.VMEM((16, 128), F32),
        pltpu.VMEM((16, 128), F32),
        pltpu.VMEM((10, 40, 128), F32),
        pltpu.VMEM((6, 40, 128), F32),
        pltpu.VMEM((128, 128), BF16),
        pltpu.VMEM((512, 256), BF16),
        pltpu.VMEM((512, 128), BF16),
        pltpu.VMEM((24, 256), F32),
        pltpu.VMEM((4 * ng + 16, 128), F32),
        pltpu.VMEM((2 * ng + 16, 128), F32),
    ]
    for extent in ((24, 256), (4 * ng, 128), (2 * ng, 128)):
        shapes += [pltpu.VMEM(extent, F32)] * 5
    for with_density in (True, False):
        halo = buffer_shapes(with_density)
        shapes += halo + halo
        tiles = 10 if with_density else 6
        shapes += [
            pltpu.VMEM((1, 128), F32),
            pltpu.VMEM((ROW, 1, 128), F32),
            pltpu.VMEM((8, 8, 128), F32),
            pltpu.VMEM((8, tiles, 8, 128), F32),
        ]
        copies = n_halo(with_density) + 4
        shapes += [pltpu.SemaphoreType.DMA((copies,)), pltpu.SemaphoreType.DMA((copies,))]
    return shapes


def solution(mesh):
    nf, ns = mesh.shape["fine"], mesh.shape["sub"]

    def body(rhs, density):
        return pl.pallas_call(
            functools.partial(kernel, nf, ns),
            out_shape=(
                jax.ShapeDtypeStruct(rhs.shape, F32),
                jax.ShapeDtypeStruct(rhs.shape, F32),
            ),
            in_specs=[pl.BlockSpec(memory_space=pltpu.VMEM)] * 2,
            out_specs=[pl.BlockSpec(memory_space=pltpu.VMEM)] * 2,
            scratch_shapes=scratch_shapes(nf // ROW),
            compiler_params=pltpu.CompilerParams(
                collective_id=0, has_side_effects=True, vmem_limit_bytes=32 * 1024 * 1024
            ),
        )(rhs, density)

    return jax.shard_map(
        body,
        mesh=mesh,
        in_specs=(P("fine", "sub", None), P("fine", "sub", None)),
        out_specs=(P("fine", "sub", None), P("fine", "sub", None)),
        check_vma=False,
    )
```

```python
import functools

import jax
import jax.numpy as jnp
from jax import lax
from jax.experimental import pallas as pl
from jax.experimental.pallas import tpu as pltpu
from jax.sharding import PartitionSpec as P

DEGREE = 4
CYCLES = 2
MESH = pl.DeviceIdType.MESH
F32 = jnp.float32
BF16 = jnp.bfloat16
ROW = 8
PLANES = (8, 4, 2)
ROWS = (32, 16, 8)


def chebyshev_constants(lower):
    upper = 2.0
    theta = 0.5 * (upper + lower)
    delta = 0.5 * (upper - lower)
    sigma = theta / delta
    ratio = 1.0 / sigma
    steps = []
    for _ in range(DEGREE - 1):
        next_ratio = 1.0 / (2.0 * sigma - ratio)
        steps.append((next_ratio * ratio, 2.0 * next_ratio / delta))
        ratio = next_ratio
    return 1.0 / theta, steps


def iota(shape, dim):
    return lax.broadcasted_iota(jnp.int32, shape, dim)


def div(value, divisor):
    return value >> (divisor.bit_length() - 1)


def mod(value, divisor):
    return value & (divisor - 1)


def quot(value, divisor):
    return lax.div(value, jnp.int32(divisor))


def rest(value, divisor):
    return lax.rem(value, jnp.int32(divisor))


def roll(value, shift, axis):
    return pltpu.roll(value, shift % value.shape[axis], axis)


def invert(value):
    return pltpu.reciprocal(value, full_range=False)


def one_hot(condition):
    return jnp.where(condition, 1.0, 0.0).astype(F32)


def one_hot_matmul(value, matrix):
    count = value.shape[0]
    first = value.astype(BF16).astype(F32)
    rest = value - first
    second = rest.astype(BF16).astype(F32)
    parts = jnp.concatenate([first, second, rest - second], axis=0).astype(BF16)
    product = jnp.dot(parts, matrix, preferred_element_type=F32)
    return product[0:count] + product[count : 2 * count] + product[2 * count :]


def restrict_block(source, first, planes, rows, stride, work):
    field = source[first : first + planes, 0:rows, :]
    field = field.reshape(planes // 2, 2, rows, 128)
    work[0 : planes // 2, 0:rows, :] = field[:, 0] + field[:, 1]
    half = rows // 2
    both = (
        work[0 : planes // 2, pl.ds(0, half, stride=2), :]
        + work[0 : planes // 2, pl.ds(1, half, stride=2), :]
    )
    lane = iota(both.shape, 2)
    even = mod(div(lane, stride), 2) == 0
    other = jnp.where(even, roll(both, -stride, 2), roll(both, stride, 2))
    return (both + other) * 0.125


def fine_coefficients(level, dens, coef, low, high):
    own = ROWS[level]
    scale = 2.0 * 0.25**level
    stride = 2**level
    face_z, face_x, face_y, diagonal, inverse = coef
    shape = (own + 16, 128)

    def compress(value):
        tail = jnp.where(
            iota((8, 128), 0) < 4, value[own : own + 8], value[own + 8 : own + 16]
        )
        return jnp.concatenate([value[0:own], tail], axis=0)

    def plane(p, down):
        here = dens[p + 1]
        above = dens[p + 2]
        lane = iota(shape, 1)
        right = roll(here, -1, 0)
        up = scale * invert(jnp.maximum(here + above, 0.1))
        x_face = scale * invert(jnp.maximum(here + right, 0.1))
        ahead = jnp.where(lane >= 128 - stride, 0.0, roll(here, -stride, 1))
        behind = jnp.where(lane < stride, 0.0, roll(here, stride, 1))
        y_face = scale * invert(jnp.maximum(here + ahead, 0.1))
        y_back = scale * invert(jnp.maximum(here + behind, 0.1))
        diag = up + down + x_face + roll(x_face, 1, 0) + y_face + y_back
        inside = here > 0.0
        face_z[p] = compress(jnp.where(inside & (above > 0.0), up, 0.0))
        face_x[p] = compress(jnp.where(inside & (right > 0.0), x_face, 0.0))
        face_y[p] = compress(jnp.where(lane >= 128 - stride, 0.0, y_face))
        diagonal[p] = compress(diag)
        inverse[p] = compress(invert(diag))
        return up

    lowest = scale * invert(jnp.maximum(dens[low] + dens[low + 1], 0.1))
    lax.fori_loop(low, high, plane, lowest, unroll=True)


def fine_apply(field, p, coef, q, stride):
    face_z, face_x, face_y, diagonal, _ = coef
    here = field[p]
    x_face = face_x[q]
    y_face = face_y[q]
    result = diagonal[q] * here
    result = result - face_z[q] * field[p + 1] - face_z[q - 1] * field[p - 1]
    result = result - x_face * roll(here, -1, 0) - roll(x_face * here, 1, 0)
    result = result - y_face * roll(here, -stride, 1) - roll(y_face * here, stride, 1)
    return result


def fine_smooth(level, source, coef, remain, updates, answer):
    planes = PLANES[level] + 8
    stride = 2**level
    inverse = coef[4]
    first, steps = chebyshev_constants(0.5)
    d0, d1, d2 = updates

    def start(p, carry):
        d0[p] = source[p] * inverse[p] * first
        return carry

    lax.fori_loop(0, planes, start, 0, unroll=True)
    chain = (d0, d1, d2)
    for sweep in range(3):
        old = chain[sweep]
        keep, add = steps[sweep]

        def step(p, carry, sweep=sweep, old=old, keep=keep, add=add):
            left = source[p] if sweep == 0 else remain[p]
            left = left - fine_apply(old, p, coef, p, stride)
            new = keep * old[p] + add * (left * inverse[p])
            if sweep < 2:
                remain[p] = left
                chain[sweep + 1][p] = new
            else:
                answer[p] = d0[p] + d1[p] + d2[p] + new
            return carry

        lax.fori_loop(sweep + 1, planes - sweep - 1, step, 0, unroll=True)


def packed_coefficients(dens, ny, nx, scale):
    rows = dens.shape[0]
    z = iota(dens.shape, 0)
    lane = iota(dens.shape, 1)
    y = mod(lane, ny)
    x = div(lane, ny)
    scale = 2.0 * scale

    def neighbour(shift, axis, outside):
        return jnp.where(outside, 0.0, roll(dens, shift, axis))

    above = neighbour(-1, 0, z == rows - 1)
    below = neighbour(1, 0, z == 0)
    right = neighbour(-ny, 1, x >= nx - 1)
    left = neighbour(ny, 1, x == 0)
    ahead = neighbour(-1, 1, y == ny - 1)
    behind = neighbour(1, 1, y == 0)

    def face(other):
        return scale * invert(jnp.maximum(dens + other, 0.1))

    up, x_face, y_face = face(above), face(right), face(ahead)
    diagonal = up + face(below) + x_face + face(left) + y_face + face(behind)
    inside = dens > 0.0

    def inner(value, other):
        return jnp.where(inside & (other > 0.0), value, 0.0)

    return (
        inner(up, above),
        inner(x_face, right),
        inner(y_face, ahead),
        jnp.where(inside, diagonal, 0.0),
        jnp.where(inside, invert(diagonal), 0.0),
    )


def packed_apply(field, coef, ny):
    face_z, face_x, face_y, diagonal, _ = coef
    result = diagonal * field
    result = result - face_z * roll(field, -1, 0) - roll(face_z * field, 1, 0)
    result = result - face_x * roll(field, -ny, 1) - roll(face_x * field, ny, 1)
    result = result - face_y * roll(field, -1, 1) - roll(face_y * field, 1, 1)
    return result


def packed_smooth(source, coef, ny, lower):
    first, steps = chebyshev_constants(lower)
    inverse = coef[4]
    update = source * inverse * first
    answer = update
    for keep, add in steps:
        source = source - packed_apply(update, coef, ny)
        update = keep * update + add * (source * inverse)
        answer = answer + update
    return answer


PIECES = {
    ("first", 1): {
        "a": (("D0", 8, 0, 5), ("R0", 8, 0, 4), ("D1", 5, 1, 4), ("D2", 5, 3, 2))
        + (("R1", 4, 0, 4), ("R2", 4, 2, 2)),
    },
    ("first", -1): {
        "a": (("D0", 5, 13, 5), ("R0", 4, 12, 4), ("D1", 5, 9, 4), ("D2", 5, 7, 2))
        + (("R1", 4, 8, 4), ("R2", 4, 6, 2)),
    },
    ("first", 3): {"a": (("D2", 6, 0, 1),)},
    ("first", -3): {"a": (("D2", 5, 11, 1),)},
    ("second", 2): {
        "a": (("D1", 8, 0, 1), ("D2", 5, 1, 2), ("R2", 4, 0, 2)),
        "b": (("D2", 5, 1, 2), ("R2", 4, 0, 2)),
    },
    ("second", -2): {
        "a": (("D1", 5, 13, 1), ("D2", 5, 9, 2), ("R2", 4, 8, 2)),
        "b": (("D2", 5, 9, 2), ("R2", 4, 8, 2)),
    },
    ("second", 1): {
        "b": (("D0", 9, 1, 4), ("D1", 5, 1, 4), ("D2", 5, 3, 2))
        + (("R0", 9, 1, 3), ("R1", 4, 0, 4), ("R2", 4, 2, 2)),
    },
    ("second", -1): {
        "b": (("D0", 5, 13, 4), ("D1", 5, 9, 4), ("D2", 5, 7, 2))
        + (("R0", 4, 12, 3), ("R1", 4, 8, 4), ("R2", 4, 6, 2)),
    },
}


def z_messages(with_density):
    result = []
    for (stage, shift), parts in PIECES.items():
        pieces = [
            (part, piece)
            for part, listed in parts.items()
            for piece in listed
            if with_density or piece[0][0] == "R"
        ]
        if pieces:
            result.append((stage, shift, pieces))
    return result


def paired(name, tiles):
    return name[1] != "0" and tiles % 2 == 0


def piece_tiles(part, piece):
    name, _, _, count = piece
    tiles = count * (ROWS[int(name[1])] // 8 if part == "a" else 1)
    return tiles // 2 if paired(name, tiles) else tiles


def x_pieces(with_density):
    result = []
    for level in range(3):
        count = PLANES[level]
        if with_density:
            result.append(("D%d" % level, count, count // 2 if level else count))
        result.append(("R%d" % level, count, (4, 1, 1)[level]))
    return result


def buffer_shapes(with_density):
    tiles = [sum(sent for _, _, sent in x_pieces(with_density))] * 2
    for _, _, pieces in z_messages(with_density):
        tiles.append(sum(piece_tiles(part, piece) for part, piece in pieces))
    return [pltpu.VMEM((count, 8, 128), F32) for count in tiles]


def n_halo(with_density):
    return 2 + len(z_messages(with_density))


def even_lanes(tiles):
    return mod(iota((tiles, 8, 128), 2), 2) == 0


def upper_rows(tiles):
    return iota((tiles, 8, 128), 1) < 4


def pack_lanes(block):
    half = block.shape[0] // 2
    return jnp.where(even_lanes(half), block[0:half], block[half:])


def unpack_lanes(block):
    even = even_lanes(block.shape[0])
    return jnp.concatenate(
        [jnp.where(even, block, roll(block, 1, 2)), jnp.where(even, roll(block, -1, 2), block)],
        axis=0,
    )


def partners_of(place):
    k, s, _, ns = place
    i, y, half = rest(k, ROW), rest(quot(k, ROW), 8), quot(k, 8 * ROW)
    depth, side = [], []
    for delta in (4, 3, 5, 2, 6, 1, 7):
        z = rest(half * ns + s + delta, 2 * ns)
        depth.append(((quot(z, ns) * 8 + y) * ROW + i, rest(z, ns)))
        side.append((delta, ((half * 8 + rest(y + delta, 8)) * ROW + i, s)))
    return depth, side


class Phase:
    def __init__(self, refs, place, with_density, buffers, coarse, send_sem, recv_sem):
        send, recv = buffers
        self.refs = refs
        self.k, self.s, self.nf, self.ns = place
        self.dense = with_density
        self.send, self.recv = send, recv
        self.row, self.row_in, self.depth_in, self.side_in = coarse
        self.send_sem, self.recv_sem = send_sem, recv_sem
        self.started = []
        self.count = 0
        self.z = z_messages(with_density)
        self.copies = {}
        self.i = rest(self.k, ROW)
        self.g = quot(self.k, ROW)
        self.ng = self.nf // ROW
        self.y = rest(self.g, 8)
        self.z_at = quot(self.g, 8) * self.ns + self.s
        self.depth_partners, self.side_partners = partners_of(place)

    def start(self, source, target, k, s, shift=0):
        index = self.count
        self.count += 1
        copy = pltpu.make_async_remote_copy(
            src_ref=source,
            dst_ref=target,
            send_sem=self.send_sem.at[index],
            recv_sem=self.recv_sem.at[index],
            device_id=(k, s),
            device_id_type=MESH,
        )
        self.when(self.has_target(shift), copy.start)
        self.started.append((copy, shift))
        return copy

    def has_target(self, shift):
        if shift == 0:
            return None
        return self.k < self.nf - shift if shift > 0 else self.k >= -shift

    def has_source(self, shift):
        return self.has_target(-shift)

    def when(self, condition, action):
        if condition is None:
            action()
        else:
            pl.when(condition)(action)

    def start_all(self, pairs, total):
        index = self.count
        self.count += 1
        sems = {"send_sem": self.send_sem.at[index], "recv_sem": self.recv_sem.at[index]}
        for source, target, device in pairs:
            pltpu.make_async_remote_copy(
                src_ref=source,
                dst_ref=target,
                device_id=device,
                device_id_type=MESH,
                **sems,
            ).start()
        whole = pltpu.make_async_remote_copy(
            src_ref=total,
            dst_ref=total,
            device_id=pairs[0][2],
            device_id_type=MESH,
            **sems,
        )
        self.started.append((whole, 0))
        return whole

    def pack_x(self):
        for which in (0, 1):
            at = 0
            for name, count, sent in x_pieces(self.dense):
                level = int(name[1])
                lead = 5 if name[0] == "D" else 4
                row = ROWS[level] - 8 if which == 0 else 0
                block = self.refs[name][lead : lead + count, row : row + 8, :]
                if level:
                    block = pack_lanes(block)
                if block.shape[0] > sent:
                    near, far = block[0:sent], roll(block[sent:], 4, 1)
                    upper = upper_rows(sent)
                    if which == 0:
                        block = jnp.where(upper, far, near)
                    else:
                        block = jnp.where(upper, near, far)
                self.send[which][at : at + sent] = block
                at += sent

    def start_x(self):
        up, down = rest(self.s + 1, self.ns), rest(self.s + self.ns - 1, self.ns)
        self.x_copies = [
            self.start(self.send[0], self.recv[0], self.k, up),
            self.start(self.send[1], self.recv[1], self.k, down),
        ]

    def unpack_x(self):
        for copy in self.x_copies:
            copy.wait_recv()
        low_in = jnp.where(self.s > 0, 1.0, 0.0).astype(F32)
        high_in = jnp.where(self.s < self.ns - 1, 1.0, 0.0).astype(F32)
        at = 0
        for name, count, sent in x_pieces(self.dense):
            level = int(name[1])
            own = ROWS[level]
            lead = 5 if name[0] == "D" else 4
            low, high = self.recv[0][at : at + sent], self.recv[1][at : at + sent]
            at += sent
            ref = self.refs[name]
            if name[0] == "D":
                if level:
                    low, high = unpack_lanes(low), unpack_lanes(high)
                ref[lead : lead + count, own : own + 8, :] = high * high_in
                ref[lead : lead + count, own + 8 : own + 16, :] = low * low_in
                continue
            upper = upper_rows(sent)
            block = jnp.where(upper, high, low)
            if sent < (count // 2 if level else count):
                far = roll(jnp.where(upper, low, high), 4, 1)
                block = jnp.concatenate([block, far], axis=0)
            if level:
                block = unpack_lanes(block)
            ref[lead : lead + count, own : own + 8, :] = block

    def pack_z(self, stage):
        for index, (when, _, pieces) in enumerate(self.z):
            if when != stage:
                continue
            at = 0
            for part, piece in pieces:
                name, source, _, count = piece
                ref, own = self.refs[name], ROWS[int(name[1])]
                if part == "a":
                    block = ref[source : source + count, 0:own, :]
                    block = block.reshape(count * own // 8, 8, 128)
                else:
                    block = ref[source : source + count, own : own + 8, :]
                    if name[0] == "D":
                        low = ref[source : source + count, own + 8 : own + 16, :]
                        block = jnp.where(upper_rows(count), block, low)
                if paired(name, block.shape[0]):
                    block = pack_lanes(block)
                self.send[2 + index][at : at + block.shape[0]] = block
                at += block.shape[0]

    def start_z(self, stage):
        for index, (when, shift, _) in enumerate(self.z):
            if when == stage:
                target = rest(self.k + shift + self.nf, self.nf)
                self.copies[index] = self.start(
                    self.send[2 + index], self.recv[2 + index], target, self.s, shift
                )

    def unpack_z(self):
        for index, (_, shift, _) in enumerate(self.z):
            self.when(self.has_source(shift), self.copies[index].wait_recv)
        for index, (_, shift, pieces) in enumerate(self.z):
            inside = self.has_source(shift)
            at = 0
            for part, piece in pieces:
                name, _, target, count = piece
                ref, own = self.refs[name], ROWS[int(name[1])]
                sent = piece_tiles(part, piece)
                block = jnp.where(inside, self.recv[2 + index][at : at + sent], 0.0)
                at += sent
                if sent < (count * own // 8 if part == "a" else count):
                    block = unpack_lanes(block)
                if part == "a":
                    ref[target : target + count, 0:own, :] = block.reshape(count, own, 128)
                else:
                    ref[target : target + count, own : own + 8, :] = block
                    if name[0] == "D":
                        ref[target : target + count, own + 8 : own + 16, :] = block

    def pack_row(self, fields, pair, spread_row):
        for index, field in enumerate(fields):
            pillar = jnp.sum(field, axis=0).reshape(4, 8, 128)
            pair[4 * index : 4 * index + 4, :] = jnp.sum(pillar, axis=1) * 0.125**3
        spread = one_hot_matmul(pair[...], spread_row[...])[0:8]
        mine = div(iota((8, 128), 1), 16) == iota((8, 128), 0)
        row = jnp.sum(jnp.where(mine, spread, 0.0), axis=0, keepdims=True)
        self.row[...] = row
        self.row_in[self.i] = row

    def start_rows(self):
        slot = self.row_in.at[self.i]
        devices = [
            (self.g * ROW + rest(self.i + delta, ROW), self.s) for delta in (4, 3, 5, 2, 6, 1, 7)
        ]
        pairs = [(self.row, slot, device) for device in devices]
        self.row_copies = self.start_all(pairs, self.row_in.at[0 : ROW - 1])

    def start_depth(self):
        self.row_copies.wait_recv()
        line = iota((8, 128), 0)
        tile = jnp.zeros((8, 128), F32)
        for index in range(ROW):
            tile = jnp.where(line == index, self.row_in[index], tile)
        self.depth_in[self.z_at] = tile
        slot = self.depth_in.at[self.z_at]
        pairs = [(slot, slot, device) for device in self.depth_partners]
        self.depth_copies = self.start_all(pairs, self.depth_in.at[0:7])

    def start_sides(self, work, pool):
        self.depth_copies.wait_recv()
        left = iota((8, 128), 1) < 64
        slot = self.side_in.at[self.y]
        wide = []
        for half in range(2):
            tiles = [self.depth_in[4 * half + index] for index in range(4)]
            turned = [roll(tile, 64, 1) for tile in tiles]
            fields = [jnp.where(left, tiles[a], turned[a + 1]) for a in (0, 2)]
            if self.dense:
                fields += [jnp.where(left, turned[a], tiles[a + 1]) for a in (0, 2)]
            for index, field in enumerate(fields):
                slot[2 + len(fields) * half + index] = field
            wide.append(jnp.concatenate(fields, axis=1))
        wide = jnp.concatenate(wide, axis=0)
        sums = one_hot_matmul(wide, pool[0 : wide.shape[1], :])
        work[...] = sums[:, 0:128]
        line = iota((8, 128), 0)
        for half in range(2):
            four = work[pl.ds(8 * half, 4, stride=2), :] + work[pl.ds(8 * half + 1, 4, stride=2), :]
            slot[half, 0:4, :] = four * 0.125
            five = sums[8 * half : 8 * half + 8, 128:256]
            five = five + roll(five, -1, 0)
            five = (five + roll(five, -2, 0)) * (0.125 * 0.125)
            five = jnp.where(mod(line, 2) == 0, five[0:1], five[4:5])
            slot[half, 4:8, :] = five[4:8]
        part = slot.at[0:2]
        far = [(part, part, device) for delta, device in self.side_partners if delta not in (1, 7)]
        self.side_copies = [self.start_all(far, self.side_in.at[0:5, 0:2])]
        near = [(slot, slot, device) for delta, device in self.side_partners if delta in (1, 7)]
        self.side_copies.append(self.start_all(near, self.side_in.at[0:2]))

    def wait_sides(self):
        for copy in self.side_copies:
            copy.wait_recv()

    def group_fields(self, group):
        wrapped = rest(group + self.ng, self.ng)
        y, half = rest(wrapped, 8), quot(wrapped, 8)
        count = 4 if self.dense else 2
        tiles = [self.side_in[y, 2 + half * count + index] for index in range(count)]
        return [
            jnp.concatenate(tiles[at : at + 2], axis=1) for at in range(0, count, 2)
        ]

    def finish(self, first, last):
        for copy, shift in self.started[first:last]:
            self.when(self.has_target(shift), copy.wait_send)


def split_packed(value):
    left = iota(value.shape, 1) < 64
    return jnp.where(left, value, 0.0), jnp.where(left, roll(value, 64, 1), 0.0)


def build_matrices(pool, fan):
    line, lane = iota((128, 128), 0), iota((128, 128), 1)
    for half in range(4):
        x, y = div(line, 16) + 8 * (half % 2), mod(line, 16)
        rows = slice(128 * half, 128 * half + 128)
        home4 = div(x, 2) * 8 + div(y, 2) + 64 * (half // 2)
        home5 = div(x, 4) * 4 + div(y, 4) + 64 * (half // 2)
        pool[rows, 0:128] = one_hot(home4 == lane).astype(BF16)
        pool[rows, 128:256] = one_hot(home5 == lane).astype(BF16)
    three = one_hot(mod(line, 16) == div(lane, 8)).astype(BF16)
    fan[0:128, :] = three
    fan[128:256, :] = three
    fan[256:384, :] = one_hot(mod(line, 8) == div(lane, 16)).astype(BF16)
    fan[384:512, :] = one_hot(mod(line, 4) == div(lane, 32)).astype(BF16)


def kernel(nf, ns, rhs, dens, solution, residual, *scratch):
    scratch = list(scratch)

    def take(count):
        taken = scratch[:count]
        del scratch[:count]
        return taken

    refs = {}
    for name in ("D0", "D1", "D2", "R0", "R1", "R2"):
        (refs[name],) = take(1)
    fine_coef = [take(5) for _ in range(3)]
    remains = take(3)
    updates = [take(3) for _ in range(3)]
    answers = take(3)
    (work, tile_work, pair, sol, spread) = take(5)
    (spread_row, pool, fan, keep3, keep4, keep5) = take(6)
    coarse_coef = [take(5) for _ in range(3)]
    phases = []
    k, s = lax.axis_index("fine"), lax.axis_index("sub")
    for with_density in (True, False):
        count = n_halo(with_density)
        buffers = take(count), take(count)
        coarse = take(4)
        send_sem, recv_sem = take(2)
        phases.append(
            Phase(refs, (k, s, nf, ns), with_density, buffers, coarse, send_sem, recv_sem)
        )
    ng = nf // ROW
    i, g = rest(k, ROW), quot(k, ROW)

    barrier = pltpu.get_barrier_semaphore()
    partners = []
    for shift in (1, 2, 3):
        partners += [(rest(k + shift, nf), s), (rest(k + nf - shift, nf), s)]
    partners += [(g * ROW + rest(i + delta, ROW), s) for delta in range(1, ROW)]
    depth, side = partners_of((k, s, nf, ns))
    partners += depth + [device for _, device in side]
    for partner in partners:
        pl.semaphore_signal(barrier, inc=1, device_id=partner, device_id_type=MESH)

    pair[...] = jnp.zeros((16, 128), F32)

    def restrict_all(name, lead):
        for level in range(2):
            refs[name + str(level + 1)][
                lead : lead + PLANES[level + 1], 0 : ROWS[level + 1], :
            ] = restrict_block(
                refs[name + str(level)], lead, PLANES[level], ROWS[level], 2**level, work
            )

    def coefficients(level, low, high):
        fine_coefficients(level, refs["D" + str(level)], fine_coef[level], low, high)

    def smooth(level):
        fine_smooth(
            level,
            refs["R" + str(level)],
            fine_coef[level],
            remains[level],
            updates[level],
            answers[level],
        )

    line, lane = iota((128, 128), 0), iota((128, 128), 1)
    spread_row[...] = one_hot(div(line, 8) == mod(lane, 16)).astype(BF16)

    for cycle in range(CYCLES):
        phase = phases[cycle]
        if cycle == 0:
            phase.pack_row((rhs[...], dens[...]), pair, spread_row)
            pl.semaphore_wait(barrier, len(partners))
        else:
            phase.pack_row((refs["R0"][4:12, 0:32, :],), pair, spread_row)
        phase.start_rows()
        if cycle == 0:
            refs["R0"][4:12, 0:32, :] = rhs[...]
            refs["D0"][5:13, 0:32, :] = dens[...]
            restrict_all("D", 5)
        restrict_all("R", 4)
        phase.pack_x()
        phase.start_x()
        phase.pack_z("first")
        phase.start_z("first")
        phase.start_depth()
        if cycle == 0:
            build_matrices(pool, fan)
            for level in range(3):
                for name, lead in (("D", 5), ("R", 4)):
                    ref = refs[name + str(level)]
                    planes, rows, _ = ref.shape
                    blank = jnp.zeros((lead, rows, 128), F32)
                    ref[0:lead] = blank
                    ref[planes - lead : planes] = blank
            for ref in (keep4, keep5):
                rows = ref.shape[0]
                ref[0:8, :] = jnp.zeros((8, 128), F32)
                ref[rows - 8 : rows, :] = jnp.zeros((8, 128), F32)
        phase.unpack_x()
        phase.pack_z("second")
        phase.start_z("second")
        phase.start_sides(tile_work, pool)
        if cycle == 0:
            coefficients(0, 5, 11)
        else:
            phases[0].finish(0, None)
        phase.unpack_z()
        for level in (2, 1):
            if cycle == 0:
                coefficients(level, 0, PLANES[level] + 8)
            smooth(level)
        if cycle == 0:
            coefficients(0, 0, 5)
            coefficients(0, 11, 16)
        smooth(0)

        for level in (2, 1):
            rows = ROWS[level]
            planes = PLANES[level] + 2
            value = answers[level][3 : 3 + planes]
            if level == 1:
                value = value + jnp.concatenate(
                    [spread[(p + 1) // 2 : (p + 1) // 2 + 1, 0 : rows + 8, :] for p in range(planes)],
                    axis=0,
                )
            own, ends = value[:, 0:rows, :], value[:, rows : rows + 8, :]
            spread[0:planes, pl.ds(0, rows, stride=2), :] = own
            spread[0:planes, pl.ds(1, rows, stride=2), :] = own
            spread[0:planes, 2 * rows : 2 * rows + 8, :] = jnp.where(
                upper_rows(planes), ends[:, 0:1, :], ends[:, 7:8, :]
            )

        def collect(p, carry, cycle=cycle):
            step = 0.4 * (answers[0][p + 3] + spread[(p + 1) // 2])
            sol[p] = step if cycle == 0 else sol[p] + step
            return carry

        lax.fori_loop(0, PLANES[0] + 2, collect, 0, unroll=True)
        if cycle == 1:
            phase.finish(0, -2)
        phase.wait_sides()

        tiles = [phase.side_in[index % 8, index // 8] for index in range(ng)]
        line = iota((8, 128), 0)
        packed4, packed5 = [], []
        for index in range(0, ng, 2):
            packed4.append(jnp.where(line < 4, tiles[index], roll(tiles[index + 1], 4, 0)))
        for index in range(0, ng, 4):
            first = jnp.where(line < 6, tiles[index], tiles[index + 1])
            second = jnp.where(line < 6, tiles[index + 2], tiles[index + 3])
            packed5.append(jnp.where(line < 4, roll(first, 4, 0), second))
        source4, density4 = split_packed(jnp.concatenate(packed4, axis=0))
        source5, density5 = split_packed(jnp.concatenate(packed5, axis=0))
        if cycle == 0:
            low_in = jnp.where(g > 0, 1.0, 0.0).astype(F32)
            high_in = jnp.where(g < ng - 1, 1.0, 0.0).astype(F32)
            density3 = jnp.concatenate(
                [
                    phase.group_fields(g - 1)[1] * low_in,
                    phase.group_fields(g)[1],
                    phase.group_fields(g + 1)[1] * high_in,
                ],
                axis=0,
            )
            for index, (field, ny) in enumerate(
                ((density3, 16), (density4, 8), (density5, 4))
            ):
                values = packed_coefficients(field, ny, ny, 0.25 ** (3 + index))
                for ref, value in zip(coarse_coef[index], values):
                    ref[...] = value
        coef3, coef4, coef5 = ([ref[...] for ref in refs5] for refs5 in coarse_coef)
        total = jnp.sum(jnp.sum(source5, axis=0, keepdims=True), axis=1, keepdims=True)
        weight = jnp.sum(jnp.sum(coef5[3], axis=0, keepdims=True), axis=1, keepdims=True)
        n4, n5 = 4 * ng, 2 * ng
        keep5[8 : 8 + n5, :] = packed_smooth(source5, coef5, 4, 0.05) + total / weight
        keep4[8 : 8 + n4, :] = packed_smooth(source4, coef4, 8, 0.5)

        source3 = jnp.concatenate(
            [phase.group_fields(g + shift)[0] for shift in (-1, 0, 1)], axis=0
        )
        keep3[...] = packed_smooth(source3, coef3, 16, 0.5)

        row = iota((16, 512), 0)
        lane = iota((16, 512), 1)
        x3 = div(row, 2) + jnp.where(row < 12, 0, -8) + (4 * s + 4)
        inside = (x3 >= 4) & (x3 < 20)
        x_lane = jnp.where(
            lane < 256,
            div(lane, 16),
            jnp.where(lane < 384, div(mod(lane, 128), 8), div(mod(lane, 128), 4)),
        )
        x_row = jnp.where(lane < 256, x3 - 4, jnp.where(lane < 384, div(x3, 2) - 2, div(x3, 4) - 1))
        chosen = (x_lane == x_row) & inside
        picked = []
        for t in range(3):
            parts = jnp.concatenate(
                [
                    keep3[pl.ds(7 + i + t, 1), :],
                    keep4[pl.ds(quot(k + 1 + t, 2) + 7, 1), :],
                    keep5[pl.ds(quot(k + 3 + t, 4) + 7, 1), :],
                ],
                axis=1,
            )
            picked.append(jnp.where(chosen, parts, 0.0))
        lifted = one_hot_matmul(jnp.concatenate(picked, axis=0), fan[...]).reshape(3, 16, 128)

        for t in range(3):
            for tile in range(4):
                spread[t, 8 * tile : 8 * tile + 8, :] = jnp.broadcast_to(
                    lifted[t, 2 * tile : 2 * tile + 1, :], (8, 128)
                )
            spread[t, 32:40, :] = jnp.where(
                iota((8, 128), 0) < 4, lifted[t, 8:9, :], lifted[t, 15:16, :]
            )

        def advance(p, carry):
            sol[p] = sol[p] + 0.4 * spread[(p + 7) // 8]
            return carry

        lax.fori_loop(0, PLANES[0] + 2, advance, 0, unroll=True)

        def defect(p, carry, cycle=cycle):
            applied = fine_apply(sol, p + 1, fine_coef[0], p + 4, 1)
            left = rhs[p] - applied[0:32, :]
            if cycle == 0:
                refs["R0"][p + 4, 0:32, :] = left
            else:
                residual[p] = left
                solution[p] = sol[p + 1, 0:32, :]
            return carry

        lax.fori_loop(0, PLANES[0], defect, 0, unroll=True)

    phases[1].finish(-2, None)


def scratch_shapes(ng):
    shapes = []
    for level in range(3):
        shapes.append(pltpu.VMEM((PLANES[level] + 10, ROWS[level] + 16, 128), F32))
    extents = [(PLANES[level] + 8, ROWS[level] + 8, 128) for level in range(3)]
    shapes += [pltpu.VMEM(extent, F32) for extent in extents]
    for extent in extents:
        shapes += [pltpu.VMEM(extent, F32)] * 5
    shapes += [pltpu.VMEM(extent, F32) for extent in extents]
    for extent in extents:
        shapes += [pltpu.VMEM(extent, F32)] * 3
    shapes += [pltpu.VMEM(extent, F32) for extent in extents]
    shapes += [
        pltpu.VMEM((4, 32, 128), F32),
        pltpu.VMEM((16, 128), F32),
        pltpu.VMEM((16, 128), F32),
        pltpu.VMEM((10, 40, 128), F32),
        pltpu.VMEM((6, 40, 128), F32),
        pltpu.VMEM((128, 128), BF16),
        pltpu.VMEM((512, 256), BF16),
        pltpu.VMEM((512, 128), BF16),
        pltpu.VMEM((24, 256), F32),
        pltpu.VMEM((4 * ng + 16, 128), F32),
        pltpu.VMEM((2 * ng + 16, 128), F32),
    ]
    for extent in ((24, 256), (4 * ng, 128), (2 * ng, 128)):
        shapes += [pltpu.VMEM(extent, F32)] * 5
    for with_density in (True, False):
        halo = buffer_shapes(with_density)
        shapes += halo + halo
        tiles = 10 if with_density else 6
        shapes += [
            pltpu.VMEM((1, 128), F32),
            pltpu.VMEM((ROW, 1, 128), F32),
            pltpu.VMEM((8, 8, 128), F32),
            pltpu.VMEM((8, tiles, 8, 128), F32),
        ]
        copies = n_halo(with_density) + 4
        shapes += [pltpu.SemaphoreType.DMA((copies,)), pltpu.SemaphoreType.DMA((copies,))]
    return shapes


def solution(mesh):
    nf, ns = mesh.shape["fine"], mesh.shape["sub"]

    def body(rhs, density):
        return pl.pallas_call(
            functools.partial(kernel, nf, ns),
            out_shape=(
                jax.ShapeDtypeStruct(rhs.shape, F32),
                jax.ShapeDtypeStruct(rhs.shape, F32),
            ),
            in_specs=[pl.BlockSpec(memory_space=pltpu.VMEM)] * 2,
            out_specs=[pl.BlockSpec(memory_space=pltpu.VMEM)] * 2,
            scratch_shapes=scratch_shapes(nf // ROW),
            compiler_params=pltpu.CompilerParams(
                collective_id=0, has_side_effects=True, vmem_limit_bytes=32 * 1024 * 1024
            ),
        )(rhs, density)

    return jax.shard_map(
        body,
        mesh=mesh,
        in_specs=(P("fine", "sub", None), P("fine", "sub", None)),
        out_specs=(P("fine", "sub", None), P("fine", "sub", None)),
        check_vma=False,
    )
```

```python
import functools

import jax
import jax.numpy as jnp
from jax import lax
from jax.experimental import pallas as pl
from jax.experimental.pallas import tpu as pltpu
from jax.sharding import PartitionSpec as P

DEGREE = 4
CYCLES = 2
MESH = pl.DeviceIdType.MESH
F32 = jnp.float32
BF16 = jnp.bfloat16
ROW = 8
PLANES = (8, 4, 2)
ROWS = (32, 16, 8)


def chebyshev_constants(lower):
    upper = 2.0
    theta = 0.5 * (upper + lower)
    delta = 0.5 * (upper - lower)
    sigma = theta / delta
    ratio = 1.0 / sigma
    steps = []
    for _ in range(DEGREE - 1):
        next_ratio = 1.0 / (2.0 * sigma - ratio)
        steps.append((next_ratio * ratio, 2.0 * next_ratio / delta))
        ratio = next_ratio
    return 1.0 / theta, steps


def iota(shape, dim):
    return lax.broadcasted_iota(jnp.int32, shape, dim)


def div(value, divisor):
    return value >> (divisor.bit_length() - 1)


def mod(value, divisor):
    return value & (divisor - 1)


def quot(value, divisor):
    return lax.div(value, jnp.int32(divisor))


def rest(value, divisor):
    return lax.rem(value, jnp.int32(divisor))


def roll(value, shift, axis):
    return pltpu.roll(value, shift % value.shape[axis], axis)


def invert(value):
    return pltpu.reciprocal(value, full_range=False)


def one_hot(condition):
    return jnp.where(condition, 1.0, 0.0).astype(F32)


def one_hot_matmul(value, matrix):
    count = value.shape[0]
    first = value.astype(BF16).astype(F32)
    rest = value - first
    second = rest.astype(BF16).astype(F32)
    parts = jnp.concatenate([first, second, rest - second], axis=0).astype(BF16)
    product = jnp.dot(parts, matrix, preferred_element_type=F32)
    return product[0:count] + product[count : 2 * count] + product[2 * count :]


def restrict_block(source, first, planes, rows, stride, work):
    field = source[first : first + planes, 0:rows, :]
    field = field.reshape(planes // 2, 2, rows, 128)
    work[0 : planes // 2, 0:rows, :] = field[:, 0] + field[:, 1]
    half = rows // 2
    both = (
        work[0 : planes // 2, pl.ds(0, half, stride=2), :]
        + work[0 : planes // 2, pl.ds(1, half, stride=2), :]
    )
    lane = iota(both.shape, 2)
    even = mod(div(lane, stride), 2) == 0
    other = jnp.where(even, roll(both, -stride, 2), roll(both, stride, 2))
    return (both + other) * 0.125


def fine_coefficients(level, dens, coef, low, high):
    own = ROWS[level]
    scale = 2.0 * 0.25**level
    stride = 2**level
    face_z, face_x, face_y, diagonal, inverse = coef
    shape = (own + 16, 128)

    def compress(value):
        tail = jnp.where(
            iota((8, 128), 0) < 4, value[own : own + 8], value[own + 8 : own + 16]
        )
        return jnp.concatenate([value[0:own], tail], axis=0)

    def plane(p, down):
        here = dens[p + 1]
        above = dens[p + 2]
        lane = iota(shape, 1)
        right = roll(here, -1, 0)
        up = scale * invert(jnp.maximum(here + above, 0.1))
        x_face = scale * invert(jnp.maximum(here + right, 0.1))
        ahead = jnp.where(lane >= 128 - stride, 0.0, roll(here, -stride, 1))
        behind = jnp.where(lane < stride, 0.0, roll(here, stride, 1))
        y_face = scale * invert(jnp.maximum(here + ahead, 0.1))
        y_back = scale * invert(jnp.maximum(here + behind, 0.1))
        diag = up + down + x_face + roll(x_face, 1, 0) + y_face + y_back
        inside = here > 0.0
        face_z[p] = compress(jnp.where(inside & (above > 0.0), up, 0.0))
        face_x[p] = compress(jnp.where(inside & (right > 0.0), x_face, 0.0))
        face_y[p] = compress(jnp.where(lane >= 128 - stride, 0.0, y_face))
        diagonal[p] = compress(diag)
        inverse[p] = compress(invert(diag))
        return up

    lowest = scale * invert(jnp.maximum(dens[low] + dens[low + 1], 0.1))
    lax.fori_loop(low, high, plane, lowest, unroll=True)


def fine_apply(field, p, coef, q, stride):
    face_z, face_x, face_y, diagonal, _ = coef
    here = field[p]
    x_face = face_x[q]
    y_face = face_y[q]
    result = diagonal[q] * here
    result = result - face_z[q] * field[p + 1] - face_z[q - 1] * field[p - 1]
    result = result - x_face * roll(here, -1, 0) - roll(x_face * here, 1, 0)
    result = result - y_face * roll(here, -stride, 1) - roll(y_face * here, stride, 1)
    return result


def fine_smooth(level, source, coef, remain, updates, answer, inner, early):
    planes = PLANES[level] + 8
    stride = 2**level
    inverse = coef[4]
    first, steps = chebyshev_constants(0.5)
    d0, d1, d2 = updates

    def start(p, carry):
        d0[p] = source[p] * inverse[p] * first
        return carry

    def planes_of(shrink):
        low, high = shrink, planes - shrink
        if inner is None:
            return [(low, high)]
        first_in, last_in = inner[0] + shrink, inner[1] - shrink
        return [(first_in, last_in)] if early else [(low, first_in), (last_in, high)]

    for low, high in planes_of(0):
        lax.fori_loop(low, high, start, 0, unroll=True)
    chain = (d0, d1, d2)
    for sweep in range(3):
        old = chain[sweep]
        keep, add = steps[sweep]

        def step(p, carry, sweep=sweep, old=old, keep=keep, add=add):
            left = source[p] if sweep == 0 else remain[p]
            left = left - fine_apply(old, p, coef, p, stride)
            new = keep * old[p] + add * (left * inverse[p])
            if sweep < 2:
                remain[p] = left
                chain[sweep + 1][p] = new
            else:
                answer[p] = d0[p] + d1[p] + d2[p] + new
            return carry

        for low, high in planes_of(sweep + 1):
            lax.fori_loop(low, high, step, 0, unroll=True)


def packed_coefficients(dens, ny, nx, scale):
    rows = dens.shape[0]
    z = iota(dens.shape, 0)
    lane = iota(dens.shape, 1)
    y = mod(lane, ny)
    x = div(lane, ny)
    scale = 2.0 * scale

    def neighbour(shift, axis, outside):
        return jnp.where(outside, 0.0, roll(dens, shift, axis))

    above = neighbour(-1, 0, z == rows - 1)
    below = neighbour(1, 0, z == 0)
    right = neighbour(-ny, 1, x >= nx - 1)
    left = neighbour(ny, 1, x == 0)
    ahead = neighbour(-1, 1, y == ny - 1)
    behind = neighbour(1, 1, y == 0)

    def face(other):
        return scale * invert(jnp.maximum(dens + other, 0.1))

    up, x_face, y_face = face(above), face(right), face(ahead)
    diagonal = up + face(below) + x_face + face(left) + y_face + face(behind)
    inside = dens > 0.0

    def inner(value, other):
        return jnp.where(inside & (other > 0.0), value, 0.0)

    return (
        inner(up, above),
        inner(x_face, right),
        inner(y_face, ahead),
        jnp.where(inside, diagonal, 0.0),
        jnp.where(inside, invert(diagonal), 0.0),
    )


def packed_apply(field, coef, ny):
    face_z, face_x, face_y, diagonal, _ = coef
    result = diagonal * field
    result = result - face_z * roll(field, -1, 0) - roll(face_z * field, 1, 0)
    result = result - face_x * roll(field, -ny, 1) - roll(face_x * field, ny, 1)
    result = result - face_y * roll(field, -1, 1) - roll(face_y * field, 1, 1)
    return result


def packed_smooth(source, coef, ny, lower):
    first, steps = chebyshev_constants(lower)
    inverse = coef[4]
    update = source * inverse * first
    answer = update
    for keep, add in steps:
        source = source - packed_apply(update, coef, ny)
        update = keep * update + add * (source * inverse)
        answer = answer + update
    return answer


PIECES = {
    ("first", 1): {
        "a": (("D0", 8, 0, 5), ("R0", 8, 0, 4), ("D1", 5, 1, 4), ("D2", 5, 3, 2))
        + (("R1", 4, 0, 4), ("R2", 4, 2, 2)),
    },
    ("first", -1): {
        "a": (("D0", 5, 13, 5), ("R0", 4, 12, 4), ("D1", 5, 9, 4), ("D2", 5, 7, 2))
        + (("R1", 4, 8, 4), ("R2", 4, 6, 2)),
    },
    ("first", 3): {"a": (("D2", 6, 0, 1),)},
    ("first", -3): {"a": (("D2", 5, 11, 1),)},
    ("second", 2): {
        "a": (("D1", 8, 0, 1), ("D2", 5, 1, 2), ("R2", 4, 0, 2)),
        "b": (("D2", 5, 1, 2), ("R2", 4, 0, 2)),
    },
    ("second", -2): {
        "a": (("D1", 5, 13, 1), ("D2", 5, 9, 2), ("R2", 4, 8, 2)),
        "b": (("D2", 5, 9, 2), ("R2", 4, 8, 2)),
    },
    ("second", 1): {
        "b": (("D0", 9, 1, 4), ("D1", 5, 1, 4), ("D2", 5, 3, 2))
        + (("R0", 9, 1, 3), ("R1", 4, 0, 4), ("R2", 4, 2, 2)),
    },
    ("second", -1): {
        "b": (("D0", 5, 13, 4), ("D1", 5, 9, 4), ("D2", 5, 7, 2))
        + (("R0", 4, 12, 3), ("R1", 4, 8, 4), ("R2", 4, 6, 2)),
    },
}


def z_messages(with_density):
    result = []
    for (stage, shift), parts in PIECES.items():
        pieces = [
            (part, piece)
            for part, listed in parts.items()
            for piece in listed
            if with_density or piece[0][0] == "R"
        ]
        if pieces:
            result.append((stage, shift, pieces))
    return result


def paired(name, tiles):
    return name[1] != "0" and tiles % 2 == 0


def piece_tiles(part, piece):
    name, _, _, count = piece
    tiles = count * (ROWS[int(name[1])] // 8 if part == "a" else 1)
    return tiles // 2 if paired(name, tiles) else tiles


def x_pieces(with_density):
    result = []
    for level in range(3):
        count = PLANES[level]
        if with_density:
            result.append(("D%d" % level, count, count // 2 if level else count))
        result.append(("R%d" % level, count, (4, 1, 1)[level]))
    return result


def buffer_shapes(with_density):
    tiles = [sum(sent for _, _, sent in x_pieces(with_density))] * 2
    for _, _, pieces in z_messages(with_density):
        tiles.append(sum(piece_tiles(part, piece) for part, piece in pieces))
    return [pltpu.VMEM((count, 8, 128), F32) for count in tiles]


def n_halo(with_density):
    return 2 + len(z_messages(with_density))


def even_lanes(tiles):
    return mod(iota((tiles, 8, 128), 2), 2) == 0


def upper_rows(tiles):
    return iota((tiles, 8, 128), 1) < 4


def pack_lanes(block):
    half = block.shape[0] // 2
    return jnp.where(even_lanes(half), block[0:half], block[half:])


def unpack_lanes(block):
    even = even_lanes(block.shape[0])
    return jnp.concatenate(
        [jnp.where(even, block, roll(block, 1, 2)), jnp.where(even, roll(block, -1, 2), block)],
        axis=0,
    )


def partners_of(place):
    k, s, _, ns = place
    i, y, half = rest(k, ROW), rest(quot(k, ROW), 8), quot(k, 8 * ROW)
    depth, side = [], []
    for delta in (4, 3, 5, 2, 6, 1, 7):
        z = rest(half * ns + s + delta, 2 * ns)
        depth.append(((quot(z, ns) * 8 + y) * ROW + i, rest(z, ns)))
        side.append((delta, ((half * 8 + rest(y + delta, 8)) * ROW + i, s)))
    return depth, side


class Phase:
    def __init__(self, refs, place, with_density, buffers, coarse, send_sem, recv_sem):
        send, recv = buffers
        self.refs = refs
        self.k, self.s, self.nf, self.ns = place
        self.dense = with_density
        self.send, self.recv = send, recv
        self.row, self.row_in, self.depth_in, self.side_in = coarse
        self.send_sem, self.recv_sem = send_sem, recv_sem
        self.started = []
        self.count = 0
        self.z = z_messages(with_density)
        self.copies = {}
        self.i = rest(self.k, ROW)
        self.g = quot(self.k, ROW)
        self.ng = self.nf // ROW
        self.y = rest(self.g, 8)
        self.z_at = quot(self.g, 8) * self.ns + self.s
        self.depth_partners, self.side_partners = partners_of(place)

    def start(self, source, target, k, s, shift=0):
        index = self.count
        self.count += 1
        copy = pltpu.make_async_remote_copy(
            src_ref=source,
            dst_ref=target,
            send_sem=self.send_sem.at[index],
            recv_sem=self.recv_sem.at[index],
            device_id=(k, s),
            device_id_type=MESH,
        )
        self.when(self.has_target(shift), copy.start)
        self.started.append((copy, shift))
        return copy

    def has_target(self, shift):
        if shift == 0:
            return None
        return self.k < self.nf - shift if shift > 0 else self.k >= -shift

    def has_source(self, shift):
        return self.has_target(-shift)

    def when(self, condition, action):
        if condition is None:
            action()
        else:
            pl.when(condition)(action)

    def start_all(self, pairs, total):
        index = self.count
        self.count += 1
        sems = {"send_sem": self.send_sem.at[index], "recv_sem": self.recv_sem.at[index]}
        for source, target, device in pairs:
            pltpu.make_async_remote_copy(
                src_ref=source,
                dst_ref=target,
                device_id=device,
                device_id_type=MESH,
                **sems,
            ).start()
        whole = pltpu.make_async_remote_copy(
            src_ref=total,
            dst_ref=total,
            device_id=pairs[0][2],
            device_id_type=MESH,
            **sems,
        )
        self.started.append((whole, 0))
        return whole

    def pack_x(self):
        for which in (0, 1):
            at = 0
            for name, count, sent in x_pieces(self.dense):
                level = int(name[1])
                lead = 5 if name[0] == "D" else 4
                row = ROWS[level] - 8 if which == 0 else 0
                block = self.refs[name][lead : lead + count, row : row + 8, :]
                if level:
                    block = pack_lanes(block)
                if block.shape[0] > sent:
                    near, far = block[0:sent], roll(block[sent:], 4, 1)
                    upper = upper_rows(sent)
                    if which == 0:
                        block = jnp.where(upper, far, near)
                    else:
                        block = jnp.where(upper, near, far)
                self.send[which][at : at + sent] = block
                at += sent

    def start_x(self):
        up, down = rest(self.s + 1, self.ns), rest(self.s + self.ns - 1, self.ns)
        self.x_copies = [
            self.start(self.send[0], self.recv[0], self.k, up),
            self.start(self.send[1], self.recv[1], self.k, down),
        ]

    def unpack_x(self):
        for copy in self.x_copies:
            copy.wait_recv()
        low_in = jnp.where(self.s > 0, 1.0, 0.0).astype(F32)
        high_in = jnp.where(self.s < self.ns - 1, 1.0, 0.0).astype(F32)
        at = 0
        for name, count, sent in x_pieces(self.dense):
            level = int(name[1])
            own = ROWS[level]
            lead = 5 if name[0] == "D" else 4
            low, high = self.recv[0][at : at + sent], self.recv[1][at : at + sent]
            at += sent
            ref = self.refs[name]
            if name[0] == "D":
                if level:
                    low, high = unpack_lanes(low), unpack_lanes(high)
                ref[lead : lead + count, own : own + 8, :] = high * high_in
                ref[lead : lead + count, own + 8 : own + 16, :] = low * low_in
                continue
            upper = upper_rows(sent)
            block = jnp.where(upper, high, low)
            if sent < (count // 2 if level else count):
                far = roll(jnp.where(upper, low, high), 4, 1)
                block = jnp.concatenate([block, far], axis=0)
            if level:
                block = unpack_lanes(block)
            ref[lead : lead + count, own : own + 8, :] = block

    def pack_z(self, stage):
        for index, (when, _, pieces) in enumerate(self.z):
            if when != stage:
                continue
            at = 0
            for part, piece in pieces:
                name, source, _, count = piece
                ref, own = self.refs[name], ROWS[int(name[1])]
                if part == "a":
                    block = ref[source : source + count, 0:own, :]
                    block = block.reshape(count * own // 8, 8, 128)
                else:
                    block = ref[source : source + count, own : own + 8, :]
                    if name[0] == "D":
                        low = ref[source : source + count, own + 8 : own + 16, :]
                        block = jnp.where(upper_rows(count), block, low)
                if paired(name, block.shape[0]):
                    block = pack_lanes(block)
                self.send[2 + index][at : at + block.shape[0]] = block
                at += block.shape[0]

    def start_z(self, stage):
        for index, (when, shift, _) in enumerate(self.z):
            if when == stage:
                target = rest(self.k + shift + self.nf, self.nf)
                self.copies[index] = self.start(
                    self.send[2 + index], self.recv[2 + index], target, self.s, shift
                )

    def unpack_z(self):
        for index, (_, shift, _) in enumerate(self.z):
            self.when(self.has_source(shift), self.copies[index].wait_recv)
        for index, (_, shift, pieces) in enumerate(self.z):
            inside = self.has_source(shift)
            at = 0
            for part, piece in pieces:
                name, _, target, count = piece
                ref, own = self.refs[name], ROWS[int(name[1])]
                sent = piece_tiles(part, piece)
                block = jnp.where(inside, self.recv[2 + index][at : at + sent], 0.0)
                at += sent
                if sent < (count * own // 8 if part == "a" else count):
                    block = unpack_lanes(block)
                if part == "a":
                    ref[target : target + count, 0:own, :] = block.reshape(count, own, 128)
                else:
                    ref[target : target + count, own : own + 8, :] = block
                    if name[0] == "D":
                        ref[target : target + count, own + 8 : own + 16, :] = block

    def pack_row(self, fields, pair, spread_row):
        for index, field in enumerate(fields):
            pillar = jnp.sum(field, axis=0).reshape(4, 8, 128)
            pair[4 * index : 4 * index + 4, :] = jnp.sum(pillar, axis=1) * 0.125**3
        spread = one_hot_matmul(pair[...], spread_row[...])[0:8]
        mine = div(iota((8, 128), 1), 16) == iota((8, 128), 0)
        row = jnp.sum(jnp.where(mine, spread, 0.0), axis=0, keepdims=True)
        self.row[...] = row
        self.row_in[self.i] = row

    def start_rows(self):
        slot = self.row_in.at[self.i]
        devices = [
            (self.g * ROW + rest(self.i + delta, ROW), self.s) for delta in (4, 3, 5, 2, 6, 1, 7)
        ]
        pairs = [(self.row, slot, device) for device in devices]
        self.row_copies = self.start_all(pairs, self.row_in.at[0 : ROW - 1])

    def start_depth(self):
        self.row_copies.wait_recv()
        line = iota((8, 128), 0)
        tile = jnp.zeros((8, 128), F32)
        for index in range(ROW):
            tile = jnp.where(line == index, self.row_in[index], tile)
        self.depth_in[self.z_at] = tile
        slot = self.depth_in.at[self.z_at]
        pairs = [(slot, slot, device) for device in self.depth_partners]
        self.depth_copies = self.start_all(pairs, self.depth_in.at[0:7])

    def start_sides(self, work, pool):
        self.depth_copies.wait_recv()
        left = iota((8, 128), 1) < 64
        slot = self.side_in.at[self.y]
        wide = []
        for half in range(2):
            tiles = [self.depth_in[4 * half + index] for index in range(4)]
            turned = [roll(tile, 64, 1) for tile in tiles]
            fields = [jnp.where(left, tiles[a], turned[a + 1]) for a in (0, 2)]
            if self.dense:
                fields += [jnp.where(left, turned[a], tiles[a + 1]) for a in (0, 2)]
            for index, field in enumerate(fields):
                slot[2 + len(fields) * half + index] = field
            wide.append(jnp.concatenate(fields, axis=1))
        wide = jnp.concatenate(wide, axis=0)
        sums = one_hot_matmul(wide, pool[0 : wide.shape[1], :])
        work[...] = sums[:, 0:128]
        line = iota((8, 128), 0)
        for half in range(2):
            four = work[pl.ds(8 * half, 4, stride=2), :] + work[pl.ds(8 * half + 1, 4, stride=2), :]
            slot[half, 0:4, :] = four * 0.125
            five = sums[8 * half : 8 * half + 8, 128:256]
            five = five + roll(five, -1, 0)
            five = (five + roll(five, -2, 0)) * (0.125 * 0.125)
            five = jnp.where(mod(line, 2) == 0, five[0:1], five[4:5])
            slot[half, 4:8, :] = five[4:8]
        part = slot.at[0:2]
        far = [(part, part, device) for delta, device in self.side_partners if delta not in (1, 7)]
        self.side_copies = [self.start_all(far, self.side_in.at[0:5, 0:2])]
        near = [(slot, slot, device) for delta, device in self.side_partners if delta in (1, 7)]
        self.side_copies.append(self.start_all(near, self.side_in.at[0:2]))

    def wait_sides(self):
        for copy in self.side_copies:
            copy.wait_recv()

    def group_fields(self, group):
        wrapped = rest(group + self.ng, self.ng)
        y, half = rest(wrapped, 8), quot(wrapped, 8)
        count = 4 if self.dense else 2
        tiles = [self.side_in[y, 2 + half * count + index] for index in range(count)]
        return [
            jnp.concatenate(tiles[at : at + 2], axis=1) for at in range(0, count, 2)
        ]

    def finish(self, first, last):
        for copy, shift in self.started[first:last]:
            self.when(self.has_target(shift), copy.wait_send)


def split_packed(value):
    left = iota(value.shape, 1) < 64
    return jnp.where(left, value, 0.0), jnp.where(left, roll(value, 64, 1), 0.0)


def build_matrices(pool, fan):
    line, lane = iota((128, 128), 0), iota((128, 128), 1)
    for half in range(4):
        x, y = div(line, 16) + 8 * (half % 2), mod(line, 16)
        rows = slice(128 * half, 128 * half + 128)
        home4 = div(x, 2) * 8 + div(y, 2) + 64 * (half // 2)
        home5 = div(x, 4) * 4 + div(y, 4) + 64 * (half // 2)
        pool[rows, 0:128] = one_hot(home4 == lane).astype(BF16)
        pool[rows, 128:256] = one_hot(home5 == lane).astype(BF16)
    three = one_hot(mod(line, 16) == div(lane, 8)).astype(BF16)
    fan[0:128, :] = three
    fan[128:256, :] = three
    fan[256:384, :] = one_hot(mod(line, 8) == div(lane, 16)).astype(BF16)
    fan[384:512, :] = one_hot(mod(line, 4) == div(lane, 32)).astype(BF16)


def kernel(nf, ns, rhs, dens, solution, residual, *scratch):
    scratch = list(scratch)

    def take(count):
        taken = scratch[:count]
        del scratch[:count]
        return taken

    refs = {}
    for name in ("D0", "D1", "D2", "R0", "R1", "R2"):
        (refs[name],) = take(1)
    fine_coef = [take(5) for _ in range(3)]
    remains = take(3)
    updates = [take(3) for _ in range(3)]
    answers = take(3)
    (work, tile_work, pair, sol, spread) = take(5)
    (spread_row, pool, fan, keep3, keep4, keep5) = take(6)
    coarse_coef = [take(5) for _ in range(3)]
    phases = []
    k, s = lax.axis_index("fine"), lax.axis_index("sub")
    for with_density in (True, False):
        count = n_halo(with_density)
        buffers = take(count), take(count)
        coarse = take(4)
        send_sem, recv_sem = take(2)
        phases.append(
            Phase(refs, (k, s, nf, ns), with_density, buffers, coarse, send_sem, recv_sem)
        )
    ng = nf // ROW
    i, g = rest(k, ROW), quot(k, ROW)

    barrier = pltpu.get_barrier_semaphore()
    partners = []
    for shift in (1, 2, 3):
        partners += [(rest(k + shift, nf), s), (rest(k + nf - shift, nf), s)]
    partners += [(g * ROW + rest(i + delta, ROW), s) for delta in range(1, ROW)]
    depth, side = partners_of((k, s, nf, ns))
    partners += depth + [device for _, device in side]
    for partner in partners:
        pl.semaphore_signal(barrier, inc=1, device_id=partner, device_id_type=MESH)

    pair[...] = jnp.zeros((16, 128), F32)

    def restrict_all(name, lead):
        for level in range(2):
            refs[name + str(level + 1)][
                lead : lead + PLANES[level + 1], 0 : ROWS[level + 1], :
            ] = restrict_block(
                refs[name + str(level)], lead, PLANES[level], ROWS[level], 2**level, work
            )

    def coefficients(level, low, high):
        fine_coefficients(level, refs["D" + str(level)], fine_coef[level], low, high)

    def smooth(level, inner=None, early=False):
        fine_smooth(
            level,
            refs["R" + str(level)],
            fine_coef[level],
            remains[level],
            updates[level],
            answers[level],
            inner,
            early,
        )

    line, lane = iota((128, 128), 0), iota((128, 128), 1)
    spread_row[...] = one_hot(div(line, 8) == mod(lane, 16)).astype(BF16)

    for cycle in range(CYCLES):
        phase = phases[cycle]
        if cycle == 0:
            refs["R0"][4:12, 0:32, :] = rhs[...]
            refs["D0"][5:13, 0:32, :] = dens[...]
            restrict_all("D", 5)
        restrict_all("R", 4)
        phase.pack_x()
        if cycle == 0:
            pl.semaphore_wait(barrier, len(partners))
        phase.start_x()
        if cycle == 0:
            phase.pack_row((rhs[...], dens[...]), pair, spread_row)
        else:
            phase.pack_row((refs["R0"][4:12, 0:32, :],), pair, spread_row)
        phase.start_rows()
        phase.pack_z("first")
        phase.start_z("first")
        phase.unpack_x()
        phase.pack_z("second")
        phase.start_z("second")
        phase.start_depth()
        if cycle == 0:
            build_matrices(pool, fan)
            for level in range(3):
                for name, lead in (("D", 5), ("R", 4)):
                    ref = refs[name + str(level)]
                    planes, rows, _ = ref.shape
                    blank = jnp.zeros((lead, rows, 128), F32)
                    ref[0:lead] = blank
                    ref[planes - lead : planes] = blank
            for ref in (keep4, keep5):
                rows = ref.shape[0]
                ref[0:8, :] = jnp.zeros((8, 128), F32)
                ref[rows - 8 : rows, :] = jnp.zeros((8, 128), F32)
        phase.start_sides(tile_work, pool)
        inner = (5, 11) if cycle == 0 else (4, 12)
        if cycle == 0:
            coefficients(0, 5, 11)
        else:
            phases[0].finish(0, None)
        smooth(0, inner, True)
        phase.unpack_z()
        for level in (2, 1):
            if cycle == 0:
                coefficients(level, 0, PLANES[level] + 8)
            smooth(level)
        if cycle == 0:
            coefficients(0, 0, 5)
            coefficients(0, 11, 16)
        smooth(0, inner)

        for level in (2, 1):
            rows = ROWS[level]
            planes = PLANES[level] + 2
            value = answers[level][3 : 3 + planes]
            if level == 1:
                value = value + jnp.concatenate(
                    [spread[(p + 1) // 2 : (p + 1) // 2 + 1, 0 : rows + 8, :] for p in range(planes)],
                    axis=0,
                )
            own, ends = value[:, 0:rows, :], value[:, rows : rows + 8, :]
            spread[0:planes, pl.ds(0, rows, stride=2), :] = own
            spread[0:planes, pl.ds(1, rows, stride=2), :] = own
            spread[0:planes, 2 * rows : 2 * rows + 8, :] = jnp.where(
                upper_rows(planes), ends[:, 0:1, :], ends[:, 7:8, :]
            )

        def collect(p, carry, cycle=cycle):
            step = 0.4 * (answers[0][p + 3] + spread[(p + 1) // 2])
            sol[p] = step if cycle == 0 else sol[p] + step
            return carry

        lax.fori_loop(0, PLANES[0] + 2, collect, 0, unroll=True)
        if cycle == 1:
            phase.finish(0, -2)
        phase.wait_sides()

        tiles = [phase.side_in[index % 8, index // 8] for index in range(ng)]
        line = iota((8, 128), 0)
        packed4, packed5 = [], []
        for index in range(0, ng, 2):
            packed4.append(jnp.where(line < 4, tiles[index], roll(tiles[index + 1], 4, 0)))
        for index in range(0, ng, 4):
            first = jnp.where(line < 6, tiles[index], tiles[index + 1])
            second = jnp.where(line < 6, tiles[index + 2], tiles[index + 3])
            packed5.append(jnp.where(line < 4, roll(first, 4, 0), second))
        source4, density4 = split_packed(jnp.concatenate(packed4, axis=0))
        source5, density5 = split_packed(jnp.concatenate(packed5, axis=0))
        if cycle == 0:
            low_in = jnp.where(g > 0, 1.0, 0.0).astype(F32)
            high_in = jnp.where(g < ng - 1, 1.0, 0.0).astype(F32)
            density3 = jnp.concatenate(
                [
                    phase.group_fields(g - 1)[1] * low_in,
                    phase.group_fields(g)[1],
                    phase.group_fields(g + 1)[1] * high_in,
                ],
                axis=0,
            )
            for index, (field, ny) in enumerate(
                ((density3, 16), (density4, 8), (density5, 4))
            ):
                values = packed_coefficients(field, ny, ny, 0.25 ** (3 + index))
                for ref, value in zip(coarse_coef[index], values):
                    ref[...] = value
        coef3, coef4, coef5 = ([ref[...] for ref in refs5] for refs5 in coarse_coef)
        total = jnp.sum(jnp.sum(source5, axis=0, keepdims=True), axis=1, keepdims=True)
        weight = jnp.sum(jnp.sum(coef5[3], axis=0, keepdims=True), axis=1, keepdims=True)
        n4, n5 = 4 * ng, 2 * ng
        keep5[8 : 8 + n5, :] = packed_smooth(source5, coef5, 4, 0.05) + total / weight
        keep4[8 : 8 + n4, :] = packed_smooth(source4, coef4, 8, 0.5)

        source3 = jnp.concatenate(
            [phase.group_fields(g + shift)[0] for shift in (-1, 0, 1)], axis=0
        )
        keep3[...] = packed_smooth(source3, coef3, 16, 0.5)

        row = iota((16, 512), 0)
        lane = iota((16, 512), 1)
        x3 = div(row, 2) + jnp.where(row < 12, 0, -8) + (4 * s + 4)
        inside = (x3 >= 4) & (x3 < 20)
        x_lane = jnp.where(
            lane < 256,
            div(lane, 16),
            jnp.where(lane < 384, div(mod(lane, 128), 8), div(mod(lane, 128), 4)),
        )
        x_row = jnp.where(lane < 256, x3 - 4, jnp.where(lane < 384, div(x3, 2) - 2, div(x3, 4) - 1))
        chosen = (x_lane == x_row) & inside
        picked = []
        for t in range(3):
            parts = jnp.concatenate(
                [
                    keep3[pl.ds(7 + i + t, 1), :],
                    keep4[pl.ds(quot(k + 1 + t, 2) + 7, 1), :],
                    keep5[pl.ds(quot(k + 3 + t, 4) + 7, 1), :],
                ],
                axis=1,
            )
            picked.append(jnp.where(chosen, parts, 0.0))
        lifted = one_hot_matmul(jnp.concatenate(picked, axis=0), fan[...]).reshape(3, 16, 128)

        for t in range(3):
            for tile in range(4):
                spread[t, 8 * tile : 8 * tile + 8, :] = jnp.broadcast_to(
                    lifted[t, 2 * tile : 2 * tile + 1, :], (8, 128)
                )
            spread[t, 32:40, :] = jnp.where(
                iota((8, 128), 0) < 4, lifted[t, 8:9, :], lifted[t, 15:16, :]
            )

        def advance(p, carry):
            sol[p] = sol[p] + 0.4 * spread[(p + 7) // 8]
            return carry

        lax.fori_loop(0, PLANES[0] + 2, advance, 0, unroll=True)

        def defect(p, carry, cycle=cycle):
            applied = fine_apply(sol, p + 1, fine_coef[0], p + 4, 1)
            left = rhs[p] - applied[0:32, :]
            if cycle == 0:
                refs["R0"][p + 4, 0:32, :] = left
            else:
                residual[p] = left
                solution[p] = sol[p + 1, 0:32, :]
            return carry

        lax.fori_loop(0, PLANES[0], defect, 0, unroll=True)

    phases[1].finish(-2, None)


def scratch_shapes(ng):
    shapes = []
    for level in range(3):
        shapes.append(pltpu.VMEM((PLANES[level] + 10, ROWS[level] + 16, 128), F32))
    extents = [(PLANES[level] + 8, ROWS[level] + 8, 128) for level in range(3)]
    shapes += [pltpu.VMEM(extent, F32) for extent in extents]
    for extent in extents:
        shapes += [pltpu.VMEM(extent, F32)] * 5
    shapes += [pltpu.VMEM(extent, F32) for extent in extents]
    for extent in extents:
        shapes += [pltpu.VMEM(extent, F32)] * 3
    shapes += [pltpu.VMEM(extent, F32) for extent in extents]
    shapes += [
        pltpu.VMEM((4, 32, 128), F32),
        pltpu.VMEM((16, 128), F32),
        pltpu.VMEM((16, 128), F32),
        pltpu.VMEM((10, 40, 128), F32),
        pltpu.VMEM((6, 40, 128), F32),
        pltpu.VMEM((128, 128), BF16),
        pltpu.VMEM((512, 256), BF16),
        pltpu.VMEM((512, 128), BF16),
        pltpu.VMEM((24, 256), F32),
        pltpu.VMEM((4 * ng + 16, 128), F32),
        pltpu.VMEM((2 * ng + 16, 128), F32),
    ]
    for extent in ((24, 256), (4 * ng, 128), (2 * ng, 128)):
        shapes += [pltpu.VMEM(extent, F32)] * 5
    for with_density in (True, False):
        halo = buffer_shapes(with_density)
        shapes += halo + halo
        tiles = 10 if with_density else 6
        shapes += [
            pltpu.VMEM((1, 128), F32),
            pltpu.VMEM((ROW, 1, 128), F32),
            pltpu.VMEM((8, 8, 128), F32),
            pltpu.VMEM((8, tiles, 8, 128), F32),
        ]
        copies = n_halo(with_density) + 4
        shapes += [pltpu.SemaphoreType.DMA((copies,)), pltpu.SemaphoreType.DMA((copies,))]
    return shapes


def solution(mesh):
    nf, ns = mesh.shape["fine"], mesh.shape["sub"]

    def body(rhs, density):
        return pl.pallas_call(
            functools.partial(kernel, nf, ns),
            out_shape=(
                jax.ShapeDtypeStruct(rhs.shape, F32),
                jax.ShapeDtypeStruct(rhs.shape, F32),
            ),
            in_specs=[pl.BlockSpec(memory_space=pltpu.VMEM)] * 2,
            out_specs=[pl.BlockSpec(memory_space=pltpu.VMEM)] * 2,
            scratch_shapes=scratch_shapes(nf // ROW),
            compiler_params=pltpu.CompilerParams(
                collective_id=0, has_side_effects=True, vmem_limit_bytes=32 * 1024 * 1024
            ),
        )(rhs, density)

    return jax.shard_map(
        body,
        mesh=mesh,
        in_specs=(P("fine", "sub", None), P("fine", "sub", None)),
        out_specs=(P("fine", "sub", None), P("fine", "sub", None)),
        check_vma=False,
    )
```

```python
import functools

import jax
import jax.numpy as jnp
from jax import lax
from jax.experimental import pallas as pl
from jax.experimental.pallas import tpu as pltpu
from jax.sharding import PartitionSpec as P

DEGREE = 4
CYCLES = 2
MESH = pl.DeviceIdType.MESH
F32 = jnp.float32
BF16 = jnp.bfloat16
ROW = 8
PLANES = (8, 4, 2)
ROWS = (32, 16, 8)


def chebyshev_constants(lower):
    upper = 2.0
    theta = 0.5 * (upper + lower)
    delta = 0.5 * (upper - lower)
    sigma = theta / delta
    ratio = 1.0 / sigma
    steps = []
    for _ in range(DEGREE - 1):
        next_ratio = 1.0 / (2.0 * sigma - ratio)
        steps.append((next_ratio * ratio, 2.0 * next_ratio / delta))
        ratio = next_ratio
    return 1.0 / theta, steps


def iota(shape, dim):
    return lax.broadcasted_iota(jnp.int32, shape, dim)


def div(value, divisor):
    return value >> (divisor.bit_length() - 1)


def mod(value, divisor):
    return value & (divisor - 1)


def quot(value, divisor):
    return lax.div(value, jnp.int32(divisor))


def rest(value, divisor):
    return lax.rem(value, jnp.int32(divisor))


def roll(value, shift, axis):
    return pltpu.roll(value, shift % value.shape[axis], axis)


def invert(value):
    return pltpu.reciprocal(value, full_range=False)


def one_hot(condition):
    return jnp.where(condition, 1.0, 0.0).astype(F32)


def one_hot_matmul(value, matrix):
    count = value.shape[0]
    first = value.astype(BF16).astype(F32)
    rest = value - first
    second = rest.astype(BF16).astype(F32)
    parts = jnp.concatenate([first, second, rest - second], axis=0).astype(BF16)
    product = jnp.dot(parts, matrix, preferred_element_type=F32)
    return product[0:count] + product[count : 2 * count] + product[2 * count :]


def restrict_block(source, first, planes, rows, stride, work):
    field = source[first : first + planes, 0:rows, :]
    field = field.reshape(planes // 2, 2, rows, 128)
    work[0 : planes // 2, 0:rows, :] = field[:, 0] + field[:, 1]
    half = rows // 2
    both = (
        work[0 : planes // 2, pl.ds(0, half, stride=2), :]
        + work[0 : planes // 2, pl.ds(1, half, stride=2), :]
    )
    lane = iota(both.shape, 2)
    even = mod(div(lane, stride), 2) == 0
    other = jnp.where(even, roll(both, -stride, 2), roll(both, stride, 2))
    return (both + other) * 0.125


def fine_coefficients(level, dens, coef, low, high):
    own = ROWS[level]
    scale = 2.0 * 0.25**level
    stride = 2**level
    face_z, face_x, face_y, diagonal, inverse = coef
    shape = (own + 16, 128)

    def compress(value):
        tail = jnp.where(
            iota((8, 128), 0) < 4, value[own : own + 8], value[own + 8 : own + 16]
        )
        return jnp.concatenate([value[0:own], tail], axis=0)

    def plane(p, down):
        here = dens[p + 1]
        above = dens[p + 2]
        lane = iota(shape, 1)
        right = roll(here, -1, 0)
        up = scale * invert(jnp.maximum(here + above, 0.1))
        x_face = scale * invert(jnp.maximum(here + right, 0.1))
        ahead = jnp.where(lane >= 128 - stride, 0.0, roll(here, -stride, 1))
        behind = jnp.where(lane < stride, 0.0, roll(here, stride, 1))
        y_face = scale * invert(jnp.maximum(here + ahead, 0.1))
        y_back = scale * invert(jnp.maximum(here + behind, 0.1))
        diag = up + down + x_face + roll(x_face, 1, 0) + y_face + y_back
        inside = here > 0.0
        face_z[p] = compress(jnp.where(inside & (above > 0.0), up, 0.0))
        face_x[p] = compress(jnp.where(inside & (right > 0.0), x_face, 0.0))
        face_y[p] = compress(jnp.where(lane >= 128 - stride, 0.0, y_face))
        diagonal[p] = compress(diag)
        inverse[p] = compress(invert(diag))
        return up

    lowest = scale * invert(jnp.maximum(dens[low] + dens[low + 1], 0.1))
    lax.fori_loop(low, high, plane, lowest, unroll=True)


def fine_apply(field, p, coef, q, stride):
    face_z, face_x, face_y, diagonal, _ = coef
    here = field[p]
    x_face = face_x[q]
    y_face = face_y[q]
    result = diagonal[q] * here
    result = result - face_z[q] * field[p + 1] - face_z[q - 1] * field[p - 1]
    result = result - x_face * roll(here, -1, 0) - roll(x_face * here, 1, 0)
    result = result - y_face * roll(here, -stride, 1) - roll(y_face * here, stride, 1)
    return result


def fine_smooth(level, source, coef, remain, updates, answer, inner, early):
    planes = PLANES[level] + 8
    stride = 2**level
    inverse = coef[4]
    first, steps = chebyshev_constants(0.5)
    d0, d1, d2 = updates

    def start(p, carry):
        d0[p] = source[p] * inverse[p] * first
        return carry

    def planes_of(shrink):
        low, high = shrink, planes - shrink
        if inner is None:
            return [(low, high)]
        first_in, last_in = inner[0] + shrink, inner[1] - shrink
        return [(first_in, last_in)] if early else [(low, first_in), (last_in, high)]

    for low, high in planes_of(0):
        lax.fori_loop(low, high, start, 0, unroll=True)
    chain = (d0, d1, d2)
    for sweep in range(3):
        old = chain[sweep]
        keep, add = steps[sweep]

        def step(p, carry, sweep=sweep, old=old, keep=keep, add=add):
            left = source[p] if sweep == 0 else remain[p]
            left = left - fine_apply(old, p, coef, p, stride)
            new = keep * old[p] + add * (left * inverse[p])
            if sweep < 2:
                remain[p] = left
                chain[sweep + 1][p] = new
            else:
                answer[p] = d0[p] + d1[p] + d2[p] + new
            return carry

        for low, high in planes_of(sweep + 1):
            lax.fori_loop(low, high, step, 0, unroll=True)


def packed_coefficients(dens, ny, nx, scale):
    rows = dens.shape[0]
    z = iota(dens.shape, 0)
    lane = iota(dens.shape, 1)
    y = mod(lane, ny)
    x = div(lane, ny)
    scale = 2.0 * scale

    def neighbour(shift, axis, outside):
        return jnp.where(outside, 0.0, roll(dens, shift, axis))

    above = neighbour(-1, 0, z == rows - 1)
    below = neighbour(1, 0, z == 0)
    right = neighbour(-ny, 1, x >= nx - 1)
    left = neighbour(ny, 1, x == 0)
    ahead = neighbour(-1, 1, y == ny - 1)
    behind = neighbour(1, 1, y == 0)

    def face(other):
        return scale * invert(jnp.maximum(dens + other, 0.1))

    up, x_face, y_face = face(above), face(right), face(ahead)
    diagonal = up + face(below) + x_face + face(left) + y_face + face(behind)
    inside = dens > 0.0

    def inner(value, other):
        return jnp.where(inside & (other > 0.0), value, 0.0)

    return (
        inner(up, above),
        inner(x_face, right),
        inner(y_face, ahead),
        jnp.where(inside, diagonal, 0.0),
        jnp.where(inside, invert(diagonal), 0.0),
    )


def packed_apply(field, coef, ny):
    face_z, face_x, face_y, diagonal, _ = coef
    result = diagonal * field
    result = result - face_z * roll(field, -1, 0) - roll(face_z * field, 1, 0)
    result = result - face_x * roll(field, -ny, 1) - roll(face_x * field, ny, 1)
    result = result - face_y * roll(field, -1, 1) - roll(face_y * field, 1, 1)
    return result


def packed_smooth(source, coef, ny, lower):
    first, steps = chebyshev_constants(lower)
    inverse = coef[4]
    update = source * inverse * first
    answer = update
    for keep, add in steps:
        source = source - packed_apply(update, coef, ny)
        update = keep * update + add * (source * inverse)
        answer = answer + update
    return answer


PIECES = {
    ("first", 1): {
        "a": (("D0", 8, 0, 5), ("R0", 8, 0, 4), ("D1", 5, 1, 4), ("D2", 5, 3, 2))
        + (("R1", 4, 0, 4), ("R2", 4, 2, 2)),
    },
    ("first", -1): {
        "a": (("D0", 5, 13, 5), ("R0", 4, 12, 4), ("D1", 5, 9, 4), ("D2", 5, 7, 2))
        + (("R1", 4, 8, 4), ("R2", 4, 6, 2)),
    },
    ("first", 3): {"a": (("D2", 6, 0, 1),)},
    ("first", -3): {"a": (("D2", 5, 11, 1),)},
    ("second", 2): {
        "a": (("D1", 8, 0, 1), ("D2", 5, 1, 2), ("R2", 4, 0, 2)),
        "b": (("D2", 5, 1, 2), ("R2", 4, 0, 2)),
    },
    ("second", -2): {
        "a": (("D1", 5, 13, 1), ("D2", 5, 9, 2), ("R2", 4, 8, 2)),
        "b": (("D2", 5, 9, 2), ("R2", 4, 8, 2)),
    },
    ("second", 1): {
        "b": (("D0", 9, 1, 4), ("D1", 5, 1, 4), ("D2", 5, 3, 2))
        + (("R0", 9, 1, 3), ("R1", 4, 0, 4), ("R2", 4, 2, 2)),
    },
    ("second", -1): {
        "b": (("D0", 5, 13, 4), ("D1", 5, 9, 4), ("D2", 5, 7, 2))
        + (("R0", 4, 12, 3), ("R1", 4, 8, 4), ("R2", 4, 6, 2)),
    },
}


def z_messages(with_density):
    result = []
    for (stage, shift), parts in PIECES.items():
        pieces = [
            (part, piece)
            for part, listed in parts.items()
            for piece in listed
            if with_density or piece[0][0] == "R"
        ]
        if pieces:
            result.append((stage, shift, pieces))
    return result


def paired(name, tiles):
    return name[1] != "0" and tiles % 2 == 0


def piece_tiles(part, piece):
    name, _, _, count = piece
    tiles = count * (ROWS[int(name[1])] // 8 if part == "a" else 1)
    return tiles // 2 if paired(name, tiles) else tiles


def x_pieces(with_density):
    result = []
    for level in range(3):
        count = PLANES[level]
        if with_density:
            result.append(("D%d" % level, count, count // 2 if level else count))
        result.append(("R%d" % level, count, (4, 1, 1)[level]))
    return result


def buffer_shapes(with_density):
    tiles = [sum(sent for _, _, sent in x_pieces(with_density))] * 2
    for _, _, pieces in z_messages(with_density):
        tiles.append(sum(piece_tiles(part, piece) for part, piece in pieces))
    return [pltpu.VMEM((count, 8, 128), F32) for count in tiles]


def n_halo(with_density):
    return 2 + len(z_messages(with_density))


def even_lanes(tiles):
    return mod(iota((tiles, 8, 128), 2), 2) == 0


def upper_rows(tiles):
    return iota((tiles, 8, 128), 1) < 4


def pack_lanes(block):
    half = block.shape[0] // 2
    return jnp.where(even_lanes(half), block[0:half], block[half:])


def unpack_lanes(block):
    even = even_lanes(block.shape[0])
    return jnp.concatenate(
        [jnp.where(even, block, roll(block, 1, 2)), jnp.where(even, roll(block, -1, 2), block)],
        axis=0,
    )


def partners_of(place):
    k, s, _, ns = place
    i, y, half = rest(k, ROW), rest(quot(k, ROW), 8), quot(k, 8 * ROW)
    depth, side = [], []
    for delta in (4, 3, 5, 2, 6, 1, 7):
        z = rest(half * ns + s + delta, 2 * ns)
        depth.append(((quot(z, ns) * 8 + y) * ROW + i, rest(z, ns)))
        side.append((delta, ((half * 8 + rest(y + delta, 8)) * ROW + i, s)))
    return depth, side


class Phase:
    def __init__(self, refs, place, with_density, buffers, coarse, send_sem, recv_sem):
        send, recv = buffers
        self.refs = refs
        self.k, self.s, self.nf, self.ns = place
        self.dense = with_density
        self.send, self.recv = send, recv
        self.row, self.row_in, self.depth_in, self.side_in = coarse
        self.send_sem, self.recv_sem = send_sem, recv_sem
        self.started = []
        self.count = 0
        self.z = z_messages(with_density)
        self.copies = {}
        self.i = rest(self.k, ROW)
        self.g = quot(self.k, ROW)
        self.ng = self.nf // ROW
        self.y = rest(self.g, 8)
        self.z_at = quot(self.g, 8) * self.ns + self.s
        self.depth_partners, self.side_partners = partners_of(place)

    def start(self, source, target, k, s, shift=0):
        index = self.count
        self.count += 1
        copy = pltpu.make_async_remote_copy(
            src_ref=source,
            dst_ref=target,
            send_sem=self.send_sem.at[index],
            recv_sem=self.recv_sem.at[index],
            device_id=(k, s),
            device_id_type=MESH,
        )
        self.when(self.has_target(shift), copy.start)
        self.started.append((copy, shift))
        return copy

    def has_target(self, shift):
        if shift == 0:
            return None
        return self.k < self.nf - shift if shift > 0 else self.k >= -shift

    def has_source(self, shift):
        return self.has_target(-shift)

    def when(self, condition, action):
        if condition is None:
            action()
        else:
            pl.when(condition)(action)

    def start_all(self, pairs, total):
        index = self.count
        self.count += 1
        sems = {"send_sem": self.send_sem.at[index], "recv_sem": self.recv_sem.at[index]}
        for source, target, device in pairs:
            pltpu.make_async_remote_copy(
                src_ref=source,
                dst_ref=target,
                device_id=device,
                device_id_type=MESH,
                **sems,
            ).start()
        whole = pltpu.make_async_remote_copy(
            src_ref=total,
            dst_ref=total,
            device_id=pairs[0][2],
            device_id_type=MESH,
            **sems,
        )
        self.started.append((whole, 0))
        return whole

    def pack_x(self):
        for which in (0, 1):
            at = 0
            for name, count, sent in x_pieces(self.dense):
                level = int(name[1])
                lead = 5 if name[0] == "D" else 4
                row = ROWS[level] - 8 if which == 0 else 0
                block = self.refs[name][lead : lead + count, row : row + 8, :]
                if level:
                    block = pack_lanes(block)
                if block.shape[0] > sent:
                    near, far = block[0:sent], roll(block[sent:], 4, 1)
                    upper = upper_rows(sent)
                    if which == 0:
                        block = jnp.where(upper, far, near)
                    else:
                        block = jnp.where(upper, near, far)
                self.send[which][at : at + sent] = block
                at += sent

    def start_x(self):
        up, down = rest(self.s + 1, self.ns), rest(self.s + self.ns - 1, self.ns)
        self.x_copies = [
            self.start(self.send[0], self.recv[0], self.k, up),
            self.start(self.send[1], self.recv[1], self.k, down),
        ]

    def unpack_x(self):
        for copy in self.x_copies:
            copy.wait_recv()
        low_in = jnp.where(self.s > 0, 1.0, 0.0).astype(F32)
        high_in = jnp.where(self.s < self.ns - 1, 1.0, 0.0).astype(F32)
        at = 0
        for name, count, sent in x_pieces(self.dense):
            level = int(name[1])
            own = ROWS[level]
            lead = 5 if name[0] == "D" else 4
            low, high = self.recv[0][at : at + sent], self.recv[1][at : at + sent]
            at += sent
            ref = self.refs[name]
            if name[0] == "D":
                if level:
                    low, high = unpack_lanes(low), unpack_lanes(high)
                ref[lead : lead + count, own : own + 8, :] = high * high_in
                ref[lead : lead + count, own + 8 : own + 16, :] = low * low_in
                continue
            upper = upper_rows(sent)
            block = jnp.where(upper, high, low)
            if sent < (count // 2 if level else count):
                far = roll(jnp.where(upper, low, high), 4, 1)
                block = jnp.concatenate([block, far], axis=0)
            if level:
                block = unpack_lanes(block)
            ref[lead : lead + count, own : own + 8, :] = block

    def pack_z(self, stage):
        for index, (when, _, pieces) in enumerate(self.z):
            if when != stage:
                continue
            at = 0
            for part, piece in pieces:
                name, source, _, count = piece
                ref, own = self.refs[name], ROWS[int(name[1])]
                if part == "a":
                    block = ref[source : source + count, 0:own, :]
                    block = block.reshape(count * own // 8, 8, 128)
                else:
                    block = ref[source : source + count, own : own + 8, :]
                    if name[0] == "D":
                        low = ref[source : source + count, own + 8 : own + 16, :]
                        block = jnp.where(upper_rows(count), block, low)
                if paired(name, block.shape[0]):
                    block = pack_lanes(block)
                self.send[2 + index][at : at + block.shape[0]] = block
                at += block.shape[0]

    def start_z(self, stage):
        for index, (when, shift, _) in enumerate(self.z):
            if when == stage:
                target = rest(self.k + shift + self.nf, self.nf)
                self.copies[index] = self.start(
                    self.send[2 + index], self.recv[2 + index], target, self.s, shift
                )

    def unpack_z(self):
        for index, (_, shift, _) in enumerate(self.z):
            self.when(self.has_source(shift), self.copies[index].wait_recv)
        for index, (_, shift, pieces) in enumerate(self.z):
            inside = self.has_source(shift)
            at = 0
            for part, piece in pieces:
                name, _, target, count = piece
                ref, own = self.refs[name], ROWS[int(name[1])]
                sent = piece_tiles(part, piece)
                block = jnp.where(inside, self.recv[2 + index][at : at + sent], 0.0)
                at += sent
                if sent < (count * own // 8 if part == "a" else count):
                    block = unpack_lanes(block)
                if part == "a":
                    ref[target : target + count, 0:own, :] = block.reshape(count, own, 128)
                else:
                    ref[target : target + count, own : own + 8, :] = block
                    if name[0] == "D":
                        ref[target : target + count, own + 8 : own + 16, :] = block

    def pack_row(self, fields, pair, spread_row):
        for index, field in enumerate(fields):
            pillar = jnp.sum(field, axis=0).reshape(4, 8, 128)
            pair[4 * index : 4 * index + 4, :] = jnp.sum(pillar, axis=1) * 0.125**3
        spread = one_hot_matmul(pair[...], spread_row[...])[0:8]
        mine = div(iota((8, 128), 1), 16) == iota((8, 128), 0)
        row = jnp.sum(jnp.where(mine, spread, 0.0), axis=0, keepdims=True)
        self.row[...] = row
        self.row_in[self.i] = row

    def start_rows(self):
        slot = self.row_in.at[self.i]
        devices = [
            (self.g * ROW + rest(self.i + delta, ROW), self.s) for delta in (4, 3, 5, 2, 6, 1, 7)
        ]
        pairs = [(self.row, slot, device) for device in devices]
        self.row_copies = self.start_all(pairs, self.row_in.at[0 : ROW - 1])

    def start_depth(self):
        self.row_copies.wait_recv()
        line = iota((8, 128), 0)
        tile = jnp.zeros((8, 128), F32)
        for index in range(ROW):
            tile = jnp.where(line == index, self.row_in[index], tile)
        self.depth_in[self.z_at] = tile
        slot = self.depth_in.at[self.z_at]
        pairs = [(slot, slot, device) for device in self.depth_partners]
        self.depth_copies = self.start_all(pairs, self.depth_in.at[0:7])

    def start_sides(self, work, pool):
        self.depth_copies.wait_recv()
        left = iota((8, 128), 1) < 64
        slot = self.side_in.at[self.y]
        wide = []
        for half in range(2):
            tiles = [self.depth_in[4 * half + index] for index in range(4)]
            turned = [roll(tile, 64, 1) for tile in tiles]
            fields = [jnp.where(left, tiles[a], turned[a + 1]) for a in (0, 2)]
            if self.dense:
                fields += [jnp.where(left, turned[a], tiles[a + 1]) for a in (0, 2)]
            for index, field in enumerate(fields):
                slot[2 + len(fields) * half + index] = field
            wide.append(jnp.concatenate(fields, axis=1))
        wide = jnp.concatenate(wide, axis=0)
        sums = one_hot_matmul(wide, pool[0 : wide.shape[1], :])
        work[...] = sums[:, 0:128]
        line = iota((8, 128), 0)
        for half in range(2):
            four = work[pl.ds(8 * half, 4, stride=2), :] + work[pl.ds(8 * half + 1, 4, stride=2), :]
            slot[half, 0:4, :] = four * 0.125
            five = sums[8 * half : 8 * half + 8, 128:256]
            five = five + roll(five, -1, 0)
            five = (five + roll(five, -2, 0)) * (0.125 * 0.125)
            five = jnp.where(mod(line, 2) == 0, five[0:1], five[4:5])
            slot[half, 4:8, :] = five[4:8]
        part = slot.at[0:2]
        far = [(part, part, device) for delta, device in self.side_partners if delta not in (1, 7)]
        self.side_copies = [self.start_all(far, self.side_in.at[0:5, 0:2])]
        near = [(slot, slot, device) for delta, device in self.side_partners if delta in (1, 7)]
        self.side_copies.append(self.start_all(near, self.side_in.at[0:2]))

    def wait_sides(self):
        for copy in self.side_copies:
            copy.wait_recv()

    def group_fields(self, group):
        wrapped = rest(group + self.ng, self.ng)
        y, half = rest(wrapped, 8), quot(wrapped, 8)
        count = 4 if self.dense else 2
        tiles = [self.side_in[y, 2 + half * count + index] for index in range(count)]
        return [
            jnp.concatenate(tiles[at : at + 2], axis=1) for at in range(0, count, 2)
        ]

    def finish(self, first, last):
        for copy, shift in self.started[first:last]:
            self.when(self.has_target(shift), copy.wait_send)


def split_packed(value):
    left = iota(value.shape, 1) < 64
    return jnp.where(left, value, 0.0), jnp.where(left, roll(value, 64, 1), 0.0)


def build_matrices(pool, fan):
    line, lane = iota((128, 128), 0), iota((128, 128), 1)
    for half in range(4):
        x, y = div(line, 16) + 8 * (half % 2), mod(line, 16)
        rows = slice(128 * half, 128 * half + 128)
        home4 = div(x, 2) * 8 + div(y, 2) + 64 * (half // 2)
        home5 = div(x, 4) * 4 + div(y, 4) + 64 * (half // 2)
        pool[rows, 0:128] = one_hot(home4 == lane).astype(BF16)
        pool[rows, 128:256] = one_hot(home5 == lane).astype(BF16)
    three = one_hot(mod(line, 16) == div(lane, 8)).astype(BF16)
    fan[0:128, :] = three
    fan[128:256, :] = three
    fan[256:384, :] = one_hot(mod(line, 8) == div(lane, 16)).astype(BF16)
    fan[384:512, :] = one_hot(mod(line, 4) == div(lane, 32)).astype(BF16)


def kernel(nf, ns, rhs, dens, solution, residual, *scratch):
    scratch = list(scratch)

    def take(count):
        taken = scratch[:count]
        del scratch[:count]
        return taken

    refs = {}
    for name in ("D0", "D1", "D2", "R0", "R1", "R2"):
        (refs[name],) = take(1)
    fine_coef = [take(5) for _ in range(3)]
    remains = take(3)
    updates = [take(3) for _ in range(3)]
    answers = take(3)
    (work, tile_work, pair, sol, spread) = take(5)
    (spread_row, pool, fan, keep3, keep4, keep5) = take(6)
    coarse_coef = [take(5) for _ in range(3)]
    phases = []
    k, s = lax.axis_index("fine"), lax.axis_index("sub")
    for with_density in (True, False):
        count = n_halo(with_density)
        buffers = take(count), take(count)
        coarse = take(4)
        send_sem, recv_sem = take(2)
        phases.append(
            Phase(refs, (k, s, nf, ns), with_density, buffers, coarse, send_sem, recv_sem)
        )
    ng = nf // ROW
    i, g = rest(k, ROW), quot(k, ROW)

    barrier = pltpu.get_barrier_semaphore()
    partners = []
    for shift in (1, 2, 3):
        partners += [(rest(k + shift, nf), s), (rest(k + nf - shift, nf), s)]
    partners += [(g * ROW + rest(i + delta, ROW), s) for delta in range(1, ROW)]
    depth, side = partners_of((k, s, nf, ns))
    partners += depth + [device for _, device in side]
    for partner in partners:
        pl.semaphore_signal(barrier, inc=1, device_id=partner, device_id_type=MESH)

    pair[...] = jnp.zeros((16, 128), F32)

    def restrict_all(name, lead):
        for level in range(2):
            refs[name + str(level + 1)][
                lead : lead + PLANES[level + 1], 0 : ROWS[level + 1], :
            ] = restrict_block(
                refs[name + str(level)], lead, PLANES[level], ROWS[level], 2**level, work
            )

    def coefficients(level, low, high):
        fine_coefficients(level, refs["D" + str(level)], fine_coef[level], low, high)

    def smooth(level, inner=None, early=False):
        fine_smooth(
            level,
            refs["R" + str(level)],
            fine_coef[level],
            remains[level],
            updates[level],
            answers[level],
            inner,
            early,
        )

    line, lane = iota((128, 128), 0), iota((128, 128), 1)
    spread_row[...] = one_hot(div(line, 8) == mod(lane, 16)).astype(BF16)

    for cycle in range(CYCLES):
        phase = phases[cycle]
        if cycle == 0:
            phase.pack_row((rhs[...], dens[...]), pair, spread_row)
            pl.semaphore_wait(barrier, len(partners))
        else:
            phase.pack_row((refs["R0"][4:12, 0:32, :],), pair, spread_row)
        phase.start_rows()
        if cycle == 0:
            refs["R0"][4:12, 0:32, :] = rhs[...]
            refs["D0"][5:13, 0:32, :] = dens[...]
            restrict_all("D", 5)
        restrict_all("R", 4)
        phase.pack_x()
        phase.start_x()
        phase.pack_z("first")
        phase.start_z("first")
        phase.start_depth()
        if cycle == 0:
            build_matrices(pool, fan)
            for level in range(3):
                for name, lead in (("D", 5), ("R", 4)):
                    ref = refs[name + str(level)]
                    planes, rows, _ = ref.shape
                    blank = jnp.zeros((lead, rows, 128), F32)
                    ref[0:lead] = blank
                    ref[planes - lead : planes] = blank
            for ref in (keep4, keep5):
                rows = ref.shape[0]
                ref[0:8, :] = jnp.zeros((8, 128), F32)
                ref[rows - 8 : rows, :] = jnp.zeros((8, 128), F32)
        phase.unpack_x()
        phase.pack_z("second")
        phase.start_z("second")
        phase.start_sides(tile_work, pool)
        inner = (5, 11) if cycle == 0 else (4, 12)
        if cycle == 0:
            coefficients(0, 5, 11)
        else:
            phases[0].finish(0, None)
        smooth(0, inner, True)
        phase.unpack_z()
        for level in (2, 1):
            if cycle == 0:
                coefficients(level, 0, PLANES[level] + 8)
            smooth(level)
        if cycle == 0:
            coefficients(0, 0, 5)
            coefficients(0, 11, 16)
        smooth(0, inner)

        for level in (2, 1):
            rows = ROWS[level]
            planes = PLANES[level] + 2
            value = answers[level][3 : 3 + planes]
            if level == 1:
                value = value + jnp.concatenate(
                    [spread[(p + 1) // 2 : (p + 1) // 2 + 1, 0 : rows + 8, :] for p in range(planes)],
                    axis=0,
                )
            own, ends = value[:, 0:rows, :], value[:, rows : rows + 8, :]
            spread[0:planes, pl.ds(0, rows, stride=2), :] = own
            spread[0:planes, pl.ds(1, rows, stride=2), :] = own
            spread[0:planes, 2 * rows : 2 * rows + 8, :] = jnp.where(
                upper_rows(planes), ends[:, 0:1, :], ends[:, 7:8, :]
            )

        def collect(p, carry, cycle=cycle):
            step = 0.4 * (answers[0][p + 3] + spread[(p + 1) // 2])
            sol[p] = step if cycle == 0 else sol[p] + step
            return carry

        lax.fori_loop(0, PLANES[0] + 2, collect, 0, unroll=True)
        if cycle == 1:
            phase.finish(0, -2)
        phase.wait_sides()

        tiles = [phase.side_in[index % 8, index // 8] for index in range(ng)]
        line = iota((8, 128), 0)
        packed4, packed5 = [], []
        for index in range(0, ng, 2):
            packed4.append(jnp.where(line < 4, tiles[index], roll(tiles[index + 1], 4, 0)))
        for index in range(0, ng, 4):
            first = jnp.where(line < 6, tiles[index], tiles[index + 1])
            second = jnp.where(line < 6, tiles[index + 2], tiles[index + 3])
            packed5.append(jnp.where(line < 4, roll(first, 4, 0), second))
        source4, density4 = split_packed(jnp.concatenate(packed4, axis=0))
        source5, density5 = split_packed(jnp.concatenate(packed5, axis=0))
        if cycle == 0:
            low_in = jnp.where(g > 0, 1.0, 0.0).astype(F32)
            high_in = jnp.where(g < ng - 1, 1.0, 0.0).astype(F32)
            density3 = jnp.concatenate(
                [
                    phase.group_fields(g - 1)[1] * low_in,
                    phase.group_fields(g)[1],
                    phase.group_fields(g + 1)[1] * high_in,
                ],
                axis=0,
            )
            for index, (field, ny) in enumerate(
                ((density3, 16), (density4, 8), (density5, 4))
            ):
                values = packed_coefficients(field, ny, ny, 0.25 ** (3 + index))
                for ref, value in zip(coarse_coef[index], values):
                    ref[...] = value
        coef3, coef4, coef5 = ([ref[...] for ref in refs5] for refs5 in coarse_coef)
        total = jnp.sum(jnp.sum(source5, axis=0, keepdims=True), axis=1, keepdims=True)
        weight = jnp.sum(jnp.sum(coef5[3], axis=0, keepdims=True), axis=1, keepdims=True)
        n4, n5 = 4 * ng, 2 * ng
        keep5[8 : 8 + n5, :] = packed_smooth(source5, coef5, 4, 0.05) + total / weight
        keep4[8 : 8 + n4, :] = packed_smooth(source4, coef4, 8, 0.5)

        source3 = jnp.concatenate(
            [phase.group_fields(g + shift)[0] for shift in (-1, 0, 1)], axis=0
        )
        keep3[...] = packed_smooth(source3, coef3, 16, 0.5)

        row = iota((16, 512), 0)
        lane = iota((16, 512), 1)
        x3 = div(row, 2) + jnp.where(row < 12, 0, -8) + (4 * s + 4)
        inside = (x3 >= 4) & (x3 < 20)
        x_lane = jnp.where(
            lane < 256,
            div(lane, 16),
            jnp.where(lane < 384, div(mod(lane, 128), 8), div(mod(lane, 128), 4)),
        )
        x_row = jnp.where(lane < 256, x3 - 4, jnp.where(lane < 384, div(x3, 2) - 2, div(x3, 4) - 1))
        chosen = (x_lane == x_row) & inside
        picked = []
        for t in range(3):
            parts = jnp.concatenate(
                [
                    keep3[pl.ds(7 + i + t, 1), :],
                    keep4[pl.ds(quot(k + 1 + t, 2) + 7, 1), :],
                    keep5[pl.ds(quot(k + 3 + t, 4) + 7, 1), :],
                ],
                axis=1,
            )
            picked.append(jnp.where(chosen, parts, 0.0))
        lifted = one_hot_matmul(jnp.concatenate(picked, axis=0), fan[...]).reshape(3, 16, 128)

        for t in range(3):
            for tile in range(4):
                spread[t, 8 * tile : 8 * tile + 8, :] = jnp.broadcast_to(
                    lifted[t, 2 * tile : 2 * tile + 1, :], (8, 128)
                )
            spread[t, 32:40, :] = jnp.where(
                iota((8, 128), 0) < 4, lifted[t, 8:9, :], lifted[t, 15:16, :]
            )

        def advance(p, carry):
            sol[p] = sol[p] + 0.4 * spread[(p + 7) // 8]
            return carry

        lax.fori_loop(0, PLANES[0] + 2, advance, 0, unroll=True)

        def defect(p, carry, cycle=cycle):
            applied = fine_apply(sol, p + 1, fine_coef[0], p + 4, 1)
            left = rhs[p] - applied[0:32, :]
            if cycle == 0:
                refs["R0"][p + 4, 0:32, :] = left
            else:
                residual[p] = left
                solution[p] = sol[p + 1, 0:32, :]
            return carry

        lax.fori_loop(0, PLANES[0], defect, 0, unroll=True)

    phases[1].finish(-2, None)


def scratch_shapes(ng):
    shapes = []
    for level in range(3):
        shapes.append(pltpu.VMEM((PLANES[level] + 10, ROWS[level] + 16, 128), F32))
    extents = [(PLANES[level] + 8, ROWS[level] + 8, 128) for level in range(3)]
    shapes += [pltpu.VMEM(extent, F32) for extent in extents]
    for extent in extents:
        shapes += [pltpu.VMEM(extent, F32)] * 5
    shapes += [pltpu.VMEM(extent, F32) for extent in extents]
    for extent in extents:
        shapes += [pltpu.VMEM(extent, F32)] * 3
    shapes += [pltpu.VMEM(extent, F32) for extent in extents]
    shapes += [
        pltpu.VMEM((4, 32, 128), F32),
        pltpu.VMEM((16, 128), F32),
        pltpu.VMEM((16, 128), F32),
        pltpu.VMEM((10, 40, 128), F32),
        pltpu.VMEM((6, 40, 128), F32),
        pltpu.VMEM((128, 128), BF16),
        pltpu.VMEM((512, 256), BF16),
        pltpu.VMEM((512, 128), BF16),
        pltpu.VMEM((24, 256), F32),
        pltpu.VMEM((4 * ng + 16, 128), F32),
        pltpu.VMEM((2 * ng + 16, 128), F32),
    ]
    for extent in ((24, 256), (4 * ng, 128), (2 * ng, 128)):
        shapes += [pltpu.VMEM(extent, F32)] * 5
    for with_density in (True, False):
        halo = buffer_shapes(with_density)
        shapes += halo + halo
        tiles = 10 if with_density else 6
        shapes += [
            pltpu.VMEM((1, 128), F32),
            pltpu.VMEM((ROW, 1, 128), F32),
            pltpu.VMEM((8, 8, 128), F32),
            pltpu.VMEM((8, tiles, 8, 128), F32),
        ]
        copies = n_halo(with_density) + 4
        shapes += [pltpu.SemaphoreType.DMA((copies,)), pltpu.SemaphoreType.DMA((copies,))]
    return shapes


def solution(mesh):
    nf, ns = mesh.shape["fine"], mesh.shape["sub"]

    def body(rhs, density):
        return pl.pallas_call(
            functools.partial(kernel, nf, ns),
            out_shape=(
                jax.ShapeDtypeStruct(rhs.shape, F32),
                jax.ShapeDtypeStruct(rhs.shape, F32),
            ),
            in_specs=[pl.BlockSpec(memory_space=pltpu.VMEM)] * 2,
            out_specs=[pl.BlockSpec(memory_space=pltpu.VMEM)] * 2,
            scratch_shapes=scratch_shapes(nf // ROW),
            compiler_params=pltpu.CompilerParams(
                collective_id=0, has_side_effects=True, vmem_limit_bytes=32 * 1024 * 1024
            ),
        )(rhs, density)

    return jax.shard_map(
        body,
        mesh=mesh,
        in_specs=(P("fine", "sub", None), P("fine", "sub", None)),
        out_specs=(P("fine", "sub", None), P("fine", "sub", None)),
        check_vma=False,
    )
```

```python
import functools

import jax
import jax.numpy as jnp
from jax import lax
from jax.experimental import pallas as pl
from jax.experimental.pallas import tpu as pltpu
from jax.sharding import PartitionSpec as P

DEGREE = 4
CYCLES = 2
MESH = pl.DeviceIdType.MESH
F32 = jnp.float32
BF16 = jnp.bfloat16
ROW = 8
PLANES = (8, 4, 2)
ROWS = (32, 16, 8)


def chebyshev_constants(lower):
    upper = 2.0
    theta = 0.5 * (upper + lower)
    delta = 0.5 * (upper - lower)
    sigma = theta / delta
    ratio = 1.0 / sigma
    steps = []
    for _ in range(DEGREE - 1):
        next_ratio = 1.0 / (2.0 * sigma - ratio)
        steps.append((next_ratio * ratio, 2.0 * next_ratio / delta))
        ratio = next_ratio
    return 1.0 / theta, steps


def iota(shape, dim):
    return lax.broadcasted_iota(jnp.int32, shape, dim)


def div(value, divisor):
    return value >> (divisor.bit_length() - 1)


def mod(value, divisor):
    return value & (divisor - 1)


def quot(value, divisor):
    return lax.div(value, jnp.int32(divisor))


def rest(value, divisor):
    return lax.rem(value, jnp.int32(divisor))


def roll(value, shift, axis):
    return pltpu.roll(value, shift % value.shape[axis], axis)


def invert(value):
    return pltpu.reciprocal(value, full_range=False)


def one_hot(condition):
    return jnp.where(condition, 1.0, 0.0).astype(F32)


def one_hot_matmul(value, matrix):
    count = value.shape[0]
    first = value.astype(BF16).astype(F32)
    rest = value - first
    second = rest.astype(BF16).astype(F32)
    parts = jnp.concatenate([first, second, rest - second], axis=0).astype(BF16)
    product = jnp.dot(parts, matrix, preferred_element_type=F32)
    return product[0:count] + product[count : 2 * count] + product[2 * count :]


def restrict_block(source, first, planes, rows, stride, work):
    field = source[first : first + planes, 0:rows, :]
    field = field.reshape(planes // 2, 2, rows, 128)
    work[0 : planes // 2, 0:rows, :] = field[:, 0] + field[:, 1]
    half = rows // 2
    both = (
        work[0 : planes // 2, pl.ds(0, half, stride=2), :]
        + work[0 : planes // 2, pl.ds(1, half, stride=2), :]
    )
    lane = iota(both.shape, 2)
    even = mod(div(lane, stride), 2) == 0
    other = jnp.where(even, roll(both, -stride, 2), roll(both, stride, 2))
    return (both + other) * 0.125


def fine_coefficients(level, dens, coef, low, high):
    own = ROWS[level]
    scale = 2.0 * 0.25**level
    stride = 2**level
    face_z, face_x, face_y, diagonal, inverse = coef
    shape = (own + 16, 128)

    def compress(value):
        tail = jnp.where(
            iota((8, 128), 0) < 4, value[own : own + 8], value[own + 8 : own + 16]
        )
        return jnp.concatenate([value[0:own], tail], axis=0)

    def plane(p, down):
        here = dens[p + 1]
        above = dens[p + 2]
        lane = iota(shape, 1)
        right = roll(here, -1, 0)
        up = scale * invert(jnp.maximum(here + above, 0.1))
        x_face = scale * invert(jnp.maximum(here + right, 0.1))
        ahead = jnp.where(lane >= 128 - stride, 0.0, roll(here, -stride, 1))
        behind = jnp.where(lane < stride, 0.0, roll(here, stride, 1))
        y_face = scale * invert(jnp.maximum(here + ahead, 0.1))
        y_back = scale * invert(jnp.maximum(here + behind, 0.1))
        diag = up + down + x_face + roll(x_face, 1, 0) + y_face + y_back
        inside = here > 0.0
        face_z[p] = compress(jnp.where(inside & (above > 0.0), up, 0.0))
        face_x[p] = compress(jnp.where(inside & (right > 0.0), x_face, 0.0))
        face_y[p] = compress(jnp.where(lane >= 128 - stride, 0.0, y_face))
        diagonal[p] = compress(diag)
        inverse[p] = compress(invert(diag))
        return up

    lowest = scale * invert(jnp.maximum(dens[low] + dens[low + 1], 0.1))
    lax.fori_loop(low, high, plane, lowest, unroll=True)


def fine_apply(field, p, coef, q, stride):
    face_z, face_x, face_y, diagonal, _ = coef
    here = field[p]
    x_face = face_x[q]
    y_face = face_y[q]
    result = diagonal[q] * here
    result = result - face_z[q] * field[p + 1] - face_z[q - 1] * field[p - 1]
    result = result - x_face * roll(here, -1, 0) - roll(x_face * here, 1, 0)
    result = result - y_face * roll(here, -stride, 1) - roll(y_face * here, stride, 1)
    return result


def fine_smooth(level, source, coef, remain, updates, answer, inner, early):
    planes = PLANES[level] + 8
    stride = 2**level
    inverse = coef[4]
    first, steps = chebyshev_constants(0.5)
    d0, d1, d2 = updates

    def start(p, carry):
        d0[p] = source[p] * inverse[p] * first
        return carry

    def planes_of(shrink):
        low, high = shrink, planes - shrink
        if inner is None:
            return [(low, high)]
        first_in, last_in = inner[0] + shrink, inner[1] - shrink
        return [(first_in, last_in)] if early else [(low, first_in), (last_in, high)]

    for low, high in planes_of(0):
        lax.fori_loop(low, high, start, 0, unroll=True)
    chain = (d0, d1, d2)
    for sweep in range(3):
        old = chain[sweep]
        keep, add = steps[sweep]

        def step(p, carry, sweep=sweep, old=old, keep=keep, add=add):
            left = source[p] if sweep == 0 else remain[p]
            left = left - fine_apply(old, p, coef, p, stride)
            new = keep * old[p] + add * (left * inverse[p])
            if sweep < 2:
                remain[p] = left
                chain[sweep + 1][p] = new
            else:
                answer[p] = d0[p] + d1[p] + d2[p] + new
            return carry

        for low, high in planes_of(sweep + 1):
            lax.fori_loop(low, high, step, 0, unroll=True)


def packed_coefficients(dens, ny, nx, scale):
    rows = dens.shape[0]
    z = iota(dens.shape, 0)
    lane = iota(dens.shape, 1)
    y = mod(lane, ny)
    x = div(lane, ny)
    scale = 2.0 * scale

    def neighbour(shift, axis, outside):
        return jnp.where(outside, 0.0, roll(dens, shift, axis))

    above = neighbour(-1, 0, z == rows - 1)
    below = neighbour(1, 0, z == 0)
    right = neighbour(-ny, 1, x >= nx - 1)
    left = neighbour(ny, 1, x == 0)
    ahead = neighbour(-1, 1, y == ny - 1)
    behind = neighbour(1, 1, y == 0)

    def face(other):
        return scale * invert(jnp.maximum(dens + other, 0.1))

    up, x_face, y_face = face(above), face(right), face(ahead)
    diagonal = up + face(below) + x_face + face(left) + y_face + face(behind)
    inside = dens > 0.0

    def inner(value, other):
        return jnp.where(inside & (other > 0.0), value, 0.0)

    return (
        inner(up, above),
        inner(x_face, right),
        inner(y_face, ahead),
        jnp.where(inside, diagonal, 0.0),
        jnp.where(inside, invert(diagonal), 0.0),
    )


def packed_apply(field, coef, ny):
    face_z, face_x, face_y, diagonal, _ = coef
    result = diagonal * field
    result = result - face_z * roll(field, -1, 0) - roll(face_z * field, 1, 0)
    result = result - face_x * roll(field, -ny, 1) - roll(face_x * field, ny, 1)
    result = result - face_y * roll(field, -1, 1) - roll(face_y * field, 1, 1)
    return result


def packed_smooth(source, coef, ny, lower):
    first, steps = chebyshev_constants(lower)
    inverse = coef[4]
    update = source * inverse * first
    answer = update
    for keep, add in steps:
        source = source - packed_apply(update, coef, ny)
        update = keep * update + add * (source * inverse)
        answer = answer + update
    return answer


PIECES = {
    ("first", 1): {
        "a": (("D0", 8, 0, 5), ("R0", 8, 0, 4), ("D1", 5, 1, 4), ("D2", 5, 3, 2))
        + (("R1", 4, 0, 4), ("R2", 4, 2, 2)),
    },
    ("first", -1): {
        "a": (("D0", 5, 13, 5), ("R0", 4, 12, 4), ("D1", 5, 9, 4), ("D2", 5, 7, 2))
        + (("R1", 4, 8, 4), ("R2", 4, 6, 2)),
    },
    ("first", 3): {"a": (("D2", 6, 0, 1),)},
    ("first", -3): {"a": (("D2", 5, 11, 1),)},
    ("second", 2): {
        "a": (("D1", 8, 0, 1), ("D2", 5, 1, 2), ("R2", 4, 0, 2)),
        "b": (("D2", 5, 1, 2), ("R2", 4, 0, 2)),
    },
    ("second", -2): {
        "a": (("D1", 5, 13, 1), ("D2", 5, 9, 2), ("R2", 4, 8, 2)),
        "b": (("D2", 5, 9, 2), ("R2", 4, 8, 2)),
    },
    ("second", 1): {
        "b": (("D0", 9, 1, 4), ("D1", 5, 1, 4), ("D2", 5, 3, 2))
        + (("R0", 9, 1, 3), ("R1", 4, 0, 4), ("R2", 4, 2, 2)),
    },
    ("second", -1): {
        "b": (("D0", 5, 13, 4), ("D1", 5, 9, 4), ("D2", 5, 7, 2))
        + (("R0", 4, 12, 3), ("R1", 4, 8, 4), ("R2", 4, 6, 2)),
    },
}


def z_messages(with_density):
    result = []
    for (stage, shift), parts in PIECES.items():
        pieces = [
            (part, piece)
            for part, listed in parts.items()
            for piece in listed
            if with_density or piece[0][0] == "R"
        ]
        if pieces:
            result.append((stage, shift, pieces))
    return result


def paired(name, tiles):
    return name[1] != "0" and tiles % 2 == 0


def piece_tiles(part, piece):
    name, _, _, count = piece
    tiles = count * (ROWS[int(name[1])] // 8 if part == "a" else 1)
    return tiles // 2 if paired(name, tiles) else tiles


def x_pieces(with_density):
    result = []
    for level in range(3):
        count = PLANES[level]
        if with_density:
            result.append(("D%d" % level, count, count // 2 if level else count))
        result.append(("R%d" % level, count, (4, 1, 1)[level]))
    return result


def buffer_shapes(with_density):
    tiles = [sum(sent for _, _, sent in x_pieces(with_density))] * 2
    for _, _, pieces in z_messages(with_density):
        tiles.append(sum(piece_tiles(part, piece) for part, piece in pieces))
    return [pltpu.VMEM((count, 8, 128), F32) for count in tiles]


def n_halo(with_density):
    return 2 + len(z_messages(with_density))


def even_lanes(tiles):
    return mod(iota((tiles, 8, 128), 2), 2) == 0


def upper_rows(tiles):
    return iota((tiles, 8, 128), 1) < 4


def pack_lanes(block):
    half = block.shape[0] // 2
    return jnp.where(even_lanes(half), block[0:half], block[half:])


def unpack_lanes(block):
    even = even_lanes(block.shape[0])
    return jnp.concatenate(
        [jnp.where(even, block, roll(block, 1, 2)), jnp.where(even, roll(block, -1, 2), block)],
        axis=0,
    )


def partners_of(place):
    k, s, _, ns = place
    i, y, half = rest(k, ROW), rest(quot(k, ROW), 8), quot(k, 8 * ROW)
    depth, side = [], []
    for delta in (4, 3, 5, 2, 6, 1, 7):
        z = rest(half * ns + s + delta, 2 * ns)
        depth.append(((quot(z, ns) * 8 + y) * ROW + i, rest(z, ns)))
        side.append((delta, ((half * 8 + rest(y + delta, 8)) * ROW + i, s)))
    return depth, side


class Phase:
    def __init__(self, refs, place, with_density, buffers, coarse, send_sem, recv_sem):
        send, recv = buffers
        self.refs = refs
        self.k, self.s, self.nf, self.ns = place
        self.dense = with_density
        self.send, self.recv = send, recv
        self.row, self.row_in, self.depth_in, self.side_in = coarse
        self.send_sem, self.recv_sem = send_sem, recv_sem
        self.started = []
        self.count = 0
        self.z = z_messages(with_density)
        self.copies = {}
        self.i = rest(self.k, ROW)
        self.g = quot(self.k, ROW)
        self.ng = self.nf // ROW
        self.y = rest(self.g, 8)
        self.z_at = quot(self.g, 8) * self.ns + self.s
        self.depth_partners, self.side_partners = partners_of(place)

    def start(self, source, target, k, s, shift=0):
        index = self.count
        self.count += 1
        copy = pltpu.make_async_remote_copy(
            src_ref=source,
            dst_ref=target,
            send_sem=self.send_sem.at[index],
            recv_sem=self.recv_sem.at[index],
            device_id=(k, s),
            device_id_type=MESH,
        )
        self.when(self.has_target(shift), copy.start)
        self.started.append((copy, shift))
        return copy

    def has_target(self, shift):
        if shift == 0:
            return None
        return self.k < self.nf - shift if shift > 0 else self.k >= -shift

    def has_source(self, shift):
        return self.has_target(-shift)

    def when(self, condition, action):
        if condition is None:
            action()
        else:
            pl.when(condition)(action)

    def start_all(self, pairs, total):
        index = self.count
        self.count += 1
        sems = {"send_sem": self.send_sem.at[index], "recv_sem": self.recv_sem.at[index]}
        for source, target, device in pairs:
            pltpu.make_async_remote_copy(
                src_ref=source,
                dst_ref=target,
                device_id=device,
                device_id_type=MESH,
                **sems,
            ).start()
        whole = pltpu.make_async_remote_copy(
            src_ref=total,
            dst_ref=total,
            device_id=pairs[0][2],
            device_id_type=MESH,
            **sems,
        )
        self.started.append((whole, 0))
        return whole

    def pack_x(self):
        for which in (0, 1):
            at = 0
            for name, count, sent in x_pieces(self.dense):
                level = int(name[1])
                lead = 5 if name[0] == "D" else 4
                row = ROWS[level] - 8 if which == 0 else 0
                block = self.refs[name][lead : lead + count, row : row + 8, :]
                if level:
                    block = pack_lanes(block)
                if block.shape[0] > sent:
                    near, far = block[0:sent], roll(block[sent:], 4, 1)
                    upper = upper_rows(sent)
                    if which == 0:
                        block = jnp.where(upper, far, near)
                    else:
                        block = jnp.where(upper, near, far)
                self.send[which][at : at + sent] = block
                at += sent

    def start_x(self):
        up, down = rest(self.s + 1, self.ns), rest(self.s + self.ns - 1, self.ns)
        self.x_copies = [
            self.start(self.send[0], self.recv[0], self.k, up),
            self.start(self.send[1], self.recv[1], self.k, down),
        ]

    def unpack_x(self):
        for copy in self.x_copies:
            copy.wait_recv()
        low_in = jnp.where(self.s > 0, 1.0, 0.0).astype(F32)
        high_in = jnp.where(self.s < self.ns - 1, 1.0, 0.0).astype(F32)
        at = 0
        for name, count, sent in x_pieces(self.dense):
            level = int(name[1])
            own = ROWS[level]
            lead = 5 if name[0] == "D" else 4
            low, high = self.recv[0][at : at + sent], self.recv[1][at : at + sent]
            at += sent
            ref = self.refs[name]
            if name[0] == "D":
                if level:
                    low, high = unpack_lanes(low), unpack_lanes(high)
                ref[lead : lead + count, own : own + 8, :] = high * high_in
                ref[lead : lead + count, own + 8 : own + 16, :] = low * low_in
                continue
            upper = upper_rows(sent)
            block = jnp.where(upper, high, low)
            if sent < (count // 2 if level else count):
                far = roll(jnp.where(upper, low, high), 4, 1)
                block = jnp.concatenate([block, far], axis=0)
            if level:
                block = unpack_lanes(block)
            ref[lead : lead + count, own : own + 8, :] = block

    def pack_z(self, stage):
        for index, (when, _, pieces) in enumerate(self.z):
            if when != stage:
                continue
            at = 0
            for part, piece in pieces:
                name, source, _, count = piece
                ref, own = self.refs[name], ROWS[int(name[1])]
                if part == "a":
                    block = ref[source : source + count, 0:own, :]
                    block = block.reshape(count * own // 8, 8, 128)
                else:
                    block = ref[source : source + count, own : own + 8, :]
                    if name[0] == "D":
                        low = ref[source : source + count, own + 8 : own + 16, :]
                        block = jnp.where(upper_rows(count), block, low)
                if paired(name, block.shape[0]):
                    block = pack_lanes(block)
                self.send[2 + index][at : at + block.shape[0]] = block
                at += block.shape[0]

    def start_z(self, stage):
        for index, (when, shift, _) in enumerate(self.z):
            if when == stage:
                target = rest(self.k + shift + self.nf, self.nf)
                self.copies[index] = self.start(
                    self.send[2 + index], self.recv[2 + index], target, self.s, shift
                )

    def unpack_z(self):
        for index, (_, shift, _) in enumerate(self.z):
            self.when(self.has_source(shift), self.copies[index].wait_recv)
        for index, (_, shift, pieces) in enumerate(self.z):
            inside = self.has_source(shift)
            at = 0
            for part, piece in pieces:
                name, _, target, count = piece
                ref, own = self.refs[name], ROWS[int(name[1])]
                sent = piece_tiles(part, piece)
                block = jnp.where(inside, self.recv[2 + index][at : at + sent], 0.0)
                at += sent
                if sent < (count * own // 8 if part == "a" else count):
                    block = unpack_lanes(block)
                if part == "a":
                    ref[target : target + count, 0:own, :] = block.reshape(count, own, 128)
                else:
                    ref[target : target + count, own : own + 8, :] = block
                    if name[0] == "D":
                        ref[target : target + count, own + 8 : own + 16, :] = block

    def pack_row(self, fields, pair, spread_row):
        for index, field in enumerate(fields):
            pillar = jnp.sum(field, axis=0).reshape(4, 8, 128)
            pair[4 * index : 4 * index + 4, :] = jnp.sum(pillar, axis=1) * 0.125**3
        spread = one_hot_matmul(pair[...], spread_row[...])[0:8]
        mine = div(iota((8, 128), 1), 16) == iota((8, 128), 0)
        row = jnp.sum(jnp.where(mine, spread, 0.0), axis=0, keepdims=True)
        self.row[...] = row
        self.row_in[self.i] = row

    def start_rows(self):
        slot = self.row_in.at[self.i]
        devices = [
            (self.g * ROW + rest(self.i + delta, ROW), self.s) for delta in (4, 3, 5, 2, 6, 1, 7)
        ]
        pairs = [(self.row, slot, device) for device in devices]
        self.row_copies = self.start_all(pairs, self.row_in.at[0 : ROW - 1])

    def start_depth(self):
        self.row_copies.wait_recv()
        line = iota((8, 128), 0)
        tile = jnp.zeros((8, 128), F32)
        for index in range(ROW):
            tile = jnp.where(line == index, self.row_in[index], tile)
        self.depth_in[self.z_at] = tile
        slot = self.depth_in.at[self.z_at]
        pairs = [(slot, slot, device) for device in self.depth_partners]
        self.depth_copies = self.start_all(pairs, self.depth_in.at[0:7])

    def start_sides(self, work, pool):
        self.depth_copies.wait_recv()
        left = iota((8, 128), 1) < 64
        slot = self.side_in.at[self.y]
        wide = []
        for half in range(2):
            tiles = [self.depth_in[4 * half + index] for index in range(4)]
            turned = [roll(tile, 64, 1) for tile in tiles]
            fields = [jnp.where(left, tiles[a], turned[a + 1]) for a in (0, 2)]
            if self.dense:
                fields += [jnp.where(left, turned[a], tiles[a + 1]) for a in (0, 2)]
            for index, field in enumerate(fields):
                slot[2 + len(fields) * half + index] = field
            wide.append(jnp.concatenate(fields, axis=1))
        wide = jnp.concatenate(wide, axis=0)
        sums = one_hot_matmul(wide, pool[0 : wide.shape[1], :])
        work[...] = sums[:, 0:128]
        line = iota((8, 128), 0)
        for half in range(2):
            four = work[pl.ds(8 * half, 4, stride=2), :] + work[pl.ds(8 * half + 1, 4, stride=2), :]
            slot[half, 0:4, :] = four * 0.125
            five = sums[8 * half : 8 * half + 8, 128:256]
            five = five + roll(five, -1, 0)
            five = (five + roll(five, -2, 0)) * (0.125 * 0.125)
            five = jnp.where(mod(line, 2) == 0, five[0:1], five[4:5])
            slot[half, 4:8, :] = five[4:8]
        part = slot.at[0:2]
        far = [(part, part, device) for delta, device in self.side_partners if delta not in (1, 7)]
        self.side_copies = [self.start_all(far, self.side_in.at[0:5, 0:2])]
        near = [(slot, slot, device) for delta, device in self.side_partners if delta in (1, 7)]
        self.side_copies.append(self.start_all(near, self.side_in.at[0:2]))

    def wait_sides(self):
        for copy in self.side_copies:
            copy.wait_recv()

    def group_fields(self, group):
        wrapped = rest(group + self.ng, self.ng)
        y, half = rest(wrapped, 8), quot(wrapped, 8)
        count = 4 if self.dense else 2
        tiles = [self.side_in[y, 2 + half * count + index] for index in range(count)]
        return [
            jnp.concatenate(tiles[at : at + 2], axis=1) for at in range(0, count, 2)
        ]

    def finish(self, first, last):
        for copy, shift in self.started[first:last]:
            self.when(self.has_target(shift), copy.wait_send)


def split_packed(value):
    left = iota(value.shape, 1) < 64
    return jnp.where(left, value, 0.0), jnp.where(left, roll(value, 64, 1), 0.0)


def build_matrices(pool, fan):
    line, lane = iota((128, 128), 0), iota((128, 128), 1)
    for half in range(4):
        x, y = div(line, 16) + 8 * (half % 2), mod(line, 16)
        rows = slice(128 * half, 128 * half + 128)
        home4 = div(x, 2) * 8 + div(y, 2) + 64 * (half // 2)
        home5 = div(x, 4) * 4 + div(y, 4) + 64 * (half // 2)
        pool[rows, 0:128] = one_hot(home4 == lane).astype(BF16)
        pool[rows, 128:256] = one_hot(home5 == lane).astype(BF16)
    three = one_hot(mod(line, 16) == div(lane, 8)).astype(BF16)
    fan[0:128, :] = three
    fan[128:256, :] = three
    fan[256:384, :] = one_hot(mod(line, 8) == div(lane, 16)).astype(BF16)
    fan[384:512, :] = one_hot(mod(line, 4) == div(lane, 32)).astype(BF16)


def kernel(nf, ns, rhs, dens, solution, residual, *scratch):
    scratch = list(scratch)

    def take(count):
        taken = scratch[:count]
        del scratch[:count]
        return taken

    refs = {}
    for name in ("D0", "D1", "D2", "R0", "R1", "R2"):
        (refs[name],) = take(1)
    fine_coef = [take(5) for _ in range(3)]
    remains = take(3)
    updates = [take(3) for _ in range(3)]
    answers = take(3)
    (work, tile_work, pair, sol, spread) = take(5)
    (spread_row, pool, fan, keep3, keep4, keep5) = take(6)
    coarse_coef = [take(5) for _ in range(3)]
    phases = []
    k, s = lax.axis_index("fine"), lax.axis_index("sub")
    for with_density in (True, False):
        count = n_halo(with_density)
        buffers = take(count), take(count)
        coarse = take(4)
        send_sem, recv_sem = take(2)
        phases.append(
            Phase(refs, (k, s, nf, ns), with_density, buffers, coarse, send_sem, recv_sem)
        )
    ng = nf // ROW
    i, g = rest(k, ROW), quot(k, ROW)

    barrier = pltpu.get_barrier_semaphore()
    partners = []
    for shift in (1, 2, 3):
        partners += [(rest(k + shift, nf), s), (rest(k + nf - shift, nf), s)]
    partners += [(g * ROW + rest(i + delta, ROW), s) for delta in range(1, ROW)]
    depth, side = partners_of((k, s, nf, ns))
    partners += depth + [device for _, device in side]
    for partner in partners:
        pl.semaphore_signal(barrier, inc=1, device_id=partner, device_id_type=MESH)

    pair[...] = jnp.zeros((16, 128), F32)

    def restrict_all(name, lead):
        for level in range(2):
            refs[name + str(level + 1)][
                lead : lead + PLANES[level + 1], 0 : ROWS[level + 1], :
            ] = restrict_block(
                refs[name + str(level)], lead, PLANES[level], ROWS[level], 2**level, work
            )

    def coefficients(level, low, high):
        fine_coefficients(level, refs["D" + str(level)], fine_coef[level], low, high)

    def smooth(level, inner=None, early=False):
        fine_smooth(
            level,
            refs["R" + str(level)],
            fine_coef[level],
            remains[level],
            updates[level],
            answers[level],
            inner,
            early,
        )

    line, lane = iota((128, 128), 0), iota((128, 128), 1)
    spread_row[...] = one_hot(div(line, 8) == mod(lane, 16)).astype(BF16)

    for cycle in range(CYCLES):
        phase = phases[cycle]
        if cycle == 0:
            phase.pack_row((rhs[...], dens[...]), pair, spread_row)
            pl.semaphore_wait(barrier, len(partners))
        else:
            phase.pack_row((refs["R0"][4:12, 0:32, :],), pair, spread_row)
        phase.start_rows()
        if cycle == 0:
            refs["R0"][4:12, 0:32, :] = rhs[...]
            refs["D0"][5:13, 0:32, :] = dens[...]
            restrict_all("D", 5)
        restrict_all("R", 4)
        phase.pack_x()
        phase.start_x()
        phase.pack_z("first")
        phase.start_z("first")
        phase.start_depth()
        if cycle == 0:
            build_matrices(pool, fan)
            for level in range(3):
                for name, lead in (("D", 5), ("R", 4)):
                    ref = refs[name + str(level)]
                    planes, rows, _ = ref.shape
                    blank = jnp.zeros((lead, rows, 128), F32)
                    ref[0:lead] = blank
                    ref[planes - lead : planes] = blank
            for ref in (keep4, keep5):
                rows = ref.shape[0]
                ref[0:8, :] = jnp.zeros((8, 128), F32)
                ref[rows - 8 : rows, :] = jnp.zeros((8, 128), F32)
        phase.start_sides(tile_work, pool)
        phase.unpack_x()
        phase.pack_z("second")
        phase.start_z("second")
        inner = (5, 11) if cycle == 0 else (4, 12)
        if cycle == 0:
            coefficients(0, 5, 11)
        else:
            phases[0].finish(0, None)
        smooth(0, inner, True)
        phase.unpack_z()
        for level in (2, 1):
            if cycle == 0:
                coefficients(level, 0, PLANES[level] + 8)
            smooth(level)
        if cycle == 0:
            coefficients(0, 0, 5)
            coefficients(0, 11, 16)
        smooth(0, inner)

        for level in (2, 1):
            rows = ROWS[level]
            planes = PLANES[level] + 2
            value = answers[level][3 : 3 + planes]
            if level == 1:
                value = value + jnp.concatenate(
                    [spread[(p + 1) // 2 : (p + 1) // 2 + 1, 0 : rows + 8, :] for p in range(planes)],
                    axis=0,
                )
            own, ends = value[:, 0:rows, :], value[:, rows : rows + 8, :]
            spread[0:planes, pl.ds(0, rows, stride=2), :] = own
            spread[0:planes, pl.ds(1, rows, stride=2), :] = own
            spread[0:planes, 2 * rows : 2 * rows + 8, :] = jnp.where(
                upper_rows(planes), ends[:, 0:1, :], ends[:, 7:8, :]
            )

        def collect(p, carry, cycle=cycle):
            step = 0.4 * (answers[0][p + 3] + spread[(p + 1) // 2])
            sol[p] = step if cycle == 0 else sol[p] + step
            return carry

        lax.fori_loop(0, PLANES[0] + 2, collect, 0, unroll=True)
        if cycle == 1:
            phase.finish(0, -2)
        phase.wait_sides()

        tiles = [phase.side_in[index % 8, index // 8] for index in range(ng)]
        line = iota((8, 128), 0)
        packed4, packed5 = [], []
        for index in range(0, ng, 2):
            packed4.append(jnp.where(line < 4, tiles[index], roll(tiles[index + 1], 4, 0)))
        for index in range(0, ng, 4):
            first = jnp.where(line < 6, tiles[index], tiles[index + 1])
            second = jnp.where(line < 6, tiles[index + 2], tiles[index + 3])
            packed5.append(jnp.where(line < 4, roll(first, 4, 0), second))
        source4, density4 = split_packed(jnp.concatenate(packed4, axis=0))
        source5, density5 = split_packed(jnp.concatenate(packed5, axis=0))
        if cycle == 0:
            low_in = jnp.where(g > 0, 1.0, 0.0).astype(F32)
            high_in = jnp.where(g < ng - 1, 1.0, 0.0).astype(F32)
            density3 = jnp.concatenate(
                [
                    phase.group_fields(g - 1)[1] * low_in,
                    phase.group_fields(g)[1],
                    phase.group_fields(g + 1)[1] * high_in,
                ],
                axis=0,
            )
            for index, (field, ny) in enumerate(
                ((density3, 16), (density4, 8), (density5, 4))
            ):
                values = packed_coefficients(field, ny, ny, 0.25 ** (3 + index))
                for ref, value in zip(coarse_coef[index], values):
                    ref[...] = value
        coef3, coef4, coef5 = ([ref[...] for ref in refs5] for refs5 in coarse_coef)
        total = jnp.sum(jnp.sum(source5, axis=0, keepdims=True), axis=1, keepdims=True)
        weight = jnp.sum(jnp.sum(coef5[3], axis=0, keepdims=True), axis=1, keepdims=True)
        n4, n5 = 4 * ng, 2 * ng
        keep5[8 : 8 + n5, :] = packed_smooth(source5, coef5, 4, 0.05) + total / weight
        keep4[8 : 8 + n4, :] = packed_smooth(source4, coef4, 8, 0.5)

        source3 = jnp.concatenate(
            [phase.group_fields(g + shift)[0] for shift in (-1, 0, 1)], axis=0
        )
        keep3[...] = packed_smooth(source3, coef3, 16, 0.5)

        row = iota((16, 512), 0)
        lane = iota((16, 512), 1)
        x3 = div(row, 2) + jnp.where(row < 12, 0, -8) + (4 * s + 4)
        inside = (x3 >= 4) & (x3 < 20)
        x_lane = jnp.where(
            lane < 256,
            div(lane, 16),
            jnp.where(lane < 384, div(mod(lane, 128), 8), div(mod(lane, 128), 4)),
        )
        x_row = jnp.where(lane < 256, x3 - 4, jnp.where(lane < 384, div(x3, 2) - 2, div(x3, 4) - 1))
        chosen = (x_lane == x_row) & inside
        picked = []
        for t in range(3):
            parts = jnp.concatenate(
                [
                    keep3[pl.ds(7 + i + t, 1), :],
                    keep4[pl.ds(quot(k + 1 + t, 2) + 7, 1), :],
                    keep5[pl.ds(quot(k + 3 + t, 4) + 7, 1), :],
                ],
                axis=1,
            )
            picked.append(jnp.where(chosen, parts, 0.0))
        lifted = one_hot_matmul(jnp.concatenate(picked, axis=0), fan[...]).reshape(3, 16, 128)

        for t in range(3):
            for tile in range(4):
                spread[t, 8 * tile : 8 * tile + 8, :] = jnp.broadcast_to(
                    lifted[t, 2 * tile : 2 * tile + 1, :], (8, 128)
                )
            spread[t, 32:40, :] = jnp.where(
                iota((8, 128), 0) < 4, lifted[t, 8:9, :], lifted[t, 15:16, :]
            )

        def advance(p, carry):
            sol[p] = sol[p] + 0.4 * spread[(p + 7) // 8]
            return carry

        lax.fori_loop(0, PLANES[0] + 2, advance, 0, unroll=True)

        def defect(p, carry, cycle=cycle):
            applied = fine_apply(sol, p + 1, fine_coef[0], p + 4, 1)
            left = rhs[p] - applied[0:32, :]
            if cycle == 0:
                refs["R0"][p + 4, 0:32, :] = left
            else:
                residual[p] = left
                solution[p] = sol[p + 1, 0:32, :]
            return carry

        lax.fori_loop(0, PLANES[0], defect, 0, unroll=True)

    phases[1].finish(-2, None)


def scratch_shapes(ng):
    shapes = []
    for level in range(3):
        shapes.append(pltpu.VMEM((PLANES[level] + 10, ROWS[level] + 16, 128), F32))
    extents = [(PLANES[level] + 8, ROWS[level] + 8, 128) for level in range(3)]
    shapes += [pltpu.VMEM(extent, F32) for extent in extents]
    for extent in extents:
        shapes += [pltpu.VMEM(extent, F32)] * 5
    shapes += [pltpu.VMEM(extent, F32) for extent in extents]
    for extent in extents:
        shapes += [pltpu.VMEM(extent, F32)] * 3
    shapes += [pltpu.VMEM(extent, F32) for extent in extents]
    shapes += [
        pltpu.VMEM((4, 32, 128), F32),
        pltpu.VMEM((16, 128), F32),
        pltpu.VMEM((16, 128), F32),
        pltpu.VMEM((10, 40, 128), F32),
        pltpu.VMEM((6, 40, 128), F32),
        pltpu.VMEM((128, 128), BF16),
        pltpu.VMEM((512, 256), BF16),
        pltpu.VMEM((512, 128), BF16),
        pltpu.VMEM((24, 256), F32),
        pltpu.VMEM((4 * ng + 16, 128), F32),
        pltpu.VMEM((2 * ng + 16, 128), F32),
    ]
    for extent in ((24, 256), (4 * ng, 128), (2 * ng, 128)):
        shapes += [pltpu.VMEM(extent, F32)] * 5
    for with_density in (True, False):
        halo = buffer_shapes(with_density)
        shapes += halo + halo
        tiles = 10 if with_density else 6
        shapes += [
            pltpu.VMEM((1, 128), F32),
            pltpu.VMEM((ROW, 1, 128), F32),
            pltpu.VMEM((8, 8, 128), F32),
            pltpu.VMEM((8, tiles, 8, 128), F32),
        ]
        copies = n_halo(with_density) + 4
        shapes += [pltpu.SemaphoreType.DMA((copies,)), pltpu.SemaphoreType.DMA((copies,))]
    return shapes


def solution(mesh):
    nf, ns = mesh.shape["fine"], mesh.shape["sub"]

    def body(rhs, density):
        return pl.pallas_call(
            functools.partial(kernel, nf, ns),
            out_shape=(
                jax.ShapeDtypeStruct(rhs.shape, F32),
                jax.ShapeDtypeStruct(rhs.shape, F32),
            ),
            in_specs=[pl.BlockSpec(memory_space=pltpu.VMEM)] * 2,
            out_specs=[pl.BlockSpec(memory_space=pltpu.VMEM)] * 2,
            scratch_shapes=scratch_shapes(nf // ROW),
            compiler_params=pltpu.CompilerParams(
                collective_id=0, has_side_effects=True, vmem_limit_bytes=32 * 1024 * 1024
            ),
        )(rhs, density)

    return jax.shard_map(
        body,
        mesh=mesh,
        in_specs=(P("fine", "sub", None), P("fine", "sub", None)),
        out_specs=(P("fine", "sub", None), P("fine", "sub", None)),
        check_vma=False,
    )
```
